32 devices in a mesh: groups: 2 (over x), seq: 8 (over z, y), tp: 2 (over core).
Axes of the slice: x: 2, y: 2, z: 4, core: 2. Of those that a mesh axis runs over, the one named last changes fastest.
Arguments:
- queries: bfloat16 [16384, 4096], P(('groups', 'seq'), 'tp'), parts along dimension 0, may hold values from -6 to 6
- keys: bfloat16 [16384, 4096], P(('groups', 'seq'), 'tp'), parts along dimension 0, may hold values from -6 to 6
- values: bfloat16 [16384, 4096], P(('groups', 'seq'), 'tp'), parts along dimension 0, may hold values from -6 to 6
- log_decay: float32 [16384, 32], P(('groups', 'seq'), 'tp'), parts along dimension 0, may hold values from -1 to 0, as said below
- gate: bfloat16 [16384, 4096], P(('groups', 'seq'), 'tp'), parts along dimension 0, may hold values from -6 to 6
- gain: bfloat16 [4096], P('tp'), may hold values from 0.099609375 to 1.8984375
- doc_lengths: int32 [16], P('groups'), parts along dimension 0, may hold values from 1 to 4096, 8192 in all
- owner_ids: int32 [16], P('groups'), parts along dimension 0, may hold values from 0 to 7, each once
Outputs:
- mixed: bfloat16 [16384, 4096], P(('groups', 'seq'), 'tp'), parts along dimension 0
- owner_states: bfloat16 [16, 32, 128, 128], P(('groups', 'seq'), 'tp'), parts along dimension 0
The draws below stay inside these ranges and needn't reach their ends.
There are 2 independent parts, one for each index of `groups`. The reference program is written for one: setup_inputs(seed, part) draws one part's arguments, and reference() takes and returns one part's arrays. A program takes and returns all parts, laid end to end along the dimension named above; an argument that names none is the same for every part. Nothing has to cross between parts.
Inputs may be any that keep to these rules, and one draw needn't show every extreme that they name: `doc_lengths`: positive lengths summing to 8192; the longest prompt has exactly 4096 tokens. `owner_ids`: a permutation of the owner slots. `log_decay`: negative.
All inputs are finite; a program needn't handle non-finite values.
Results may differ from the reference program's by a relative error of at most 0.0049.
Values may be sent and summed in bfloat16 or wider, within the bound.
No kernel may reach another device: no remote copies, remote signals or barrier semaphores. Data moves between devices by JAX's collectives and lax.ppermute only.
A program may use at most 192 MiB of HBM per device.

```python
import math
import jax
import jax.numpy as jnp
import numpy as np
from jax import lax

HEAD_GROUP = 32
DH = 128
BLK = 512
TOK_DEV = 1024
PACKED_TOKENS = 8192
DOCS = 8


def draw_log_decay(key, part):
    key = jax.random.fold_in(key, 17)
    selected_items = jax.random.split(key, 7)
    span_count = PACKED_TOKENS // TOK_DEV
    slow_heads = jax.random.uniform(selected_items[0], (HEAD_GROUP,)) < 0.5
    slow_rate = jnp.exp(jax.random.uniform(selected_items[1], (HEAD_GROUP,), minval=jnp.log(0.2), maxval=jnp.log(1.5))) / PACKED_TOKENS
    fast_rate = jnp.exp(jax.random.uniform(selected_items[2], (HEAD_GROUP,), minval=jnp.log(1.0 / 400.0), maxval=jnp.log(1.0 / 30.0)))
    head_decay_rate = jnp.where(slow_heads, slow_rate, fast_rate)
    shard_multiplier = jnp.exp(jax.random.uniform(selected_items[3], (span_count, HEAD_GROUP), minval=-0.69, maxval=0.69))
    shard_multiplier = jnp.repeat(shard_multiplier, TOK_DEV, axis=0)
    jitter_level = jax.random.uniform(selected_items[4], (PACKED_TOKENS, HEAD_GROUP), minval=0.5, maxval=1.5)
    spike_events = jax.random.uniform(selected_items[5], (PACKED_TOKENS, HEAD_GROUP)) < 4.0 / PACKED_TOKENS
    spike_falloff = jnp.log(jax.random.uniform(selected_items[6], (PACKED_TOKENS, HEAD_GROUP), minval=0.5, maxval=0.8))
    final_output = -head_decay_rate[None, :] * shard_multiplier * jitter_level + jnp.where(spike_events, spike_falloff, 0.0)
    return final_output.astype(jnp.float32)


def steps_of(key, extent, cuts, smallest, largest):
    factor_of = 1.0
    for position, shards_of in cuts:
        draws = jax.random.uniform(jax.random.fold_in(jax.random.fold_in(key, 6), position), (shards_of,), jnp.float32, smallest / len(cuts), largest / len(cuts))
        factor_of = factor_of * jnp.repeat(jnp.exp(draws), extent[position] // shards_of).reshape((-1,) + (1,) * (len(extent) - 1 - position))
    return factor_of


def split_up(amount, total, limit, skew):
    portions = [(1 << 20) // math.isqrt(rank ** skew) + 1 for rank in range(2, amount + 1)]
    surplus, holding = total - limit - (amount - 1), [1] * (amount - 1)
    while surplus > 0:
        candidates = [i for i in range(amount - 1) if holding[i] < limit]
        whole, budget = sum([portions[i] for i in candidates]), surplus
        for i in candidates:
            extra = min(limit - holding[i], max(1, budget * portions[i] // whole), surplus)
            holding[i] = holding[i] + extra
            surplus = surplus - extra
    return np.array([limit] + holding)


def uneven(own_key, count, total, limit, slope):
    if count == 2:
        one = jax.random.randint(own_key, (), max(1, total - limit), min(limit, total - 1) + 1)
        return jnp.stack([one, total - one])
    tallies = jnp.asarray(split_up(count, total, limit, slope), jnp.int32)
    couples = (count - 1) // 2
    source_of, receiver = tallies[1:1 + 2 * couples:2], tallies[2:2 + 2 * couples:2]
    slack = jnp.minimum(source_of - 1, limit - receiver)
    passed = jax.random.randint(jax.random.fold_in(own_key, 1), (couples,), 0, 1 << 20) % (slack + 1)
    tallies = tallies.at[1:1 + 2 * couples:2].set(source_of - passed).at[2:2 + 2 * couples:2].set(receiver + passed)
    return tallies[jax.random.permutation(jax.random.fold_in(own_key, 2), count)]


def bell_draw(key, shape, deviation, limit, shards=(), kind=jnp.bfloat16):
    level = steps_of(key, shape, shards, -0.22, 0.18) if shards else 1.0
    result = jax.random.normal(key, shape, jnp.float32) * deviation * level
    return jnp.minimum(jnp.maximum(result, -limit), limit).astype(kind)


def setup_inputs(seed: int = 0, part: int = 0) -> dict:
    arg_keys = jax.random.split(jax.random.key(seed), 9)
    part_splits = jax.random.split(jax.random.fold_in(arg_keys[8], part), 9)
    return {
        "queries": bell_draw(part_splits[0], (PACKED_TOKENS, HEAD_GROUP * DH), 1.0, 6.0, ((0, 8), (1, 2))),
        "keys": bell_draw(part_splits[1], (PACKED_TOKENS, HEAD_GROUP * DH), 1.0, 6.0, ((0, 8), (1, 2))),
        "values": bell_draw(part_splits[2], (PACKED_TOKENS, HEAD_GROUP * DH), 1.0, 6.0, ((0, 8), (1, 2))),
        "log_decay": draw_log_decay(jax.random.fold_in(jax.random.fold_in(arg_keys[8], part), 71), part),
        "gate": bell_draw(part_splits[4], (PACKED_TOKENS, HEAD_GROUP * DH), 1.0, 6.0, ((0, 8), (1, 2))),
        "gain": jnp.clip(1.0 + 0.18 * jax.random.normal(arg_keys[5], (HEAD_GROUP * DH,), jnp.float32), 0.099609375, 1.8984375).astype(jnp.bfloat16),
        "doc_lengths": uneven(part_splits[6], DOCS, PACKED_TOKENS, PACKED_TOKENS // 2, 2).astype(jnp.int32),
        "owner_ids": jax.random.permutation(part_splits[7], DOCS).astype(jnp.int32),
    }


highest_prec = lax.Precision.HIGHEST

def segment_ids(doc_lengths, positions):
    doc_ends = jnp.cumsum(doc_lengths).astype(jnp.int32)
    return lax.optimization_barrier(jnp.sum((positions[:, None] >= doc_ends[None, :]).astype(jnp.int32), axis=1)).astype(jnp.int32)

def block_intra(query_part, key_part, value_part, decay_part, seg_part, key_scale):
    index_row = jnp.arange(seg_part.shape[0], dtype=jnp.int32)
    causal = (index_row[None, :] <= index_row[:, None]) & (seg_part[:, None] == seg_part[None, :])
    scores = jnp.einsum('ihd,jhd->hij', query_part.astype(jnp.float32), key_part.astype(jnp.float32), precision=highest_prec) * key_scale
    cum_heads = decay_part.T
    exponent = jnp.where(causal[None], cum_heads[:, :, None] - cum_heads[:, None, :], -1e+30)
    weights = lax.optimization_barrier((scores * jnp.exp(exponent)).astype(jnp.bfloat16)).astype(jnp.float32)
    return jnp.einsum('hij,jhd->ihd', weights, value_part.astype(jnp.float32), precision=highest_prec)

def block_inter(query_part, carried, decay_part, seg_part, prev_seg):
    keep_carry = (seg_part == prev_seg).astype(jnp.float32)
    carry_weight = jnp.exp(decay_part) * keep_carry[:, None]
    product = jnp.einsum('ihd,hde->ihe', query_part.astype(jnp.float32), carried, precision=highest_prec)
    return product * carry_weight[:, :, None]

def block_state(carried, key_part, value_part, decay_part, seg_part, prev_seg, key_scale):
    last_cum = decay_part[-1]
    same_doc = (seg_part == seg_part[-1]).astype(jnp.float32)
    weighted = key_part.astype(jnp.float32) * key_scale * jnp.exp(last_cum[None, :] - decay_part)[:, :, None] * same_doc[:, None, None]
    weighted = lax.optimization_barrier(weighted.astype(jnp.bfloat16)).astype(jnp.float32)
    no_reset = (seg_part[-1] == prev_seg).astype(jnp.float32)
    outer_sum = jnp.einsum('jhd,jhe->hde', weighted, value_part.astype(jnp.float32), precision=highest_prec)
    return (jnp.exp(last_cum) * no_reset)[:, None, None] * carried + outer_sum

def final_state(start_state, key_part, value_part, decay_part, seg_part, prev_seg, inner_index, doc_index, key_scale):
    index_row = jnp.arange(seg_part.shape[0], dtype=jnp.int32)
    end_decay = lax.dynamic_index_in_dim(decay_part, inner_index, 0, keepdims=False)
    taken = (index_row <= inner_index) & (seg_part == doc_index)
    exponent = jnp.where(taken[:, None], end_decay[None, :] - decay_part, -1e+30)
    weighted = key_part.astype(jnp.float32) * key_scale * jnp.exp(exponent)[:, :, None]
    weighted = lax.optimization_barrier(weighted.astype(jnp.bfloat16)).astype(jnp.float32)
    entry_rate = jnp.exp(end_decay) * jnp.where(prev_seg == doc_index, 1.0, 0.0)
    outer_sum = jnp.einsum('jhd,jhe->hde', weighted, value_part.astype(jnp.float32), precision=highest_prec)
    return (entry_rate[:, None, None] * start_state + outer_sum).astype(jnp.bfloat16)

def norm_gate(attended, gate, gain):
    count_rows = attended.shape[0]
    heads_here = attended.shape[1]
    square_mean = lax.optimization_barrier(jnp.mean(attended * attended, axis=-1, keepdims=True))
    gate_part = jax.nn.sigmoid(gate.reshape(count_rows, heads_here, -1).astype(jnp.float32))
    gain_part = gain.reshape(heads_here, -1).astype(jnp.float32)
    final_output = attended * lax.rsqrt(square_mean + 1e-06) * gain_part[None] * gate_part
    return final_output.reshape(count_rows, -1).astype(jnp.bfloat16)

def reference(queries, keys, values, log_decay, gate, gain, doc_lengths, owner_ids):
    key_scale = DH ** (-0.5)
    nblock = PACKED_TOKENS // BLK
    positions = jnp.arange(PACKED_TOKENS, dtype=jnp.int32)
    segment = segment_ids(doc_lengths, positions)
    segment_blk = segment.reshape(nblock, BLK)
    seg_before = jnp.concatenate([jnp.zeros((1,), jnp.int32), segment_blk[:-1, -1]]).astype(jnp.int32)
    query_blk = queries.reshape(nblock, BLK, HEAD_GROUP, DH)
    key_blk = keys.reshape(nblock, BLK, HEAD_GROUP, DH)
    value_blk = values.reshape(nblock, BLK, HEAD_GROUP, DH)
    cum_decay = jnp.cumsum(log_decay.reshape(nblock, BLK, HEAD_GROUP), axis=1)

    def advance(carried, inputs):
        query_part, key_part, value_part, decay_part, seg_part, prev_seg = inputs
        attended = block_intra(query_part, key_part, value_part, decay_part, seg_part, key_scale)
        attended = attended + block_inter(query_part, carried, decay_part, seg_part, prev_seg)
        updated = block_state(carried, key_part, value_part, decay_part, seg_part, prev_seg, key_scale)
        return (updated, (attended, carried))
    start_zero = jnp.zeros((HEAD_GROUP, DH, DH), jnp.float32)
    _, (attended, starts) = lax.scan(advance, start_zero, (query_blk, key_blk, value_blk, cum_decay, segment_blk, seg_before))
    mixed = norm_gate(attended.reshape(PACKED_TOKENS, HEAD_GROUP, DH), gate, gain)
    doc_ends = jnp.cumsum(doc_lengths).astype(jnp.int32)

    def finish(doc_index):
        end_pos = (doc_ends[doc_index] - 1).astype(jnp.int32)
        block_index = (end_pos // BLK).astype(jnp.int32)
        inner_index = (end_pos - block_index * BLK).astype(jnp.int32)

        def pick(source):
            return lax.dynamic_index_in_dim(source, block_index, 0, keepdims=False)
        return final_state(pick(starts), pick(key_blk), pick(value_blk), pick(cum_decay), pick(segment_blk), pick(seg_before), inner_index, doc_index, key_scale)
    finals = lax.map(finish, jnp.arange(DOCS, dtype=jnp.int32))
    owner_states = jnp.zeros_like(finals).at[owner_ids].set(finals)
    return (mixed, owner_states)
```

```python
import functools
import math

import jax
import jax.numpy as jnp
from jax import lax
from jax.experimental import pallas as pl
from jax.experimental.pallas import tpu as pltpu
from jax.sharding import PartitionSpec as P

BLK = 512
SIDE = 3
EXTRA = 16
NEG = -1e30
LOG2E = math.log2(math.e)
F32, BF16 = jnp.float32, jnp.bfloat16


def dot(a, b, contract=((1,), (0,))):
    return lax.dot_general(a, b, (contract, ((), ())), preferred_element_type=F32)


def iota(shape, dim):
    return lax.broadcasted_iota(jnp.int32, shape, dim)


def read_ends(len_ref, count):
    ends, total = [], jnp.int32(0)
    for d in range(count):
        total = total + len_ref[d]
        ends.append(total)
    return ends


def run_end(ends, pos):
    best = ends[-1]
    for e in reversed(ends[:-1]):
        best = jnp.where(e > pos, e, best)
    return best


def run_start(ends, pos):
    best = jnp.zeros_like(pos)
    for e in ends[:-1]:
        best = jnp.where(e <= pos, e, best)
    return best


def split3(x):
    hi = x.astype(BF16)
    rest = x - hi.astype(F32)
    mid = rest.astype(BF16)
    return hi, mid, (rest - mid.astype(F32)).astype(BF16)


def fill_cums(ld_ref, crow_ref, ccol_ref):
    heads, rows = ld_ref.shape
    upper = (iota((BLK, BLK), 0) <= iota((BLK, BLK), 1)).astype(F32).astype(BF16)
    lower = (iota((BLK, BLK), 0) >= iota((BLK, BLK), 1)).astype(F32).astype(BF16)
    base_row = jnp.zeros((heads, 1), F32)
    base_col = jnp.zeros((1, heads), F32)
    for b in range(rows // BLK):
        part = ld_ref[:, b * BLK : (b + 1) * BLK] * LOG2E
        row = jnp.zeros((heads, BLK), F32)
        col = jnp.zeros((BLK, heads), F32)
        for piece in reversed(split3(part)):
            row = row + dot(piece, upper)
            col = col + dot(lower, piece, ((1,), (1,)))
        row, col = row + base_row, col + base_col
        crow_ref[:, b * BLK : (b + 1) * BLK] = row
        ccol_ref[b * BLK : (b + 1) * BLK, :] = col
        base_row, base_col = row[:, BLK - 1 :], col[BLK - 1 :, :]


def pieces_kernel(scale, slots, by_owner, len_ref, own_ref, ld_ref, k_ref, v_ref, out_ref, *rest):
    heads, rows = ld_ref.shape
    count = len_ref.shape[0]
    if by_owner:
        crow_ref, ccol_ref, w_ref = rest
        first_ref = None
    else:
        crow_ref, ccol_ref, w_ref, first_ref = rest
    step = pl.program_id(0)
    hp = k_ref.shape[1] // 128

    @pl.when(step == 0)
    def _():
        fill_cums(ld_ref, crow_ref, ccol_ref)
        first = lax.axis_index("seq") * rows
        last = first + rows - 1
        ends = read_ends(len_ref, count)
        starts = [jnp.int32(0)] + ends[:-1]
        lows = [jnp.int32(0)] * slots
        highs = [jnp.int32(-1)] * slots
        place = jnp.int32(0)
        for d in range(count):
            here = (ends[d] > first) & (ends[d] <= last)
            low = jnp.maximum(starts[d] - first, 0)
            high = ends[d] - 1 - first
            for s in range(slots):
                if by_owner:
                    mine = here & (place >= SIDE) & (own_ref[d] == s)
                else:
                    mine = here & (place == s - 1)
                lows[s] = jnp.where(mine, low, lows[s])
                highs[s] = jnp.where(mine, high, highs[s])
            place = place + here.astype(jnp.int32)
        if not by_owner:
            lows[0] = jnp.maximum(run_start(ends, last) - first, 0)
            highs[0] = jnp.int32(rows - 1)
        at = iota((heads, rows), 1)
        cum = crow_ref[...]
        for s in range(slots):
            end_cum = jnp.sum(jnp.where(at == highs[s], cum, 0.0), axis=1, keepdims=True)
            inside = (at >= lows[s]) & (at <= highs[s])
            w_ref[s] = jnp.exp2(jnp.where(inside, end_cum - cum, NEG) + math.log2(scale))
        if not by_owner:
            stop = jnp.minimum(run_end(ends, first) - 1 - first, rows - 1)
            goes_on = (run_start(ends, first) < first).astype(F32)
            stop_cum = jnp.sum(jnp.where(at == stop, cum, 0.0), axis=1, keepdims=True)
            first_ref[...] = jnp.broadcast_to(jnp.exp2(stop_cum) * goes_on, (heads, 128))

    for i in range(hp):
        h = step * hp + i
        flipped = k_ref[:, i * 128 : (i + 1) * 128].astype(F32).T
        value = v_ref[:, i * 128 : (i + 1) * 128]
        for s in range(slots):
            weighted = (flipped * w_ref[s, pl.ds(h, 1), :]).astype(BF16)
            state = dot(weighted, value).astype(BF16)
            if by_owner:
                out_ref[s, i] = state
            else:
                at = (s * hp + i) * 128
                out_ref[0, at : at + 128, :] = state
    if not by_owner:
        rate = first_ref[pl.ds(step * hp, hp), :]
        high = rate.astype(BF16).astype(F32)
        pad = jnp.zeros((EXTRA // 2 - hp, 128), F32)
        tail = jnp.concatenate([high, pad, rate - high, pad], axis=0) if hp < EXTRA // 2 else jnp.concatenate([high, rate - high], axis=0)
        out_ref[0, slots * hp * 128 :, :] = tail.astype(BF16)


def piece_states(doc_lengths, owner_ids, decay_rows, keys, values, spread, slots, by_owner):
    heads, rows = decay_rows.shape
    hp = heads // spread
    whole = lambda shape: pl.BlockSpec(shape, lambda j: (0,) * len(shape))
    smem = pl.BlockSpec(memory_space=pltpu.SMEM)
    wide = pl.BlockSpec((rows, hp * 128), lambda j: (0, j))
    if by_owner:
        out = jax.ShapeDtypeStruct((slots, heads, 128, 128), BF16)
        out_spec = pl.BlockSpec((slots, hp, 128, 128), lambda j: (0, j, 0, 0))
    else:
        size = slots * hp * 128 + EXTRA
        out = jax.ShapeDtypeStruct((spread, size, 128), BF16)
        out_spec = pl.BlockSpec((1, size, 128), lambda j: (j, 0, 0))
    scratch = [pltpu.VMEM((slots, heads, rows), F32)]
    if not by_owner:
        scratch.append(pltpu.VMEM((heads, 128), F32))
    return pl.pallas_call(
        functools.partial(pieces_kernel, 128**-0.5, slots, by_owner),
        grid=(spread,),
        in_specs=[smem, smem, whole((heads, rows)), wide, wide],
        out_specs=[out_spec, whole((heads, rows)), whole((rows, heads))],
        out_shape=[
            out,
            jax.ShapeDtypeStruct((heads, rows), F32),
            jax.ShapeDtypeStruct((rows, heads), F32),
        ],
        scratch_shapes=scratch,
        compiler_params=pltpu.CompilerParams(vmem_limit_bytes=48 * 2**20),
        name="piece_states",
    )(doc_lengths, owner_ids, decay_rows, keys, values)


def head_column(ccol_ref, h):
    cols = ccol_ref[...]
    return jnp.sum(jnp.where(iota(cols.shape, 1) == h, cols, 0.0), axis=1, keepdims=True)


def blocks_kernel(scale, len_ref, q_ref, k_ref, v_ref, crow_ref, ccol_ref, out_ref, bias_ref):
    rows = q_ref.shape[0]
    count = len_ref.shape[0]
    step = pl.program_id(0)
    hb = q_ref.shape[1] // 128
    nblock = rows // BLK
    half = BLK // 2
    first = lax.axis_index("seq") * rows
    ends = read_ends(len_ref, count)

    @pl.when(step == 0)
    def _():
        for b in range(nblock):
            t_pos = first + b * BLK + iota((BLK, 1), 0)
            start = run_start(ends, t_pos)
            s_pos = first + b * BLK + iota((BLK, BLK), 1)
            keep = (s_pos <= t_pos) & (s_pos >= start)
            bias_ref[b * BLK : (b + 1) * BLK, :] = jnp.where(keep, math.log2(scale), NEG)

    for i in range(hb):
        h = step * hb + i
        col_all = head_column(ccol_ref, h)
        row_all = crow_ref[pl.ds(h, 1), :]
        lanes = slice(i * 128, (i + 1) * 128)
        carried = None
        for b in range(nblock):
            r0 = b * BLK
            key = k_ref[r0 : r0 + BLK, lanes]
            value = v_ref[r0 : r0 + BLK, lanes]
            if b > 0:
                before = first + r0 - 1
                reach = run_end(ends, before) - (first + r0)
                base = row_all[:, r0 - 1 : r0]
            for part in range(2):
                t0 = r0 + part * half
                width = (part + 1) * half
                query = q_ref[t0 : t0 + half, lanes]
                col = col_all[t0 : t0 + half]
                row = row_all[:, r0 : r0 + width]
                scores = dot(query, key[:width], ((1,), (1,)))
                decay = jnp.exp2((col - row) + bias_ref[t0 : t0 + half, :width])
                att = dot((scores * decay).astype(BF16), value[:width])
                if b > 0:
                    at = part * half + iota((half, 1), 0)
                    lead = jnp.exp2(jnp.where(at < reach, col - base, NEG))
                    att = att + lead * dot(query, carried_bf)
                out_ref[t0 : t0 + half, lanes] = att
            if b + 1 < nblock:
                last = first + r0 + BLK - 1
                since = run_start(ends, last) - (first + r0)
                row = row_all[:, r0 : r0 + BLK]
                total = row[:, BLK - 1 :]
                inside = iota((1, BLK), 1) >= since
                weight = jnp.exp2(jnp.where(inside, total - row, NEG) + math.log2(scale))
                weighted = (key.astype(F32).T * weight).astype(BF16)
                fresh = dot(weighted, value)
                if b > 0:
                    fresh = fresh + carried * jnp.exp2(jnp.where(BLK <= reach, total - base, NEG))
                carried = fresh
                carried_bf = carried.astype(BF16)


def block_attention(doc_lengths, queries, keys, values, crow, ccol):
    heads, rows = crow.shape
    hb = 2
    whole = lambda shape: pl.BlockSpec(shape, lambda j: (0,) * len(shape))
    wide = pl.BlockSpec((rows, hb * 128), lambda j: (0, j))
    return pl.pallas_call(
        functools.partial(blocks_kernel, 128**-0.5),
        grid=(heads // hb,),
        in_specs=[
            pl.BlockSpec(memory_space=pltpu.SMEM),
            wide,
            wide,
            wide,
            whole((heads, rows)),
            whole((rows, heads)),
        ],
        out_specs=wide,
        out_shape=jax.ShapeDtypeStruct((rows, heads * 128), F32),
        scratch_shapes=[pltpu.VMEM((rows, BLK), F32)],
        compiler_params=pltpu.CompilerParams(vmem_limit_bytes=48 * 2**20),
        cost_estimate=pl.CostEstimate(
            flops=heads * rows * BLK * 128 * 4, bytes_accessed=rows * heads * 128 * 10, transcendentals=heads * rows * BLK
        ),
        name="block_attention",
    )(doc_lengths, queries, keys, values, crow, ccol)


def scan_kernel(slots, rows, len_ref, own_ref, in_ref, enter_ref, final_ref, state_ref):
    spread, hp = enter_ref.shape[0], enter_ref.shape[1]
    count = len_ref.shape[0]
    ends = read_ends(len_ref, count)
    tail = slots * hp * 128

    def rate(e, i):
        extra = in_ref[e, tail:, :].astype(F32)
        return extra[i : i + 1, :] + extra[EXTRA // 2 + i : EXTRA // 2 + i + 1, :]

    def piece(e, s, i):
        return in_ref[e, pl.ds((s * hp + i) * 128, 128), :].astype(F32)

    for i in range(hp):
        state = jnp.zeros((128, 128), F32)
        for e in range(spread):
            state_ref[e, i] = state
            enter_ref[e, i] = state.astype(BF16)
            inner = jnp.int32(0)
            for d in range(count):
                inner = inner + ((ends[d] > e * rows) & (ends[d] < (e + 1) * rows)).astype(jnp.int32)
            passes = (inner == 0).astype(F32)
            state = state * (rate(e, i) * passes) + piece(e, 0, i)

    place, previous = jnp.int32(0), jnp.int32(-1)
    for d in range(count):
        device = (ends[d] - 1) // rows
        place = jnp.where(device == previous, place + 1, 0)
        previous = device
        at_end = ends[d] == (device + 1) * rows
        slot = jnp.where(at_end, 0, jnp.minimum(place, SIDE - 1) + 1)
        enters = (place == 0).astype(F32)
        for i in range(hp):
            start = pl.multiple_of((slot * hp + i) * 128, 128)
            local = in_ref[device, pl.ds(start, 128), :].astype(F32)
            state = local + state_ref[device, i] * (rate(device, i) * enters)
            final_ref[own_ref[d], i] = state.astype(BF16)


def scan_states(doc_lengths, owner_ids, parcels, slots, hp, rows):
    spread = parcels.shape[0]
    smem = pl.BlockSpec(memory_space=pltpu.SMEM)
    vmem = pl.BlockSpec(memory_space=pltpu.VMEM)
    shape = jax.ShapeDtypeStruct((spread, hp, 128, 128), BF16)
    return pl.pallas_call(
        functools.partial(scan_kernel, slots, rows),
        in_specs=[smem, smem, vmem],
        out_specs=[vmem, vmem],
        out_shape=[shape, shape],
        scratch_shapes=[pltpu.VMEM((spread, hp, 128, 128), F32)],
        compiler_params=pltpu.CompilerParams(vmem_limit_bytes=48 * 2**20),
        name="scan_states",
    )(doc_lengths, owner_ids, parcels)


def mix_kernel(len_ref, q_ref, enter_ref, local_ref, gate_ref, gain_ref, ccol_ref, out_ref):
    rows = q_ref.shape[0]
    step = pl.program_id(0)
    hb = q_ref.shape[1] // 128
    first = lax.axis_index("seq") * rows
    reach = run_end(read_ends(len_ref, len_ref.shape[0]), first - 1) - first
    at = iota((rows, 1), 0)
    for i in range(hb):
        lanes = slice(i * 128, (i + 1) * 128)
        col = head_column(ccol_ref, step * hb + i)
        lead = jnp.exp2(jnp.where(at < reach, col, NEG))
        att = local_ref[:, lanes] + lead * dot(q_ref[:, lanes], enter_ref[i])
        mean = jnp.mean(att * att, axis=1, keepdims=True)
        gate = 1.0 / (1.0 + jnp.exp(-gate_ref[:, lanes].astype(F32)))
        gain = gain_ref[:, lanes].astype(F32)
        out_ref[:, lanes] = (att * lax.rsqrt(mean + 1e-06) * gain * gate).astype(BF16)


def mix(doc_lengths, queries, entering, local, gate, gain, ccol):
    rows, heads = ccol.shape
    hb = 2
    wide = pl.BlockSpec((rows, hb * 128), lambda j: (0, j))
    return pl.pallas_call(
        mix_kernel,
        grid=(heads // hb,),
        in_specs=[
            pl.BlockSpec(memory_space=pltpu.SMEM),
            wide,
            pl.BlockSpec((hb, 128, 128), lambda j: (j, 0, 0)),
            wide,
            wide,
            pl.BlockSpec((1, hb * 128), lambda j: (0, j)),
            pl.BlockSpec((rows, heads), lambda j: (0, 0)),
        ],
        out_specs=wide,
        out_shape=jax.ShapeDtypeStruct((rows, heads * 128), BF16),
        compiler_params=pltpu.CompilerParams(vmem_limit_bytes=48 * 2**20),
        cost_estimate=pl.CostEstimate(
            flops=rows * heads * 128 * 256, bytes_accessed=rows * heads * 128 * 10, transcendentals=rows * heads * 128
        ),
        name="mix",
    )(doc_lengths, queries, entering, local, gate, gain.reshape(1, -1), ccol)


def swap(x):
    return lax.all_to_all(x, "seq", split_axis=0, concat_axis=0, tiled=True)


def crowded(doc_lengths, spread, rows, groups):
    count = doc_lengths.shape[0]
    index = jnp.arange(count, dtype=jnp.int32)
    ends = jnp.sum(jnp.where(index[None, :] <= index[:, None], doc_lengths[None, :], 0), axis=1)
    inner = (ends[None, :] // rows == jnp.arange(spread, dtype=jnp.int32)[:, None]) & (ends % rows != 0)[None, :]
    over = (jnp.max(jnp.sum(inner.astype(F32), axis=1)) > SIDE).astype(F32).reshape(1)
    seen = over
    for shift in range(1, groups):
        seen = seen + lax.ppermute(over, "groups", [(g, (g + shift) % groups) for g in range(groups)])
    return seen[0] > 0


def on_device(spread, groups, queries, keys, values, log_decay, gate, gain, doc_lengths, owner_ids):
    rows, heads = log_decay.shape
    hp = heads // spread
    slots = SIDE + 1
    decay_rows = log_decay.T
    over = crowded(doc_lengths, spread, rows, groups)
    parcels, crow, ccol = piece_states(doc_lengths, owner_ids, decay_rows, keys, values, spread, slots, False)
    parcels = swap(parcels)
    local = block_attention(doc_lengths, queries, keys, values, crow, ccol)
    entering, finals = scan_states(doc_lengths, owner_ids, parcels, slots, hp, rows)
    entering = swap(entering).reshape(heads, 128, 128)
    entering, finals = lax.optimization_barrier((entering, finals))
    owned = swap(finals).reshape(1, heads, 128, 128)
    mixed = mix(doc_lengths, queries, entering, local, gate, gain, ccol)

    def send_rest(owned):
        rest, _, _ = piece_states(doc_lengths, owner_ids, decay_rows, keys, values, spread, spread, True)
        rest = swap(rest)
        me = lax.axis_index("seq")
        index = jnp.arange(owner_ids.shape[0], dtype=jnp.int32)
        ends = jnp.cumsum(doc_lengths)
        doc = jnp.sum(jnp.where(owner_ids == me, index, 0))
        source = (ends - 1) // rows
        mine = source[doc]
        ahead = jnp.sum(((source == mine) & (index < doc)).astype(jnp.int32))
        late = (ahead >= SIDE) & (ends[doc] % rows != 0)
        return jnp.where(late, lax.dynamic_index_in_dim(rest, mine, 0, True), owned)

    owned = lax.cond(over, send_rest, lambda owned: owned, owned)
    return mixed, owned


def solution(mesh):
    placed = (
        P(("groups", "seq"), "tp"),
        P(("groups", "seq"), "tp"),
        P(("groups", "seq"), "tp"),
        P(("groups", "seq"), "tp"),
        P(("groups", "seq"), "tp"),
        P("tp"),
        P("groups"),
        P("groups"),
    )
    return jax.shard_map(
        functools.partial(on_device, mesh.shape["seq"], mesh.shape["groups"]),
        mesh=mesh,
        in_specs=placed,
        out_specs=(P(("groups", "seq"), "tp"), P(("groups", "seq"), "tp", None, None)),
        check_vma=False,
    )
```

```python
import functools
import math

import jax
import jax.numpy as jnp
from jax import lax
from jax.experimental import pallas as pl
from jax.experimental.pallas import tpu as pltpu
from jax.sharding import PartitionSpec as P

BLK = 512
SIDE = 3
EXTRA = 16
NEG = -1e30
LOG2E = math.log2(math.e)
SCALE = 128**-0.5
F32, BF16 = jnp.float32, jnp.bfloat16
SMEM = pl.BlockSpec(memory_space=pltpu.SMEM)
VMEM = pl.BlockSpec(memory_space=pltpu.VMEM)
LIMIT = pltpu.CompilerParams(vmem_limit_bytes=48 * 2**20)


def dot(a, b, contract=((1,), (0,))):
    return lax.dot_general(a, b, (contract, ((), ())), preferred_element_type=F32)


def iota(shape, dim):
    return lax.broadcasted_iota(jnp.int32, shape, dim)


def read_ends(len_ref, count):
    ends, total = [], jnp.int32(0)
    for d in range(count):
        total = total + len_ref[d]
        ends.append(total)
    return ends


def run_end(ends, pos):
    best = ends[-1]
    for e in reversed(ends[:-1]):
        best = jnp.where(e > pos, e, best)
    return best


def run_start(ends, pos):
    best = jnp.zeros_like(pos)
    for e in ends[:-1]:
        best = jnp.where(e <= pos, e, best)
    return best


def split3(x):
    hi = x.astype(BF16)
    rest = x - hi.astype(F32)
    mid = rest.astype(BF16)
    return hi, mid, (rest - mid.astype(F32)).astype(BF16)


def cum_rows(ld_ref, crow_ref):
    heads, rows = ld_ref.shape
    upper = (iota((BLK, BLK), 0) <= iota((BLK, BLK), 1)).astype(F32).astype(BF16)
    base = jnp.zeros((heads, 1), F32)
    for b in range(rows // BLK):
        part = ld_ref[:, b * BLK : (b + 1) * BLK] * LOG2E
        row = jnp.zeros((heads, BLK), F32)
        for piece in reversed(split3(part)):
            row = row + dot(piece, upper)
        row = row + base
        crow_ref[:, b * BLK : (b + 1) * BLK] = row
        base = row[:, BLK - 1 :]


def value_at(cum, at, index):
    return jnp.sum(jnp.where(at == index, cum, 0.0), axis=1, keepdims=True)


def span_weights(cum, at, low, high):
    inside = (at >= low) & (at <= high)
    return jnp.exp2(jnp.where(inside, value_at(cum, at, high) - cum, NEG) + math.log2(SCALE))


def last_kernel(len_ref, ld_ref, k_ref, v_ref, out_ref, crow_ref, w_ref, first_ref):
    heads, rows = ld_ref.shape
    step = pl.program_id(0)
    hp = k_ref.shape[1] // 128

    @pl.when(step == 0)
    def _():
        cum_rows(ld_ref, crow_ref)
        first = lax.axis_index("seq") * rows
        ends = read_ends(len_ref, len_ref.shape[0])
        at = iota((heads, rows), 1)
        cum = crow_ref[...]
        low = jnp.maximum(run_start(ends, first + rows - 1) - first, 0)
        w_ref[...] = span_weights(cum, at, low, rows - 1)
        stop = jnp.minimum(run_end(ends, first) - 1 - first, rows - 1)
        goes_on = (run_start(ends, first) < first).astype(F32)
        first_ref[...] = jnp.broadcast_to(jnp.exp2(value_at(cum, at, stop)) * goes_on, (heads, 128))

    for i in range(hp):
        lanes = slice(i * 128, (i + 1) * 128)
        flipped = k_ref[:, lanes].T.astype(F32)
        weighted = (flipped * w_ref[pl.ds(step * hp + i, 1), :]).astype(BF16)
        out_ref[0, lanes, :] = dot(weighted, v_ref[:, lanes]).astype(BF16)
    rate = first_ref[pl.ds(step * hp, hp), :]
    high = rate.astype(BF16).astype(F32)
    pad = jnp.zeros((EXTRA - 2 * hp, 128), F32)
    out_ref[0, hp * 128 :, :] = jnp.concatenate([high, rate - high, pad], axis=0).astype(BF16)


def whole(shape):
    return pl.BlockSpec(shape, lambda j: (0,) * len(shape))


def last_pieces(doc_lengths, decay_rows, keys, values, members):
    heads, rows = decay_rows.shape
    hp = heads // members
    wide = pl.BlockSpec((rows, hp * 128), lambda j: (0, j))
    size = hp * 128 + EXTRA
    return pl.pallas_call(
        last_kernel,
        grid=(members,),
        in_specs=[SMEM, whole((heads, rows)), wide, wide],
        out_specs=[pl.BlockSpec((1, size, 128), lambda j: (j, 0, 0)), whole((heads, rows))],
        out_shape=[
            jax.ShapeDtypeStruct((members, size, 128), BF16),
            jax.ShapeDtypeStruct((heads, rows), F32),
        ],
        scratch_shapes=[pltpu.VMEM((heads, rows), F32), pltpu.VMEM((heads, 128), F32)],
        compiler_params=LIMIT,
        cost_estimate=pl.CostEstimate(
            flops=heads * rows * 128 * 256, bytes_accessed=rows * heads * 128 * 4, transcendentals=heads * rows
        ),
        name="last_pieces",
    )(doc_lengths, decay_rows, keys, values)


def side_kernel(slots, by_owner, len_ref, own_ref, ld_ref, crow_ref, k_ref, v_ref, out_ref, ccol_ref, w_ref):
    heads, rows = crow_ref.shape
    step = pl.program_id(0)
    hp = k_ref.shape[1] // 128

    @pl.when(step == 0)
    def _():
        lower = (iota((BLK, BLK), 0) >= iota((BLK, BLK), 1)).astype(F32).astype(BF16)
        base = jnp.zeros((1, heads), F32)
        for b in range(rows // BLK):
            part = ld_ref[:, b * BLK : (b + 1) * BLK] * LOG2E
            col = jnp.zeros((BLK, heads), F32)
            for piece in reversed(split3(part)):
                col = col + dot(lower, piece, ((1,), (1,)))
            col = col + base
            ccol_ref[b * BLK : (b + 1) * BLK, :] = col
            base = col[BLK - 1 :, :]
        first = lax.axis_index("seq") * rows
        last = first + rows - 1
        ends = read_ends(len_ref, len_ref.shape[0])
        starts = [jnp.int32(0)] + ends[:-1]
        lows = [jnp.int32(0)] * slots
        highs = [jnp.int32(-1)] * slots
        place = jnp.int32(0)
        for d in range(len(ends)):
            here = (ends[d] > first) & (ends[d] <= last)
            low = jnp.maximum(starts[d] - first, 0)
            for s in range(slots):
                mine = here & ((place >= SIDE) & (own_ref[d] == s) if by_owner else (place == s))
                lows[s] = jnp.where(mine, low, lows[s])
                highs[s] = jnp.where(mine, ends[d] - 1 - first, highs[s])
            place = place + here.astype(jnp.int32)
        at = iota((heads, rows), 1)
        cum = crow_ref[...]
        for s in range(slots):
            w_ref[s] = span_weights(cum, at, lows[s], highs[s])

    for i in range(hp):
        lanes = slice(i * 128, (i + 1) * 128)
        flipped = k_ref[:, lanes].T.astype(F32)
        for s in range(slots):
            weighted = (flipped * w_ref[s, pl.ds(step * hp + i, 1), :]).astype(BF16)
            state = dot(weighted, v_ref[:, lanes]).astype(BF16)
            if by_owner:
                out_ref[s, i] = state
            else:
                at = (s * hp + i) * 128
                out_ref[0, at : at + 128, :] = state


def side_pieces(doc_lengths, owner_ids, decay_rows, crow, keys, values, members, slots, by_owner):
    heads, rows = crow.shape
    hp = heads // members
    wide = pl.BlockSpec((rows, hp * 128), lambda j: (0, j))
    if by_owner:
        out = jax.ShapeDtypeStruct((slots, heads, 128, 128), BF16)
        out_spec = pl.BlockSpec((slots, hp, 128, 128), lambda j: (0, j, 0, 0))
    else:
        out = jax.ShapeDtypeStruct((members, slots * hp * 128, 128), BF16)
        out_spec = pl.BlockSpec((1, slots * hp * 128, 128), lambda j: (j, 0, 0))
    return pl.pallas_call(
        functools.partial(side_kernel, slots, by_owner),
        grid=(members,),
        in_specs=[SMEM, SMEM, whole((heads, rows)), whole((heads, rows)), wide, wide],
        out_specs=[out_spec, whole((rows, heads))],
        out_shape=[out, jax.ShapeDtypeStruct((rows, heads), F32)],
        scratch_shapes=[pltpu.VMEM((slots, heads, rows), F32)],
        compiler_params=LIMIT,
        cost_estimate=pl.CostEstimate(
            flops=slots * heads * rows * 128 * 256, bytes_accessed=rows * heads * 128 * 4, transcendentals=heads * rows
        ),
        name="side_pieces",
    )(doc_lengths, owner_ids, decay_rows, crow, keys, values)


def head_column(ccol_ref, h):
    cols = ccol_ref[...]
    return jnp.sum(jnp.where(iota(cols.shape, 1) == h, cols, 0.0), axis=1, keepdims=True)


def blocks_kernel(len_ref, q_ref, k_ref, v_ref, crow_ref, ccol_ref, out_ref, bias_ref):
    rows = q_ref.shape[0]
    count = len_ref.shape[0]
    step = pl.program_id(0)
    hb = q_ref.shape[1] // 128
    nblock = rows // BLK
    half = BLK // 2
    first = lax.axis_index("seq") * rows
    ends = read_ends(len_ref, count)

    @pl.when(step == 0)
    def _():
        for b in range(nblock):
            t_pos = first + b * BLK + iota((BLK, 1), 0)
            start = run_start(ends, t_pos)
            s_pos = first + b * BLK + iota((BLK, BLK), 1)
            keep = (s_pos <= t_pos) & (s_pos >= start)
            bias_ref[b * BLK : (b + 1) * BLK, :] = jnp.where(keep, math.log2(SCALE), NEG)

    for i in range(hb):
        h = step * hb + i
        col_all = head_column(ccol_ref, h)
        row_all = crow_ref[pl.ds(h, 1), :]
        lanes = slice(i * 128, (i + 1) * 128)
        carried = None
        for b in range(nblock):
            r0 = b * BLK
            key = k_ref[r0 : r0 + BLK, lanes]
            value = v_ref[r0 : r0 + BLK, lanes]
            if b > 0:
                before = first + r0 - 1
                reach = run_end(ends, before) - (first + r0)
                base = row_all[:, r0 - 1 : r0]
            for part in range(2):
                t0 = r0 + part * half
                width = (part + 1) * half
                query = q_ref[t0 : t0 + half, lanes]
                col = col_all[t0 : t0 + half]
                row = row_all[:, r0 : r0 + width]
                scores = dot(query, key[:width], ((1,), (1,)))
                decay = jnp.exp2((col - row) + bias_ref[t0 : t0 + half, :width])
                att = dot((scores * decay).astype(BF16), value[:width])
                if b > 0:
                    at = part * half + iota((half, 1), 0)
                    lead = jnp.exp2(jnp.where(at < reach, col - base, NEG))
                    att = att + lead * dot(query, carried_bf)
                out_ref[t0 : t0 + half, lanes] = att
            if b + 1 < nblock:
                last = first + r0 + BLK - 1
                since = run_start(ends, last) - (first + r0)
                row = row_all[:, r0 : r0 + BLK]
                total = row[:, BLK - 1 :]
                inside = iota((1, BLK), 1) >= since
                weight = jnp.exp2(jnp.where(inside, total - row, NEG) + math.log2(SCALE))
                weighted = (key.astype(F32).T * weight).astype(BF16)
                fresh = dot(weighted, value)
                if b > 0:
                    fresh = fresh + carried * jnp.exp2(jnp.where(BLK <= reach, total - base, NEG))
                carried = fresh
                carried_bf = carried.astype(BF16)


def block_attention(doc_lengths, queries, keys, values, crow, ccol):
    heads, rows = crow.shape
    hb = 2
    wide = pl.BlockSpec((rows, hb * 128), lambda j: (0, j))
    return pl.pallas_call(
        blocks_kernel,
        grid=(heads // hb,),
        in_specs=[
            SMEM,
            wide,
            wide,
            wide,
            whole((heads, rows)),
            whole((rows, heads)),
        ],
        out_specs=wide,
        out_shape=jax.ShapeDtypeStruct((rows, heads * 128), F32),
        scratch_shapes=[pltpu.VMEM((rows, BLK), F32)],
        compiler_params=LIMIT,
        cost_estimate=pl.CostEstimate(
            flops=heads * rows * BLK * 128 * 4, bytes_accessed=rows * heads * 128 * 10, transcendentals=heads * rows * BLK
        ),
        name="block_attention",
    )(doc_lengths, queries, keys, values, crow, ccol)


def decay_of(last_ref, e, i, hp):
    extra = last_ref[e, hp * 128 :, :].astype(F32)
    return extra[i : i + 1, :] + extra[hp + i : hp + i + 1, :]


def scan_quad(rows, len_ref, last_ref, state, i, hp, note):
    members = last_ref.shape[0]
    ends = read_ends(len_ref, len_ref.shape[0])
    base = lax.axis_index("seq") // members * members
    for e in range(members):
        note(e, state)
        low = (base + e) * rows
        inner = jnp.int32(0)
        for end in ends:
            inner = inner + ((end > low) & (end < low + rows)).astype(jnp.int32)
        passes = (inner == 0).astype(F32)
        piece = last_ref[e, i * 128 : (i + 1) * 128, :].astype(F32)
        state = state * (decay_of(last_ref, e, i, hp) * passes) + piece
    return state


def leave_kernel(rows, len_ref, last_ref, in_ref, out_ref):
    hp = in_ref.shape[0]
    for i in range(hp):
        state = scan_quad(rows, len_ref, last_ref, in_ref[i].astype(F32), i, hp, lambda e, x: None)
        out_ref[i] = state.astype(BF16)


def leave_quad(doc_lengths, last, coming, rows):
    return pl.pallas_call(
        functools.partial(leave_kernel, rows),
        in_specs=[SMEM, VMEM, VMEM],
        out_specs=VMEM,
        out_shape=jax.ShapeDtypeStruct(coming.shape, BF16),
        compiler_params=LIMIT,
        name="leave_quad",
    )(doc_lengths, last, coming)


def enter_kernel(rows, len_ref, last_ref, in_ref, out_ref):
    hp = in_ref.shape[0]

    def note(i, e, state):
        out_ref[e, i] = state.astype(BF16)

    for i in range(hp):
        scan_quad(rows, len_ref, last_ref, in_ref[i].astype(F32), i, hp, functools.partial(note, i))


def enter_states(doc_lengths, last, coming, rows):
    return pl.pallas_call(
        functools.partial(enter_kernel, rows),
        in_specs=[SMEM, VMEM, VMEM],
        out_specs=VMEM,
        out_shape=jax.ShapeDtypeStruct((last.shape[0],) + coming.shape, BF16),
        compiler_params=LIMIT,
        name="enter_states",
    )(doc_lengths, last, coming)


def final_kernel(rows, len_ref, own_ref, last_ref, side_ref, in_ref, out_ref, state_ref):
    hp = in_ref.shape[0]
    members = last_ref.shape[0]
    ends = read_ends(len_ref, len_ref.shape[0])
    base = lax.axis_index("seq") // members * members

    def note(i, e, state):
        state_ref[e, i] = state

    for i in range(hp):
        scan_quad(rows, len_ref, last_ref, in_ref[i].astype(F32), i, hp, functools.partial(note, i))
    out_ref[...] = jnp.zeros_like(out_ref)
    place, previous = jnp.int32(0), jnp.int32(-1)
    for d in range(len(ends)):
        device = (ends[d] - 1) // rows
        place = jnp.where(device == previous, place + 1, 0)
        previous = device
        at_end = ends[d] == (device + 1) * rows
        enters = (place == 0).astype(F32)
        mine = device // members * members == base
        e = device - base

        def put(i, local):
            state = local.astype(F32) + state_ref[e, i] * (decay_of(last_ref, e, i, hp) * enters)
            out_ref[own_ref[d], i] = state.astype(BF16)

        @pl.when(mine & at_end)
        def _():
            for i in range(hp):
                put(i, last_ref[e, i * 128 : (i + 1) * 128, :])

        @pl.when(mine & jnp.logical_not(at_end))
        def _():
            for i in range(hp):
                row = pl.multiple_of((jnp.minimum(place, SIDE - 1) * hp + i) * 128, 128)
                put(i, side_ref[e, pl.ds(row, 128), :])


def final_states(doc_lengths, owner_ids, last, side, coming, rows, spread):
    return pl.pallas_call(
        functools.partial(final_kernel, rows),
        in_specs=[SMEM, SMEM, VMEM, VMEM, VMEM],
        out_specs=VMEM,
        out_shape=jax.ShapeDtypeStruct((spread,) + coming.shape, BF16),
        scratch_shapes=[pltpu.VMEM((last.shape[0],) + coming.shape, F32)],
        compiler_params=LIMIT,
        name="final_states",
    )(doc_lengths, owner_ids, last, side, coming)


def mix_kernel(len_ref, q_ref, enter_ref, local_ref, gate_ref, gain_ref, ccol_ref, out_ref):
    rows = q_ref.shape[0]
    step = pl.program_id(0)
    hb = q_ref.shape[1] // 128
    first = lax.axis_index("seq") * rows
    reach = run_end(read_ends(len_ref, len_ref.shape[0]), first - 1) - first
    at = iota((rows, 1), 0)
    for i in range(hb):
        lanes = slice(i * 128, (i + 1) * 128)
        col = head_column(ccol_ref, step * hb + i)
        lead = jnp.exp2(jnp.where(at < reach, col, NEG))
        att = local_ref[:, lanes] + lead * dot(q_ref[:, lanes], enter_ref[i])
        mean = jnp.mean(att * att, axis=1, keepdims=True)
        gate = 1.0 / (1.0 + jnp.exp(-gate_ref[:, lanes].astype(F32)))
        gain = gain_ref[:, lanes].astype(F32)
        out_ref[:, lanes] = (att * lax.rsqrt(mean + 1e-06) * gain * gate).astype(BF16)


def mix(doc_lengths, queries, entering, local, gate, gain, ccol):
    rows, heads = ccol.shape
    hb = 2
    wide = pl.BlockSpec((rows, hb * 128), lambda j: (0, j))
    return pl.pallas_call(
        mix_kernel,
        grid=(heads // hb,),
        in_specs=[
            SMEM,
            wide,
            pl.BlockSpec((hb, 128, 128), lambda j: (j, 0, 0)),
            wide,
            wide,
            pl.BlockSpec((1, hb * 128), lambda j: (0, j)),
            pl.BlockSpec((rows, heads), lambda j: (0, 0)),
        ],
        out_specs=wide,
        out_shape=jax.ShapeDtypeStruct((rows, heads * 128), BF16),
        compiler_params=LIMIT,
        cost_estimate=pl.CostEstimate(
            flops=rows * heads * 128 * 256, bytes_accessed=rows * heads * 128 * 10, transcendentals=rows * heads * 128
        ),
        name="mix",
    )(doc_lengths, queries, entering, local, gate, gain.reshape(1, -1), ccol)


def swap(x, groups=None):
    return lax.all_to_all(x, "seq", split_axis=0, concat_axis=0, axis_index_groups=groups, tiled=True)


def crowded(doc_lengths, spread, rows, groups):
    count = doc_lengths.shape[0]
    index = jnp.arange(count, dtype=jnp.int32)
    ends = jnp.sum(jnp.where(index[None, :] <= index[:, None], doc_lengths[None, :], 0), axis=1)
    inner = (ends[None, :] // rows == jnp.arange(spread, dtype=jnp.int32)[:, None]) & (ends % rows != 0)[None, :]
    over = (jnp.max(jnp.sum(inner.astype(F32), axis=1)) > SIDE).astype(F32).reshape(1)
    seen = over
    for shift in range(1, groups):
        seen = seen + lax.ppermute(over, "groups", [(g, (g + shift) % groups) for g in range(groups)])
    return seen[0] > 0


def own_final(doc_lengths, owner_ids, rows):
    index = jnp.arange(owner_ids.shape[0], dtype=jnp.int32)
    ends = jnp.sum(jnp.where(index[None, :] <= index[:, None], doc_lengths[None, :], 0), axis=1)
    mine = owner_ids == lax.axis_index("seq")
    source = (ends - 1) // rows
    device = jnp.sum(jnp.where(mine, source, 0))
    doc = jnp.sum(jnp.where(mine, index, 0))
    ahead = jnp.sum(((source == device) & (index < doc)).astype(jnp.int32))
    inner = jnp.sum(jnp.where(mine, ends, 0)) != (device + 1) * rows
    return device, (ahead >= SIDE) & inner


def on_device(spread, groups, queries, keys, values, log_decay, gate, gain, doc_lengths, owner_ids):
    rows, heads = log_decay.shape
    members = 4
    quads = spread // members
    hp = heads // members
    near = [[q * members + m for m in range(members)] for q in range(quads)]
    onward = [(s, s + members) for s in range(spread - members)]
    decay_rows = log_decay.T

    last, crow = last_pieces(doc_lengths, decay_rows, keys, values, members)
    last = swap(last, near)
    side, ccol = side_pieces(doc_lengths, owner_ids, decay_rows, crow, keys, values, members, SIDE, False)
    last, side = lax.optimization_barrier((last, side))
    side = swap(side, near)

    coming = jnp.zeros((hp, 128, 128), BF16)
    for _ in range(quads - 1):
        leaving = leave_quad(doc_lengths, last, coming, rows)
        coming = lax.ppermute(leaving, "seq", onward)
    crow_after, _ = lax.optimization_barrier((crow, leaving))
    local = block_attention(doc_lengths, queries, keys, values, crow_after, ccol)
    over = crowded(doc_lengths, spread, rows, groups)
    device, late = own_final(doc_lengths, owner_ids, rows)
    coming, local, over, device, late = lax.optimization_barrier((coming, local, over, device, late))

    entering = swap(enter_states(doc_lengths, last, coming, rows), near).reshape(heads, 128, 128)
    finals = final_states(doc_lengths, owner_ids, last, side, coming, rows, spread)
    entering, finals = lax.optimization_barrier((entering, finals))
    owned = swap(finals).reshape(quads, heads, 128, 128)
    mixed = mix(doc_lengths, queries, entering, local, gate, gain, ccol)
    owned = lax.dynamic_index_in_dim(owned, device // members, 0, True)

    def send_rest(owned):
        rest, _ = side_pieces(doc_lengths, owner_ids, decay_rows, crow, keys, values, heads, spread, True)
        rest = swap(rest)
        return jnp.where(late, lax.dynamic_index_in_dim(rest, device, 0, True), owned)

    owned = lax.cond(over, send_rest, lambda owned: owned, owned)
    return mixed, owned


def solution(mesh):
    placed = (
        P(("groups", "seq"), "tp"),
        P(("groups", "seq"), "tp"),
        P(("groups", "seq"), "tp"),
        P(("groups", "seq"), "tp"),
        P(("groups", "seq"), "tp"),
        P("tp"),
        P("groups"),
        P("groups"),
    )
    return jax.shard_map(
        functools.partial(on_device, mesh.shape["seq"], mesh.shape["groups"]),
        mesh=mesh,
        in_specs=placed,
        out_specs=(P(("groups", "seq"), "tp"), P(("groups", "seq"), "tp", None, None)),
        check_vma=False,
    )
```

```python
import functools
import math

import jax
import jax.numpy as jnp
from jax import lax
from jax.experimental import pallas as pl
from jax.experimental.pallas import tpu as pltpu
from jax.sharding import PartitionSpec as P

BLK = 512
SIDE = 3
EXTRA = 16
CHUNK = 256
EARLY = 6
NEG = -1e30
LOG2E = math.log2(math.e)
SCALE = 128**-0.5
F32, BF16 = jnp.float32, jnp.bfloat16
SMEM = pl.BlockSpec(memory_space=pltpu.SMEM)
VMEM = pl.BlockSpec(memory_space=pltpu.VMEM)
LIMIT = pltpu.CompilerParams(vmem_limit_bytes=60 * 2**20)


def dot(a, b, contract=((1,), (0,))):
    return lax.dot_general(a, b, (contract, ((), ())), preferred_element_type=F32)


def iota(shape, dim):
    return lax.broadcasted_iota(jnp.int32, shape, dim)


def read_ends(len_ref, count):
    ends, total = [], jnp.int32(0)
    for d in range(count):
        total = total + len_ref[d]
        ends.append(total)
    return ends


def run_end(ends, pos):
    best = ends[-1]
    for e in reversed(ends[:-1]):
        best = jnp.where(e > pos, e, best)
    return best


def run_start(ends, pos):
    best = jnp.zeros_like(pos)
    for e in ends[:-1]:
        best = jnp.where(e <= pos, e, best)
    return best


def split3(x):
    hi = x.astype(BF16)
    rest = x - hi.astype(F32)
    mid = rest.astype(BF16)
    return hi, mid, (rest - mid.astype(F32)).astype(BF16)


def cum_rows(ld_ref, crow_ref):
    heads, rows = ld_ref.shape
    upper = (iota((BLK, BLK), 0) <= iota((BLK, BLK), 1)).astype(F32).astype(BF16)
    base = jnp.zeros((heads, 1), F32)
    for b in range(rows // BLK):
        part = ld_ref[:, b * BLK : (b + 1) * BLK] * LOG2E
        sums = dot(jnp.concatenate(split3(part), axis=0), upper)
        row = sums[2 * heads :] + sums[heads : 2 * heads] + sums[:heads] + base
        crow_ref[:, b * BLK : (b + 1) * BLK] = row
        base = row[:, BLK - 1 :]


def value_at(cum, at, index):
    return jnp.sum(jnp.where(at == index, cum, 0.0), axis=1, keepdims=True)


def span_weights(cum, at, low, high):
    inside = (at >= low) & (at <= high)
    return jnp.exp2(jnp.where(inside, value_at(cum, at, high) - cum, NEG) + math.log2(SCALE))


def weigh(keys, w_ref, h):
    flipped = keys.T.astype(F32)
    weights = [jnp.broadcast_to(w_ref[pl.ds(h + j, 1), :], (128, keys.shape[0])) for j in range(2)]
    return (flipped * jnp.concatenate(weights, axis=0)).astype(BF16)


def last_kernel(len_ref, ld_ref, k_ref, v_ref, out_ref, crow_ref, w_ref, first_ref):
    heads, rows = ld_ref.shape
    step = pl.program_id(0)
    hp = k_ref.shape[1] // 128

    @pl.when(step == 0)
    def _():
        cum_rows(ld_ref, crow_ref)
        first = lax.axis_index("seq") * rows
        ends = read_ends(len_ref, len_ref.shape[0])
        at = iota((heads, rows), 1)
        cum = crow_ref[...]
        low = jnp.maximum(run_start(ends, first + rows - 1) - first, 0)
        w_ref[...] = span_weights(cum, at, low, rows - 1)
        stop = jnp.minimum(run_end(ends, first) - 1 - first, rows - 1)
        goes_on = (run_start(ends, first) < first).astype(F32)
        first_ref[...] = jnp.broadcast_to(jnp.exp2(value_at(cum, at, stop)) * goes_on, (heads, 128))

    for i in range(0, hp, 2):
        lanes = slice(i * 128, (i + 2) * 128)
        states = dot(weigh(k_ref[:, lanes], w_ref, step * hp + i), v_ref[:, lanes])
        out_ref[0, i * 128 : (i + 1) * 128, :] = states[:128, :128].astype(BF16)
        out_ref[0, (i + 1) * 128 : (i + 2) * 128, :] = states[128:, 128:].astype(BF16)
    rate = first_ref[pl.ds(step * hp, hp), :]
    high = rate.astype(BF16).astype(F32)
    pad = jnp.zeros((EXTRA - 2 * hp, 128), F32)
    out_ref[0, hp * 128 :, :] = jnp.concatenate([high, rate - high, pad], axis=0).astype(BF16)


def whole(shape):
    return pl.BlockSpec(shape, lambda j: (0,) * len(shape))


def last_pieces(doc_lengths, decay_rows, keys, values, members):
    heads, rows = decay_rows.shape
    hp = heads // members
    wide = pl.BlockSpec((rows, hp * 128), lambda j: (0, j))
    size = hp * 128 + EXTRA
    return pl.pallas_call(
        last_kernel,
        grid=(members,),
        in_specs=[SMEM, whole((heads, rows)), wide, wide],
        out_specs=[pl.BlockSpec((1, size, 128), lambda j: (j, 0, 0)), whole((heads, rows))],
        out_shape=[
            jax.ShapeDtypeStruct((members, size, 128), BF16),
            jax.ShapeDtypeStruct((heads, rows), F32),
        ],
        scratch_shapes=[pltpu.VMEM((heads, rows), F32), pltpu.VMEM((heads, 128), F32)],
        compiler_params=LIMIT,
        cost_estimate=pl.CostEstimate(
            flops=heads * rows * 128 * 256, bytes_accessed=rows * heads * 128 * 4, transcendentals=heads * rows
        ),
        name="last_pieces",
    )(doc_lengths, decay_rows, keys, values)


def side_kernel(slots, by_owner, len_ref, own_ref, ld_ref, crow_ref, k_ref, v_ref, out_ref, ccol_ref, flag_ref, w_ref, keep_ref):
    heads, rows = crow_ref.shape
    step = pl.program_id(0)
    hp = k_ref.shape[1] // 128

    @pl.when(step == 0)
    def _():
        lower = (iota((BLK, BLK), 0) >= iota((BLK, BLK), 1)).astype(F32).astype(BF16)
        base = jnp.zeros((1, heads), F32)
        for b in range(rows // BLK):
            part = ld_ref[:, b * BLK : (b + 1) * BLK] * LOG2E
            col = jnp.zeros((BLK, heads), F32)
            for piece in reversed(split3(part)):
                col = col + dot(lower, piece, ((1,), (1,)))
            col = col + base
            ccol_ref[b * BLK : (b + 1) * BLK, :] = col
            base = col[BLK - 1 :, :]
        me = lax.axis_index("seq")
        first = me * rows
        last = first + rows - 1
        ends = read_ends(len_ref, len_ref.shape[0])
        starts = [jnp.int32(0)] + ends[:-1]
        lows = [jnp.int32(0)] * slots
        highs = [jnp.int32(-1)] * slots
        place, rank, previous = jnp.int32(0), jnp.int32(0), jnp.int32(-1)
        crowded, owned_in, owned_late = jnp.int32(0), jnp.int32(0), jnp.int32(0)
        for d in range(len(ends)):
            here = (ends[d] > first) & (ends[d] <= last)
            low = jnp.maximum(starts[d] - first, 0)
            for s in range(slots):
                mine = here & ((place >= SIDE) & (own_ref[d] == s) if by_owner else (place == s))
                lows[s] = jnp.where(mine, low, lows[s])
                highs[s] = jnp.where(mine, ends[d] - 1 - first, highs[s])
            place = place + here.astype(jnp.int32)
            device = (ends[d] - 1) // rows
            rank = jnp.where(device == previous, rank + 1, 0)
            previous = device
            late = ((rank >= SIDE) & (ends[d] != (device + 1) * rows)).astype(jnp.int32)
            crowded = jnp.maximum(crowded, late)
            owned_in = jnp.where(own_ref[d] == me, device, owned_in)
            owned_late = jnp.where(own_ref[d] == me, late, owned_late)
        flag_ref[0] = owned_in
        flag_ref[1] = owned_late
        flag_ref[2] = crowded
        at = iota((heads, rows), 1)
        cum = crow_ref[...]
        row_at = iota((16, rows), 1)
        total = jnp.zeros((heads, rows), F32)
        for s in range(slots):
            total = total + span_weights(cum, at, lows[s], highs[s])
            inside = (row_at >= lows[s]) & (row_at <= highs[s])
            keep_ref[s] = jnp.where(inside, 1.0, 0.0).astype(BF16)
        w_ref[...] = total

    for i in range(0, hp, 2):
        lanes = slice(i * 128, (i + 2) * 128)
        weighted = weigh(k_ref[:, lanes], w_ref, step * hp + i).reshape(16, 16, rows)
        for s in range(slots):
            kept = (weighted * keep_ref[s][None]).reshape(256, rows)
            states = dot(kept, v_ref[:, lanes])
            for j in range(2):
                state = states[j * 128 : (j + 1) * 128, j * 128 : (j + 1) * 128].astype(BF16)
                if by_owner:
                    out_ref[s, i + j] = state
                else:
                    at = (s * hp + i + j) * 128
                    out_ref[0, at : at + 128, :] = state


def side_pieces(doc_lengths, owner_ids, decay_rows, crow, keys, values, members, slots, by_owner):
    heads, rows = crow.shape
    hp = heads // members
    wide = pl.BlockSpec((rows, hp * 128), lambda j: (0, j))
    if by_owner:
        out = jax.ShapeDtypeStruct((slots, heads, 128, 128), BF16)
        out_spec = pl.BlockSpec((slots, hp, 128, 128), lambda j: (0, j, 0, 0))
    else:
        out = jax.ShapeDtypeStruct((members, slots * hp * 128, 128), BF16)
        out_spec = pl.BlockSpec((1, slots * hp * 128, 128), lambda j: (j, 0, 0))
    return pl.pallas_call(
        functools.partial(side_kernel, slots, by_owner),
        grid=(members,),
        in_specs=[SMEM, SMEM, whole((heads, rows)), whole((heads, rows)), wide, wide],
        out_specs=[out_spec, whole((rows, heads)), SMEM],
        out_shape=[out, jax.ShapeDtypeStruct((rows, heads), F32), jax.ShapeDtypeStruct((4,), jnp.int32)],
        scratch_shapes=[pltpu.VMEM((heads, rows), F32), pltpu.VMEM((slots, 16, rows), BF16)],
        compiler_params=LIMIT,
        cost_estimate=pl.CostEstimate(
            flops=slots * heads * rows * 128 * 256, bytes_accessed=rows * heads * 128 * 4, transcendentals=heads * rows
        ),
        name="side_pieces",
    )(doc_lengths, owner_ids, decay_rows, crow, keys, values)


def head_column(ccol_ref, h):
    cols = ccol_ref[...]
    return jnp.sum(jnp.where(iota(cols.shape, 1) == h, cols, 0.0), axis=1, keepdims=True)


def fill_bias(first, ends, bias_ref):
    for c in range(bias_ref.shape[0] // CHUNK):
        base = first + c * CHUNK
        t_pos = base + iota((CHUNK, 1), 0)
        start = run_start(ends, t_pos)
        s_pos = base + iota((CHUNK, CHUNK), 1)
        keep = (s_pos <= t_pos) & (s_pos >= start)
        bias_ref[c * CHUNK : (c + 1) * CHUNK, :] = jnp.where(keep, math.log2(SCALE), NEG)


def attend(first, ends, q_ref, k_ref, v_ref, lanes, row_all, col_all, bias_ref, state, emit):
    rows = q_ref.shape[0]
    half = CHUNK // 2
    for c in range(rows // CHUNK):
        r0 = c * CHUNK
        key = k_ref[r0 : r0 + CHUNK, lanes]
        value = v_ref[r0 : r0 + CHUNK, lanes]
        row = row_all[:, r0 : r0 + CHUNK]
        base = row_all[:, r0 - 1 : r0] if c else jnp.zeros((1, 1), F32)
        reach = run_end(ends, first + r0 - 1) - (first + r0)
        state_bf = None if state is None else state.astype(BF16)
        for part in range(2):
            t0 = r0 + part * half
            width = (part + 1) * half
            query = q_ref[t0 : t0 + half, lanes]
            col = col_all[t0 : t0 + half]
            scores = dot(query, key[:width], ((1,), (1,)))
            decay = jnp.exp2((col - row[:, :width]) + bias_ref[t0 : t0 + half, :width])
            att = dot((scores * decay).astype(BF16), value[:width])
            if state is not None:
                at = part * half + iota((half, 1), 0)
                lead = jnp.exp2(jnp.where(at < reach, col - base, NEG))
                att = att + lead * dot(query, state_bf)
            emit(t0, half, att)
        if r0 + CHUNK < rows:
            since = run_start(ends, first + r0 + CHUNK - 1) - (first + r0)
            total = row[:, CHUNK - 1 :]
            inside = iota((1, CHUNK), 1) >= since
            weight = jnp.exp2(jnp.where(inside, total - row, NEG) + math.log2(SCALE))
            fresh = dot((key.T.astype(F32) * weight).astype(BF16), value)
            if state is not None:
                fresh = fresh + state * jnp.exp2(jnp.where(CHUNK <= reach, total - base, NEG))
            state = fresh


def early_kernel(len_ref, q_ref, k_ref, v_ref, crow_ref, ccol_ref, out_ref, bias_ref):
    rows = q_ref.shape[0]
    step = pl.program_id(0)
    first = lax.axis_index("seq") * rows
    ends = read_ends(len_ref, len_ref.shape[0])

    @pl.when(step == 0)
    def _():
        fill_bias(first, ends, bias_ref)

    for i in range(2):
        h = step * 2 + i
        lanes = slice(i * 128, (i + 1) * 128)

        def emit(t0, size, att):
            out_ref[t0 : t0 + size, lanes] = att

        attend(
            first, ends, q_ref, k_ref, v_ref, lanes, crow_ref[pl.ds(h, 1), :], head_column(ccol_ref, h), bias_ref, None, emit
        )


def early_attention(doc_lengths, queries, keys, values, crow, ccol):
    heads, rows = crow.shape
    wide = pl.BlockSpec((rows, 256), lambda j: (0, j))
    return pl.pallas_call(
        early_kernel,
        grid=(EARLY // 2,),
        in_specs=[SMEM, wide, wide, wide, whole((heads, rows)), whole((rows, heads))],
        out_specs=wide,
        out_shape=jax.ShapeDtypeStruct((rows, EARLY * 128), F32),
        scratch_shapes=[pltpu.VMEM((rows, CHUNK), F32)],
        compiler_params=LIMIT,
        cost_estimate=pl.CostEstimate(
            flops=EARLY * rows * CHUNK * 128 * 8, bytes_accessed=rows * EARLY * 128 * 10, transcendentals=EARLY * rows * CHUNK
        ),
        name="early_attention",
    )(doc_lengths, queries, keys, values, crow, ccol)


def decay_of(last_ref, e, i, hp):
    extra = last_ref[e, hp * 128 :, :].astype(F32)
    return extra[i : i + 1, :] + extra[hp + i : hp + i + 1, :]


def scan_quad(rows, len_ref, last_ref, state, i, hp, note):
    members = last_ref.shape[0]
    ends = read_ends(len_ref, len_ref.shape[0])
    base = lax.axis_index("seq") // members * members
    for e in range(members):
        note(e, state)
        low = (base + e) * rows
        inner = jnp.int32(0)
        for end in ends:
            inner = inner + ((end > low) & (end < low + rows)).astype(jnp.int32)
        passes = (inner == 0).astype(F32)
        piece = last_ref[e, i * 128 : (i + 1) * 128, :].astype(F32)
        state = state * (decay_of(last_ref, e, i, hp) * passes) + piece
    return state


def leave_kernel(rows, len_ref, last_ref, in_ref, out_ref):
    hp = in_ref.shape[0]
    for i in range(hp):
        state = scan_quad(rows, len_ref, last_ref, in_ref[i].astype(F32), i, hp, lambda e, x: None)
        out_ref[i] = state.astype(BF16)


def leave_quad(doc_lengths, last, coming, rows):
    return pl.pallas_call(
        functools.partial(leave_kernel, rows),
        in_specs=[SMEM, VMEM, VMEM],
        out_specs=VMEM,
        out_shape=jax.ShapeDtypeStruct(coming.shape, BF16),
        compiler_params=LIMIT,
        name="leave_quad",
    )(doc_lengths, last, coming)


def enter_kernel(rows, len_ref, last_ref, in_ref, out_ref):
    hp = in_ref.shape[0]

    def note(i, e, state):
        out_ref[e, i] = state.astype(BF16)

    for i in range(hp):
        scan_quad(rows, len_ref, last_ref, in_ref[i].astype(F32), i, hp, functools.partial(note, i))


def enter_states(doc_lengths, last, coming, rows):
    return pl.pallas_call(
        functools.partial(enter_kernel, rows),
        in_specs=[SMEM, VMEM, VMEM],
        out_specs=VMEM,
        out_shape=jax.ShapeDtypeStruct((last.shape[0],) + coming.shape, BF16),
        compiler_params=LIMIT,
        name="enter_states",
    )(doc_lengths, last, coming)


def final_kernel(rows, len_ref, own_ref, last_ref, side_ref, in_ref, out_ref, state_ref):
    hp = in_ref.shape[0]
    members = last_ref.shape[0]
    ends = read_ends(len_ref, len_ref.shape[0])
    base = lax.axis_index("seq") // members * members

    def note(i, e, state):
        state_ref[e, i] = state

    for i in range(hp):
        scan_quad(rows, len_ref, last_ref, in_ref[i].astype(F32), i, hp, functools.partial(note, i))
    out_ref[...] = jnp.zeros_like(out_ref)
    place, previous = jnp.int32(0), jnp.int32(-1)
    for d in range(len(ends)):
        device = (ends[d] - 1) // rows
        place = jnp.where(device == previous, place + 1, 0)
        previous = device
        at_end = ends[d] == (device + 1) * rows
        enters = (place == 0).astype(F32)
        mine = device // members * members == base
        e = device - base

        def put(i, local):
            state = local.astype(F32) + state_ref[e, i] * (decay_of(last_ref, e, i, hp) * enters)
            out_ref[own_ref[d], i] = state.astype(BF16)

        @pl.when(mine & at_end)
        def _():
            for i in range(hp):
                put(i, last_ref[e, i * 128 : (i + 1) * 128, :])

        @pl.when(mine & jnp.logical_not(at_end))
        def _():
            for i in range(hp):
                row = pl.multiple_of((jnp.minimum(place, SIDE - 1) * hp + i) * 128, 128)
                put(i, side_ref[e, pl.ds(row, 128), :])


def final_states(doc_lengths, owner_ids, last, side, coming, rows, spread):
    return pl.pallas_call(
        functools.partial(final_kernel, rows),
        in_specs=[SMEM, SMEM, VMEM, VMEM, VMEM],
        out_specs=VMEM,
        out_shape=jax.ShapeDtypeStruct((spread,) + coming.shape, BF16),
        scratch_shapes=[pltpu.VMEM((last.shape[0],) + coming.shape, F32)],
        compiler_params=LIMIT,
        name="final_states",
    )(doc_lengths, owner_ids, last, side, coming)


def finish_kernel(
    len_ref, q_ref, k_ref, v_ref, enter_ref, local_ref, gate_ref, gain_ref, crow_ref, ccol_ref, out_ref, bias_ref
):
    rows = q_ref.shape[0]
    step = pl.program_id(0)
    first = lax.axis_index("seq") * rows
    ends = read_ends(len_ref, len_ref.shape[0])

    def emit(lanes, t0, size, att):
        mean = jnp.mean(att * att, axis=1, keepdims=True)
        gate = 1.0 / (1.0 + jnp.exp(-gate_ref[t0 : t0 + size, lanes].astype(F32)))
        gain = gain_ref[:, lanes].astype(F32)
        out_ref[t0 : t0 + size, lanes] = (att * lax.rsqrt(mean + 1e-06) * gain * gate).astype(BF16)

    @pl.when(step == 0)
    def _():
        fill_bias(first, ends, bias_ref)

    @pl.when(step < EARLY // 2)
    def _():
        reach = run_end(ends, first - 1) - first
        for i in range(2):
            lanes = slice(i * 128, (i + 1) * 128)
            col_all = head_column(ccol_ref, step * 2 + i)
            for t0 in range(0, rows, CHUNK):
                at = t0 + iota((CHUNK, 1), 0)
                lead = jnp.exp2(jnp.where(at < reach, col_all[t0 : t0 + CHUNK], NEG))
                carry = dot(q_ref[t0 : t0 + CHUNK, lanes], enter_ref[i])
                emit(lanes, t0, CHUNK, local_ref[t0 : t0 + CHUNK, lanes] + lead * carry)

    @pl.when(step >= EARLY // 2)
    def _():
        for i in range(2):
            h = step * 2 + i
            lanes = slice(i * 128, (i + 1) * 128)
            row_all, col_all = crow_ref[pl.ds(h, 1), :], head_column(ccol_ref, h)
            state = enter_ref[i].astype(F32)
            attend(
                first, ends, q_ref, k_ref, v_ref, lanes, row_all, col_all, bias_ref, state, functools.partial(emit, lanes)
            )


def finish(doc_lengths, queries, keys, values, entering, local, gate, gain, crow, ccol):
    heads, rows = crow.shape
    pairs = EARLY // 2
    wide = pl.BlockSpec((rows, 256), lambda j: (0, j))
    late = pl.BlockSpec((rows, 256), lambda j: (0, jnp.maximum(j, pairs)))
    return pl.pallas_call(
        finish_kernel,
        grid=(heads // 2,),
        in_specs=[
            SMEM,
            wide,
            late,
            late,
            pl.BlockSpec((2, 128, 128), lambda j: (j, 0, 0)),
            pl.BlockSpec((rows, 256), lambda j: (0, jnp.minimum(j, pairs - 1))),
            wide,
            pl.BlockSpec((1, 256), lambda j: (0, j)),
            whole((heads, rows)),
            whole((rows, heads)),
        ],
        out_specs=wide,
        out_shape=jax.ShapeDtypeStruct((rows, heads * 128), BF16),
        scratch_shapes=[pltpu.VMEM((rows, CHUNK), F32)],
        compiler_params=LIMIT,
        cost_estimate=pl.CostEstimate(
            flops=heads * rows * CHUNK * 128 * 8, bytes_accessed=rows * heads * 128 * 10, transcendentals=heads * rows * CHUNK
        ),
        name="finish",
    )(doc_lengths, queries, keys, values, entering, local, gate, gain.reshape(1, -1), crow, ccol)


def pick_kernel(quad_ref, late_ref, in_ref, rest_ref, out_ref):
    out_ref[...] = in_ref[...]

    @pl.when(late_ref[0] > 0)
    def _():
        out_ref[...] = rest_ref[...]


def pick_owned(quad, late, arrived, rest):
    shape = rest.shape
    block = lambda index: pl.BlockSpec(shape, index)
    return pl.pallas_call(
        pick_kernel,
        grid_spec=pltpu.PrefetchScalarGridSpec(
            num_scalar_prefetch=2,
            grid=(1,),
            in_specs=[block(lambda j, quad, late: (quad[0], 0, 0, 0)), block(lambda j, quad, late: (0, 0, 0, 0))],
            out_specs=block(lambda j, quad, late: (0, 0, 0, 0)),
        ),
        out_shape=jax.ShapeDtypeStruct(shape, BF16),
        compiler_params=LIMIT,
        name="pick_owned",
    )(quad, late, arrived, rest)


def swap(x, groups=None):
    return lax.all_to_all(x, "seq", split_axis=0, concat_axis=0, axis_index_groups=groups, tiled=True)


def on_device(spread, queries, keys, values, log_decay, gate, gain, doc_lengths, owner_ids):
    rows, heads = log_decay.shape
    members = 4
    quads = spread // members
    hp = heads // members
    near = [[q * members + m for m in range(members)] for q in range(quads)]
    onward = [(s, s + members) for s in range(spread - members)]
    decay_rows = log_decay.T

    last, crow = last_pieces(doc_lengths, decay_rows, keys, values, members)
    last = swap(last, near)
    side, ccol, flags = side_pieces(doc_lengths, owner_ids, decay_rows, crow, keys, values, members, SIDE, False)
    last, side = lax.optimization_barrier((last, side))
    side = swap(side, near)

    coming = jnp.zeros((hp, 128, 128), BF16)
    for _ in range(quads - 1):
        leaving = leave_quad(doc_lengths, last, coming, rows)
        coming = lax.ppermute(leaving, "seq", onward)
    crow_after, _ = lax.optimization_barrier((crow, leaving))
    local = early_attention(doc_lengths, queries, keys, values, crow_after, ccol)

    def send_rest():
        rest, _, _ = side_pieces(
            doc_lengths, owner_ids, decay_rows, crow_after, keys, values, heads // 2, spread, True
        )
        return lax.dynamic_index_in_dim(swap(rest), flags[0], 0, True)

    rest = lax.cond(flags[2] > 0, send_rest, lambda: jnp.zeros((1, heads, 128, 128), BF16))
    coming, local, rest = lax.optimization_barrier((coming, local, rest))

    entering = swap(enter_states(doc_lengths, last, coming, rows), near).reshape(heads, 128, 128)
    finals = final_states(doc_lengths, owner_ids, last, side, coming, rows, spread)
    arrived = swap(finals).reshape(quads, heads, 128, 128)
    entering, _ = lax.optimization_barrier((entering, finals))
    mixed = finish(doc_lengths, queries, keys, values, entering, local, gate, gain, crow, ccol)
    owned = pick_owned((flags[0] // members).reshape(1), flags[1].reshape(1), arrived, rest)
    return mixed, owned


def solution(mesh):
    placed = (
        P(("groups", "seq"), "tp"),
        P(("groups", "seq"), "tp"),
        P(("groups", "seq"), "tp"),
        P(("groups", "seq"), "tp"),
        P(("groups", "seq"), "tp"),
        P("tp"),
        P("groups"),
        P("groups"),
    )
    return jax.shard_map(
        functools.partial(on_device, mesh.shape["seq"]),
        mesh=mesh,
        in_specs=placed,
        out_specs=(P(("groups", "seq"), "tp"), P(("groups", "seq"), "tp", None, None)),
        check_vma=False,
    )
```

```python
import functools
import math

import jax
import jax.numpy as jnp
from jax import lax
from jax.experimental import pallas as pl
from jax.experimental.pallas import tpu as pltpu
from jax.sharding import PartitionSpec as P

BLK = 512
SIDE = 3
EXTRA = 16
CHUNK = 128
MEMBERS = 4
EARLY = 4
NEG = -1e30
LOG2E = math.log2(math.e)
SCALE = 128**-0.5
F32, BF16 = jnp.float32, jnp.bfloat16
SMEM = pl.BlockSpec(memory_space=pltpu.SMEM)
VMEM = pl.BlockSpec(memory_space=pltpu.VMEM)
LIMIT = pltpu.CompilerParams(vmem_limit_bytes=60 * 2**20)
SMALL = pltpu.CompilerParams(vmem_limit_bytes=48 * 2**20)


def dot(a, b, contract=((1,), (0,))):
    return lax.dot_general(a, b, (contract, ((), ())), preferred_element_type=F32)


def iota(shape, dim):
    return lax.broadcasted_iota(jnp.int32, shape, dim)


def read_ends(len_ref, count):
    ends, total = [], jnp.int32(0)
    for d in range(count):
        total = total + len_ref[d]
        ends.append(total)
    return ends


def run_end(ends, pos):
    best = ends[-1]
    for e in reversed(ends[:-1]):
        best = jnp.where(e > pos, e, best)
    return best


def run_start(ends, pos):
    best = jnp.zeros_like(pos)
    for e in ends[:-1]:
        best = jnp.where(e <= pos, e, best)
    return best


def split3(x):
    hi = x.astype(BF16)
    rest = x - hi.astype(F32)
    mid = rest.astype(BF16)
    return hi, mid, (rest - mid.astype(F32)).astype(BF16)


def cum_rows(ld_ref, crow_ref):
    heads, rows = ld_ref.shape
    upper = (iota((BLK, BLK), 0) <= iota((BLK, BLK), 1)).astype(F32).astype(BF16)
    base = jnp.zeros((heads, 1), F32)
    for b in range(rows // BLK):
        part = ld_ref[:, b * BLK : (b + 1) * BLK] * LOG2E
        sums = dot(jnp.concatenate(split3(part), axis=0), upper)
        row = sums[2 * heads :] + sums[heads : 2 * heads] + sums[:heads] + base
        crow_ref[:, b * BLK : (b + 1) * BLK] = row
        base = row[:, BLK - 1 :]


def value_at(cum, at, index):
    return jnp.sum(jnp.where(at == index, cum, 0.0), axis=1, keepdims=True)


def span_weights(cum, at, low, high):
    inside = (at >= low) & (at <= high)
    return jnp.exp2(jnp.where(inside, value_at(cum, at, high) - cum, NEG) + math.log2(SCALE))


def weigh(flipped, w_ref, h):
    weights = [jnp.broadcast_to(w_ref[pl.ds(h + j, 1), :], (128, flipped.shape[1])) for j in range(2)]
    return (flipped.astype(F32) * jnp.concatenate(weights, axis=0)).astype(BF16)


def last_kernel(len_ref, ld_ref, k_ref, v_ref, out_ref, crow_ref, kt_ref, w_ref, first_ref):
    heads, rows = ld_ref.shape
    step = pl.program_id(0)
    hp = k_ref.shape[1] // 128

    @pl.when(step == 0)
    def _():
        cum_rows(ld_ref, crow_ref)
        first = lax.axis_index("seq") * rows
        ends = read_ends(len_ref, len_ref.shape[0])
        at = iota((heads, rows), 1)
        cum = crow_ref[...]
        low = jnp.maximum(run_start(ends, first + rows - 1) - first, 0)
        w_ref[...] = span_weights(cum, at, low, rows - 1)
        stop = jnp.minimum(run_end(ends, first) - 1 - first, rows - 1)
        goes_on = (run_start(ends, first) < first).astype(F32)
        first_ref[...] = jnp.broadcast_to(jnp.exp2(value_at(cum, at, stop)) * goes_on, (heads, 128))

    for i in range(0, hp, 2):
        lanes = slice(i * 128, (i + 2) * 128)
        flipped = k_ref[:, lanes].T
        kt_ref[lanes, :] = flipped
        states = dot(weigh(flipped, w_ref, step * hp + i), v_ref[:, lanes])
        out_ref[0, i * 128 : (i + 1) * 128, :] = states[:128, :128].astype(BF16)
        out_ref[0, (i + 1) * 128 : (i + 2) * 128, :] = states[128:, 128:].astype(BF16)
    rate = first_ref[pl.ds(step * hp, hp), :]
    high = rate.astype(BF16).astype(F32)
    pad = jnp.zeros((EXTRA - 2 * hp, 128), F32)
    out_ref[0, hp * 128 :, :] = jnp.concatenate([high, rate - high, pad], axis=0).astype(BF16)


def whole(shape):
    return pl.BlockSpec(shape, lambda j: (0,) * len(shape))


def last_pieces(doc_lengths, decay_rows, keys, values, members):
    heads, rows = decay_rows.shape
    hp = heads // members
    wide = pl.BlockSpec((rows, hp * 128), lambda j: (0, j))
    size = hp * 128 + EXTRA
    return pl.pallas_call(
        last_kernel,
        grid=(members,),
        in_specs=[SMEM, whole((heads, rows)), wide, wide],
        out_specs=[
            pl.BlockSpec((1, size, 128), lambda j: (j, 0, 0)),
            whole((heads, rows)),
            pl.BlockSpec((hp * 128, rows), lambda j: (j, 0)),
        ],
        out_shape=[
            jax.ShapeDtypeStruct((members, size, 128), BF16),
            jax.ShapeDtypeStruct((heads, rows), F32),
            jax.ShapeDtypeStruct((heads * 128, rows), BF16),
        ],
        scratch_shapes=[pltpu.VMEM((heads, rows), F32), pltpu.VMEM((heads, 128), F32)],
        compiler_params=LIMIT,
        cost_estimate=pl.CostEstimate(
            flops=heads * rows * 128 * 256, bytes_accessed=rows * heads * 128 * 6, transcendentals=heads * rows
        ),
        name="last_pieces",
    )(doc_lengths, decay_rows, keys, values)


def side_kernel(slots, by_owner, len_ref, own_ref, ld_ref, crow_ref, kt_ref, v_ref, out_ref, ccol_ref, flag_ref, w_ref, keep_ref):
    heads, rows = crow_ref.shape
    step = pl.program_id(0)
    hp = v_ref.shape[1] // 128

    @pl.when(step == 0)
    def _():
        lower = (iota((BLK, BLK), 0) >= iota((BLK, BLK), 1)).astype(F32).astype(BF16)
        base = jnp.zeros((1, heads), F32)
        for b in range(rows // BLK):
            part = ld_ref[:, b * BLK : (b + 1) * BLK] * LOG2E
            col = jnp.zeros((BLK, heads), F32)
            for piece in reversed(split3(part)):
                col = col + dot(lower, piece, ((1,), (1,)))
            col = col + base
            ccol_ref[b * BLK : (b + 1) * BLK, :] = col
            base = col[BLK - 1 :, :]
        me = lax.axis_index("seq")
        first = me * rows
        last = first + rows - 1
        ends = read_ends(len_ref, len_ref.shape[0])
        starts = [jnp.int32(0)] + ends[:-1]
        lows = [jnp.int32(0)] * slots
        highs = [jnp.int32(-1)] * slots
        place, rank, previous = jnp.int32(0), jnp.int32(0), jnp.int32(-1)
        crowded, owned_in, owned_late = jnp.int32(0), jnp.int32(0), jnp.int32(0)
        for d in range(len(ends)):
            here = (ends[d] > first) & (ends[d] <= last)
            low = jnp.maximum(starts[d] - first, 0)
            for s in range(slots):
                mine = here & ((place >= SIDE) & (own_ref[d] == s) if by_owner else (place == s))
                lows[s] = jnp.where(mine, low, lows[s])
                highs[s] = jnp.where(mine, ends[d] - 1 - first, highs[s])
            place = place + here.astype(jnp.int32)
            device = (ends[d] - 1) // rows
            rank = jnp.where(device == previous, rank + 1, 0)
            previous = device
            late = ((rank >= SIDE) & (ends[d] != (device + 1) * rows)).astype(jnp.int32)
            crowded = jnp.maximum(crowded, late)
            owned_in = jnp.where(own_ref[d] == me, device, owned_in)
            owned_late = jnp.where(own_ref[d] == me, late, owned_late)
        flag_ref[0] = owned_in // MEMBERS
        flag_ref[1] = owned_late
        flag_ref[2] = crowded
        flag_ref[3] = owned_in
        at = iota((heads, rows), 1)
        cum = crow_ref[...]
        row_at = iota((16, rows), 1)
        total = jnp.zeros((heads, rows), F32)
        for s in range(slots):
            total = total + span_weights(cum, at, lows[s], highs[s])
            inside = (row_at >= lows[s]) & (row_at <= highs[s])
            keep_ref[s] = jnp.where(inside, 1.0, 0.0).astype(BF16)
        w_ref[...] = total

    for i in range(0, hp, 2):
        lanes = slice(i * 128, (i + 2) * 128)
        weighted = weigh(kt_ref[lanes, :], w_ref, step * hp + i).reshape(16, 16, rows)
        for s in range(slots):
            kept = (weighted * keep_ref[s][None]).reshape(256, rows)
            states = dot(kept, v_ref[:, lanes])
            for j in range(2):
                state = states[j * 128 : (j + 1) * 128, j * 128 : (j + 1) * 128].astype(BF16)
                if by_owner:
                    out_ref[s, i + j] = state
                else:
                    at = (s * hp + i + j) * 128
                    out_ref[0, at : at + 128, :] = state


def side_pieces(doc_lengths, owner_ids, decay_rows, crow, flipped, values, members, slots, by_owner):
    heads, rows = crow.shape
    hp = heads // members
    wide = pl.BlockSpec((rows, hp * 128), lambda j: (0, j))
    if by_owner:
        out = jax.ShapeDtypeStruct((slots, heads, 128, 128), BF16)
        out_spec = pl.BlockSpec((slots, hp, 128, 128), lambda j: (0, j, 0, 0))
    else:
        out = jax.ShapeDtypeStruct((members, slots * hp * 128, 128), BF16)
        out_spec = pl.BlockSpec((1, slots * hp * 128, 128), lambda j: (j, 0, 0))
    return pl.pallas_call(
        functools.partial(side_kernel, slots, by_owner),
        grid=(members,),
        in_specs=[
            SMEM,
            SMEM,
            whole((heads, rows)),
            whole((heads, rows)),
            pl.BlockSpec((hp * 128, rows), lambda j: (j, 0)),
            wide,
        ],
        out_specs=[out_spec, whole((rows, heads)), SMEM],
        out_shape=[out, jax.ShapeDtypeStruct((rows, heads), F32), jax.ShapeDtypeStruct((4,), jnp.int32)],
        scratch_shapes=[pltpu.VMEM((heads, rows), F32), pltpu.VMEM((slots, 16, rows), BF16)],
        compiler_params=LIMIT,
        cost_estimate=pl.CostEstimate(
            flops=slots * heads * rows * 128 * 256, bytes_accessed=rows * heads * 128 * 4, transcendentals=heads * rows
        ),
        name="side_pieces",
    )(doc_lengths, owner_ids, decay_rows, crow, flipped, values)


def head_column(ccol_ref, h):
    cols = ccol_ref[...]
    return jnp.sum(jnp.where(iota(cols.shape, 1) == h, cols, 0.0), axis=1, keepdims=True)


def fill_bias(first, ends, bias_ref):
    for c in range(bias_ref.shape[0] // CHUNK):
        base = first + c * CHUNK
        t_pos = base + iota((CHUNK, 1), 0)
        start = run_start(ends, t_pos)
        s_pos = base + iota((CHUNK, CHUNK), 1)
        keep = (s_pos <= t_pos) & (s_pos >= start)
        bias_ref[c * CHUNK : (c + 1) * CHUNK, :] = jnp.where(keep, math.log2(SCALE), NEG)


def attend(first, ends, q_ref, kt_ref, v_ref, lanes, row_all, col_all, bias_ref, state, emit):
    rows = q_ref.shape[0]
    for r0 in range(0, rows, CHUNK):
        span = slice(r0, r0 + CHUNK)
        query, flipped, value = q_ref[span, lanes], kt_ref[lanes, span], v_ref[span, lanes]
        row, col = row_all[:, span], col_all[span]
        base = row_all[:, r0 - 1 : r0] if r0 else jnp.zeros((1, 1), F32)
        reach = run_end(ends, first + r0 - 1) - (first + r0)
        decay = jnp.exp2((col - row) + bias_ref[span, :])
        if state is None:
            att = dot((dot(query, flipped) * decay).astype(BF16), value)
        else:
            both = dot(query, jnp.concatenate([flipped, state.astype(BF16)], axis=1))
            lead = jnp.exp2(jnp.where(iota((CHUNK, 1), 0) < reach, col - base, NEG))
            att = dot((both[:, :CHUNK] * decay).astype(BF16), value) + lead * both[:, CHUNK:]
        emit(r0, CHUNK, att)
        if r0 + CHUNK < rows:
            since = run_start(ends, first + r0 + CHUNK - 1) - (first + r0)
            total = row[:, CHUNK - 1 :]
            inside = iota((1, CHUNK), 1) >= since
            weight = jnp.exp2(jnp.where(inside, total - row, NEG) + math.log2(SCALE))
            fresh = dot((flipped.astype(F32) * weight).astype(BF16), value)
            if state is not None:
                fresh = fresh + state * jnp.exp2(jnp.where(CHUNK <= reach, total - base, NEG))
            state = fresh


def early_kernel(pairs_before, len_ref, q_ref, kt_ref, v_ref, crow_ref, ccol_ref, out_ref, bias_ref):
    rows = q_ref.shape[0]
    step = pl.program_id(0)
    first = lax.axis_index("seq") * rows
    ends = read_ends(len_ref, len_ref.shape[0])

    @pl.when(step == 0)
    def _():
        fill_bias(first, ends, bias_ref)

    for i in range(2):
        h = (step + pairs_before) * 2 + i
        lanes = slice(i * 128, (i + 1) * 128)

        def emit(t0, size, att):
            out_ref[t0 : t0 + size, lanes] = att

        row_all, col_all = crow_ref[pl.ds(h, 1), :], head_column(ccol_ref, h)
        attend(first, ends, q_ref, kt_ref, v_ref, lanes, row_all, col_all, bias_ref, None, emit)


def early_attention(doc_lengths, queries, flipped, values, crow, ccol, heads_before):
    heads, rows = crow.shape
    skip = heads_before // 2
    wide = pl.BlockSpec((rows, 256), lambda j: (0, j + skip))
    return pl.pallas_call(
        functools.partial(early_kernel, skip),
        grid=(EARLY // 2,),
        in_specs=[
            SMEM,
            wide,
            pl.BlockSpec((256, rows), lambda j: (j + skip, 0)),
            wide,
            whole((heads, rows)),
            whole((rows, heads)),
        ],
        out_specs=pl.BlockSpec((rows, 256), lambda j: (0, j)),
        out_shape=jax.ShapeDtypeStruct((rows, EARLY * 128), F32),
        scratch_shapes=[pltpu.VMEM((rows, CHUNK), F32)],
        compiler_params=LIMIT,
        cost_estimate=pl.CostEstimate(
            flops=EARLY * rows * CHUNK * 128 * 8, bytes_accessed=rows * EARLY * 128 * 10, transcendentals=EARLY * rows * CHUNK
        ),
        name="early_attention",
    )(doc_lengths, queries, flipped, values, crow, ccol)


def decay_of(last_ref, e, i, hp):
    extra = last_ref[e, hp * 128 :, :].astype(F32)
    return extra[i : i + 1, :] + extra[hp + i : hp + i + 1, :]


def scan_quad(rows, len_ref, last_ref, state, i, hp, note):
    members = last_ref.shape[0]
    ends = read_ends(len_ref, len_ref.shape[0])
    base = lax.axis_index("seq") // members * members
    for e in range(members):
        note(e, state)
        low = (base + e) * rows
        inner = jnp.int32(0)
        for end in ends:
            inner = inner + ((end > low) & (end < low + rows)).astype(jnp.int32)
        passes = (inner == 0).astype(F32)
        piece = last_ref[e, i * 128 : (i + 1) * 128, :].astype(F32)
        state = state * (decay_of(last_ref, e, i, hp) * passes) + piece
    return state


def leave_kernel(rows, len_ref, last_ref, *refs):
    out_ref = refs[-1]
    hp = out_ref.shape[0]
    for i in range(hp):
        state = refs[0][i].astype(F32) if len(refs) > 1 else jnp.zeros((128, 128), F32)
        state = scan_quad(rows, len_ref, last_ref, state, i, hp, lambda e, x: None)
        out_ref[i] = state.astype(BF16)


def leave_quad(doc_lengths, last, coming, rows, hp):
    return pl.pallas_call(
        functools.partial(leave_kernel, rows),
        in_specs=[SMEM] + [VMEM] * (1 + len(coming)),
        out_specs=VMEM,
        out_shape=jax.ShapeDtypeStruct((hp, 128, 128), BF16),
        compiler_params=SMALL,
        name="leave_quad",
    )(doc_lengths, last, *coming)


def enter_kernel(rows, len_ref, last_ref, in_ref, *refs):
    out_refs, state_ref = refs[:-1], refs[-1]
    hp = in_ref.shape[0]

    def note(i, e, state):
        state_ref[e, i] = state

    for i in range(hp):
        scan_quad(rows, len_ref, last_ref, in_ref[i].astype(F32), i, hp, functools.partial(note, i))
    me = lax.axis_index("seq") % len(out_refs)
    for x, out_ref in enumerate(out_refs):
        out_ref[...] = state_ref[me ^ x].astype(BF16)


def enter_states(doc_lengths, last, coming, rows):
    members = last.shape[0]
    return pl.pallas_call(
        functools.partial(enter_kernel, rows),
        in_specs=[SMEM, VMEM, VMEM],
        out_specs=[VMEM] * members,
        out_shape=[jax.ShapeDtypeStruct(coming.shape, BF16)] * members,
        scratch_shapes=[pltpu.VMEM((members,) + coming.shape, F32)],
        compiler_params=SMALL,
        name="enter_states",
    )(doc_lengths, last, coming)


def final_kernel(rows, len_ref, own_ref, last_ref, side_ref, in_ref, out_ref, state_ref):
    hp = in_ref.shape[0]
    members = last_ref.shape[0]
    ends = read_ends(len_ref, len_ref.shape[0])
    base = lax.axis_index("seq") // members * members

    def note(i, e, state):
        state_ref[e, i] = state

    for i in range(hp):
        scan_quad(rows, len_ref, last_ref, in_ref[i].astype(F32), i, hp, functools.partial(note, i))
    out_ref[...] = jnp.zeros_like(out_ref)
    place, previous = jnp.int32(0), jnp.int32(-1)
    for d in range(len(ends)):
        device = (ends[d] - 1) // rows
        place = jnp.where(device == previous, place + 1, 0)
        previous = device
        at_end = ends[d] == (device + 1) * rows
        enters = (place == 0).astype(F32)
        mine = device // members * members == base
        e = device - base

        def put(i, local):
            state = local.astype(F32) + state_ref[e, i] * (decay_of(last_ref, e, i, hp) * enters)
            out_ref[own_ref[d], i] = state.astype(BF16)

        @pl.when(mine & at_end)
        def _():
            for i in range(hp):
                put(i, last_ref[e, i * 128 : (i + 1) * 128, :])

        @pl.when(mine & jnp.logical_not(at_end))
        def _():
            for i in range(hp):
                row = pl.multiple_of((jnp.minimum(place, SIDE - 1) * hp + i) * 128, 128)
                put(i, side_ref[e, pl.ds(row, 128), :])


def final_states(doc_lengths, owner_ids, last, side, coming, rows, spread):
    return pl.pallas_call(
        functools.partial(final_kernel, rows),
        in_specs=[SMEM, SMEM, VMEM, VMEM, VMEM],
        out_specs=VMEM,
        out_shape=jax.ShapeDtypeStruct((spread,) + coming.shape, BF16),
        scratch_shapes=[pltpu.VMEM((last.shape[0],) + coming.shape, F32)],
        compiler_params=SMALL,
        name="final_states",
    )(doc_lengths, owner_ids, last, side, coming)


def finish_kernel(
    len_ref, q_ref, kt_ref, v_ref, e0, e1, e2, e3, local1_ref, local2_ref, gate_ref, gain_ref, crow_ref, ccol_ref, out_ref, bias_ref
):
    rows = q_ref.shape[0]
    step = pl.program_id(0)
    me = lax.axis_index("seq")
    first = me * rows
    ends = read_ends(len_ref, len_ref.shape[0])
    hp = e0.shape[0]

    def entering(h):
        far = (h // hp) ^ (me % MEMBERS)
        state = e0[h % hp]
        for x, ref in ((1, e1), (2, e2), (3, e3)):
            state = jnp.where(far == x, ref[h % hp], state)
        return state

    def emit(lanes, t0, size, att):
        mean = jnp.mean(att * att, axis=1, keepdims=True)
        gate = 0.5 + 0.5 * jnp.tanh(0.5 * gate_ref[t0 : t0 + size, lanes].astype(F32))
        gain = gain_ref[:, lanes].astype(F32)
        out_ref[t0 : t0 + size, lanes] = (att * lax.rsqrt(mean + 1e-06) * (gain * gate)).astype(BF16)

    def add_carry(local_ref):
        reach = run_end(ends, first - 1) - first
        for i in range(2):
            lanes = slice(i * 128, (i + 1) * 128)
            col_all = head_column(ccol_ref, step * 2 + i)
            state = entering(step * 2 + i)
            for t0 in range(0, rows, 256):
                at = t0 + iota((256, 1), 0)
                lead = jnp.exp2(jnp.where(at < reach, col_all[t0 : t0 + 256], NEG))
                carry = dot(q_ref[t0 : t0 + 256, lanes], state)
                emit(lanes, t0, 256, local_ref[t0 : t0 + 256, lanes] + lead * carry)

    @pl.when(step == 0)
    def _():
        fill_bias(first, ends, bias_ref)

    @pl.when(step < EARLY // 2)
    def _():
        add_carry(local1_ref)

    @pl.when((step >= EARLY // 2) & (step < EARLY))
    def _():
        add_carry(local2_ref)

    @pl.when(step >= EARLY)
    def _():
        for i in range(2):
            h = step * 2 + i
            lanes = slice(i * 128, (i + 1) * 128)
            row_all, col_all = crow_ref[pl.ds(h, 1), :], head_column(ccol_ref, h)
            state = entering(h).astype(F32)
            attend(
                first, ends, q_ref, kt_ref, v_ref, lanes, row_all, col_all, bias_ref, state, functools.partial(emit, lanes)
            )


def finish(doc_lengths, queries, flipped, values, entering, local1, local2, gate, gain, crow, ccol):
    heads, rows = crow.shape
    pairs = EARLY // 2
    wide = pl.BlockSpec((rows, 256), lambda j: (0, j))
    return pl.pallas_call(
        finish_kernel,
        grid=(heads // 2,),
        in_specs=[
            SMEM,
            wide,
            pl.BlockSpec((256, rows), lambda j: (jnp.maximum(j, EARLY), 0)),
            pl.BlockSpec((rows, 256), lambda j: (0, jnp.maximum(j, EARLY))),
        ]
        + [whole(e.shape) for e in entering]
        + [
            pl.BlockSpec((rows, 256), lambda j: (0, jnp.minimum(j, pairs - 1))),
            pl.BlockSpec((rows, 256), lambda j: (0, jnp.clip(j - pairs, 0, pairs - 1))),
            wide,
            pl.BlockSpec((1, 256), lambda j: (0, j)),
            whole((heads, rows)),
            whole((rows, heads)),
        ],
        out_specs=wide,
        out_shape=jax.ShapeDtypeStruct((rows, heads * 128), BF16),
        scratch_shapes=[pltpu.VMEM((rows, CHUNK), F32)],
        compiler_params=LIMIT,
        cost_estimate=pl.CostEstimate(
            flops=heads * rows * CHUNK * 128 * 8, bytes_accessed=rows * heads * 128 * 10, transcendentals=heads * rows * CHUNK
        ),
        name="finish",
    )(doc_lengths, queries, flipped, values, *entering, local1, local2, gate, gain.reshape(1, -1), crow, ccol)


def swap(x, groups=None):
    return lax.all_to_all(x, "seq", split_axis=0, concat_axis=0, axis_index_groups=groups, tiled=True)


def on_device(spread, queries, keys, values, log_decay, gate, gain, doc_lengths, owner_ids):
    rows, heads = log_decay.shape
    quads = spread // MEMBERS
    hp = heads // MEMBERS
    near = [[q * MEMBERS + m for m in range(MEMBERS)] for q in range(quads)]
    onward = [(s, s + MEMBERS) for s in range(spread - MEMBERS)]
    decay_rows = log_decay.T

    last, crow, flipped = last_pieces(doc_lengths, decay_rows, keys, values, MEMBERS)
    last = swap(last, near)
    side, ccol, flags = side_pieces(doc_lengths, owner_ids, decay_rows, crow, flipped, values, MEMBERS, SIDE, False)
    last, side = lax.optimization_barrier((last, side))

    coming = []
    for _ in range(quads - 1):
        leaving = leave_quad(doc_lengths, last, coming, rows, hp)
        coming = [lax.ppermute(leaving, "seq", onward)]
    side, crow_1, leaving = lax.optimization_barrier((side, crow, leaving))
    side = swap(side, near)
    local1 = early_attention(doc_lengths, queries, flipped, values, crow_1, ccol, 0)

    def send_rest():
        rest, _, _ = side_pieces(
            doc_lengths, owner_ids, decay_rows, crow_1, flipped, values, heads // 2, spread, True
        )
        return lax.dynamic_index_in_dim(swap(rest), flags[3], 0, True)

    coming, local1 = lax.optimization_barrier((coming[0], local1))
    entering = enter_states(doc_lengths, last, coming, rows)
    crow_2, entering = lax.optimization_barrier((crow_1, entering))
    entering = [entering[0]] + [
        lax.ppermute(entering[x], "seq", [(s, s ^ x) for s in range(spread)]) for x in range(1, MEMBERS)
    ]
    local2 = early_attention(doc_lengths, queries, flipped, values, crow_2, ccol, EARLY)
    rest = lax.cond(flags[2] > 0, send_rest, lambda: jnp.zeros((1, heads, 128, 128), BF16))
    side, local2, rest = lax.optimization_barrier((side, local2, rest))
    finals = final_states(doc_lengths, owner_ids, last, side, coming, rows, spread)
    arrived = swap(finals).reshape(quads, heads, 128, 128)
    entering, _ = lax.optimization_barrier((entering, finals))
    mixed = finish(doc_lengths, queries, flipped, values, entering, local1, local2, gate, gain, crow, ccol)
    arrived = lax.dynamic_slice(arrived, (flags[0], 0, 0, 0), (1, heads, 128, 128))
    return mixed, jnp.where(flags[1] > 0, rest, arrived)


def solution(mesh):
    placed = (
        P(("groups", "seq"), "tp"),
        P(("groups", "seq"), "tp"),
        P(("groups", "seq"), "tp"),
        P(("groups", "seq"), "tp"),
        P(("groups", "seq"), "tp"),
        P("tp"),
        P("groups"),
        P("groups"),
    )
    return jax.shard_map(
        functools.partial(on_device, mesh.shape["seq"]),
        mesh=mesh,
        in_specs=placed,
        out_specs=(P(("groups", "seq"), "tp"), P(("groups", "seq"), "tp", None, None)),
        check_vma=False,
    )
```

```python
import functools
import math

import jax
import jax.numpy as jnp
from jax import lax
from jax.experimental import pallas as pl
from jax.experimental.pallas import tpu as pltpu
from jax.sharding import PartitionSpec as P

BLK = 512
SIDE = 3
EXTRA = 16
CHUNK = 256
MEMBERS = 4
EARLY = (4, 4, 2)
NEG = -1e30
LOG2E = math.log2(math.e)
SCALE = 128**-0.5
F32, BF16 = jnp.float32, jnp.bfloat16
SMEM = pl.BlockSpec(memory_space=pltpu.SMEM)
VMEM = pl.BlockSpec(memory_space=pltpu.VMEM)
LIMIT = pltpu.CompilerParams(vmem_limit_bytes=60 * 2**20)
SMALL = pltpu.CompilerParams(vmem_limit_bytes=48 * 2**20)


def dot(a, b, contract=((1,), (0,))):
    return lax.dot_general(a, b, (contract, ((), ())), preferred_element_type=F32)


def iota(shape, dim):
    return lax.broadcasted_iota(jnp.int32, shape, dim)


def read_ends(len_ref, count):
    ends, total = [], jnp.int32(0)
    for d in range(count):
        total = total + len_ref[d]
        ends.append(total)
    return ends


def run_end(ends, pos):
    best = ends[-1]
    for e in reversed(ends[:-1]):
        best = jnp.where(e > pos, e, best)
    return best


def run_start(ends, pos):
    best = jnp.zeros_like(pos)
    for e in ends[:-1]:
        best = jnp.where(e <= pos, e, best)
    return best


def split3(x):
    hi = x.astype(BF16)
    rest = x - hi.astype(F32)
    mid = rest.astype(BF16)
    return hi, mid, (rest - mid.astype(F32)).astype(BF16)


def cum_rows(ld_ref, crow_ref):
    heads, rows = ld_ref.shape
    upper = (iota((BLK, BLK), 0) <= iota((BLK, BLK), 1)).astype(F32).astype(BF16)
    base = jnp.zeros((heads, 1), F32)
    for b in range(rows // BLK):
        part = ld_ref[:, b * BLK : (b + 1) * BLK] * LOG2E
        sums = dot(jnp.concatenate(split3(part), axis=0), upper)
        row = sums[2 * heads :] + sums[heads : 2 * heads] + sums[:heads] + base
        crow_ref[:, b * BLK : (b + 1) * BLK] = row
        base = row[:, BLK - 1 :]


def value_at(cum, at, index):
    return jnp.sum(jnp.where(at == index, cum, 0.0), axis=1, keepdims=True)


def span_weights(cum, at, low, high):
    inside = (at >= low) & (at <= high)
    return jnp.exp2(jnp.where(inside, value_at(cum, at, high) - cum, NEG) + math.log2(SCALE))


def weigh(flipped, w_ref, h):
    weights = [jnp.broadcast_to(w_ref[pl.ds(h + j, 1), :], (128, flipped.shape[1])) for j in range(2)]
    return (flipped.astype(F32) * jnp.concatenate(weights, axis=0)).astype(BF16)


def whole(shape):
    return pl.BlockSpec(shape, lambda j: (0,) * len(shape))


def pieces_kernel(by_owner, len_ref, own_ref, ld_ref, k_ref, v_ref, *refs):
    if by_owner:
        side_ref, crow_ref, w_ref, keep_ref = refs
    else:
        side_ref, crow_ref, flag_ref = refs[:3]
        last_refs = refs[3 : 3 + MEMBERS]
        w_ref, keep_ref, first_ref = refs[3 + MEMBERS :]
    heads, rows = crow_ref.shape
    slots = keep_ref.shape[0]
    step = pl.program_id(0)
    hp = v_ref.shape[1] // 128
    me = lax.axis_index("seq")

    @pl.when(step == 0)
    def _():
        cum_rows(ld_ref, crow_ref)
        first = me * rows
        last = first + rows - 1
        ends = read_ends(len_ref, len_ref.shape[0])
        starts = [jnp.int32(0)] + ends[:-1]
        lows = [jnp.int32(0)] * slots
        highs = [jnp.int32(-1)] * slots
        place, rank, previous = jnp.int32(0), jnp.int32(0), jnp.int32(-1)
        crowded, owned_in, owned_late = jnp.int32(0), jnp.int32(0), jnp.int32(0)
        for d in range(len(ends)):
            here = (ends[d] > first) & (ends[d] <= last)
            low = jnp.maximum(starts[d] - first, 0)
            for s in range(slots):
                mine = here & ((place >= SIDE) & (own_ref[d] == s) if by_owner else (place == s))
                lows[s] = jnp.where(mine, low, lows[s])
                highs[s] = jnp.where(mine, ends[d] - 1 - first, highs[s])
            place = place + here.astype(jnp.int32)
            device = (ends[d] - 1) // rows
            rank = jnp.where(device == previous, rank + 1, 0)
            previous = device
            late = ((rank >= SIDE) & (ends[d] != (device + 1) * rows)).astype(jnp.int32)
            crowded = jnp.maximum(crowded, late)
            owned_in = jnp.where(own_ref[d] == me, device, owned_in)
            owned_late = jnp.where(own_ref[d] == me, late, owned_late)
        if not by_owner:
            lows[SIDE] = jnp.maximum(run_start(ends, last) - first, 0)
            highs[SIDE] = jnp.int32(rows - 1)
            flag_ref[0] = owned_in // MEMBERS
            flag_ref[1] = owned_late
            flag_ref[2] = crowded
            flag_ref[3] = owned_in
        at = iota((heads, rows), 1)
        cum = crow_ref[...]
        row_at = iota((16, rows), 1)
        total = jnp.zeros((heads, rows), F32)
        for s in range(slots):
            total = total + span_weights(cum, at, lows[s], highs[s])
            inside = (row_at >= lows[s]) & (row_at <= highs[s])
            keep_ref[s] = jnp.where(inside, 1.0, 0.0).astype(BF16)
        w_ref[...] = total
        if not by_owner:
            stop = jnp.minimum(run_end(ends, first) - 1 - first, rows - 1)
            goes_on = (run_start(ends, first) < first).astype(F32)
            first_ref[...] = jnp.broadcast_to(jnp.exp2(value_at(cum, at, stop)) * goes_on, (heads, 128))

    weighted = []
    for i in range(0, hp, 2):
        flipped = k_ref[:, i * 128 : (i + 2) * 128].T
        weighted.append(weigh(flipped, w_ref, step * hp + i).reshape(16, 16, rows))
    last_states = []
    for i in range(0, hp, 2):
        value = v_ref[:, i * 128 : (i + 2) * 128]
        for s in range(slots):
            kept = (weighted[i // 2] * keep_ref[s][None]).reshape(256, rows)
            states = dot(kept, value)
            for j in range(2):
                state = states[j * 128 : (j + 1) * 128, j * 128 : (j + 1) * 128].astype(BF16)
                if by_owner:
                    side_ref[s, i + j] = state
                elif s < SIDE:
                    at = (s * hp + i + j) * 128
                    side_ref[0, at : at + 128, :] = state
                else:
                    last_states.append(state)
    if not by_owner:
        rate = first_ref[pl.ds(step * hp, hp), :]
        high = rate.astype(BF16).astype(F32)
        pad = jnp.zeros((EXTRA - 2 * hp, 128), F32)
        tail = jnp.concatenate([high, rate - high, pad], axis=0).astype(BF16)
        for x, last_ref in enumerate(last_refs):

            @pl.when((step ^ (me % MEMBERS)) == x)
            def _():
                for i in range(hp):
                    last_ref[i * 128 : (i + 1) * 128, :] = last_states[i]
                last_ref[hp * 128 :, :] = tail


def piece_states(doc_lengths, owner_ids, decay_rows, keys, values, spread=0):
    heads, rows = decay_rows.shape
    by_owner = spread > 0
    hp = 2 if by_owner else heads // MEMBERS
    slots = spread if by_owner else SIDE + 1
    wide = pl.BlockSpec((rows, hp * 128), lambda j: (0, j))
    scratch = [pltpu.VMEM((heads, rows), F32), pltpu.VMEM((slots, 16, rows), BF16)]
    if by_owner:
        shapes = [jax.ShapeDtypeStruct((slots, heads, 128, 128), BF16), jax.ShapeDtypeStruct((heads, rows), F32)]
        specs = [pl.BlockSpec((slots, hp, 128, 128), lambda j: (0, j, 0, 0)), whole((heads, rows))]
    else:
        last = (hp * 128 + EXTRA, 128)
        shapes = [
            jax.ShapeDtypeStruct((MEMBERS, SIDE * hp * 128, 128), BF16),
            jax.ShapeDtypeStruct((heads, rows), F32),
            jax.ShapeDtypeStruct((4,), jnp.int32),
        ] + [jax.ShapeDtypeStruct(last, BF16)] * MEMBERS
        specs = [pl.BlockSpec((1, SIDE * hp * 128, 128), lambda j: (j, 0, 0)), whole((heads, rows)), SMEM]
        specs += [whole(last)] * MEMBERS
        scratch.append(pltpu.VMEM((heads, 128), F32))
    return pl.pallas_call(
        functools.partial(pieces_kernel, by_owner),
        grid=(heads // hp,),
        in_specs=[SMEM, SMEM, whole((heads, rows)), wide, wide],
        out_specs=specs,
        out_shape=shapes,
        scratch_shapes=scratch,
        compiler_params=LIMIT,
        cost_estimate=pl.CostEstimate(
            flops=slots * heads * rows * 128 * 256, bytes_accessed=rows * heads * 128 * 4, transcendentals=heads * rows
        ),
        name="piece_states",
    )(doc_lengths, owner_ids, decay_rows, keys, values)


def head_column(ccol_ref, h):
    cols = ccol_ref[...]
    return jnp.sum(jnp.where(iota(cols.shape, 1) == h, cols, 0.0), axis=1, keepdims=True)


def fill_columns(crow_ref, ccol_ref):
    heads, rows = crow_ref.shape
    for r0 in range(0, rows, 128):
        part = crow_ref[:, r0 : r0 + 128]
        part = jnp.concatenate([part, jnp.zeros((128 - heads, 128), F32)], axis=0)
        ccol_ref[r0 : r0 + 128, :] = part.T


def fill_bias(first, ends, bias_ref):
    for c in range(bias_ref.shape[0] // CHUNK):
        base = first + c * CHUNK
        t_pos = base + iota((CHUNK, 1), 0)
        start = run_start(ends, t_pos)
        s_pos = base + iota((CHUNK, CHUNK), 1)
        keep = (s_pos <= t_pos) & (s_pos >= start)
        bias_ref[c * CHUNK : (c + 1) * CHUNK, :] = jnp.where(keep, math.log2(SCALE), NEG)


def attend(first, ends, q_ref, k_ref, v_ref, h, crow_ref, ccol_ref, bias_ref, states, emit):
    rows = q_ref.shape[0]
    pair = range(2)
    half = CHUNK // 2
    lanes = [slice(i * 128, (i + 1) * 128) for i in pair]
    row_all = [crow_ref[pl.ds(h + i, 1), :] for i in pair]
    col_all = [head_column(ccol_ref, h + i) for i in pair]
    starts = range(0, rows, CHUNK)
    spans = [slice(r0, r0 + CHUNK) for r0 in starts]
    reach = [run_end(ends, first + r0 - 1) - (first + r0) for r0 in starts]
    base = [[row_all[i][:, r0 - 1 : r0] if r0 else jnp.zeros((1, 1), F32) for r0 in starts] for i in pair]

    fresh = [[], []]
    for c, r0 in enumerate(starts[:-1]):
        since = run_start(ends, first + r0 + CHUNK - 1) - (first + r0)
        inside = iota((1, CHUNK), 1) >= since
        for i in pair:
            row = row_all[i][:, spans[c]]
            weight = jnp.exp2(jnp.where(inside, row[:, CHUNK - 1 :] - row, NEG) + math.log2(SCALE))
            flipped = k_ref[spans[c], lanes[i]].T
            fresh[i].append(dot((flipped.astype(F32) * weight).astype(BF16), v_ref[spans[c], lanes[i]]))
    carried = []
    for i in pair:
        state = None if states is None else states[i]
        chain = [None if state is None else state.astype(BF16)]
        for c in range(len(starts) - 1):
            if state is None:
                state = fresh[i][c]
            else:
                total = row_all[i][:, starts[c] + CHUNK - 1 : starts[c] + CHUNK]
                state = fresh[i][c] + state * jnp.exp2(jnp.where(CHUNK <= reach[c], total - base[i][c], NEG))
            chain.append(state.astype(BF16))
        carried.append(chain)

    def products(c):
        result = []
        for i in pair:
            query = q_ref[spans[c], lanes[i]]
            scores = dot(query, k_ref[spans[c], lanes[i]], ((1,), (1,)))
            result.append((scores, None if carried[i][c] is None else dot(query, carried[i][c])))
        return result

    ahead = products(0)
    for c, r0 in enumerate(starts):
        current = ahead
        if c + 1 < len(starts):
            ahead = products(c + 1)
        for part in range(2):
            t0, width = part * half, (part + 1) * half
            rows_here = slice(r0 + t0, r0 + t0 + half)
            for i in pair:
                scores, carry = current[i]
                col = col_all[i][rows_here]
                decay = jnp.exp2((col - row_all[i][:, r0 : r0 + width]) + bias_ref[rows_here, :width])
                weights = (scores[t0 : t0 + half, :width] * decay).astype(BF16)
                att = dot(weights, v_ref[r0 : r0 + width, lanes[i]])
                if carry is not None:
                    lead = jnp.exp2(jnp.where(t0 + iota((half, 1), 0) < reach[c], col - base[i][c], NEG))
                    att = att + lead * carry[t0 : t0 + half]
                emit(lanes[i], r0 + t0, half, att)


def early_kernel(pairs_before, len_ref, q_ref, k_ref, v_ref, crow_ref, *refs):
    out_ref, bias_ref, ccol_ref = refs[-3:]
    rows = q_ref.shape[0]
    step = pl.program_id(0)
    first = lax.axis_index("seq") * rows
    ends = read_ends(len_ref, len_ref.shape[0])

    @pl.when(step == 0)
    def _():
        fill_bias(first, ends, bias_ref)
        fill_columns(crow_ref, ccol_ref)

    def emit(lanes, t0, size, att):
        out_ref[t0 : t0 + size, lanes] = att

    attend(first, ends, q_ref, k_ref, v_ref, (step + pairs_before) * 2, crow_ref, ccol_ref, bias_ref, None, emit)


def early_attention(doc_lengths, queries, keys, values, crow, before, part):
    heads, rows = crow.shape
    skip = sum(EARLY[:part]) // 2
    wide = pl.BlockSpec((rows, 256), lambda j: (0, j + skip))
    count = EARLY[part]
    return pl.pallas_call(
        functools.partial(early_kernel, skip),
        grid=(count // 2,),
        in_specs=[SMEM, wide, wide, wide, whole((heads, rows))] + [pl.BlockSpec(memory_space=pl.ANY)] * len(before),
        out_specs=wide,
        out_shape=jax.ShapeDtypeStruct((rows, sum(EARLY) * 128), F32),
        input_output_aliases={5: 0} if before else {},
        scratch_shapes=[pltpu.VMEM((rows, CHUNK), F32), pltpu.VMEM((rows, 128), F32)],
        compiler_params=LIMIT,
        cost_estimate=pl.CostEstimate(
            flops=count * rows * CHUNK * 128 * 8, bytes_accessed=rows * count * 128 * 10, transcendentals=count * rows * CHUNK
        ),
        name="early_attention",
    )(doc_lengths, queries, keys, values, crow, *before)


def gather_last(refs, last_ref):
    me = lax.axis_index("seq") % MEMBERS
    for x, ref in enumerate(refs):
        last_ref[me ^ x] = ref[...]


def decay_of(last_ref, e, i, hp):
    extra = last_ref[e, hp * 128 :, :].astype(F32)
    return extra[i : i + 1, :] + extra[hp + i : hp + i + 1, :]


def scan_quad(rows, len_ref, last_ref, state, i, hp, note):
    members = last_ref.shape[0]
    ends = read_ends(len_ref, len_ref.shape[0])
    base = lax.axis_index("seq") // members * members
    for e in range(members):
        note(e, state)
        low = (base + e) * rows
        inner = jnp.int32(0)
        for end in ends:
            inner = inner + ((end > low) & (end < low + rows)).astype(jnp.int32)
        passes = (inner == 0).astype(F32)
        piece = last_ref[e, i * 128 : (i + 1) * 128, :].astype(F32)
        state = state * (decay_of(last_ref, e, i, hp) * passes) + piece
    return state


def leave_kernel(rows, len_ref, *refs):
    out_ref, last_ref = refs[-2:]
    gather_last(refs[:MEMBERS], last_ref)
    hp = out_ref.shape[0]
    for i in range(hp):
        state = jnp.zeros((128, 128), F32)
        if len(refs) > MEMBERS + 2:
            state = refs[MEMBERS][i].astype(F32)
        state = scan_quad(rows, len_ref, last_ref, state, i, hp, lambda e, x: None)
        out_ref[i] = state.astype(BF16)


def leave_quad(doc_lengths, last, coming, rows, hp):
    return pl.pallas_call(
        functools.partial(leave_kernel, rows),
        in_specs=[SMEM] + [VMEM] * (MEMBERS + len(coming)),
        out_specs=VMEM,
        out_shape=jax.ShapeDtypeStruct((hp, 128, 128), BF16),
        scratch_shapes=[pltpu.VMEM((MEMBERS,) + last[0].shape, BF16)],
        compiler_params=SMALL,
        name="leave_quad",
    )(doc_lengths, *last, *coming)


def enter_kernel(rows, len_ref, *refs):
    in_ref, out_refs, last_ref, state_ref = refs[MEMBERS], refs[MEMBERS + 1 : -2], refs[-2], refs[-1]
    gather_last(refs[:MEMBERS], last_ref)
    hp = in_ref.shape[0]

    def note(i, e, state):
        state_ref[e, i] = state

    for i in range(hp):
        scan_quad(rows, len_ref, last_ref, in_ref[i].astype(F32), i, hp, functools.partial(note, i))
    me = lax.axis_index("seq") % MEMBERS
    for x, out_ref in enumerate(out_refs):
        out_ref[...] = state_ref[me ^ x].astype(BF16)


def enter_states(doc_lengths, last, coming, rows):
    return pl.pallas_call(
        functools.partial(enter_kernel, rows),
        in_specs=[SMEM] + [VMEM] * (MEMBERS + 1),
        out_specs=[VMEM] * MEMBERS,
        out_shape=[jax.ShapeDtypeStruct(coming.shape, BF16)] * MEMBERS,
        scratch_shapes=[
            pltpu.VMEM((MEMBERS,) + last[0].shape, BF16),
            pltpu.VMEM((MEMBERS,) + coming.shape, F32),
        ],
        compiler_params=SMALL,
        name="enter_states",
    )(doc_lengths, *last, coming)


def final_kernel(rows, len_ref, own_ref, *refs):
    side_ref, in_ref, out_ref, last_ref, state_ref = refs[MEMBERS:]
    gather_last(refs[:MEMBERS], last_ref)
    hp = in_ref.shape[0]
    ends = read_ends(len_ref, len_ref.shape[0])
    base = lax.axis_index("seq") // MEMBERS * MEMBERS

    def note(i, e, state):
        state_ref[e, i] = state

    for i in range(hp):
        scan_quad(rows, len_ref, last_ref, in_ref[i].astype(F32), i, hp, functools.partial(note, i))
    out_ref[...] = jnp.zeros_like(out_ref)
    place, previous = jnp.int32(0), jnp.int32(-1)
    for d in range(len(ends)):
        device = (ends[d] - 1) // rows
        place = jnp.where(device == previous, place + 1, 0)
        previous = device
        at_end = ends[d] == (device + 1) * rows
        enters = (place == 0).astype(F32)
        mine = device // MEMBERS * MEMBERS == base
        e = device - base

        def put(i, local):
            state = local.astype(F32) + state_ref[e, i] * (decay_of(last_ref, e, i, hp) * enters)
            out_ref[own_ref[d], i] = state.astype(BF16)

        @pl.when(mine & at_end)
        def _():
            for i in range(hp):
                put(i, last_ref[e, i * 128 : (i + 1) * 128, :])

        @pl.when(mine & jnp.logical_not(at_end))
        def _():
            for i in range(hp):
                row = pl.multiple_of((jnp.minimum(place, SIDE - 1) * hp + i) * 128, 128)
                put(i, side_ref[e, pl.ds(row, 128), :])


def final_states(doc_lengths, owner_ids, last, side, coming, rows, spread):
    return pl.pallas_call(
        functools.partial(final_kernel, rows),
        in_specs=[SMEM, SMEM] + [VMEM] * (MEMBERS + 2),
        out_specs=VMEM,
        out_shape=jax.ShapeDtypeStruct((spread,) + coming.shape, BF16),
        scratch_shapes=[
            pltpu.VMEM((MEMBERS,) + last[0].shape, BF16),
            pltpu.VMEM((MEMBERS,) + coming.shape, F32),
        ],
        compiler_params=SMALL,
        name="final_states",
    )(doc_lengths, owner_ids, *last, side, coming)


def finish_kernel(
    len_ref, q_ref, k_ref, v_ref, e0, e1, e2, e3, local_ref, gate_ref, gain_ref, crow_ref, out_ref, bias_ref, ccol_ref
):
    rows = q_ref.shape[0]
    step = pl.program_id(0)
    me = lax.axis_index("seq")
    first = me * rows
    ends = read_ends(len_ref, len_ref.shape[0])
    hp = e0.shape[0]
    pairs = sum(EARLY) // 2

    def entering(h):
        far = (h // hp) ^ (me % MEMBERS)
        state = e0[h % hp]
        for x, ref in ((1, e1), (2, e2), (3, e3)):
            state = jnp.where(far == x, ref[h % hp], state)
        return state

    def emit(lanes, t0, size, att):
        mean = jnp.mean(att * att, axis=1, keepdims=True)
        gate = 0.5 + 0.5 * jnp.tanh(0.5 * gate_ref[t0 : t0 + size, lanes].astype(F32))
        gain = gain_ref[:, lanes].astype(F32)
        out_ref[t0 : t0 + size, lanes] = (att * lax.rsqrt(mean + 1e-06) * (gain * gate)).astype(BF16)

    @pl.when(step == 0)
    def _():
        fill_bias(first, ends, bias_ref)
        fill_columns(crow_ref, ccol_ref)

    @pl.when(step < pairs)
    def _():
        reach = run_end(ends, first - 1) - first
        cols = [head_column(ccol_ref, step * 2 + i) for i in range(2)]
        states = [entering(step * 2 + i) for i in range(2)]
        lanes = [slice(i * 128, (i + 1) * 128) for i in range(2)]
        for t0 in range(0, rows, 256):
            carry = [dot(q_ref[t0 : t0 + 256, lanes[i]], states[i]) for i in range(2)]
            at = t0 + iota((256, 1), 0)
            for i in range(2):
                lead = jnp.exp2(jnp.where(at < reach, cols[i][t0 : t0 + 256], NEG))
                emit(lanes[i], t0, 256, local_ref[t0 : t0 + 256, lanes[i]] + lead * carry[i])

    @pl.when(step >= pairs)
    def _():
        states = [entering(step * 2 + i).astype(F32) for i in range(2)]
        attend(first, ends, q_ref, k_ref, v_ref, step * 2, crow_ref, ccol_ref, bias_ref, states, emit)


def finish(doc_lengths, queries, keys, values, entering, local, gate, gain, crow):
    heads, rows = crow.shape
    pairs = sum(EARLY) // 2
    wide = pl.BlockSpec((rows, 256), lambda j: (0, j))
    late = pl.BlockSpec((rows, 256), lambda j: (0, jnp.maximum(j, pairs)))
    return pl.pallas_call(
        finish_kernel,
        grid=(heads // 2,),
        in_specs=[SMEM, wide, late, late]
        + [whole(e.shape) for e in entering]
        + [
            pl.BlockSpec((rows, 256), lambda j: (0, jnp.minimum(j, pairs - 1))),
            wide,
            pl.BlockSpec((1, 256), lambda j: (0, j)),
            whole((heads, rows)),
        ],
        out_specs=wide,
        out_shape=jax.ShapeDtypeStruct((rows, heads * 128), BF16),
        scratch_shapes=[pltpu.VMEM((rows, CHUNK), F32), pltpu.VMEM((rows, 128), F32)],
        compiler_params=LIMIT,
        cost_estimate=pl.CostEstimate(
            flops=heads * rows * CHUNK * 128 * 8, bytes_accessed=rows * heads * 128 * 10, transcendentals=heads * rows * CHUNK
        ),
        name="finish",
    )(doc_lengths, queries, keys, values, *entering, local, gate, gain.reshape(1, -1), crow)


def swap(x, groups=None):
    return lax.all_to_all(x, "seq", split_axis=0, concat_axis=0, axis_index_groups=groups, tiled=True)


def by_distance(parcels, spread):
    return [parcels[0]] + [
        lax.ppermute(parcels[x], "seq", [(s, s ^ x) for s in range(spread)]) for x in range(1, MEMBERS)
    ]


def on_device(spread, queries, keys, values, log_decay, gate, gain, doc_lengths, owner_ids):
    rows, heads = log_decay.shape
    quads = spread // MEMBERS
    hp = heads // MEMBERS
    near = [[q * MEMBERS + m for m in range(MEMBERS)] for q in range(quads)]
    onward = [(s, s + MEMBERS) for s in range(spread - MEMBERS)]
    decay_rows = log_decay.T
    early = functools.partial(early_attention, doc_lengths, queries, keys, values)
    barrier = lax.optimization_barrier

    side, crow, flags, *last = piece_states(doc_lengths, owner_ids, decay_rows, keys, values)
    side = swap(side, near)
    last = by_distance(last, spread)
    local = early(crow, [], 0)
    last, local = barrier((last, local))

    coming = []
    for _ in range(quads - 1):
        leaving = leave_quad(doc_lengths, last, coming, rows, hp)
        coming = [lax.ppermute(leaving, "seq", onward)]
    crow_1, leaving = barrier((crow, leaving))
    local = early(crow_1, [local], 1)
    coming, local = barrier((coming[0], local))

    entering = enter_states(doc_lengths, last, coming, rows)
    crow_2, entering = barrier((crow_1, entering))
    entering = by_distance(entering, spread)
    local = early(crow_2, [local], 2)

    def send_rest():
        rest, _ = piece_states(doc_lengths, owner_ids, decay_rows, keys, values, spread)
        return lax.dynamic_index_in_dim(swap(rest), flags[3], 0, True)

    rest = lax.cond(flags[2] > 0, send_rest, lambda: jnp.zeros((1, heads, 128, 128), BF16))
    side, local, rest, entering = barrier((side, local, rest, entering))
    finals = final_states(doc_lengths, owner_ids, last, side, coming, rows, spread)
    arrived = swap(finals).reshape(quads, heads, 128, 128)
    entering, _ = barrier((entering, finals))
    mixed = finish(doc_lengths, queries, keys, values, entering, local, gate, gain, crow)
    arrived = lax.dynamic_slice(arrived, (flags[0], 0, 0, 0), (1, heads, 128, 128))
    return mixed, jnp.where(flags[1] > 0, rest, arrived)


def solution(mesh):
    placed = (
        P(("groups", "seq"), "tp"),
        P(("groups", "seq"), "tp"),
        P(("groups", "seq"), "tp"),
        P(("groups", "seq"), "tp"),
        P(("groups", "seq"), "tp"),
        P("tp"),
        P("groups"),
        P("groups"),
    )
    return jax.shard_map(
        functools.partial(on_device, mesh.shape["seq"]),
        mesh=mesh,
        in_specs=placed,
        out_specs=(P(("groups", "seq"), "tp"), P(("groups", "seq"), "tp", None, None)),
        check_vma=False,
    )
```

```python
import functools
import math

import jax
import jax.numpy as jnp
from jax import lax
from jax.experimental import pallas as pl
from jax.experimental.pallas import tpu as pltpu
from jax.sharding import PartitionSpec as P

BLK = 512
SIDE = 3
EXTRA = 16
CHUNK = 256
MEMBERS = 4
NEG = -1e30
LOG2E = math.log2(math.e)
SCALE = 128**-0.5
F32, BF16 = jnp.float32, jnp.bfloat16
SMEM = pl.BlockSpec(memory_space=pltpu.SMEM)
VMEM = pl.BlockSpec(memory_space=pltpu.VMEM)
LIMIT = pltpu.CompilerParams(vmem_limit_bytes=60 * 2**20)
SMALL = pltpu.CompilerParams(vmem_limit_bytes=48 * 2**20)


def dot(a, b, contract=((1,), (0,))):
    return lax.dot_general(a, b, (contract, ((), ())), preferred_element_type=F32)


def iota(shape, dim):
    return lax.broadcasted_iota(jnp.int32, shape, dim)


def read_ends(len_ref, count):
    ends, total = [], jnp.int32(0)
    for d in range(count):
        total = total + len_ref[d]
        ends.append(total)
    return ends


def run_end(ends, pos):
    best = ends[-1]
    for e in reversed(ends[:-1]):
        best = jnp.where(e > pos, e, best)
    return best


def run_start(ends, pos):
    best = jnp.zeros_like(pos)
    for e in ends[:-1]:
        best = jnp.where(e <= pos, e, best)
    return best


def split3(x):
    hi = x.astype(BF16)
    rest = x - hi.astype(F32)
    mid = rest.astype(BF16)
    return hi, mid, (rest - mid.astype(F32)).astype(BF16)


def cum_rows(ld_ref, crow_ref):
    heads, rows = ld_ref.shape
    upper = (iota((BLK, BLK), 0) <= iota((BLK, BLK), 1)).astype(F32).astype(BF16)
    base = jnp.zeros((heads, 1), F32)
    for b in range(rows // BLK):
        part = ld_ref[:, b * BLK : (b + 1) * BLK] * LOG2E
        sums = dot(jnp.concatenate(split3(part), axis=0), upper)
        row = sums[2 * heads :] + sums[heads : 2 * heads] + sums[:heads] + base
        crow_ref[:, b * BLK : (b + 1) * BLK] = row
        base = row[:, BLK - 1 :]


def value_at(cum, at, index):
    return jnp.sum(jnp.where(at == index, cum, 0.0), axis=1, keepdims=True)


def span_weights(cum, at, low, high):
    inside = (at >= low) & (at <= high)
    return jnp.exp2(jnp.where(inside, value_at(cum, at, high) - cum, NEG) + math.log2(SCALE))


def weigh(flipped, w_ref, h):
    weights = [jnp.broadcast_to(w_ref[pl.ds(h + j, 1), :], (128, flipped.shape[1])) for j in range(2)]
    return (flipped.astype(F32) * jnp.concatenate(weights, axis=0)).astype(BF16)


def whole(shape):
    return pl.BlockSpec(shape, lambda j: (0,) * len(shape))


def pieces_kernel(by_owner, len_ref, own_ref, ld_ref, k_ref, v_ref, *refs):
    if by_owner:
        side_ref, crow_ref, w_ref, keep_ref = refs
    else:
        side_ref, crow_ref, flag_ref = refs[:3]
        last_refs = refs[3 : 3 + MEMBERS]
        w_ref, keep_ref, first_ref = refs[3 + MEMBERS :]
    heads, rows = crow_ref.shape
    slots = keep_ref.shape[0]
    step = pl.program_id(0)
    hp = v_ref.shape[1] // 128
    me = lax.axis_index("seq")

    @pl.when(step == 0)
    def _():
        cum_rows(ld_ref, crow_ref)
        first = me * rows
        last = first + rows - 1
        ends = read_ends(len_ref, len_ref.shape[0])
        starts = [jnp.int32(0)] + ends[:-1]
        lows = [jnp.int32(0)] * slots
        highs = [jnp.int32(-1)] * slots
        place, rank, previous = jnp.int32(0), jnp.int32(0), jnp.int32(-1)
        crowded, owned_in, owned_late = jnp.int32(0), jnp.int32(0), jnp.int32(0)
        for d in range(len(ends)):
            here = (ends[d] > first) & (ends[d] <= last)
            low = jnp.maximum(starts[d] - first, 0)
            for s in range(slots):
                mine = here & ((place >= SIDE) & (own_ref[d] == s) if by_owner else (place == s))
                lows[s] = jnp.where(mine, low, lows[s])
                highs[s] = jnp.where(mine, ends[d] - 1 - first, highs[s])
            place = place + here.astype(jnp.int32)
            device = (ends[d] - 1) // rows
            rank = jnp.where(device == previous, rank + 1, 0)
            previous = device
            late = ((rank >= SIDE) & (ends[d] != (device + 1) * rows)).astype(jnp.int32)
            crowded = jnp.maximum(crowded, late)
            owned_in = jnp.where(own_ref[d] == me, device, owned_in)
            owned_late = jnp.where(own_ref[d] == me, late, owned_late)
        if not by_owner:
            lows[SIDE] = jnp.maximum(run_start(ends, last) - first, 0)
            highs[SIDE] = jnp.int32(rows - 1)
            flag_ref[0] = owned_in // MEMBERS
            flag_ref[1] = owned_late
            flag_ref[2] = crowded
            flag_ref[3] = owned_in
        at = iota((heads, rows), 1)
        cum = crow_ref[...]
        row_at = iota((16, rows), 1)
        total = jnp.zeros((heads, rows), F32)
        for s in range(slots):
            total = total + span_weights(cum, at, lows[s], highs[s])
            inside = (row_at >= lows[s]) & (row_at <= highs[s])
            keep_ref[s] = jnp.where(inside, 1.0, 0.0).astype(BF16)
        w_ref[...] = total
        if not by_owner:
            stop = jnp.minimum(run_end(ends, first) - 1 - first, rows - 1)
            goes_on = (run_start(ends, first) < first).astype(F32)
            first_ref[...] = jnp.broadcast_to(jnp.exp2(value_at(cum, at, stop)) * goes_on, (heads, 128))

    weighted = []
    for i in range(0, hp, 2):
        flipped = k_ref[:, i * 128 : (i + 2) * 128].T
        weighted.append(weigh(flipped, w_ref, step * hp + i).reshape(16, 16, rows))
    last_states = []
    for i in range(0, hp, 2):
        value = v_ref[:, i * 128 : (i + 2) * 128]
        for s in range(slots):
            kept = (weighted[i // 2] * keep_ref[s][None]).reshape(256, rows)
            states = dot(kept, value)
            for j in range(2):
                state = states[j * 128 : (j + 1) * 128, j * 128 : (j + 1) * 128].astype(BF16)
                if by_owner:
                    side_ref[s, i + j] = state
                elif s < SIDE:
                    at = (s * hp + i + j) * 128
                    side_ref[0, at : at + 128, :] = state
                else:
                    last_states.append(state)
    if not by_owner:
        rate = first_ref[pl.ds(step * hp, hp), :]
        high = rate.astype(BF16).astype(F32)
        pad = jnp.zeros((EXTRA - 2 * hp, 128), F32)
        tail = jnp.concatenate([high, rate - high, pad], axis=0).astype(BF16)
        for x, last_ref in enumerate(last_refs):

            @pl.when((step ^ (me % MEMBERS)) == x)
            def _():
                for i in range(hp):
                    last_ref[i * 128 : (i + 1) * 128, :] = last_states[i]
                last_ref[hp * 128 :, :] = tail


def piece_states(doc_lengths, owner_ids, decay_rows, keys, values, spread=0):
    heads, rows = decay_rows.shape
    by_owner = spread > 0
    hp = 2 if by_owner else heads // MEMBERS
    slots = spread if by_owner else SIDE + 1
    wide = pl.BlockSpec((rows, hp * 128), lambda j: (0, j))
    scratch = [pltpu.VMEM((heads, rows), F32), pltpu.VMEM((slots, 16, rows), BF16)]
    if by_owner:
        shapes = [jax.ShapeDtypeStruct((slots, heads, 128, 128), BF16), jax.ShapeDtypeStruct((heads, rows), F32)]
        specs = [pl.BlockSpec((slots, hp, 128, 128), lambda j: (0, j, 0, 0)), whole((heads, rows))]
    else:
        last = (hp * 128 + EXTRA, 128)
        shapes = [
            jax.ShapeDtypeStruct((MEMBERS, SIDE * hp * 128, 128), BF16),
            jax.ShapeDtypeStruct((heads, rows), F32),
            jax.ShapeDtypeStruct((4,), jnp.int32),
        ] + [jax.ShapeDtypeStruct(last, BF16)] * MEMBERS
        specs = [pl.BlockSpec((1, SIDE * hp * 128, 128), lambda j: (j, 0, 0)), whole((heads, rows)), SMEM]
        specs += [whole(last)] * MEMBERS
        scratch.append(pltpu.VMEM((heads, 128), F32))
    return pl.pallas_call(
        functools.partial(pieces_kernel, by_owner),
        grid=(heads // hp,),
        in_specs=[SMEM, SMEM, whole((heads, rows)), wide, wide],
        out_specs=specs,
        out_shape=shapes,
        scratch_shapes=scratch,
        compiler_params=LIMIT,
        cost_estimate=pl.CostEstimate(
            flops=slots * heads * rows * 128 * 256, bytes_accessed=rows * heads * 128 * 4, transcendentals=heads * rows
        ),
        name="piece_states",
    )(doc_lengths, owner_ids, decay_rows, keys, values)


def head_column(ccol_ref, h):
    cols = ccol_ref[...]
    return jnp.sum(jnp.where(iota(cols.shape, 1) == h, cols, 0.0), axis=1, keepdims=True)


def fill_columns(crow_ref, ccol_ref):
    heads, rows = crow_ref.shape
    for r0 in range(0, rows, 128):
        part = crow_ref[:, r0 : r0 + 128]
        part = jnp.concatenate([part, jnp.zeros((128 - heads, 128), F32)], axis=0)
        ccol_ref[r0 : r0 + 128, :] = part.T


def fill_bias(first, ends, bias_ref):
    for c in range(bias_ref.shape[0] // CHUNK):
        base = first + c * CHUNK
        t_pos = base + iota((CHUNK, 1), 0)
        start = run_start(ends, t_pos)
        s_pos = base + iota((CHUNK, CHUNK), 1)
        keep = (s_pos <= t_pos) & (s_pos >= start)
        bias_ref[c * CHUNK : (c + 1) * CHUNK, :] = jnp.where(keep, math.log2(SCALE), NEG)


def attend(first, ends, q_ref, k_ref, v_ref, h, crow_ref, ccol_ref, bias_ref, states, emit):
    rows = q_ref.shape[0]
    pair = range(2)
    half = CHUNK // 2
    lanes = [slice(i * 128, (i + 1) * 128) for i in pair]
    row_all = [crow_ref[pl.ds(h + i, 1), :] for i in pair]
    col_all = [head_column(ccol_ref, h + i) for i in pair]
    starts = range(0, rows, CHUNK)
    spans = [slice(r0, r0 + CHUNK) for r0 in starts]
    reach = [run_end(ends, first + r0 - 1) - (first + r0) for r0 in starts]
    base = [[row_all[i][:, r0 - 1 : r0] if r0 else jnp.zeros((1, 1), F32) for r0 in starts] for i in pair]

    fresh = [[], []]
    for c, r0 in enumerate(starts[:-1]):
        since = run_start(ends, first + r0 + CHUNK - 1) - (first + r0)
        inside = iota((1, CHUNK), 1) >= since
        for i in pair:
            row = row_all[i][:, spans[c]]
            weight = jnp.exp2(jnp.where(inside, row[:, CHUNK - 1 :] - row, NEG) + math.log2(SCALE))
            flipped = k_ref[spans[c], lanes[i]].T
            fresh[i].append(dot((flipped.astype(F32) * weight).astype(BF16), v_ref[spans[c], lanes[i]]))
    carried = []
    for i in pair:
        state, chain = states[i], [states[i].astype(BF16)]
        for c in range(len(starts) - 1):
            total = row_all[i][:, starts[c] + CHUNK - 1 : starts[c] + CHUNK]
            state = fresh[i][c] + state * jnp.exp2(jnp.where(CHUNK <= reach[c], total - base[i][c], NEG))
            chain.append(state.astype(BF16))
        carried.append(chain)

    def products(c):
        result = []
        for i in pair:
            query = q_ref[spans[c], lanes[i]]
            scores = dot(query, k_ref[spans[c], lanes[i]], ((1,), (1,)))
            result.append((scores, dot(query, carried[i][c])))
        return result

    ahead = products(0)
    for c, r0 in enumerate(starts):
        current = ahead
        if c + 1 < len(starts):
            ahead = products(c + 1)
        for part in range(2):
            t0, width = part * half, (part + 1) * half
            rows_here = slice(r0 + t0, r0 + t0 + half)
            for i in pair:
                scores, carry = current[i]
                col = col_all[i][rows_here]
                decay = jnp.exp2((col - row_all[i][:, r0 : r0 + width]) + bias_ref[rows_here, :width])
                weights = (scores[t0 : t0 + half, :width] * decay).astype(BF16)
                att = dot(weights, v_ref[r0 : r0 + width, lanes[i]])
                lead = jnp.exp2(jnp.where(t0 + iota((half, 1), 0) < reach[c], col - base[i][c], NEG))
                emit(lanes[i], r0 + t0, half, att + lead * carry[t0 : t0 + half])


def gather_last(refs, last_ref):
    me = lax.axis_index("seq") % MEMBERS
    for x, ref in enumerate(refs):
        last_ref[me ^ x] = ref[...]


def decay_of(last_ref, e, i, hp):
    extra = last_ref[e, hp * 128 :, :].astype(F32)
    return extra[i : i + 1, :] + extra[hp + i : hp + i + 1, :]


def scan_quad(rows, len_ref, last_ref, state, i, hp, note):
    members = last_ref.shape[0]
    ends = read_ends(len_ref, len_ref.shape[0])
    base = lax.axis_index("seq") // members * members
    for e in range(members):
        note(e, state)
        low = (base + e) * rows
        inner = jnp.int32(0)
        for end in ends:
            inner = inner + ((end > low) & (end < low + rows)).astype(jnp.int32)
        passes = (inner == 0).astype(F32)
        piece = last_ref[e, i * 128 : (i + 1) * 128, :].astype(F32)
        state = state * (decay_of(last_ref, e, i, hp) * passes) + piece
    return state


def leave_kernel(rows, len_ref, *refs):
    out_ref, last_ref = refs[-2:]
    gather_last(refs[:MEMBERS], last_ref)
    hp = out_ref.shape[0]
    for i in range(hp):
        state = jnp.zeros((128, 128), F32)
        if len(refs) > MEMBERS + 2:
            state = refs[MEMBERS][i].astype(F32)
        state = scan_quad(rows, len_ref, last_ref, state, i, hp, lambda e, x: None)
        out_ref[i] = state.astype(BF16)


def leave_quad(doc_lengths, last, coming, rows, hp):
    return pl.pallas_call(
        functools.partial(leave_kernel, rows),
        in_specs=[SMEM] + [VMEM] * (MEMBERS + len(coming)),
        out_specs=VMEM,
        out_shape=jax.ShapeDtypeStruct((hp, 128, 128), BF16),
        scratch_shapes=[pltpu.VMEM((MEMBERS,) + last[0].shape, BF16)],
        compiler_params=SMALL,
        name="leave_quad",
    )(doc_lengths, *last, *coming)


def enter_kernel(rows, len_ref, *refs):
    in_ref, out_refs, last_ref, state_ref = refs[MEMBERS], refs[MEMBERS + 1 : -2], refs[-2], refs[-1]
    gather_last(refs[:MEMBERS], last_ref)
    hp = in_ref.shape[0]

    def note(i, e, state):
        state_ref[e, i] = state

    for i in range(hp):
        scan_quad(rows, len_ref, last_ref, in_ref[i].astype(F32), i, hp, functools.partial(note, i))
    me = lax.axis_index("seq") % MEMBERS
    for x, out_ref in enumerate(out_refs):
        out_ref[...] = state_ref[me ^ x].astype(BF16)


def enter_states(doc_lengths, last, coming, rows):
    return pl.pallas_call(
        functools.partial(enter_kernel, rows),
        in_specs=[SMEM] + [VMEM] * (MEMBERS + 1),
        out_specs=[VMEM] * MEMBERS,
        out_shape=[jax.ShapeDtypeStruct(coming.shape, BF16)] * MEMBERS,
        scratch_shapes=[
            pltpu.VMEM((MEMBERS,) + last[0].shape, BF16),
            pltpu.VMEM((MEMBERS,) + coming.shape, F32),
        ],
        compiler_params=SMALL,
        name="enter_states",
    )(doc_lengths, *last, coming)


def final_kernel(rows, len_ref, own_ref, *refs):
    side_ref, in_ref, out_ref, last_ref, state_ref = refs[MEMBERS:]
    gather_last(refs[:MEMBERS], last_ref)
    hp = in_ref.shape[0]
    ends = read_ends(len_ref, len_ref.shape[0])
    base = lax.axis_index("seq") // MEMBERS * MEMBERS

    def note(i, e, state):
        state_ref[e, i] = state

    for i in range(hp):
        scan_quad(rows, len_ref, last_ref, in_ref[i].astype(F32), i, hp, functools.partial(note, i))
    out_ref[...] = jnp.zeros_like(out_ref)
    place, previous = jnp.int32(0), jnp.int32(-1)
    for d in range(len(ends)):
        device = (ends[d] - 1) // rows
        place = jnp.where(device == previous, place + 1, 0)
        previous = device
        at_end = ends[d] == (device + 1) * rows
        enters = (place == 0).astype(F32)
        mine = device // MEMBERS * MEMBERS == base
        e = device - base

        def put(i, local):
            state = local.astype(F32) + state_ref[e, i] * (decay_of(last_ref, e, i, hp) * enters)
            out_ref[own_ref[d], i] = state.astype(BF16)

        @pl.when(mine & at_end)
        def _():
            for i in range(hp):
                put(i, last_ref[e, i * 128 : (i + 1) * 128, :])

        @pl.when(mine & jnp.logical_not(at_end))
        def _():
            for i in range(hp):
                row = pl.multiple_of((jnp.minimum(place, SIDE - 1) * hp + i) * 128, 128)
                put(i, side_ref[e, pl.ds(row, 128), :])


def final_states(doc_lengths, owner_ids, last, side, coming, rows, spread):
    return pl.pallas_call(
        functools.partial(final_kernel, rows),
        in_specs=[SMEM, SMEM] + [VMEM] * (MEMBERS + 2),
        out_specs=VMEM,
        out_shape=jax.ShapeDtypeStruct((spread,) + coming.shape, BF16),
        scratch_shapes=[
            pltpu.VMEM((MEMBERS,) + last[0].shape, BF16),
            pltpu.VMEM((MEMBERS,) + coming.shape, F32),
        ],
        compiler_params=SMALL,
        name="final_states",
    )(doc_lengths, owner_ids, *last, side, coming)


def finish_kernel(len_ref, q_ref, k_ref, v_ref, e0, e1, e2, e3, gate_ref, gain_ref, crow_ref, out_ref, bias_ref, ccol_ref):
    rows = q_ref.shape[0]
    step = pl.program_id(0)
    me = lax.axis_index("seq")
    first = me * rows
    ends = read_ends(len_ref, len_ref.shape[0])
    hp = e0.shape[0]

    def entering(h):
        far = (h // hp) ^ (me % MEMBERS)
        state = e0[h % hp]
        for x, ref in ((1, e1), (2, e2), (3, e3)):
            state = jnp.where(far == x, ref[h % hp], state)
        return state

    def emit(lanes, t0, size, att):
        mean = jnp.mean(att * att, axis=1, keepdims=True)
        gate = 0.5 + 0.5 * jnp.tanh(0.5 * gate_ref[t0 : t0 + size, lanes].astype(F32))
        gain = gain_ref[:, lanes].astype(F32)
        out_ref[t0 : t0 + size, lanes] = (att * lax.rsqrt(mean + 1e-06) * (gain * gate)).astype(BF16)

    @pl.when(step == 0)
    def _():
        fill_bias(first, ends, bias_ref)
        fill_columns(crow_ref, ccol_ref)

    states = [entering(step * 2 + i).astype(F32) for i in range(2)]
    attend(first, ends, q_ref, k_ref, v_ref, step * 2, crow_ref, ccol_ref, bias_ref, states, emit)


def finish(doc_lengths, queries, keys, values, entering, gate, gain, crow):
    heads, rows = crow.shape
    wide = pl.BlockSpec((rows, 256), lambda j: (0, j))
    return pl.pallas_call(
        finish_kernel,
        grid=(heads // 2,),
        in_specs=[SMEM, wide, wide, wide]
        + [whole(e.shape) for e in entering]
        + [wide, pl.BlockSpec((1, 256), lambda j: (0, j)), whole((heads, rows))],
        out_specs=wide,
        out_shape=jax.ShapeDtypeStruct((rows, heads * 128), BF16),
        scratch_shapes=[pltpu.VMEM((rows, CHUNK), F32), pltpu.VMEM((rows, 128), F32)],
        compiler_params=pltpu.CompilerParams(vmem_limit_bytes=57 * 2**20),
        cost_estimate=pl.CostEstimate(
            flops=heads * rows * CHUNK * 128 * 8, bytes_accessed=rows * heads * 128 * 10, transcendentals=heads * rows * CHUNK
        ),
        name="finish",
    )(doc_lengths, queries, keys, values, *entering, gate, gain, crow)


def swap(x, groups=None):
    return lax.all_to_all(x, "seq", split_axis=0, concat_axis=0, axis_index_groups=groups, tiled=True)


def by_distance(parcels, spread):
    return [parcels[0]] + [
        lax.ppermute(parcels[x], "seq", [(s, s ^ x) for s in range(spread)]) for x in range(1, MEMBERS)
    ]


def on_device(spread, queries, keys, values, log_decay, gate, gain, doc_lengths, owner_ids):
    rows, heads = log_decay.shape
    quads = spread // MEMBERS
    hp = heads // MEMBERS
    near = [[q * MEMBERS + m for m in range(MEMBERS)] for q in range(quads)]
    onward = [(s, s + MEMBERS) for s in range(spread - MEMBERS)]
    decay_rows = log_decay.T
    barrier = lax.optimization_barrier

    side, crow, flags, *last = piece_states(doc_lengths, owner_ids, decay_rows, keys, values)
    side = swap(side, near)
    last = by_distance(last, spread)

    coming = []
    for _ in range(quads - 1):
        leaving = leave_quad(doc_lengths, last, coming, rows, hp)
        coming = [lax.ppermute(leaving, "seq", onward)]
    flags, gain, leaving = barrier((flags, gain, leaving))
    gain = gain.reshape(1, -1)

    def send_rest():
        rest, _ = piece_states(doc_lengths, owner_ids, decay_rows, keys, values, spread)
        return lax.dynamic_index_in_dim(swap(rest), flags[3], 0, True)

    rest = lax.cond(flags[2] > 0, send_rest, lambda: jnp.zeros((1, heads, 128, 128), BF16))
    from_quad = [flags[0] == q for q in range(1, quads)]
    coming, rest, gain, late, from_quad = barrier((coming[0], rest, gain, flags[1] > 0, from_quad))

    entering = by_distance(enter_states(doc_lengths, last, coming, rows), spread)
    finals = final_states(doc_lengths, owner_ids, last, side, coming, rows, spread)
    arrived = swap(finals).reshape(quads, 1, heads, 128, 128)
    entering, _ = barrier((entering, finals))
    mixed = finish(doc_lengths, queries, keys, values, entering, gate, gain, crow)
    owned = arrived[0]
    for q in range(1, quads):
        owned = jnp.where(from_quad[q - 1], arrived[q], owned)
    return mixed, jnp.where(late, rest, owned)


def solution(mesh):
    placed = (
        P(("groups", "seq"), "tp"),
        P(("groups", "seq"), "tp"),
        P(("groups", "seq"), "tp"),
        P(("groups", "seq"), "tp"),
        P(("groups", "seq"), "tp"),
        P("tp"),
        P("groups"),
        P("groups"),
    )
    return jax.shard_map(
        functools.partial(on_device, mesh.shape["seq"]),
        mesh=mesh,
        in_specs=placed,
        out_specs=(P(("groups", "seq"), "tp"), P(("groups", "seq"), "tp", None, None)),
        check_vma=False,
    )
```

```python
import functools
import math

import jax
import jax.numpy as jnp
from jax import lax
from jax.experimental import pallas as pl
from jax.experimental.pallas import tpu as pltpu
from jax.sharding import PartitionSpec as P

BLK = 512
SIDE = 3
SENT = (2, 1)
EXTRA = 16
CHUNK = 256
MEMBERS = 4
NEG = -1e30
LOG2E = math.log2(math.e)
SCALE = 128**-0.5
F32, BF16 = jnp.float32, jnp.bfloat16
SMEM = pl.BlockSpec(memory_space=pltpu.SMEM)
VMEM = pl.BlockSpec(memory_space=pltpu.VMEM)
LIMIT = pltpu.CompilerParams(vmem_limit_bytes=60 * 2**20)
SMALL = pltpu.CompilerParams(vmem_limit_bytes=48 * 2**20)


def dot(a, b, contract=((1,), (0,))):
    return lax.dot_general(a, b, (contract, ((), ())), preferred_element_type=F32)


def iota(shape, dim):
    return lax.broadcasted_iota(jnp.int32, shape, dim)


def read_ends(len_ref, count):
    ends, total = [], jnp.int32(0)
    for d in range(count):
        total = total + len_ref[d]
        ends.append(total)
    return ends


def run_end(ends, pos):
    best = ends[-1]
    for e in reversed(ends[:-1]):
        best = jnp.where(e > pos, e, best)
    return best


def run_start(ends, pos):
    best = jnp.zeros_like(pos)
    for e in ends[:-1]:
        best = jnp.where(e <= pos, e, best)
    return best


def split3(x):
    hi = x.astype(BF16)
    rest = x - hi.astype(F32)
    mid = rest.astype(BF16)
    return hi, mid, (rest - mid.astype(F32)).astype(BF16)


def cum_rows(ld_ref, crow_ref):
    heads, rows = ld_ref.shape
    upper = (iota((BLK, BLK), 0) <= iota((BLK, BLK), 1)).astype(F32).astype(BF16)
    base = jnp.zeros((heads, 1), F32)
    for b in range(rows // BLK):
        part = ld_ref[:, b * BLK : (b + 1) * BLK] * LOG2E
        sums = dot(jnp.concatenate(split3(part), axis=0), upper)
        row = sums[2 * heads :] + sums[heads : 2 * heads] + sums[:heads] + base
        crow_ref[:, b * BLK : (b + 1) * BLK] = row
        base = row[:, BLK - 1 :]


def value_at(cum, at, index):
    return jnp.sum(jnp.where(at == index, cum, 0.0), axis=1, keepdims=True)


def span_weights(cum, at, low, high):
    inside = (at >= low) & (at <= high)
    return jnp.exp2(jnp.where(inside, value_at(cum, at, high) - cum, NEG) + math.log2(SCALE))


def weigh(flipped, w_ref, h):
    weights = [jnp.broadcast_to(w_ref[pl.ds(h + j, 1), :], (128, flipped.shape[1])) for j in range(2)]
    return (flipped.astype(F32) * jnp.concatenate(weights, axis=0)).astype(BF16)


def whole(shape):
    return pl.BlockSpec(shape, lambda j: (0,) * len(shape))


def pieces_kernel(by_owner, len_ref, own_ref, ld_ref, k_ref, v_ref, *refs):
    if by_owner:
        side_ref, crow_ref, w_ref, keep_ref = refs
    else:
        side_refs, crow_ref, flag_ref = refs[:2], refs[2], refs[3]
        last_refs = refs[4 : 4 + MEMBERS]
        w_ref, keep_ref, first_ref = refs[4 + MEMBERS :]
    heads, rows = crow_ref.shape
    slots = keep_ref.shape[0]
    step = pl.program_id(0)
    hp = v_ref.shape[1] // 128
    me = lax.axis_index("seq")

    @pl.when(step == 0)
    def _():
        cum_rows(ld_ref, crow_ref)
        first = me * rows
        last = first + rows - 1
        ends = read_ends(len_ref, len_ref.shape[0])
        starts = [jnp.int32(0)] + ends[:-1]
        lows = [jnp.int32(0)] * slots
        highs = [jnp.int32(-1)] * slots
        place, rank, previous = jnp.int32(0), jnp.int32(0), jnp.int32(-1)
        crowded, owned_in, owned_late = jnp.int32(0), jnp.int32(0), jnp.int32(0)
        for d in range(len(ends)):
            here = (ends[d] > first) & (ends[d] <= last)
            low = jnp.maximum(starts[d] - first, 0)
            for s in range(slots):
                mine = here & ((place >= SIDE) & (own_ref[d] == s) if by_owner else (place == s))
                lows[s] = jnp.where(mine, low, lows[s])
                highs[s] = jnp.where(mine, ends[d] - 1 - first, highs[s])
            place = place + here.astype(jnp.int32)
            device = (ends[d] - 1) // rows
            rank = jnp.where(device == previous, rank + 1, 0)
            previous = device
            late = ((rank >= SIDE) & (ends[d] != (device + 1) * rows)).astype(jnp.int32)
            crowded = jnp.maximum(crowded, late)
            owned_in = jnp.where(own_ref[d] == me, device, owned_in)
            owned_late = jnp.where(own_ref[d] == me, late, owned_late)
        if not by_owner:
            lows[SIDE] = jnp.maximum(run_start(ends, last) - first, 0)
            highs[SIDE] = jnp.int32(rows - 1)
            flag_ref[0] = owned_in // MEMBERS
            flag_ref[1] = owned_late
            flag_ref[2] = crowded
            flag_ref[3] = owned_in
        at = iota((heads, rows), 1)
        cum = crow_ref[...]
        row_at = iota((16, rows), 1)
        total = jnp.zeros((heads, rows), F32)
        for s in range(slots):
            total = total + span_weights(cum, at, lows[s], highs[s])
            inside = (row_at >= lows[s]) & (row_at <= highs[s])
            keep_ref[s] = jnp.where(inside, 1.0, 0.0).astype(BF16)
        w_ref[...] = total
        if not by_owner:
            stop = jnp.minimum(run_end(ends, first) - 1 - first, rows - 1)
            goes_on = (run_start(ends, first) < first).astype(F32)
            first_ref[...] = jnp.broadcast_to(jnp.exp2(value_at(cum, at, stop)) * goes_on, (heads, 128))

    weighted = []
    for i in range(0, hp, 2):
        flipped = k_ref[:, i * 128 : (i + 2) * 128].T
        weighted.append(weigh(flipped, w_ref, step * hp + i).reshape(16, 16, rows))
    last_states = []
    for i in range(0, hp, 2):
        value = v_ref[:, i * 128 : (i + 2) * 128]
        for s in range(slots):
            kept = (weighted[i // 2] * keep_ref[s][None]).reshape(256, rows)
            states = dot(kept, value)
            for j in range(2):
                state = states[j * 128 : (j + 1) * 128, j * 128 : (j + 1) * 128].astype(BF16)
                if by_owner:
                    side_ref[s, i + j] = state
                elif s < SIDE:
                    part, slot = (0, s) if s < SENT[0] else (1, s - SENT[0])
                    at = (slot * hp + i + j) * 128
                    side_refs[part][0, at : at + 128, :] = state
                else:
                    last_states.append(state)
    if not by_owner:
        rate = first_ref[pl.ds(step * hp, hp), :]
        high = rate.astype(BF16).astype(F32)
        pad = jnp.zeros((EXTRA - 2 * hp, 128), F32)
        tail = jnp.concatenate([high, rate - high, pad], axis=0).astype(BF16)
        for x, last_ref in enumerate(last_refs):

            @pl.when((step ^ (me % MEMBERS)) == x)
            def _():
                for i in range(hp):
                    last_ref[i * 128 : (i + 1) * 128, :] = last_states[i]
                last_ref[hp * 128 :, :] = tail


def piece_states(doc_lengths, owner_ids, decay_rows, keys, values, spread=0):
    heads, rows = decay_rows.shape
    by_owner = spread > 0
    hp = 2 if by_owner else heads // MEMBERS
    slots = spread if by_owner else SIDE + 1
    wide = pl.BlockSpec((rows, hp * 128), lambda j: (0, j))
    scratch = [pltpu.VMEM((heads, rows), F32), pltpu.VMEM((slots, 16, rows), BF16)]
    if by_owner:
        shapes = [jax.ShapeDtypeStruct((slots, heads, 128, 128), BF16), jax.ShapeDtypeStruct((heads, rows), F32)]
        specs = [pl.BlockSpec((slots, hp, 128, 128), lambda j: (0, j, 0, 0)), whole((heads, rows))]
    else:
        last = (hp * 128 + EXTRA, 128)
        shapes = [
            *[jax.ShapeDtypeStruct((MEMBERS, n * hp * 128, 128), BF16) for n in SENT],
            jax.ShapeDtypeStruct((heads, rows), F32),
            jax.ShapeDtypeStruct((4,), jnp.int32),
            *[jax.ShapeDtypeStruct(last, BF16)] * MEMBERS,
        ]
        specs = [pl.BlockSpec((1, n * hp * 128, 128), lambda j: (j, 0, 0)) for n in SENT]
        specs += [whole((heads, rows)), SMEM] + [whole(last)] * MEMBERS
        scratch.append(pltpu.VMEM((heads, 128), F32))
    return pl.pallas_call(
        functools.partial(pieces_kernel, by_owner),
        grid=(heads // hp,),
        in_specs=[SMEM, SMEM, whole((heads, rows)), wide, wide],
        out_specs=specs,
        out_shape=shapes,
        scratch_shapes=scratch,
        compiler_params=LIMIT,
        cost_estimate=pl.CostEstimate(
            flops=slots * heads * rows * 128 * 256, bytes_accessed=rows * heads * 128 * 4, transcendentals=heads * rows
        ),
        name="piece_states",
    )(doc_lengths, owner_ids, decay_rows, keys, values)


def head_column(ccol_ref, h):
    cols = ccol_ref[...]
    return jnp.sum(jnp.where(iota(cols.shape, 1) == h, cols, 0.0), axis=1, keepdims=True)


def fill_columns(crow_ref, ccol_ref):
    heads, rows = crow_ref.shape
    for r0 in range(0, rows, 128):
        part = crow_ref[:, r0 : r0 + 128]
        part = jnp.concatenate([part, jnp.zeros((128 - heads, 128), F32)], axis=0)
        ccol_ref[r0 : r0 + 128, :] = part.T


def fill_bias(first, ends, bias_ref):
    for c in range(bias_ref.shape[0] // CHUNK):
        base = first + c * CHUNK
        t_pos = base + iota((CHUNK, 1), 0)
        start = run_start(ends, t_pos)
        s_pos = base + iota((CHUNK, CHUNK), 1)
        keep = (s_pos <= t_pos) & (s_pos >= start)
        bias_ref[c * CHUNK : (c + 1) * CHUNK, :] = jnp.where(keep, math.log2(SCALE), NEG)


def attend(first, ends, q_ref, k_ref, v_ref, h, crow_ref, ccol_ref, bias_ref, states, emit):
    rows = q_ref.shape[0]
    pair = range(2)
    half = CHUNK // 2
    lanes = [slice(i * 128, (i + 1) * 128) for i in pair]
    row_all = [crow_ref[pl.ds(h + i, 1), :] for i in pair]
    col_all = [head_column(ccol_ref, h + i) for i in pair]
    starts = range(0, rows, CHUNK)
    spans = [slice(r0, r0 + CHUNK) for r0 in starts]
    reach = [run_end(ends, first + r0 - 1) - (first + r0) for r0 in starts]
    base = [[row_all[i][:, r0 - 1 : r0] if r0 else jnp.zeros((1, 1), F32) for r0 in starts] for i in pair]

    fresh = [[], []]
    for c, r0 in enumerate(starts[:-1]):
        since = run_start(ends, first + r0 + CHUNK - 1) - (first + r0)
        inside = iota((1, CHUNK), 1) >= since
        for i in pair:
            row = row_all[i][:, spans[c]]
            weight = jnp.exp2(jnp.where(inside, row[:, CHUNK - 1 :] - row, NEG) + math.log2(SCALE))
            flipped = k_ref[spans[c], lanes[i]].T
            fresh[i].append(dot((flipped.astype(F32) * weight).astype(BF16), v_ref[spans[c], lanes[i]]))
    carried = []
    for i in pair:
        state, chain = states[i], [states[i].astype(BF16)]
        for c in range(len(starts) - 1):
            total = row_all[i][:, starts[c] + CHUNK - 1 : starts[c] + CHUNK]
            state = fresh[i][c] + state * jnp.exp2(jnp.where(CHUNK <= reach[c], total - base[i][c], NEG))
            chain.append(state.astype(BF16))
        carried.append(chain)

    def products(c):
        result = []
        for i in pair:
            query = q_ref[spans[c], lanes[i]]
            scores = dot(query, k_ref[spans[c], lanes[i]], ((1,), (1,)))
            result.append((scores, dot(query, carried[i][c])))
        return result

    ahead = products(0)
    for c, r0 in enumerate(starts):
        current = ahead
        if c + 1 < len(starts):
            ahead = products(c + 1)
        for part in range(2):
            t0, width = part * half, (part + 1) * half
            rows_here = slice(r0 + t0, r0 + t0 + half)
            for i in pair:
                scores, carry = current[i]
                col = col_all[i][rows_here]
                decay = jnp.exp2((col - row_all[i][:, r0 : r0 + width]) + bias_ref[rows_here, :width])
                weights = (scores[t0 : t0 + half, :width] * decay).astype(BF16)
                att = dot(weights, v_ref[r0 : r0 + width, lanes[i]])
                lead = jnp.exp2(jnp.where(t0 + iota((half, 1), 0) < reach[c], col - base[i][c], NEG))
                emit(lanes[i], r0 + t0, half, att + lead * carry[t0 : t0 + half])


def gather_last(refs, last_ref):
    me = lax.axis_index("seq") % MEMBERS
    for x, ref in enumerate(refs):
        last_ref[me ^ x] = ref[...]


def decay_of(last_ref, e, i, hp):
    extra = last_ref[e, hp * 128 :, :].astype(F32)
    return extra[i : i + 1, :] + extra[hp + i : hp + i + 1, :]


def scan_quad(rows, len_ref, last_ref, state, i, hp, note):
    members = last_ref.shape[0]
    ends = read_ends(len_ref, len_ref.shape[0])
    base = lax.axis_index("seq") // members * members
    for e in range(members):
        note(e, state)
        low = (base + e) * rows
        inner = jnp.int32(0)
        for end in ends:
            inner = inner + ((end > low) & (end < low + rows)).astype(jnp.int32)
        passes = (inner == 0).astype(F32)
        piece = last_ref[e, i * 128 : (i + 1) * 128, :].astype(F32)
        state = state * (decay_of(last_ref, e, i, hp) * passes) + piece
    return state


def leave_kernel(rows, len_ref, *refs):
    out_ref, last_ref = refs[-2:]
    gather_last(refs[:MEMBERS], last_ref)
    hp = out_ref.shape[0]
    for i in range(hp):
        state = jnp.zeros((128, 128), F32)
        if len(refs) > MEMBERS + 2:
            state = refs[MEMBERS][i].astype(F32)
        state = scan_quad(rows, len_ref, last_ref, state, i, hp, lambda e, x: None)
        out_ref[i] = state.astype(BF16)


def leave_quad(doc_lengths, last, coming, rows, hp):
    return pl.pallas_call(
        functools.partial(leave_kernel, rows),
        in_specs=[SMEM] + [VMEM] * (MEMBERS + len(coming)),
        out_specs=VMEM,
        out_shape=jax.ShapeDtypeStruct((hp, 128, 128), BF16),
        scratch_shapes=[pltpu.VMEM((MEMBERS,) + last[0].shape, BF16)],
        compiler_params=SMALL,
        name="leave_quad",
    )(doc_lengths, *last, *coming)


def enter_kernel(rows, len_ref, *refs):
    in_ref, out_refs, last_ref, state_ref = refs[MEMBERS], refs[MEMBERS + 1 : -2], refs[-2], refs[-1]
    gather_last(refs[:MEMBERS], last_ref)
    hp = in_ref.shape[0]

    def note(i, e, state):
        state_ref[e, i] = state

    for i in range(hp):
        scan_quad(rows, len_ref, last_ref, in_ref[i].astype(F32), i, hp, functools.partial(note, i))
    me = lax.axis_index("seq") % MEMBERS
    for x, out_ref in enumerate(out_refs):
        out_ref[...] = state_ref[me ^ x].astype(BF16)


def enter_states(doc_lengths, last, coming, rows):
    return pl.pallas_call(
        functools.partial(enter_kernel, rows),
        in_specs=[SMEM] + [VMEM] * (MEMBERS + 1),
        out_specs=[VMEM] * MEMBERS,
        out_shape=[jax.ShapeDtypeStruct(coming.shape, BF16)] * MEMBERS,
        scratch_shapes=[
            pltpu.VMEM((MEMBERS,) + last[0].shape, BF16),
            pltpu.VMEM((MEMBERS,) + coming.shape, F32),
        ],
        compiler_params=SMALL,
        name="enter_states",
    )(doc_lengths, *last, coming)


def final_kernel(rows, len_ref, own_ref, *refs):
    side1_ref, side2_ref, in_ref, out_ref, last_ref, state_ref = refs[MEMBERS:]
    gather_last(refs[:MEMBERS], last_ref)
    hp = in_ref.shape[0]
    ends = read_ends(len_ref, len_ref.shape[0])
    base = lax.axis_index("seq") // MEMBERS * MEMBERS

    def note(i, e, state):
        state_ref[e, i] = state

    for i in range(hp):
        scan_quad(rows, len_ref, last_ref, in_ref[i].astype(F32), i, hp, functools.partial(note, i))
    out_ref[...] = jnp.zeros_like(out_ref)
    place, previous = jnp.int32(0), jnp.int32(-1)
    for d in range(len(ends)):
        device = (ends[d] - 1) // rows
        place = jnp.where(device == previous, place + 1, 0)
        previous = device
        at_end = ends[d] == (device + 1) * rows
        enters = (place == 0).astype(F32)
        mine = device // MEMBERS * MEMBERS == base
        e = device - base

        def put(i, local):
            state = local.astype(F32) + state_ref[e, i] * (decay_of(last_ref, e, i, hp) * enters)
            out_ref[own_ref[d], i] = state.astype(BF16)

        @pl.when(mine & at_end)
        def _():
            for i in range(hp):
                put(i, last_ref[e, i * 128 : (i + 1) * 128, :])

        @pl.when(mine & jnp.logical_not(at_end) & (place < SENT[0]))
        def _():
            for i in range(hp):
                put(i, side1_ref[e, pl.ds(pl.multiple_of((place * hp + i) * 128, 128), 128), :])

        @pl.when(mine & jnp.logical_not(at_end) & (place >= SENT[0]))
        def _():
            slot = jnp.minimum(place - SENT[0], SENT[1] - 1)
            for i in range(hp):
                put(i, side2_ref[e, pl.ds(pl.multiple_of((slot * hp + i) * 128, 128), 128), :])


def final_states(doc_lengths, owner_ids, last, side, coming, rows, spread):
    return pl.pallas_call(
        functools.partial(final_kernel, rows),
        in_specs=[SMEM, SMEM] + [VMEM] * (MEMBERS + 3),
        out_specs=VMEM,
        out_shape=jax.ShapeDtypeStruct((spread,) + coming.shape, BF16),
        scratch_shapes=[
            pltpu.VMEM((MEMBERS,) + last[0].shape, BF16),
            pltpu.VMEM((MEMBERS,) + coming.shape, F32),
        ],
        compiler_params=SMALL,
        name="final_states",
    )(doc_lengths, owner_ids, *last, *side, coming)


def finish_kernel(len_ref, q_ref, k_ref, v_ref, e0, e1, e2, e3, gate_ref, gain_ref, crow_ref, out_ref, bias_ref, ccol_ref):
    rows = q_ref.shape[0]
    step = pl.program_id(0)
    me = lax.axis_index("seq")
    first = me * rows
    ends = read_ends(len_ref, len_ref.shape[0])
    hp = e0.shape[0]

    def entering(h):
        far = (h // hp) ^ (me % MEMBERS)
        state = e0[h % hp]
        for x, ref in ((1, e1), (2, e2), (3, e3)):
            state = jnp.where(far == x, ref[h % hp], state)
        return state

    def emit(lanes, t0, size, att):
        mean = jnp.mean(att * att, axis=1, keepdims=True)
        gate = 0.5 + 0.5 * jnp.tanh(0.5 * gate_ref[t0 : t0 + size, lanes].astype(F32))
        gain = gain_ref[:, lanes].astype(F32)
        out_ref[t0 : t0 + size, lanes] = (att * lax.rsqrt(mean + 1e-06) * (gain * gate)).astype(BF16)

    @pl.when(step == 0)
    def _():
        fill_bias(first, ends, bias_ref)
        fill_columns(crow_ref, ccol_ref)

    states = [entering(step * 2 + i).astype(F32) for i in range(2)]
    attend(first, ends, q_ref, k_ref, v_ref, step * 2, crow_ref, ccol_ref, bias_ref, states, emit)


def finish(doc_lengths, queries, keys, values, entering, gate, gain, crow):
    heads, rows = crow.shape
    wide = pl.BlockSpec((rows, 256), lambda j: (0, j))
    return pl.pallas_call(
        finish_kernel,
        grid=(heads // 2,),
        in_specs=[SMEM, wide, wide, wide]
        + [whole(e.shape) for e in entering]
        + [wide, pl.BlockSpec((1, 256), lambda j: (0, j)), whole((heads, rows))],
        out_specs=wide,
        out_shape=jax.ShapeDtypeStruct((rows, heads * 128), BF16),
        scratch_shapes=[pltpu.VMEM((rows, CHUNK), F32), pltpu.VMEM((rows, 128), F32)],
        compiler_params=pltpu.CompilerParams(vmem_limit_bytes=54 * 2**20),
        cost_estimate=pl.CostEstimate(
            flops=heads * rows * CHUNK * 128 * 8, bytes_accessed=rows * heads * 128 * 10, transcendentals=heads * rows * CHUNK
        ),
        name="finish",
    )(doc_lengths, queries, keys, values, *entering, gate, gain, crow)


def swap(x, groups=None):
    return lax.all_to_all(x, "seq", split_axis=0, concat_axis=0, axis_index_groups=groups, tiled=True)


def by_distance(parcels, spread):
    return [parcels[0]] + [
        lax.ppermute(parcels[x], "seq", [(s, s ^ x) for s in range(spread)]) for x in range(1, MEMBERS)
    ]


def on_device(spread, queries, keys, values, log_decay, gate, gain, doc_lengths, owner_ids):
    rows, heads = log_decay.shape
    quads = spread // MEMBERS
    hp = heads // MEMBERS
    near = [[q * MEMBERS + m for m in range(MEMBERS)] for q in range(quads)]
    onward = [(s, s + MEMBERS) for s in range(spread - MEMBERS)]
    decay_rows = log_decay.T
    barrier = lax.optimization_barrier

    side1, side2, crow, flags, *last = piece_states(doc_lengths, owner_ids, decay_rows, keys, values)
    last = by_distance(last, spread)
    side1, last[1] = barrier((side1, last[1]))
    side1 = swap(side1, near)
    side2, side1 = barrier((side2, side1))
    side2 = swap(side2, near)

    coming = []
    for _ in range(quads - 1):
        leaving = leave_quad(doc_lengths, last, coming, rows, hp)
        coming = [lax.ppermute(leaving, "seq", onward)]
    flags, gain, leaving = barrier((flags, gain, leaving))
    gain = gain.reshape(1, -1)

    def send_rest():
        rest, _ = piece_states(doc_lengths, owner_ids, decay_rows, keys, values, spread)
        return lax.dynamic_index_in_dim(swap(rest), flags[3], 0, True)

    rest = lax.cond(flags[2] > 0, send_rest, lambda: jnp.zeros((1, heads, 128, 128), BF16))
    from_quad = [flags[0] == q for q in range(1, quads)]
    coming, rest, gain, late, from_quad = barrier((coming[0], rest, gain, flags[1] > 0, from_quad))

    entering = by_distance(enter_states(doc_lengths, last, coming, rows), spread)
    finals = final_states(doc_lengths, owner_ids, last, [side1, side2], coming, rows, spread)
    entering, finals = barrier((entering, finals))
    arrived = swap(finals).reshape(quads, 1, heads, 128, 128)
    mixed = finish(doc_lengths, queries, keys, values, entering, gate, gain, crow)
    owned = arrived[0]
    for q in range(1, quads):
        owned = jnp.where(from_quad[q - 1], arrived[q], owned)
    return mixed, jnp.where(late, rest, owned)


def solution(mesh):
    placed = (
        P(("groups", "seq"), "tp"),
        P(("groups", "seq"), "tp"),
        P(("groups", "seq"), "tp"),
        P(("groups", "seq"), "tp"),
        P(("groups", "seq"), "tp"),
        P("tp"),
        P("groups"),
        P("groups"),
    )
    return jax.shard_map(
        functools.partial(on_device, mesh.shape["seq"]),
        mesh=mesh,
        in_specs=placed,
        out_specs=(P(("groups", "seq"), "tp"), P(("groups", "seq"), "tp", None, None)),
        check_vma=False,
    )
```

```python
import functools
import math

import jax
import jax.numpy as jnp
from jax import lax
from jax.experimental import pallas as pl
from jax.experimental.pallas import tpu as pltpu
from jax.sharding import PartitionSpec as P

BLK = 512
SIDE = 3
SENT = (2, 1)
EXTRA = 16
CHUNK = 256
MEMBERS = 4
TILE = 256
EARLY = (4, 4)
NEG = -1e30
LOG2E = math.log2(math.e)
SCALE = 128**-0.5
F32, BF16 = jnp.float32, jnp.bfloat16
SMEM = pl.BlockSpec(memory_space=pltpu.SMEM)
VMEM = pl.BlockSpec(memory_space=pltpu.VMEM)
LIMIT = pltpu.CompilerParams(vmem_limit_bytes=60 * 2**20)
SMALL = pltpu.CompilerParams(vmem_limit_bytes=48 * 2**20)


def dot(a, b, contract=((1,), (0,))):
    return lax.dot_general(a, b, (contract, ((), ())), preferred_element_type=F32)


def iota(shape, dim):
    return lax.broadcasted_iota(jnp.int32, shape, dim)


def read_ends(len_ref, count):
    ends, total = [], jnp.int32(0)
    for d in range(count):
        total = total + len_ref[d]
        ends.append(total)
    return ends


def run_end(ends, pos):
    best = ends[-1]
    for e in reversed(ends[:-1]):
        best = jnp.where(e > pos, e, best)
    return best


def run_start(ends, pos):
    best = jnp.zeros_like(pos)
    for e in ends[:-1]:
        best = jnp.where(e <= pos, e, best)
    return best


def split3(x):
    hi = x.astype(BF16)
    rest = x - hi.astype(F32)
    mid = rest.astype(BF16)
    return hi, mid, (rest - mid.astype(F32)).astype(BF16)


def cum_rows(ld_ref, crow_ref):
    heads, rows = ld_ref.shape
    upper = (iota((BLK, BLK), 0) <= iota((BLK, BLK), 1)).astype(F32).astype(BF16)
    base = jnp.zeros((heads, 1), F32)
    for b in range(rows // BLK):
        part = ld_ref[:, b * BLK : (b + 1) * BLK] * LOG2E
        sums = dot(jnp.concatenate(split3(part), axis=0), upper)
        row = sums[2 * heads :] + sums[heads : 2 * heads] + sums[:heads] + base
        crow_ref[:, b * BLK : (b + 1) * BLK] = row
        base = row[:, BLK - 1 :]


def value_at(cum, at, index):
    return jnp.sum(jnp.where(at == index, cum, 0.0), axis=1, keepdims=True)


def span_weights(cum, at, low, high):
    inside = (at >= low) & (at <= high)
    return jnp.exp2(jnp.where(inside, value_at(cum, at, high) - cum, NEG) + math.log2(SCALE))


def weigh(flipped, w_ref, h):
    weights = [jnp.broadcast_to(w_ref[pl.ds(h + j, 1), :], (128, flipped.shape[1])) for j in range(2)]
    return (flipped.astype(F32) * jnp.concatenate(weights, axis=0)).astype(BF16)


def whole(shape):
    return pl.BlockSpec(shape, lambda j: (0,) * len(shape))


def pieces_kernel(by_owner, len_ref, own_ref, ld_ref, k_ref, v_ref, *refs):
    if by_owner:
        side_ref, crow_ref, w_ref, keep_ref = refs
        slots = keep_ref.shape[0]
    else:
        side_refs, crow_ref, flag_ref = refs[:2], refs[2], refs[3]
        last_refs = refs[4 : 4 + MEMBERS]
        w_ref, first_ref, high_ref, weighted_ref, prefix_ref = refs[4 + MEMBERS :]
        slots = SIDE
    heads, rows = crow_ref.shape
    step = pl.program_id(0)
    hp = v_ref.shape[1] // 128
    me = lax.axis_index("seq")

    @pl.when(step == 0)
    def _():
        cum_rows(ld_ref, crow_ref)
        first = me * rows
        last = first + rows - 1
        ends = read_ends(len_ref, len_ref.shape[0])
        starts = [jnp.int32(0)] + ends[:-1]
        lows = [jnp.int32(0)] * slots
        highs = [jnp.int32(-1)] * slots
        place, rank, previous = jnp.int32(0), jnp.int32(0), jnp.int32(-1)
        crowded, owned_in, owned_late = jnp.int32(0), jnp.int32(0), jnp.int32(0)
        for d in range(len(ends)):
            here = (ends[d] > first) & (ends[d] <= last)
            low = jnp.maximum(starts[d] - first, 0)
            for s in range(slots):
                mine = here & ((place >= SIDE) & (own_ref[d] == s) if by_owner else (place == s))
                lows[s] = jnp.where(mine, low, lows[s])
                highs[s] = jnp.where(mine, ends[d] - 1 - first, highs[s])
            place = place + here.astype(jnp.int32)
            device = (ends[d] - 1) // rows
            rank = jnp.where(device == previous, rank + 1, 0)
            previous = device
            late = ((rank >= SIDE) & (ends[d] != (device + 1) * rows)).astype(jnp.int32)
            crowded = jnp.maximum(crowded, late)
            owned_in = jnp.where(own_ref[d] == me, device, owned_in)
            owned_late = jnp.where(own_ref[d] == me, late, owned_late)
        at = iota((heads, rows), 1)
        cum = crow_ref[...]
        total = jnp.zeros((heads, rows), F32)
        for s in range(slots):
            total = total + span_weights(cum, at, lows[s], highs[s])
        if by_owner:
            row_at = iota((16, rows), 1)
            for s in range(slots):
                inside = (row_at >= lows[s]) & (row_at <= highs[s])
                keep_ref[s] = jnp.where(inside, 1.0, 0.0).astype(BF16)
        else:
            total = total + span_weights(cum, at, jnp.maximum(run_start(ends, last) - first, 0), rows - 1)
            flag_ref[0] = owned_in // MEMBERS
            flag_ref[1] = owned_late
            flag_ref[2] = crowded
            flag_ref[3] = owned_in
            high = jnp.int32(-1)
            for s in range(slots):
                high = jnp.maximum(high, highs[s])
                high_ref[s] = high
            stop = jnp.minimum(run_end(ends, first) - 1 - first, rows - 1)
            goes_on = (run_start(ends, first) < first).astype(F32)
            first_ref[...] = jnp.broadcast_to(jnp.exp2(value_at(cum, at, stop)) * goes_on, (heads, 128))
        w_ref[...] = total

    def own(states, j):
        return states[j * 128 : (j + 1) * 128, j * 128 : (j + 1) * 128]

    if by_owner:
        weighted = weigh(k_ref[...].T, w_ref, step * hp).reshape(16, 16, rows)
        for s in range(slots):
            states = dot((weighted * keep_ref[s][None]).reshape(256, rows), v_ref[...])
            for j in range(2):
                side_ref[s, j] = own(states, j).astype(BF16)
        return

    pairs = range(0, hp, 2)
    lanes = {i: slice(i * 128, (i + 2) * 128) for i in pairs}
    for i in pairs:
        weighted_ref[lanes[i], :] = weigh(k_ref[:, lanes[i]].T, w_ref, step * hp + i)
    totals = {}
    for i in pairs:
        sums = [jnp.zeros((128, 128), F32)] * 2
        for t in range(rows // TILE):
            span = slice(t * TILE, (t + 1) * TILE)
            states = dot(weighted_ref[lanes[i], span], v_ref[span, lanes[i]])
            for j in range(2):
                prefix_ref[t, i + j] = sums[j]
                sums[j] = sums[j] + own(states, j)
        totals[i] = sums
    ended = {i: [jnp.zeros((128, 128), F32)] * 2 for i in pairs}
    for s in range(slots):
        high = high_ref[s]
        tile = jnp.maximum(high, 0) // TILE
        start = pl.multiple_of(tile * TILE, TILE)
        keep = jnp.where(start + iota((16, TILE), 1) <= high, 1.0, 0.0).astype(BF16)
        part, slot = (0, s) if s < SENT[0] else (1, s - SENT[0])
        for i in pairs:
            kept = weighted_ref[lanes[i], pl.ds(start, TILE)].reshape(16, 16, TILE) * keep[None]
            states = dot(kept.reshape(256, TILE), v_ref[pl.ds(start, TILE), lanes[i]])
            for j in range(2):
                until = own(states, j) + prefix_ref[tile, i + j]
                at = (slot * hp + i + j) * 128
                side_refs[part][0, at : at + 128, :] = (until - ended[i][j]).astype(BF16)
                ended[i][j] = until
    rate = first_ref[pl.ds(step * hp, hp), :]
    high = rate.astype(BF16).astype(F32)
    pad = jnp.zeros((EXTRA - 2 * hp, 128), F32)
    tail = jnp.concatenate([high, rate - high, pad], axis=0).astype(BF16)
    last_states = [(totals[i][j] - ended[i][j]).astype(BF16) for i in pairs for j in range(2)]
    for x, last_ref in enumerate(last_refs):

        @pl.when((step ^ (me % MEMBERS)) == x)
        def _():
            for i in range(hp):
                last_ref[i * 128 : (i + 1) * 128, :] = last_states[i]
            last_ref[hp * 128 :, :] = tail


def piece_states(doc_lengths, owner_ids, decay_rows, keys, values, spread=0):
    heads, rows = decay_rows.shape
    by_owner = spread > 0
    hp = 2 if by_owner else heads // MEMBERS
    wide = pl.BlockSpec((rows, hp * 128), lambda j: (0, j))
    scratch = [pltpu.VMEM((heads, rows), F32)]
    if by_owner:
        shapes = [jax.ShapeDtypeStruct((spread, heads, 128, 128), BF16), jax.ShapeDtypeStruct((heads, rows), F32)]
        specs = [pl.BlockSpec((spread, hp, 128, 128), lambda j: (0, j, 0, 0)), whole((heads, rows))]
        scratch.append(pltpu.VMEM((spread, 16, rows), BF16))
    else:
        last = (hp * 128 + EXTRA, 128)
        shapes = [
            *[jax.ShapeDtypeStruct((MEMBERS, n * hp * 128, 128), BF16) for n in SENT],
            jax.ShapeDtypeStruct((heads, rows), F32),
            jax.ShapeDtypeStruct((4,), jnp.int32),
            *[jax.ShapeDtypeStruct(last, BF16)] * MEMBERS,
        ]
        specs = [pl.BlockSpec((1, n * hp * 128, 128), lambda j: (j, 0, 0)) for n in SENT]
        specs += [whole((heads, rows)), SMEM] + [whole(last)] * MEMBERS
        scratch += [
            pltpu.VMEM((heads, 128), F32),
            pltpu.SMEM((SIDE,), jnp.int32),
            pltpu.VMEM((hp * 128, rows), BF16),
            pltpu.VMEM((rows // TILE, hp, 128, 128), F32),
        ]
    return pl.pallas_call(
        functools.partial(pieces_kernel, by_owner),
        grid=(heads // hp,),
        in_specs=[SMEM, SMEM, whole((heads, rows)), wide, wide],
        out_specs=specs,
        out_shape=shapes,
        scratch_shapes=scratch,
        compiler_params=LIMIT,
        cost_estimate=pl.CostEstimate(
            flops=2 * heads * rows * 128 * 256, bytes_accessed=rows * heads * 128 * 4, transcendentals=heads * rows
        ),
        name="piece_states",
    )(doc_lengths, owner_ids, decay_rows, keys, values)


def head_column(ccol_ref, h):
    cols = ccol_ref[...]
    return jnp.sum(jnp.where(iota(cols.shape, 1) == h, cols, 0.0), axis=1, keepdims=True)


def fill_columns(crow_ref, ccol_ref):
    heads, rows = crow_ref.shape
    for r0 in range(0, rows, 128):
        part = crow_ref[:, r0 : r0 + 128]
        part = jnp.concatenate([part, jnp.zeros((128 - heads, 128), F32)], axis=0)
        ccol_ref[r0 : r0 + 128, :] = part.T


def fill_bias(first, ends, bias_ref):
    for c in range(bias_ref.shape[0] // CHUNK):
        base = first + c * CHUNK
        t_pos = base + iota((CHUNK, 1), 0)
        start = run_start(ends, t_pos)
        s_pos = base + iota((CHUNK, CHUNK), 1)
        keep = (s_pos <= t_pos) & (s_pos >= start)
        bias_ref[c * CHUNK : (c + 1) * CHUNK, :] = jnp.where(keep, math.log2(SCALE), NEG)


def attend(first, ends, q_ref, k_ref, v_ref, h, crow_ref, ccol_ref, bias_ref, states, emit):
    rows = q_ref.shape[0]
    pair = range(2)
    half = CHUNK // 2
    lanes = [slice(i * 128, (i + 1) * 128) for i in pair]
    row_all = [crow_ref[pl.ds(h + i, 1), :] for i in pair]
    col_all = [head_column(ccol_ref, h + i) for i in pair]
    starts = range(0, rows, CHUNK)
    spans = [slice(r0, r0 + CHUNK) for r0 in starts]
    reach = [run_end(ends, first + r0 - 1) - (first + r0) for r0 in starts]
    base = [[row_all[i][:, r0 - 1 : r0] if r0 else jnp.zeros((1, 1), F32) for r0 in starts] for i in pair]

    fresh = [[], []]
    for c, r0 in enumerate(starts[:-1]):
        since = run_start(ends, first + r0 + CHUNK - 1) - (first + r0)
        inside = iota((1, CHUNK), 1) >= since
        for i in pair:
            row = row_all[i][:, spans[c]]
            weight = jnp.exp2(jnp.where(inside, row[:, CHUNK - 1 :] - row, NEG) + math.log2(SCALE))
            flipped = k_ref[spans[c], lanes[i]].T
            fresh[i].append(dot((flipped.astype(F32) * weight).astype(BF16), v_ref[spans[c], lanes[i]]))
    carried = []
    for i in pair:
        state = None if states is None else states[i]
        chain = [None if state is None else state.astype(BF16)]
        for c in range(len(starts) - 1):
            if state is None:
                state = fresh[i][c]
            else:
                total = row_all[i][:, starts[c] + CHUNK - 1 : starts[c] + CHUNK]
                state = fresh[i][c] + state * jnp.exp2(jnp.where(CHUNK <= reach[c], total - base[i][c], NEG))
            chain.append(state.astype(BF16))
        carried.append(chain)

    def products(c):
        result = []
        for i in pair:
            query = q_ref[spans[c], lanes[i]]
            scores = dot(query, k_ref[spans[c], lanes[i]], ((1,), (1,)))
            result.append((scores, None if carried[i][c] is None else dot(query, carried[i][c])))
        return result

    ahead = products(0)
    for c, r0 in enumerate(starts):
        current = ahead
        if c + 1 < len(starts):
            ahead = products(c + 1)
        for part in range(2):
            t0, width = part * half, (part + 1) * half
            rows_here = slice(r0 + t0, r0 + t0 + half)
            for i in pair:
                scores, carry = current[i]
                col = col_all[i][rows_here]
                decay = jnp.exp2((col - row_all[i][:, r0 : r0 + width]) + bias_ref[rows_here, :width])
                weights = (scores[t0 : t0 + half, :width] * decay).astype(BF16)
                att = dot(weights, v_ref[r0 : r0 + width, lanes[i]])
                if carry is not None:
                    lead = jnp.exp2(jnp.where(t0 + iota((half, 1), 0) < reach[c], col - base[i][c], NEG))
                    att = att + lead * carry[t0 : t0 + half]
                emit(lanes[i], r0 + t0, half, att)


def early_kernel(pairs_before, len_ref, q_ref, k_ref, v_ref, crow_ref, *refs):
    out_ref, bias_ref, ccol_ref = refs[-3:]
    rows = q_ref.shape[0]
    step = pl.program_id(0)
    first = lax.axis_index("seq") * rows
    ends = read_ends(len_ref, len_ref.shape[0])

    @pl.when(step == 0)
    def _():
        fill_bias(first, ends, bias_ref)
        fill_columns(crow_ref, ccol_ref)

    def emit(lanes, t0, size, att):
        out_ref[t0 : t0 + size, lanes] = att

    attend(first, ends, q_ref, k_ref, v_ref, (step + pairs_before) * 2, crow_ref, ccol_ref, bias_ref, None, emit)


def early_attention(doc_lengths, queries, keys, values, crow, before, part):
    heads, rows = crow.shape
    skip = sum(EARLY[:part]) // 2
    wide = pl.BlockSpec((rows, 256), lambda j: (0, j + skip))
    count = EARLY[part]
    return pl.pallas_call(
        functools.partial(early_kernel, skip),
        grid=(count // 2,),
        in_specs=[SMEM, wide, wide, wide, whole((heads, rows))] + [pl.BlockSpec(memory_space=pl.ANY)] * len(before),
        out_specs=wide,
        out_shape=jax.ShapeDtypeStruct((rows, sum(EARLY) * 128), F32),
        input_output_aliases={5: 0} if before else {},
        scratch_shapes=[pltpu.VMEM((rows, CHUNK), F32), pltpu.VMEM((rows, 128), F32)],
        compiler_params=LIMIT,
        cost_estimate=pl.CostEstimate(
            flops=count * rows * CHUNK * 128 * 8, bytes_accessed=rows * count * 128 * 10, transcendentals=count * rows * CHUNK
        ),
        name="early_attention",
    )(doc_lengths, queries, keys, values, crow, *before)


def gather_last(refs, last_ref):
    me = lax.axis_index("seq") % MEMBERS
    for x, ref in enumerate(refs):
        last_ref[me ^ x] = ref[...]


def decay_of(last_ref, e, i, hp):
    extra = last_ref[e, hp * 128 :, :].astype(F32)
    return extra[i : i + 1, :] + extra[hp + i : hp + i + 1, :]


def scan_quad(rows, len_ref, last_ref, state, i, hp, note):
    members = last_ref.shape[0]
    ends = read_ends(len_ref, len_ref.shape[0])
    base = lax.axis_index("seq") // members * members
    for e in range(members):
        note(e, state)
        low = (base + e) * rows
        inner = jnp.int32(0)
        for end in ends:
            inner = inner + ((end > low) & (end < low + rows)).astype(jnp.int32)
        passes = (inner == 0).astype(F32)
        piece = last_ref[e, i * 128 : (i + 1) * 128, :].astype(F32)
        state = state * (decay_of(last_ref, e, i, hp) * passes) + piece
    return state


def leave_kernel(rows, len_ref, *refs):
    out_ref, last_ref = refs[-2:]
    gather_last(refs[:MEMBERS], last_ref)
    hp = out_ref.shape[0]
    for i in range(hp):
        state = jnp.zeros((128, 128), F32)
        if len(refs) > MEMBERS + 2:
            state = refs[MEMBERS][i].astype(F32)
        state = scan_quad(rows, len_ref, last_ref, state, i, hp, lambda e, x: None)
        out_ref[i] = state.astype(BF16)


def leave_quad(doc_lengths, last, coming, rows, hp):
    return pl.pallas_call(
        functools.partial(leave_kernel, rows),
        in_specs=[SMEM] + [VMEM] * (MEMBERS + len(coming)),
        out_specs=VMEM,
        out_shape=jax.ShapeDtypeStruct((hp, 128, 128), BF16),
        scratch_shapes=[pltpu.VMEM((MEMBERS,) + last[0].shape, BF16)],
        compiler_params=SMALL,
        name="leave_quad",
    )(doc_lengths, *last, *coming)


def enter_kernel(rows, len_ref, *refs):
    in_ref, out_refs, last_ref, state_ref = refs[MEMBERS], refs[MEMBERS + 1 : -2], refs[-2], refs[-1]
    gather_last(refs[:MEMBERS], last_ref)
    hp = in_ref.shape[0]

    def note(i, e, state):
        state_ref[e, i] = state

    for i in range(hp):
        scan_quad(rows, len_ref, last_ref, in_ref[i].astype(F32), i, hp, functools.partial(note, i))
    me = lax.axis_index("seq") % MEMBERS
    for x, out_ref in enumerate(out_refs):
        out_ref[...] = state_ref[me ^ x].astype(BF16)


def enter_states(doc_lengths, last, coming, rows):
    return pl.pallas_call(
        functools.partial(enter_kernel, rows),
        in_specs=[SMEM] + [VMEM] * (MEMBERS + 1),
        out_specs=[VMEM] * MEMBERS,
        out_shape=[jax.ShapeDtypeStruct(coming.shape, BF16)] * MEMBERS,
        scratch_shapes=[
            pltpu.VMEM((MEMBERS,) + last[0].shape, BF16),
            pltpu.VMEM((MEMBERS,) + coming.shape, F32),
        ],
        compiler_params=SMALL,
        name="enter_states",
    )(doc_lengths, *last, coming)


def final_kernel(rows, len_ref, own_ref, *refs):
    side1_ref, side2_ref, in_ref, out_ref, last_ref, state_ref = refs[MEMBERS:]
    gather_last(refs[:MEMBERS], last_ref)
    hp = in_ref.shape[0]
    ends = read_ends(len_ref, len_ref.shape[0])
    base = lax.axis_index("seq") // MEMBERS * MEMBERS

    def note(i, e, state):
        state_ref[e, i] = state

    for i in range(hp):
        scan_quad(rows, len_ref, last_ref, in_ref[i].astype(F32), i, hp, functools.partial(note, i))
    out_ref[...] = jnp.zeros_like(out_ref)
    place, previous = jnp.int32(0), jnp.int32(-1)
    for d in range(len(ends)):
        device = (ends[d] - 1) // rows
        place = jnp.where(device == previous, place + 1, 0)
        previous = device
        at_end = ends[d] == (device + 1) * rows
        enters = (place == 0).astype(F32)
        mine = device // MEMBERS * MEMBERS == base
        e = device - base

        def put(i, local):
            state = local.astype(F32) + state_ref[e, i] * (decay_of(last_ref, e, i, hp) * enters)
            out_ref[own_ref[d], i] = state.astype(BF16)

        @pl.when(mine & at_end)
        def _():
            for i in range(hp):
                put(i, last_ref[e, i * 128 : (i + 1) * 128, :])

        @pl.when(mine & jnp.logical_not(at_end) & (place < SENT[0]))
        def _():
            for i in range(hp):
                put(i, side1_ref[e, pl.ds(pl.multiple_of((place * hp + i) * 128, 128), 128), :])

        @pl.when(mine & jnp.logical_not(at_end) & (place >= SENT[0]))
        def _():
            slot = jnp.minimum(place - SENT[0], SENT[1] - 1)
            for i in range(hp):
                put(i, side2_ref[e, pl.ds(pl.multiple_of((slot * hp + i) * 128, 128), 128), :])


def final_states(doc_lengths, owner_ids, last, side, coming, rows, spread):
    return pl.pallas_call(
        functools.partial(final_kernel, rows),
        in_specs=[SMEM, SMEM] + [VMEM] * (MEMBERS + 3),
        out_specs=VMEM,
        out_shape=jax.ShapeDtypeStruct((spread,) + coming.shape, BF16),
        scratch_shapes=[
            pltpu.VMEM((MEMBERS,) + last[0].shape, BF16),
            pltpu.VMEM((MEMBERS,) + coming.shape, F32),
        ],
        compiler_params=SMALL,
        name="final_states",
    )(doc_lengths, owner_ids, *last, *side, coming)


def finish_kernel(
    len_ref, q_ref, k_ref, v_ref, e0, e1, e2, e3, local_ref, gate_ref, gain_ref, crow_ref, out_ref, bias_ref, ccol_ref
):
    rows = q_ref.shape[0]
    step = pl.program_id(0)
    me = lax.axis_index("seq")
    first = me * rows
    ends = read_ends(len_ref, len_ref.shape[0])
    hp = e0.shape[0]
    pairs = sum(EARLY) // 2

    def entering(h):
        far = (h // hp) ^ (me % MEMBERS)
        state = e0[h % hp]
        for x, ref in ((1, e1), (2, e2), (3, e3)):
            state = jnp.where(far == x, ref[h % hp], state)
        return state

    def emit(lanes, t0, size, att):
        mean = jnp.mean(att * att, axis=1, keepdims=True)
        gate = 0.5 + 0.5 * jnp.tanh(0.5 * gate_ref[t0 : t0 + size, lanes].astype(F32))
        gain = gain_ref[:, lanes].astype(F32)
        out_ref[t0 : t0 + size, lanes] = (att * lax.rsqrt(mean + 1e-06) * (gain * gate)).astype(BF16)

    @pl.when(step == 0)
    def _():
        fill_bias(first, ends, bias_ref)
        fill_columns(crow_ref, ccol_ref)

    @pl.when(step < pairs)
    def _():
        reach = run_end(ends, first - 1) - first
        cols = [head_column(ccol_ref, step * 2 + i) for i in range(2)]
        states = [entering(step * 2 + i) for i in range(2)]
        lanes = [slice(i * 128, (i + 1) * 128) for i in range(2)]
        for t0 in range(0, rows, 256):
            carry = [dot(q_ref[t0 : t0 + 256, lanes[i]], states[i]) for i in range(2)]
            at = t0 + iota((256, 1), 0)
            for i in range(2):
                lead = jnp.exp2(jnp.where(at < reach, cols[i][t0 : t0 + 256], NEG))
                emit(lanes[i], t0, 256, local_ref[t0 : t0 + 256, lanes[i]] + lead * carry[i])

    @pl.when(step >= pairs)
    def _():
        states = [entering(step * 2 + i).astype(F32) for i in range(2)]
        attend(first, ends, q_ref, k_ref, v_ref, step * 2, crow_ref, ccol_ref, bias_ref, states, emit)


def finish(doc_lengths, queries, keys, values, entering, local, gate, gain, crow):
    heads, rows = crow.shape
    pairs = sum(EARLY) // 2
    wide = pl.BlockSpec((rows, 256), lambda j: (0, j))
    late = pl.BlockSpec((rows, 256), lambda j: (0, jnp.maximum(j, pairs)))
    return pl.pallas_call(
        finish_kernel,
        grid=(heads // 2,),
        in_specs=[SMEM, wide, late, late]
        + [whole(e.shape) for e in entering]
        + [
            pl.BlockSpec((rows, 256), lambda j: (0, jnp.minimum(j, pairs - 1))),
            wide,
            pl.BlockSpec((1, 256), lambda j: (0, j)),
            whole((heads, rows)),
        ],
        out_specs=wide,
        out_shape=jax.ShapeDtypeStruct((rows, heads * 128), BF16),
        scratch_shapes=[pltpu.VMEM((rows, CHUNK), F32), pltpu.VMEM((rows, 128), F32)],
        compiler_params=LIMIT,
        cost_estimate=pl.CostEstimate(
            flops=heads * rows * CHUNK * 128 * 8, bytes_accessed=rows * heads * 128 * 10, transcendentals=heads * rows * CHUNK
        ),
        name="finish",
    )(doc_lengths, queries, keys, values, *entering, local, gate, gain, crow)


def swap(x, groups=None):
    return lax.all_to_all(x, "seq", split_axis=0, concat_axis=0, axis_index_groups=groups, tiled=True)


def by_distance(parcels, spread):
    return [parcels[0]] + [
        lax.ppermute(parcels[x], "seq", [(s, s ^ x) for s in range(spread)]) for x in range(1, MEMBERS)
    ]


def on_device(spread, queries, keys, values, log_decay, gate, gain, doc_lengths, owner_ids):
    rows, heads = log_decay.shape
    quads = spread // MEMBERS
    hp = heads // MEMBERS
    near = [[q * MEMBERS + m for m in range(MEMBERS)] for q in range(quads)]
    onward = [(s, s + MEMBERS) for s in range(spread - MEMBERS)]
    decay_rows = log_decay.T
    barrier = lax.optimization_barrier

    side1, side2, crow, flags, *last = piece_states(doc_lengths, owner_ids, decay_rows, keys, values)
    early = functools.partial(early_attention, doc_lengths, queries, keys, values)
    last = by_distance(last, spread)
    side1, last[1] = barrier((side1, last[1]))
    side1 = swap(side1, near)
    local = early(crow, [], 0)
    last, local = barrier((last, local))

    coming = []
    for _ in range(quads - 1):
        leaving = leave_quad(doc_lengths, last, coming, rows, hp)
        coming = [lax.ppermute(leaving, "seq", onward)]
    crow_1, leaving = barrier((crow, leaving))
    local = early(crow_1, [local], 1)
    side1, side2, local, flags, gain = barrier((side1, side2, local, flags, gain))
    side2 = swap(side2, near)
    gain = gain.reshape(1, -1)

    def send_rest():
        rest, _ = piece_states(doc_lengths, owner_ids, decay_rows, keys, values, spread)
        return lax.dynamic_index_in_dim(swap(rest), flags[3], 0, True)

    rest = lax.cond(flags[2] > 0, send_rest, lambda: jnp.zeros((1, heads, 128, 128), BF16))
    from_quad = [flags[0] == q for q in range(1, quads)]
    coming, rest, gain, late, from_quad, local = barrier((coming[0], rest, gain, flags[1] > 0, from_quad, local))

    entering = by_distance(enter_states(doc_lengths, last, coming, rows), spread)
    finals = final_states(doc_lengths, owner_ids, last, [side1, side2], coming, rows, spread)
    entering[1], finals = barrier((entering[1], finals))
    arrived = swap(finals).reshape(quads, 1, heads, 128, 128)
    entering, finals = barrier((entering, finals))
    mixed = finish(doc_lengths, queries, keys, values, entering, local, gate, gain, crow)
    owned = arrived[0]
    for q in range(1, quads):
        owned = jnp.where(from_quad[q - 1], arrived[q], owned)
    return mixed, jnp.where(late, rest, owned)


def solution(mesh):
    placed = (
        P(("groups", "seq"), "tp"),
        P(("groups", "seq"), "tp"),
        P(("groups", "seq"), "tp"),
        P(("groups", "seq"), "tp"),
        P(("groups", "seq"), "tp"),
        P("tp"),
        P("groups"),
        P("groups"),
    )
    return jax.shard_map(
        functools.partial(on_device, mesh.shape["seq"]),
        mesh=mesh,
        in_specs=placed,
        out_specs=(P(("groups", "seq"), "tp"), P(("groups", "seq"), "tp", None, None)),
        check_vma=False,
    )
```

```python
import functools
import math

import jax
import jax.numpy as jnp
from jax import lax
from jax.experimental import pallas as pl
from jax.experimental.pallas import tpu as pltpu
from jax.sharding import PartitionSpec as P

BLK = 512
SIDE = 3
EXTRA = 16
CHUNK = 256
MEMBERS = 4
TILE = 256
EARLY = (8,)
NEG = -1e30
LOG2E = math.log2(math.e)
SCALE = 128**-0.5
F32, BF16 = jnp.float32, jnp.bfloat16
SMEM = pl.BlockSpec(memory_space=pltpu.SMEM)
VMEM = pl.BlockSpec(memory_space=pltpu.VMEM)
LIMIT = pltpu.CompilerParams(vmem_limit_bytes=60 * 2**20)
SMALL = pltpu.CompilerParams(vmem_limit_bytes=48 * 2**20)


def dot(a, b, contract=((1,), (0,))):
    return lax.dot_general(a, b, (contract, ((), ())), preferred_element_type=F32)


def iota(shape, dim):
    return lax.broadcasted_iota(jnp.int32, shape, dim)


def read_ends(len_ref, count):
    ends, total = [], jnp.int32(0)
    for d in range(count):
        total = total + len_ref[d]
        ends.append(total)
    return ends


def run_end(ends, pos):
    best = ends[-1]
    for e in reversed(ends[:-1]):
        best = jnp.where(e > pos, e, best)
    return best


def run_start(ends, pos):
    best = jnp.zeros_like(pos)
    for e in ends[:-1]:
        best = jnp.where(e <= pos, e, best)
    return best


def split3(x):
    hi = x.astype(BF16)
    rest = x - hi.astype(F32)
    mid = rest.astype(BF16)
    return hi, mid, (rest - mid.astype(F32)).astype(BF16)


def cum_rows(ld_ref, crow_ref):
    heads, rows = ld_ref.shape
    upper = (iota((BLK, BLK), 0) <= iota((BLK, BLK), 1)).astype(F32).astype(BF16)
    base = jnp.zeros((heads, 1), F32)
    for b in range(rows // BLK):
        part = ld_ref[:, b * BLK : (b + 1) * BLK] * LOG2E
        sums = dot(jnp.concatenate(split3(part), axis=0), upper)
        row = sums[2 * heads :] + sums[heads : 2 * heads] + sums[:heads] + base
        crow_ref[:, b * BLK : (b + 1) * BLK] = row
        base = row[:, BLK - 1 :]


def value_at(cum, at, index):
    return jnp.sum(jnp.where(at == index, cum, 0.0), axis=1, keepdims=True)


def span_weights(cum, at, low, high):
    inside = (at >= low) & (at <= high)
    return jnp.exp2(jnp.where(inside, value_at(cum, at, high) - cum, NEG) + math.log2(SCALE))


def weigh(flipped, w_ref, h):
    weights = [jnp.broadcast_to(w_ref[pl.ds(h + j, 1), :], (128, flipped.shape[1])) for j in range(2)]
    return (flipped.astype(F32) * jnp.concatenate(weights, axis=0)).astype(BF16)


def whole(shape):
    return pl.BlockSpec(shape, lambda j: (0,) * len(shape))


def pieces_kernel(by_owner, len_ref, own_ref, ld_ref, k_ref, v_ref, *refs):
    if by_owner:
        side_ref, crow_ref, w_ref, keep_ref = refs
        slots = keep_ref.shape[0]
    else:
        side_ref, crow_ref, flag_ref = refs[:3]
        last_refs = refs[3 : 3 + MEMBERS]
        w_ref, first_ref, high_ref, weighted_ref, prefix_ref = refs[3 + MEMBERS :]
        slots = SIDE
    heads, rows = crow_ref.shape
    step = pl.program_id(0)
    hp = v_ref.shape[1] // 128
    me = lax.axis_index("seq")

    @pl.when(step == 0)
    def _():
        cum_rows(ld_ref, crow_ref)
        first = me * rows
        last = first + rows - 1
        ends = read_ends(len_ref, len_ref.shape[0])
        starts = [jnp.int32(0)] + ends[:-1]
        lows = [jnp.int32(0)] * slots
        highs = [jnp.int32(-1)] * slots
        place, rank, previous = jnp.int32(0), jnp.int32(0), jnp.int32(-1)
        crowded, owned_in, owned_late = jnp.int32(0), jnp.int32(0), jnp.int32(0)
        for d in range(len(ends)):
            here = (ends[d] > first) & (ends[d] <= last)
            low = jnp.maximum(starts[d] - first, 0)
            for s in range(slots):
                mine = here & ((place >= SIDE) & (own_ref[d] == s) if by_owner else (place == s))
                lows[s] = jnp.where(mine, low, lows[s])
                highs[s] = jnp.where(mine, ends[d] - 1 - first, highs[s])
            place = place + here.astype(jnp.int32)
            device = (ends[d] - 1) // rows
            rank = jnp.where(device == previous, rank + 1, 0)
            previous = device
            late = ((rank >= SIDE) & (ends[d] != (device + 1) * rows)).astype(jnp.int32)
            crowded = jnp.maximum(crowded, late)
            owned_in = jnp.where(own_ref[d] == me, device, owned_in)
            owned_late = jnp.where(own_ref[d] == me, late, owned_late)
        at = iota((heads, rows), 1)
        cum = crow_ref[...]
        total = jnp.zeros((heads, rows), F32)
        for s in range(slots):
            total = total + span_weights(cum, at, lows[s], highs[s])
        if by_owner:
            row_at = iota((16, rows), 1)
            for s in range(slots):
                inside = (row_at >= lows[s]) & (row_at <= highs[s])
                keep_ref[s] = jnp.where(inside, 1.0, 0.0).astype(BF16)
        else:
            total = total + span_weights(cum, at, jnp.maximum(run_start(ends, last) - first, 0), rows - 1)
            flag_ref[0] = owned_in // MEMBERS
            flag_ref[1] = owned_late
            flag_ref[2] = crowded
            flag_ref[3] = owned_in
            high = jnp.int32(-1)
            for s in range(slots):
                high = jnp.maximum(high, highs[s])
                high_ref[s] = high
            stop = jnp.minimum(run_end(ends, first) - 1 - first, rows - 1)
            goes_on = (run_start(ends, first) < first).astype(F32)
            first_ref[...] = jnp.broadcast_to(jnp.exp2(value_at(cum, at, stop)) * goes_on, (heads, 128))
        w_ref[...] = total

    def own(states, j):
        return states[j * 128 : (j + 1) * 128, j * 128 : (j + 1) * 128]

    if by_owner:
        weighted = weigh(k_ref[...].T, w_ref, step * hp).reshape(16, 16, rows)
        for s in range(slots):
            states = dot((weighted * keep_ref[s][None]).reshape(256, rows), v_ref[...])
            for j in range(2):
                side_ref[s, j] = own(states, j).astype(BF16)
        return

    pairs = range(0, hp, 2)
    lanes = {i: slice(i * 128, (i + 2) * 128) for i in pairs}
    for i in pairs:
        weighted_ref[lanes[i], :] = weigh(k_ref[:, lanes[i]].T, w_ref, step * hp + i)
    totals = {}
    for i in pairs:
        sums = [jnp.zeros((128, 128), F32)] * 2
        for t in range(rows // TILE):
            span = slice(t * TILE, (t + 1) * TILE)
            states = dot(weighted_ref[lanes[i], span], v_ref[span, lanes[i]])
            for j in range(2):
                prefix_ref[t, i + j] = sums[j]
                sums[j] = sums[j] + own(states, j)
        totals[i] = sums
    ended = {i: [jnp.zeros((128, 128), F32)] * 2 for i in pairs}
    for s in range(slots):
        high = high_ref[s]
        tile = jnp.maximum(high, 0) // TILE
        start = pl.multiple_of(tile * TILE, TILE)
        keep = jnp.where(start + iota((16, TILE), 1) <= high, 1.0, 0.0).astype(BF16)
        for i in pairs:
            kept = weighted_ref[lanes[i], pl.ds(start, TILE)].reshape(16, 16, TILE) * keep[None]
            states = dot(kept.reshape(256, TILE), v_ref[pl.ds(start, TILE), lanes[i]])
            for j in range(2):
                until = own(states, j) + prefix_ref[tile, i + j]
                at = (s * hp + i + j) * 128
                side_ref[0, at : at + 128, :] = (until - ended[i][j]).astype(BF16)
                ended[i][j] = until
    rate = first_ref[pl.ds(step * hp, hp), :]
    high = rate.astype(BF16).astype(F32)
    pad = jnp.zeros((EXTRA - 2 * hp, 128), F32)
    tail = jnp.concatenate([high, rate - high, pad], axis=0).astype(BF16)
    last_states = [(totals[i][j] - ended[i][j]).astype(BF16) for i in pairs for j in range(2)]
    for x, last_ref in enumerate(last_refs):

        @pl.when((step ^ (me % MEMBERS)) == x)
        def _():
            for i in range(hp):
                last_ref[i * 128 : (i + 1) * 128, :] = last_states[i]
            last_ref[hp * 128 :, :] = tail


def piece_states(doc_lengths, owner_ids, decay_rows, keys, values, spread=0):
    heads, rows = decay_rows.shape
    by_owner = spread > 0
    hp = 2 if by_owner else heads // MEMBERS
    wide = pl.BlockSpec((rows, hp * 128), lambda j: (0, j))
    scratch = [pltpu.VMEM((heads, rows), F32)]
    if by_owner:
        shapes = [jax.ShapeDtypeStruct((spread, heads, 128, 128), BF16), jax.ShapeDtypeStruct((heads, rows), F32)]
        specs = [pl.BlockSpec((spread, hp, 128, 128), lambda j: (0, j, 0, 0)), whole((heads, rows))]
        scratch.append(pltpu.VMEM((spread, 16, rows), BF16))
    else:
        last = (hp * 128 + EXTRA, 128)
        shapes = [
            jax.ShapeDtypeStruct((MEMBERS, SIDE * hp * 128, 128), BF16),
            jax.ShapeDtypeStruct((heads, rows), F32),
            jax.ShapeDtypeStruct((4,), jnp.int32),
            *[jax.ShapeDtypeStruct(last, BF16)] * MEMBERS,
        ]
        specs = [pl.BlockSpec((1, SIDE * hp * 128, 128), lambda j: (j, 0, 0)), whole((heads, rows)), SMEM]
        specs += [whole(last)] * MEMBERS
        scratch += [
            pltpu.VMEM((heads, 128), F32),
            pltpu.SMEM((SIDE,), jnp.int32),
            pltpu.VMEM((hp * 128, rows), BF16),
            pltpu.VMEM((rows // TILE, hp, 128, 128), F32),
        ]
    return pl.pallas_call(
        functools.partial(pieces_kernel, by_owner),
        grid=(heads // hp,),
        in_specs=[SMEM, SMEM, whole((heads, rows)), wide, wide],
        out_specs=specs,
        out_shape=shapes,
        scratch_shapes=scratch,
        compiler_params=LIMIT,
        cost_estimate=pl.CostEstimate(
            flops=2 * heads * rows * 128 * 256, bytes_accessed=rows * heads * 128 * 4, transcendentals=heads * rows
        ),
        name="piece_states",
    )(doc_lengths, owner_ids, decay_rows, keys, values)


def head_column(ccol_ref, h):
    cols = ccol_ref[...]
    return jnp.sum(jnp.where(iota(cols.shape, 1) == h, cols, 0.0), axis=1, keepdims=True)


def fill_columns(crow_ref, ccol_ref):
    heads, rows = crow_ref.shape
    for r0 in range(0, rows, 128):
        part = crow_ref[:, r0 : r0 + 128]
        part = jnp.concatenate([part, jnp.zeros((128 - heads, 128), F32)], axis=0)
        ccol_ref[r0 : r0 + 128, :] = part.T


def fill_bias(first, ends, bias_ref):
    for c in range(bias_ref.shape[0] // CHUNK):
        base = first + c * CHUNK
        t_pos = base + iota((CHUNK, 1), 0)
        start = run_start(ends, t_pos)
        s_pos = base + iota((CHUNK, CHUNK), 1)
        keep = (s_pos <= t_pos) & (s_pos >= start)
        bias_ref[c * CHUNK : (c + 1) * CHUNK, :] = jnp.where(keep, math.log2(SCALE), NEG)


def attend(first, ends, q_ref, k_ref, v_ref, h, crow_ref, ccol_ref, bias_ref, states, emit):
    rows = q_ref.shape[0]
    pair = range(2)
    half = CHUNK // 2
    lanes = [slice(i * 128, (i + 1) * 128) for i in pair]
    row_all = [crow_ref[pl.ds(h + i, 1), :] for i in pair]
    col_all = [head_column(ccol_ref, h + i) for i in pair]
    starts = range(0, rows, CHUNK)
    spans = [slice(r0, r0 + CHUNK) for r0 in starts]
    reach = [run_end(ends, first + r0 - 1) - (first + r0) for r0 in starts]
    base = [[row_all[i][:, r0 - 1 : r0] if r0 else jnp.zeros((1, 1), F32) for r0 in starts] for i in pair]

    fresh = [[], []]
    for c, r0 in enumerate(starts[:-1]):
        since = run_start(ends, first + r0 + CHUNK - 1) - (first + r0)
        inside = iota((1, CHUNK), 1) >= since
        for i in pair:
            row = row_all[i][:, spans[c]]
            weight = jnp.exp2(jnp.where(inside, row[:, CHUNK - 1 :] - row, NEG) + math.log2(SCALE))
            flipped = k_ref[spans[c], lanes[i]].T
            fresh[i].append(dot((flipped.astype(F32) * weight).astype(BF16), v_ref[spans[c], lanes[i]]))
    carried = []
    for i in pair:
        state = None if states is None else states[i]
        chain = [None if state is None else state.astype(BF16)]
        for c in range(len(starts) - 1):
            if state is None:
                state = fresh[i][c]
            else:
                total = row_all[i][:, starts[c] + CHUNK - 1 : starts[c] + CHUNK]
                state = fresh[i][c] + state * jnp.exp2(jnp.where(CHUNK <= reach[c], total - base[i][c], NEG))
            chain.append(state.astype(BF16))
        carried.append(chain)

    def products(c):
        result = []
        for i in pair:
            query = q_ref[spans[c], lanes[i]]
            scores = dot(query, k_ref[spans[c], lanes[i]], ((1,), (1,)))
            result.append((scores, None if carried[i][c] is None else dot(query, carried[i][c])))
        return result

    ahead = products(0)
    for c, r0 in enumerate(starts):
        current = ahead
        if c + 1 < len(starts):
            ahead = products(c + 1)
        for part in range(2):
            t0, width = part * half, (part + 1) * half
            rows_here = slice(r0 + t0, r0 + t0 + half)
            for i in pair:
                scores, carry = current[i]
                col = col_all[i][rows_here]
                decay = jnp.exp2((col - row_all[i][:, r0 : r0 + width]) + bias_ref[rows_here, :width])
                weights = (scores[t0 : t0 + half, :width] * decay).astype(BF16)
                att = dot(weights, v_ref[r0 : r0 + width, lanes[i]])
                if carry is not None:
                    lead = jnp.exp2(jnp.where(t0 + iota((half, 1), 0) < reach[c], col - base[i][c], NEG))
                    att = att + lead * carry[t0 : t0 + half]
                emit(lanes[i], r0 + t0, half, att)


def early_kernel(pairs_before, len_ref, q_ref, k_ref, v_ref, crow_ref, *refs):
    out_ref, bias_ref, ccol_ref = refs[-3:]
    rows = q_ref.shape[0]
    step = pl.program_id(0)
    first = lax.axis_index("seq") * rows
    ends = read_ends(len_ref, len_ref.shape[0])

    @pl.when(step == 0)
    def _():
        fill_bias(first, ends, bias_ref)
        fill_columns(crow_ref, ccol_ref)

    def emit(lanes, t0, size, att):
        out_ref[t0 : t0 + size, lanes] = att

    attend(first, ends, q_ref, k_ref, v_ref, (step + pairs_before) * 2, crow_ref, ccol_ref, bias_ref, None, emit)


def early_attention(doc_lengths, queries, keys, values, crow, before, part):
    heads, rows = crow.shape
    skip = sum(EARLY[:part]) // 2
    wide = pl.BlockSpec((rows, 256), lambda j: (0, j + skip))
    count = EARLY[part]
    return pl.pallas_call(
        functools.partial(early_kernel, skip),
        grid=(count // 2,),
        in_specs=[SMEM, wide, wide, wide, whole((heads, rows))] + [pl.BlockSpec(memory_space=pl.ANY)] * len(before),
        out_specs=wide,
        out_shape=jax.ShapeDtypeStruct((rows, sum(EARLY) * 128), F32),
        input_output_aliases={5: 0} if before else {},
        scratch_shapes=[pltpu.VMEM((rows, CHUNK), F32), pltpu.VMEM((rows, 128), F32)],
        compiler_params=LIMIT,
        cost_estimate=pl.CostEstimate(
            flops=count * rows * CHUNK * 128 * 8, bytes_accessed=rows * count * 128 * 10, transcendentals=count * rows * CHUNK
        ),
        name="early_attention",
    )(doc_lengths, queries, keys, values, crow, *before)


def from_before(in_ref, i):
    quad = lax.axis_index("seq") // MEMBERS
    return in_ref[jnp.maximum(quad - 1, 0), i].astype(F32) * (quad > 0).astype(F32)


def gather_last(refs, last_ref):
    me = lax.axis_index("seq") % MEMBERS
    for x, ref in enumerate(refs):
        last_ref[me ^ x] = ref[...]


def decay_of(last_ref, e, i, hp):
    extra = last_ref[e, hp * 128 :, :].astype(F32)
    return extra[i : i + 1, :] + extra[hp + i : hp + i + 1, :]


def scan_quad(rows, len_ref, last_ref, state, i, hp, note):
    members = last_ref.shape[0]
    ends = read_ends(len_ref, len_ref.shape[0])
    base = lax.axis_index("seq") // members * members
    for e in range(members):
        note(e, state)
        low = (base + e) * rows
        inner = jnp.int32(0)
        for end in ends:
            inner = inner + ((end > low) & (end < low + rows)).astype(jnp.int32)
        passes = (inner == 0).astype(F32)
        piece = last_ref[e, i * 128 : (i + 1) * 128, :].astype(F32)
        state = state * (decay_of(last_ref, e, i, hp) * passes) + piece
    return state


def leave_kernel(rows, len_ref, *refs):
    out_ref, last_ref = refs[-2:]
    gather_last(refs[:MEMBERS], last_ref)
    hp = out_ref.shape[0]
    for i in range(hp):
        state = jnp.zeros((128, 128), F32)
        if len(refs) > MEMBERS + 2:
            state = from_before(refs[MEMBERS], i)
        state = scan_quad(rows, len_ref, last_ref, state, i, hp, lambda e, x: None)
        out_ref[i] = state.astype(BF16)


def leave_quad(doc_lengths, last, coming, rows, hp):
    return pl.pallas_call(
        functools.partial(leave_kernel, rows),
        in_specs=[SMEM] + [VMEM] * (MEMBERS + len(coming)),
        out_specs=VMEM,
        out_shape=jax.ShapeDtypeStruct((hp, 128, 128), BF16),
        scratch_shapes=[pltpu.VMEM((MEMBERS,) + last[0].shape, BF16)],
        compiler_params=SMALL,
        name="leave_quad",
    )(doc_lengths, *last, *coming)


def enter_kernel(rows, len_ref, *refs):
    in_ref, out_refs, last_ref, state_ref = refs[MEMBERS], refs[MEMBERS + 1 : -2], refs[-2], refs[-1]
    gather_last(refs[:MEMBERS], last_ref)
    hp = in_ref.shape[1]

    def note(i, e, state):
        state_ref[e, i] = state

    for i in range(hp):
        scan_quad(rows, len_ref, last_ref, from_before(in_ref, i), i, hp, functools.partial(note, i))
    me = lax.axis_index("seq") % MEMBERS
    for x, out_ref in enumerate(out_refs):
        out_ref[...] = state_ref[me ^ x].astype(BF16)


def enter_states(doc_lengths, last, coming, rows):
    return pl.pallas_call(
        functools.partial(enter_kernel, rows),
        in_specs=[SMEM] + [VMEM] * (MEMBERS + 1),
        out_specs=[VMEM] * MEMBERS,
        out_shape=[jax.ShapeDtypeStruct(coming.shape[1:], BF16)] * MEMBERS,
        scratch_shapes=[
            pltpu.VMEM((MEMBERS,) + last[0].shape, BF16),
            pltpu.VMEM((MEMBERS,) + coming.shape[1:], F32),
        ],
        compiler_params=SMALL,
        name="enter_states",
    )(doc_lengths, *last, coming)


def final_kernel(rows, len_ref, own_ref, *refs):
    side_ref, in_ref, out_ref, last_ref, state_ref = refs[MEMBERS:]
    gather_last(refs[:MEMBERS], last_ref)
    hp = in_ref.shape[1]
    ends = read_ends(len_ref, len_ref.shape[0])
    base = lax.axis_index("seq") // MEMBERS * MEMBERS

    def note(i, e, state):
        state_ref[e, i] = state

    for i in range(hp):
        scan_quad(rows, len_ref, last_ref, from_before(in_ref, i), i, hp, functools.partial(note, i))
    out_ref[...] = jnp.zeros_like(out_ref)
    place, previous = jnp.int32(0), jnp.int32(-1)
    for d in range(len(ends)):
        device = (ends[d] - 1) // rows
        place = jnp.where(device == previous, place + 1, 0)
        previous = device
        at_end = ends[d] == (device + 1) * rows
        enters = (place == 0).astype(F32)
        mine = device // MEMBERS * MEMBERS == base
        e = device - base

        def put(i, local):
            state = local.astype(F32) + state_ref[e, i] * (decay_of(last_ref, e, i, hp) * enters)
            out_ref[own_ref[d], i] = state.astype(BF16)

        @pl.when(mine & at_end)
        def _():
            for i in range(hp):
                put(i, last_ref[e, i * 128 : (i + 1) * 128, :])

        @pl.when(mine & jnp.logical_not(at_end))
        def _():
            for i in range(hp):
                row = pl.multiple_of((jnp.minimum(place, SIDE - 1) * hp + i) * 128, 128)
                put(i, side_ref[e, pl.ds(row, 128), :])


def final_states(doc_lengths, owner_ids, last, side, coming, rows, spread):
    return pl.pallas_call(
        functools.partial(final_kernel, rows),
        in_specs=[SMEM, SMEM] + [VMEM] * (MEMBERS + 2),
        out_specs=VMEM,
        out_shape=jax.ShapeDtypeStruct((spread,) + coming.shape[1:], BF16),
        scratch_shapes=[
            pltpu.VMEM((MEMBERS,) + last[0].shape, BF16),
            pltpu.VMEM((MEMBERS,) + coming.shape[1:], F32),
        ],
        compiler_params=SMALL,
        name="final_states",
    )(doc_lengths, owner_ids, *last, side, coming)


def finish_kernel(
    len_ref, q_ref, k_ref, v_ref, e0, e1, e2, e3, local_ref, gate_ref, gain_ref, crow_ref, out_ref, bias_ref, ccol_ref
):
    rows = q_ref.shape[0]
    step = pl.program_id(0)
    me = lax.axis_index("seq")
    first = me * rows
    ends = read_ends(len_ref, len_ref.shape[0])
    hp = e0.shape[0]
    pairs = sum(EARLY) // 2

    def entering(h):
        far = (h // hp) ^ (me % MEMBERS)
        state = e0[h % hp]
        for x, ref in ((1, e1), (2, e2), (3, e3)):
            state = jnp.where(far == x, ref[h % hp], state)
        return state

    def emit(lanes, t0, size, att):
        mean = jnp.mean(att * att, axis=1, keepdims=True)
        gate = 0.5 + 0.5 * jnp.tanh(0.5 * gate_ref[t0 : t0 + size, lanes].astype(F32))
        gain = gain_ref[:, lanes].astype(F32)
        out_ref[t0 : t0 + size, lanes] = (att * lax.rsqrt(mean + 1e-06) * (gain * gate)).astype(BF16)

    @pl.when(step == 0)
    def _():
        fill_bias(first, ends, bias_ref)
        fill_columns(crow_ref, ccol_ref)

    @pl.when(step < pairs)
    def _():
        reach = run_end(ends, first - 1) - first
        cols = [head_column(ccol_ref, step * 2 + i) for i in range(2)]
        states = [entering(step * 2 + i) for i in range(2)]
        lanes = [slice(i * 128, (i + 1) * 128) for i in range(2)]
        for t0 in range(0, rows, 256):
            carry = [dot(q_ref[t0 : t0 + 256, lanes[i]], states[i]) for i in range(2)]
            at = t0 + iota((256, 1), 0)
            for i in range(2):
                lead = jnp.exp2(jnp.where(at < reach, cols[i][t0 : t0 + 256], NEG))
                emit(lanes[i], t0, 256, local_ref[t0 : t0 + 256, lanes[i]] + lead * carry[i])

    @pl.when(step >= pairs)
    def _():
        states = [entering(step * 2 + i).astype(F32) for i in range(2)]
        attend(first, ends, q_ref, k_ref, v_ref, step * 2, crow_ref, ccol_ref, bias_ref, states, emit)


def finish(doc_lengths, queries, keys, values, entering, local, gate, gain, crow):
    heads, rows = crow.shape
    pairs = sum(EARLY) // 2
    wide = pl.BlockSpec((rows, 256), lambda j: (0, j))
    late = pl.BlockSpec((rows, 256), lambda j: (0, jnp.maximum(j, pairs)))
    return pl.pallas_call(
        finish_kernel,
        grid=(heads // 2,),
        in_specs=[SMEM, wide, late, late]
        + [whole(e.shape) for e in entering]
        + [
            pl.BlockSpec((rows, 256), lambda j: (0, jnp.minimum(j, pairs - 1))),
            wide,
            pl.BlockSpec((1, 256), lambda j: (0, j)),
            whole((heads, rows)),
        ],
        out_specs=wide,
        out_shape=jax.ShapeDtypeStruct((rows, heads * 128), BF16),
        scratch_shapes=[pltpu.VMEM((rows, CHUNK), F32), pltpu.VMEM((rows, 128), F32)],
        compiler_params=LIMIT,
        cost_estimate=pl.CostEstimate(
            flops=heads * rows * CHUNK * 128 * 8, bytes_accessed=rows * heads * 128 * 10, transcendentals=heads * rows * CHUNK
        ),
        name="finish",
    )(doc_lengths, queries, keys, values, *entering, local, gate, gain, crow)


def swap(x, groups=None):
    return lax.all_to_all(x, "seq", split_axis=0, concat_axis=0, axis_index_groups=groups, tiled=True)


def by_distance(parcels, spread):
    return [parcels[0]] + [
        lax.ppermute(parcels[x], "seq", [(s, s ^ x) for s in range(spread)]) for x in range(1, MEMBERS)
    ]


def on_device(spread, queries, keys, values, log_decay, gate, gain, doc_lengths, owner_ids):
    rows, heads = log_decay.shape
    quads = spread // MEMBERS
    hp = heads // MEMBERS
    near = [[q * MEMBERS + m for m in range(MEMBERS)] for q in range(quads)]
    lines = [[q * MEMBERS + m for q in range(quads)] for m in range(MEMBERS)]
    decay_rows = log_decay.T
    barrier = lax.optimization_barrier

    side, crow, flags, *last = piece_states(doc_lengths, owner_ids, decay_rows, keys, values)
    last = by_distance(last, spread)

    def send_rest():
        rest, _ = piece_states(doc_lengths, owner_ids, decay_rows, keys, values, spread)
        return lax.dynamic_index_in_dim(swap(rest), flags[3], 0, True)

    gain = gain.reshape(1, -1)
    rest = lax.cond(flags[2] > 0, send_rest, lambda: jnp.zeros((1, heads, 128, 128), BF16))
    from_quad = [flags[0] == q for q in range(1, quads)]
    last, rest, gain, late, from_quad = barrier((last, rest, gain, flags[1] > 0, from_quad))

    side, last = barrier((side, last))
    side = swap(side, near)
    coming = []
    for q in range(1, quads):
        leaving = leave_quad(doc_lengths, last, coming, rows, hp)
        coming = [lax.all_gather(leaving, "seq", axis_index_groups=lines)]
    crow_1, leaving = barrier((crow, leaving))
    local = early_attention(doc_lengths, queries, keys, values, crow_1, [], 0)
    coming, local = barrier((coming[0], local))

    entering = by_distance(enter_states(doc_lengths, last, coming, rows), spread)
    finals = final_states(doc_lengths, owner_ids, last, side, coming, rows, spread)
    entering, finals = barrier((entering, finals))
    arrived = swap(finals).reshape(quads, 1, heads, 128, 128)
    mixed = finish(doc_lengths, queries, keys, values, entering, local, gate, gain, crow)
    owned = arrived[0]
    for q in range(1, quads):
        owned = jnp.where(from_quad[q - 1], arrived[q], owned)
    return mixed, jnp.where(late, rest, owned)


def solution(mesh):
    placed = (
        P(("groups", "seq"), "tp"),
        P(("groups", "seq"), "tp"),
        P(("groups", "seq"), "tp"),
        P(("groups", "seq"), "tp"),
        P(("groups", "seq"), "tp"),
        P("tp"),
        P("groups"),
        P("groups"),
    )
    return jax.shard_map(
        functools.partial(on_device, mesh.shape["seq"]),
        mesh=mesh,
        in_specs=placed,
        out_specs=(P(("groups", "seq"), "tp"), P(("groups", "seq"), "tp", None, None)),
        check_vma=False,
    )
```

```python
import functools
import math

import jax
import jax.numpy as jnp
from jax import lax
from jax.experimental import pallas as pl
from jax.experimental.pallas import tpu as pltpu
from jax.sharding import PartitionSpec as P

BLK = 512
SIDE = 3
EXTRA = 16
CHUNK = 256
MEMBERS = 4
TILE = 256
EARLY = (8,)
NEG = -1e30
LOG2E = math.log2(math.e)
SCALE = 128**-0.5
F32, BF16 = jnp.float32, jnp.bfloat16
SMEM = pl.BlockSpec(memory_space=pltpu.SMEM)
VMEM = pl.BlockSpec(memory_space=pltpu.VMEM)
LIMIT = pltpu.CompilerParams(vmem_limit_bytes=60 * 2**20)
SMALL = pltpu.CompilerParams(vmem_limit_bytes=48 * 2**20)


def dot(a, b, contract=((1,), (0,))):
    return lax.dot_general(a, b, (contract, ((), ())), preferred_element_type=F32)


def iota(shape, dim):
    return lax.broadcasted_iota(jnp.int32, shape, dim)


def read_ends(len_ref, count):
    ends, total = [], jnp.int32(0)
    for d in range(count):
        total = total + len_ref[d]
        ends.append(total)
    return ends


def run_end(ends, pos):
    best = ends[-1]
    for e in reversed(ends[:-1]):
        best = jnp.where(e > pos, e, best)
    return best


def run_start(ends, pos):
    best = jnp.zeros_like(pos)
    for e in ends[:-1]:
        best = jnp.where(e <= pos, e, best)
    return best


def split3(x):
    hi = x.astype(BF16)
    rest = x - hi.astype(F32)
    mid = rest.astype(BF16)
    return hi, mid, (rest - mid.astype(F32)).astype(BF16)


def cum_rows(ld_ref, crow_ref):
    heads, rows = ld_ref.shape
    upper = (iota((BLK, BLK), 0) <= iota((BLK, BLK), 1)).astype(F32).astype(BF16)
    base = jnp.zeros((heads, 1), F32)
    for b in range(rows // BLK):
        part = ld_ref[:, b * BLK : (b + 1) * BLK] * LOG2E
        sums = dot(jnp.concatenate(split3(part), axis=0), upper)
        row = sums[2 * heads :] + sums[heads : 2 * heads] + sums[:heads] + base
        crow_ref[:, b * BLK : (b + 1) * BLK] = row
        base = row[:, BLK - 1 :]


def value_at(cum, at, index):
    return jnp.sum(jnp.where(at == index, cum, 0.0), axis=1, keepdims=True)


def span_weights(cum, at, low, high):
    inside = (at >= low) & (at <= high)
    return jnp.exp2(jnp.where(inside, value_at(cum, at, high) - cum, NEG) + math.log2(SCALE))


def weigh(flipped, w_ref, h):
    weights = [jnp.broadcast_to(w_ref[pl.ds(h + j, 1), :], (128, flipped.shape[1])) for j in range(2)]
    return (flipped.astype(F32) * jnp.concatenate(weights, axis=0)).astype(BF16)


def whole(shape):
    return pl.BlockSpec(shape, lambda j: (0,) * len(shape))


def pieces_kernel(rest, len_ref, own_ref, ld_ref, k_ref, v_ref, *refs):
    if rest:
        side_ref, crow_ref, w_ref, keep_ref = refs
        slots = keep_ref.shape[0]
    else:
        side_ref, crow_ref, flag_ref = refs[:3]
        last_refs = refs[3 : 3 + MEMBERS]
        w_ref, first_ref, high_ref, weighted_ref, prefix_ref = refs[3 + MEMBERS :]
        slots = SIDE
    heads, rows = crow_ref.shape
    step = pl.program_id(0)
    hp = v_ref.shape[1] // 128
    me = lax.axis_index("seq")

    @pl.when(step == 0)
    def _():
        cum_rows(ld_ref, crow_ref)
        first = me * rows
        last = first + rows - 1
        ends = read_ends(len_ref, len_ref.shape[0])
        starts = [jnp.int32(0)] + ends[:-1]
        lows = [jnp.int32(0)] * slots
        highs = [jnp.int32(-1)] * slots
        place, rank, previous = jnp.int32(0), jnp.int32(0), jnp.int32(-1)
        crowded, owned_in = jnp.int32(0), jnp.int32(0)
        for d in range(len(ends)):
            here = (ends[d] > first) & (ends[d] <= last)
            low = jnp.maximum(starts[d] - first, 0)
            for s in range(slots):
                mine = here & (place == s + (SIDE if rest else 0))
                lows[s] = jnp.where(mine, low, lows[s])
                highs[s] = jnp.where(mine, ends[d] - 1 - first, highs[s])
            place = place + here.astype(jnp.int32)
            device = (ends[d] - 1) // rows
            rank = jnp.where(device == previous, rank + 1, 0)
            previous = device
            late = ((rank >= SIDE) & (ends[d] != (device + 1) * rows)).astype(jnp.int32)
            crowded = jnp.maximum(crowded, late)
            owned_in = jnp.where(own_ref[d] == me, device, owned_in)
        at = iota((heads, rows), 1)
        cum = crow_ref[...]
        total = jnp.zeros((heads, rows), F32)
        for s in range(slots):
            total = total + span_weights(cum, at, lows[s], highs[s])
        if rest:
            row_at = iota((16, rows), 1)
            for s in range(slots):
                inside = (row_at >= lows[s]) & (row_at <= highs[s])
                keep_ref[s] = jnp.where(inside, 1.0, 0.0).astype(BF16)
        else:
            total = total + span_weights(cum, at, jnp.maximum(run_start(ends, last) - first, 0), rows - 1)
            flag_ref[0] = owned_in // MEMBERS
            flag_ref[1] = crowded
            high = jnp.int32(-1)
            for s in range(slots):
                high = jnp.maximum(high, highs[s])
                high_ref[s] = high
            stop = jnp.minimum(run_end(ends, first) - 1 - first, rows - 1)
            goes_on = (run_start(ends, first) < first).astype(F32)
            first_ref[...] = jnp.broadcast_to(jnp.exp2(value_at(cum, at, stop)) * goes_on, (heads, 128))
        w_ref[...] = total

    def own(states, j):
        return states[j * 128 : (j + 1) * 128, j * 128 : (j + 1) * 128]

    if rest:
        for i in range(0, hp, 2):
            lanes = slice(i * 128, (i + 2) * 128)
            weighted = weigh(k_ref[:, lanes].T, w_ref, step * hp + i).reshape(16, 16, rows)
            for s in range(slots):
                states = dot((weighted * keep_ref[s][None]).reshape(256, rows), v_ref[:, lanes])
                for j in range(2):
                    at = (s * hp + i + j) * 128
                    side_ref[0, at : at + 128, :] = own(states, j).astype(BF16)
        return

    pairs = range(0, hp, 2)
    lanes = {i: slice(i * 128, (i + 2) * 128) for i in pairs}
    for i in pairs:
        weighted_ref[lanes[i], :] = weigh(k_ref[:, lanes[i]].T, w_ref, step * hp + i)
    totals = {}
    for i in pairs:
        sums = [jnp.zeros((128, 128), F32)] * 2
        for t in range(rows // TILE):
            span = slice(t * TILE, (t + 1) * TILE)
            states = dot(weighted_ref[lanes[i], span], v_ref[span, lanes[i]])
            for j in range(2):
                prefix_ref[t, i + j] = sums[j]
                sums[j] = sums[j] + own(states, j)
        totals[i] = sums
    ended = {i: [jnp.zeros((128, 128), F32)] * 2 for i in pairs}
    for s in range(slots):
        high = high_ref[s]
        tile = jnp.maximum(high, 0) // TILE
        start = pl.multiple_of(tile * TILE, TILE)
        keep = jnp.where(start + iota((16, TILE), 1) <= high, 1.0, 0.0).astype(BF16)
        for i in pairs:
            kept = weighted_ref[lanes[i], pl.ds(start, TILE)].reshape(16, 16, TILE) * keep[None]
            states = dot(kept.reshape(256, TILE), v_ref[pl.ds(start, TILE), lanes[i]])
            for j in range(2):
                until = own(states, j) + prefix_ref[tile, i + j]
                at = (s * hp + i + j) * 128
                side_ref[0, at : at + 128, :] = (until - ended[i][j]).astype(BF16)
                ended[i][j] = until
    rate = first_ref[pl.ds(step * hp, hp), :]
    high = rate.astype(BF16).astype(F32)
    pad = jnp.zeros((EXTRA - 2 * hp, 128), F32)
    tail = jnp.concatenate([high, rate - high, pad], axis=0).astype(BF16)
    last_states = [(totals[i][j] - ended[i][j]).astype(BF16) for i in pairs for j in range(2)]
    for x, last_ref in enumerate(last_refs):

        @pl.when((step ^ (me % MEMBERS)) == x)
        def _():
            for i in range(hp):
                last_ref[i * 128 : (i + 1) * 128, :] = last_states[i]
            last_ref[hp * 128 :, :] = tail


def piece_states(doc_lengths, owner_ids, decay_rows, keys, values, slots):
    heads, rows = decay_rows.shape
    rest = slots > SIDE
    count = slots - SIDE if rest else slots
    hp = heads // MEMBERS
    wide = pl.BlockSpec((rows, hp * 128), lambda j: (0, j))
    side = (count * hp * 128, 128)
    shapes = [jax.ShapeDtypeStruct((MEMBERS,) + side, BF16), jax.ShapeDtypeStruct((heads, rows), F32)]
    specs = [pl.BlockSpec((1,) + side, lambda j: (j, 0, 0)), whole((heads, rows))]
    scratch = [pltpu.VMEM((heads, rows), F32)]
    if rest:
        scratch.append(pltpu.VMEM((count, 16, rows), BF16))
    else:
        last = (hp * 128 + EXTRA, 128)
        shapes += [jax.ShapeDtypeStruct((2,), jnp.int32)] + [jax.ShapeDtypeStruct(last, BF16)] * MEMBERS
        specs += [SMEM] + [whole(last)] * MEMBERS
        scratch += [
            pltpu.VMEM((heads, 128), F32),
            pltpu.SMEM((SIDE,), jnp.int32),
            pltpu.VMEM((hp * 128, rows), BF16),
            pltpu.VMEM((rows // TILE, hp, 128, 128), F32),
        ]
    return pl.pallas_call(
        functools.partial(pieces_kernel, rest),
        grid=(MEMBERS,),
        in_specs=[SMEM, SMEM, whole((heads, rows)), wide, wide],
        out_specs=specs,
        out_shape=shapes,
        scratch_shapes=scratch,
        compiler_params=LIMIT,
        cost_estimate=pl.CostEstimate(
            flops=2 * heads * rows * 128 * 256, bytes_accessed=rows * heads * 128 * 4, transcendentals=heads * rows
        ),
        name="piece_states",
    )(doc_lengths, owner_ids, decay_rows, keys, values)


def head_column(ccol_ref, h):
    cols = ccol_ref[...]
    return jnp.sum(jnp.where(iota(cols.shape, 1) == h, cols, 0.0), axis=1, keepdims=True)


def fill_columns(crow_ref, ccol_ref):
    heads, rows = crow_ref.shape
    for r0 in range(0, rows, 128):
        part = crow_ref[:, r0 : r0 + 128]
        part = jnp.concatenate([part, jnp.zeros((128 - heads, 128), F32)], axis=0)
        ccol_ref[r0 : r0 + 128, :] = part.T


def fill_bias(first, ends, bias_ref):
    for c in range(bias_ref.shape[0] // CHUNK):
        base = first + c * CHUNK
        t_pos = base + iota((CHUNK, 1), 0)
        start = run_start(ends, t_pos)
        s_pos = base + iota((CHUNK, CHUNK), 1)
        keep = (s_pos <= t_pos) & (s_pos >= start)
        bias_ref[c * CHUNK : (c + 1) * CHUNK, :] = jnp.where(keep, math.log2(SCALE), NEG)


def attend(first, ends, q_ref, k_ref, v_ref, h, crow_ref, ccol_ref, bias_ref, states, emit):
    rows = q_ref.shape[0]
    pair = range(2)
    half = CHUNK // 2
    lanes = [slice(i * 128, (i + 1) * 128) for i in pair]
    row_all = [crow_ref[pl.ds(h + i, 1), :] for i in pair]
    col_all = [head_column(ccol_ref, h + i) for i in pair]
    starts = range(0, rows, CHUNK)
    spans = [slice(r0, r0 + CHUNK) for r0 in starts]
    reach = [run_end(ends, first + r0 - 1) - (first + r0) for r0 in starts]
    base = [[row_all[i][:, r0 - 1 : r0] if r0 else jnp.zeros((1, 1), F32) for r0 in starts] for i in pair]

    fresh = [[], []]
    for c, r0 in enumerate(starts[:-1]):
        since = run_start(ends, first + r0 + CHUNK - 1) - (first + r0)
        inside = iota((1, CHUNK), 1) >= since
        for i in pair:
            row = row_all[i][:, spans[c]]
            weight = jnp.exp2(jnp.where(inside, row[:, CHUNK - 1 :] - row, NEG) + math.log2(SCALE))
            flipped = k_ref[spans[c], lanes[i]].T
            fresh[i].append(dot((flipped.astype(F32) * weight).astype(BF16), v_ref[spans[c], lanes[i]]))
    carried = []
    for i in pair:
        state = None if states is None else states[i]
        chain = [None if state is None else state.astype(BF16)]
        for c in range(len(starts) - 1):
            if state is None:
                state = fresh[i][c]
            else:
                total = row_all[i][:, starts[c] + CHUNK - 1 : starts[c] + CHUNK]
                state = fresh[i][c] + state * jnp.exp2(jnp.where(CHUNK <= reach[c], total - base[i][c], NEG))
            chain.append(state.astype(BF16))
        carried.append(chain)

    def products(c):
        result = []
        for i in pair:
            query = q_ref[spans[c], lanes[i]]
            scores = dot(query, k_ref[spans[c], lanes[i]], ((1,), (1,)))
            result.append((scores, None if carried[i][c] is None else dot(query, carried[i][c])))
        return result

    ahead = products(0)
    for c, r0 in enumerate(starts):
        current = ahead
        if c + 1 < len(starts):
            ahead = products(c + 1)
        for part in range(2):
            t0, width = part * half, (part + 1) * half
            rows_here = slice(r0 + t0, r0 + t0 + half)
            for i in pair:
                scores, carry = current[i]
                col = col_all[i][rows_here]
                decay = jnp.exp2((col - row_all[i][:, r0 : r0 + width]) + bias_ref[rows_here, :width])
                weights = (scores[t0 : t0 + half, :width] * decay).astype(BF16)
                att = dot(weights, v_ref[r0 : r0 + width, lanes[i]])
                if carry is not None:
                    lead = jnp.exp2(jnp.where(t0 + iota((half, 1), 0) < reach[c], col - base[i][c], NEG))
                    att = att + lead * carry[t0 : t0 + half]
                emit(lanes[i], r0 + t0, half, att)


def early_kernel(pairs_before, len_ref, q_ref, k_ref, v_ref, crow_ref, *refs):
    out_ref, bias_ref, ccol_ref = refs[-3:]
    rows = q_ref.shape[0]
    step = pl.program_id(0)
    first = lax.axis_index("seq") * rows
    ends = read_ends(len_ref, len_ref.shape[0])

    @pl.when(step == 0)
    def _():
        fill_bias(first, ends, bias_ref)
        fill_columns(crow_ref, ccol_ref)

    def emit(lanes, t0, size, att):
        out_ref[t0 : t0 + size, lanes] = att

    attend(first, ends, q_ref, k_ref, v_ref, (step + pairs_before) * 2, crow_ref, ccol_ref, bias_ref, None, emit)


def early_attention(doc_lengths, queries, keys, values, crow, before, part):
    heads, rows = crow.shape
    skip = sum(EARLY[:part]) // 2
    wide = pl.BlockSpec((rows, 256), lambda j: (0, j + skip))
    count = EARLY[part]
    return pl.pallas_call(
        functools.partial(early_kernel, skip),
        grid=(count // 2,),
        in_specs=[SMEM, wide, wide, wide, whole((heads, rows))] + [pl.BlockSpec(memory_space=pl.ANY)] * len(before),
        out_specs=wide,
        out_shape=jax.ShapeDtypeStruct((rows, sum(EARLY) * 128), F32),
        input_output_aliases={5: 0} if before else {},
        scratch_shapes=[pltpu.VMEM((rows, CHUNK), F32), pltpu.VMEM((rows, 128), F32)],
        compiler_params=LIMIT,
        cost_estimate=pl.CostEstimate(
            flops=count * rows * CHUNK * 128 * 8, bytes_accessed=rows * count * 128 * 10, transcendentals=count * rows * CHUNK
        ),
        name="early_attention",
    )(doc_lengths, queries, keys, values, crow, *before)


def gather_last(refs, last_ref):
    me = lax.axis_index("seq") % MEMBERS
    for x, ref in enumerate(refs):
        last_ref[me ^ x] = ref[...]


def decay_of(last_ref, e, i, hp):
    extra = last_ref[e, hp * 128 :, :].astype(F32)
    return extra[i : i + 1, :] + extra[hp + i : hp + i + 1, :]


def scan_quad(rows, len_ref, last_ref, state, i, hp, note):
    members = last_ref.shape[0]
    ends = read_ends(len_ref, len_ref.shape[0])
    base = lax.axis_index("seq") // members * members
    for e in range(members):
        note(e, state)
        low = (base + e) * rows
        inner = jnp.int32(0)
        for end in ends:
            inner = inner + ((end > low) & (end < low + rows)).astype(jnp.int32)
        passes = (inner == 0).astype(F32)
        piece = last_ref[e, i * 128 : (i + 1) * 128, :].astype(F32)
        state = state * (decay_of(last_ref, e, i, hp) * passes) + piece
    return state


def leave_kernel(rows, len_ref, *refs):
    out_ref, last_ref = refs[-2:]
    gather_last(refs[:MEMBERS], last_ref)
    hp = out_ref.shape[0]
    for i in range(hp):
        state = jnp.zeros((128, 128), F32)
        if len(refs) > MEMBERS + 2:
            state = refs[MEMBERS][i].astype(F32)
        state = scan_quad(rows, len_ref, last_ref, state, i, hp, lambda e, x: None)
        out_ref[i] = state.astype(BF16)


def leave_quad(doc_lengths, last, coming, rows, hp):
    return pl.pallas_call(
        functools.partial(leave_kernel, rows),
        in_specs=[SMEM] + [VMEM] * (MEMBERS + len(coming)),
        out_specs=VMEM,
        out_shape=jax.ShapeDtypeStruct((hp, 128, 128), BF16),
        scratch_shapes=[pltpu.VMEM((MEMBERS,) + last[0].shape, BF16)],
        compiler_params=SMALL,
        name="leave_quad",
    )(doc_lengths, *last, *coming)


def enter_kernel(rows, len_ref, *refs):
    in_ref, out_refs, last_ref, state_ref = refs[MEMBERS], refs[MEMBERS + 1 : -2], refs[-2], refs[-1]
    gather_last(refs[:MEMBERS], last_ref)
    hp = in_ref.shape[0]

    def note(i, e, state):
        state_ref[e, i] = state

    for i in range(hp):
        scan_quad(rows, len_ref, last_ref, in_ref[i].astype(F32), i, hp, functools.partial(note, i))
    me = lax.axis_index("seq") % MEMBERS
    for x, out_ref in enumerate(out_refs):
        out_ref[...] = state_ref[me ^ x].astype(BF16)


def enter_states(doc_lengths, last, coming, rows):
    return pl.pallas_call(
        functools.partial(enter_kernel, rows),
        in_specs=[SMEM] + [VMEM] * (MEMBERS + 1),
        out_specs=[VMEM] * MEMBERS,
        out_shape=[jax.ShapeDtypeStruct(coming.shape, BF16)] * MEMBERS,
        scratch_shapes=[
            pltpu.VMEM((MEMBERS,) + last[0].shape, BF16),
            pltpu.VMEM((MEMBERS,) + coming.shape, F32),
        ],
        compiler_params=SMALL,
        name="enter_states",
    )(doc_lengths, *last, coming)


def final_kernel(rows, len_ref, own_ref, *refs):
    side_ref, rest_ref, in_ref, out_ref, last_ref, state_ref, piece_ref = refs[MEMBERS:]
    gather_last(refs[:MEMBERS], last_ref)
    hp = in_ref.shape[0]
    ends = read_ends(len_ref, len_ref.shape[0])
    base = lax.axis_index("seq") // MEMBERS * MEMBERS

    def note(i, e, state):
        state_ref[e, i] = state

    for i in range(hp):
        scan_quad(rows, len_ref, last_ref, in_ref[i].astype(F32), i, hp, functools.partial(note, i))
    out_ref[...] = jnp.zeros_like(out_ref)
    place, previous = jnp.int32(0), jnp.int32(-1)
    for d in range(len(ends)):
        device = (ends[d] - 1) // rows
        place = jnp.where(device == previous, place + 1, 0)
        previous = device
        at_end = ends[d] == (device + 1) * rows
        enters = (place == 0).astype(F32)
        mine = device // MEMBERS * MEMBERS == base
        e = device - base

        def put(i, local):
            state = local.astype(F32) + state_ref[e, i] * (decay_of(last_ref, e, i, hp) * enters)
            out_ref[own_ref[d], i] = state.astype(BF16)

        @pl.when(mine & at_end)
        def _():
            for i in range(hp):
                put(i, last_ref[e, i * 128 : (i + 1) * 128, :])

        @pl.when(mine & jnp.logical_not(at_end) & (place < SIDE))
        def _():
            for i in range(hp):
                put(i, side_ref[e, pl.ds(pl.multiple_of((place * hp + i) * 128, 128), 128), :])

        @pl.when(mine & jnp.logical_not(at_end) & (place >= SIDE))
        def _():
            for i in range(hp):
                row = pl.multiple_of(((place - SIDE) * hp + i) * 128, 128)
                pltpu.sync_copy(rest_ref.at[e, pl.ds(row, 128), :], piece_ref)
                put(i, piece_ref[...])


def final_states(doc_lengths, owner_ids, last, side, rest, coming, rows, spread):
    return pl.pallas_call(
        functools.partial(final_kernel, rows),
        in_specs=[SMEM, SMEM] + [VMEM] * (MEMBERS + 1) + [pl.BlockSpec(memory_space=pl.ANY), VMEM],
        out_specs=VMEM,
        out_shape=jax.ShapeDtypeStruct((spread,) + coming.shape, BF16),
        scratch_shapes=[
            pltpu.VMEM((MEMBERS,) + last[0].shape, BF16),
            pltpu.VMEM((MEMBERS,) + coming.shape, F32),
            pltpu.VMEM((128, 128), BF16),
        ],
        compiler_params=SMALL,
        name="final_states",
    )(doc_lengths, owner_ids, *last, side, rest, coming)


def finish_kernel(
    len_ref, q_ref, k_ref, v_ref, e0, e1, e2, e3, local_ref, gate_ref, gain_ref, crow_ref, out_ref, bias_ref, ccol_ref
):
    rows = q_ref.shape[0]
    step = pl.program_id(0)
    me = lax.axis_index("seq")
    first = me * rows
    ends = read_ends(len_ref, len_ref.shape[0])
    hp = e0.shape[0]
    pairs = sum(EARLY) // 2

    def entering(h):
        far = (h // hp) ^ (me % MEMBERS)
        state = e0[h % hp]
        for x, ref in ((1, e1), (2, e2), (3, e3)):
            state = jnp.where(far == x, ref[h % hp], state)
        return state

    def emit(lanes, t0, size, att):
        mean = jnp.mean(att * att, axis=1, keepdims=True)
        gate = 0.5 + 0.5 * jnp.tanh(0.5 * gate_ref[t0 : t0 + size, lanes].astype(F32))
        gain = gain_ref[:, lanes].astype(F32)
        out_ref[t0 : t0 + size, lanes] = (att * lax.rsqrt(mean + 1e-06) * (gain * gate)).astype(BF16)

    @pl.when(step == 0)
    def _():
        fill_bias(first, ends, bias_ref)
        fill_columns(crow_ref, ccol_ref)

    @pl.when(step < pairs)
    def _():
        reach = run_end(ends, first - 1) - first
        cols = [head_column(ccol_ref, step * 2 + i) for i in range(2)]
        states = [entering(step * 2 + i) for i in range(2)]
        lanes = [slice(i * 128, (i + 1) * 128) for i in range(2)]
        for t0 in range(0, rows, 256):
            carry = [dot(q_ref[t0 : t0 + 256, lanes[i]], states[i]) for i in range(2)]
            at = t0 + iota((256, 1), 0)
            for i in range(2):
                lead = jnp.exp2(jnp.where(at < reach, cols[i][t0 : t0 + 256], NEG))
                emit(lanes[i], t0, 256, local_ref[t0 : t0 + 256, lanes[i]] + lead * carry[i])

    @pl.when(step >= pairs)
    def _():
        states = [entering(step * 2 + i).astype(F32) for i in range(2)]
        attend(first, ends, q_ref, k_ref, v_ref, step * 2, crow_ref, ccol_ref, bias_ref, states, emit)


def finish(doc_lengths, queries, keys, values, entering, local, gate, gain, crow):
    heads, rows = crow.shape
    pairs = sum(EARLY) // 2
    wide = pl.BlockSpec((rows, 256), lambda j: (0, j))
    late = pl.BlockSpec((rows, 256), lambda j: (0, jnp.maximum(j, pairs)))
    return pl.pallas_call(
        finish_kernel,
        grid=(heads // 2,),
        in_specs=[SMEM, wide, late, late]
        + [whole(e.shape) for e in entering]
        + [
            pl.BlockSpec((rows, 256), lambda j: (0, jnp.minimum(j, pairs - 1))),
            wide,
            pl.BlockSpec((1, 256), lambda j: (0, j)),
            whole((heads, rows)),
        ],
        out_specs=wide,
        out_shape=jax.ShapeDtypeStruct((rows, heads * 128), BF16),
        scratch_shapes=[pltpu.VMEM((rows, CHUNK), F32), pltpu.VMEM((rows, 128), F32)],
        compiler_params=LIMIT,
        cost_estimate=pl.CostEstimate(
            flops=heads * rows * CHUNK * 128 * 8, bytes_accessed=rows * heads * 128 * 10, transcendentals=heads * rows * CHUNK
        ),
        name="finish",
    )(doc_lengths, queries, keys, values, *entering, local, gate, gain, crow)


def swap(x, groups=None):
    return lax.all_to_all(x, "seq", split_axis=0, concat_axis=0, axis_index_groups=groups, tiled=True)


def by_distance(parcels, spread):
    return [parcels[0]] + [
        lax.ppermute(parcels[x], "seq", [(s, s ^ x) for s in range(spread)]) for x in range(1, MEMBERS)
    ]


def on_device(spread, queries, keys, values, log_decay, gate, gain, doc_lengths, owner_ids):
    rows, heads = log_decay.shape
    quads = spread // MEMBERS
    hp = heads // MEMBERS
    near = [[q * MEMBERS + m for m in range(MEMBERS)] for q in range(quads)]
    onward = [(s, s + MEMBERS) for s in range(spread - MEMBERS)]
    decay_rows = log_decay.T
    barrier = lax.optimization_barrier

    side, crow, flags, *last = piece_states(doc_lengths, owner_ids, decay_rows, keys, values, SIDE)
    last = by_distance(last, spread)
    gain = gain.reshape(1, -1)
    crowded = flags[1] > 0
    from_quad = [flags[0] == q for q in range(1, quads)]
    slots = max(doc_lengths.shape[0] - 1, SIDE + 1)

    def send_rest():
        return swap(piece_states(doc_lengths, owner_ids, decay_rows, keys, values, slots)[0], near)

    none = jnp.zeros((MEMBERS, (slots - SIDE) * hp * 128, 128), BF16)
    rest = lax.cond(crowded, send_rest, lambda: none)
    last, side, gain, rest, from_quad = barrier((last, side, gain, rest, from_quad))

    side = swap(side, near)
    coming = []
    for _ in range(quads - 1):
        leaving = leave_quad(doc_lengths, last, coming, rows, hp)
        coming = [lax.ppermute(leaving, "seq", onward)]
    crow_1, leaving = barrier((crow, leaving))
    local = early_attention(doc_lengths, queries, keys, values, crow_1, [], 0)
    coming, local, side = barrier((coming[0], local, side))

    entering = by_distance(enter_states(doc_lengths, last, coming, rows), spread)
    finals = final_states(doc_lengths, owner_ids, last, side, rest, coming, rows, spread)
    entering, finals = barrier((entering, finals))
    arrived = swap(finals).reshape(quads, 1, heads, 128, 128)
    mixed = finish(doc_lengths, queries, keys, values, entering, local, gate, gain, crow)
    owned = arrived[0]
    for q in range(1, quads):
        owned = jnp.where(from_quad[q - 1], arrived[q], owned)
    return mixed, owned


def solution(mesh):
    placed = (
        P(("groups", "seq"), "tp"),
        P(("groups", "seq"), "tp"),
        P(("groups", "seq"), "tp"),
        P(("groups", "seq"), "tp"),
        P(("groups", "seq"), "tp"),
        P("tp"),
        P("groups"),
        P("groups"),
    )
    return jax.shard_map(
        functools.partial(on_device, mesh.shape["seq"]),
        mesh=mesh,
        in_specs=placed,
        out_specs=(P(("groups", "seq"), "tp"), P(("groups", "seq"), "tp", None, None)),
        check_vma=False,
    )
```

```python
import functools
import math

import jax
import jax.numpy as jnp
from jax import lax
from jax.experimental import pallas as pl
from jax.experimental.pallas import tpu as pltpu
from jax.sharding import PartitionSpec as P

BLK = 512
SIDE = 3
EXTRA = 16
CHUNK = 256
MEMBERS = 4
TILE = 256
EARLY = (8,)
NEG = -1e30
LOG2E = math.log2(math.e)
SCALE = 128**-0.5
F32, BF16 = jnp.float32, jnp.bfloat16
SMEM = pl.BlockSpec(memory_space=pltpu.SMEM)
VMEM = pl.BlockSpec(memory_space=pltpu.VMEM)
LIMIT = pltpu.CompilerParams(vmem_limit_bytes=60 * 2**20)
SMALL = pltpu.CompilerParams(vmem_limit_bytes=48 * 2**20)


def dot(a, b, contract=((1,), (0,))):
    return lax.dot_general(a, b, (contract, ((), ())), preferred_element_type=F32)


def iota(shape, dim):
    return lax.broadcasted_iota(jnp.int32, shape, dim)


def read_ends(len_ref, count):
    ends, total = [], jnp.int32(0)
    for d in range(count):
        total = total + len_ref[d]
        ends.append(total)
    return ends


def run_end(ends, pos):
    best = ends[-1]
    for e in reversed(ends[:-1]):
        best = jnp.where(e > pos, e, best)
    return best


def run_start(ends, pos):
    best = jnp.zeros_like(pos)
    for e in ends[:-1]:
        best = jnp.where(e <= pos, e, best)
    return best


def split3(x):
    hi = x.astype(BF16)
    rest = x - hi.astype(F32)
    mid = rest.astype(BF16)
    return hi, mid, (rest - mid.astype(F32)).astype(BF16)


def cum_rows(ld_ref, crow_ref):
    heads, rows = ld_ref.shape
    upper = (iota((BLK, BLK), 0) <= iota((BLK, BLK), 1)).astype(F32).astype(BF16)
    base = jnp.zeros((heads, 1), F32)
    for b in range(rows // BLK):
        part = ld_ref[:, b * BLK : (b + 1) * BLK] * LOG2E
        sums = dot(jnp.concatenate(split3(part), axis=0), upper)
        row = sums[2 * heads :] + sums[heads : 2 * heads] + sums[:heads] + base
        crow_ref[:, b * BLK : (b + 1) * BLK] = row
        base = row[:, BLK - 1 :]


def value_at(cum, at, index):
    return jnp.sum(jnp.where(at == index, cum, 0.0), axis=1, keepdims=True)


def span_weights(cum, at, low, high):
    inside = (at >= low) & (at <= high)
    return jnp.exp2(jnp.where(inside, value_at(cum, at, high) - cum, NEG) + math.log2(SCALE))


def weigh(flipped, w_ref, h):
    weights = [jnp.broadcast_to(w_ref[pl.ds(h + j, 1), :], (128, flipped.shape[1])) for j in range(2)]
    return (flipped.astype(F32) * jnp.concatenate(weights, axis=0)).astype(BF16)


def whole(shape):
    return pl.BlockSpec(shape, lambda j: (0,) * len(shape))


def pieces_kernel(rest, len_ref, own_ref, ld_ref, k_ref, v_ref, *refs):
    if rest:
        side_ref, crow_ref, w_ref, keep_ref = refs
        slots = keep_ref.shape[0]
    else:
        side_ref, crow_ref, flag_ref = refs[:3]
        last_refs = refs[3 : 3 + MEMBERS]
        w_ref, first_ref, high_ref, weighted_ref, prefix_ref = refs[3 + MEMBERS :]
        slots = SIDE
    heads, rows = crow_ref.shape
    step = pl.program_id(0)
    hp = v_ref.shape[1] // 128
    me = lax.axis_index("seq")

    @pl.when(step == 0)
    def _():
        cum_rows(ld_ref, crow_ref)
        first = me * rows
        last = first + rows - 1
        ends = read_ends(len_ref, len_ref.shape[0])
        starts = [jnp.int32(0)] + ends[:-1]
        lows = [jnp.int32(0)] * slots
        highs = [jnp.int32(-1)] * slots
        place, rank, previous = jnp.int32(0), jnp.int32(0), jnp.int32(-1)
        crowded, owned_in = jnp.int32(0), jnp.int32(0)
        for d in range(len(ends)):
            here = (ends[d] > first) & (ends[d] <= last)
            low = jnp.maximum(starts[d] - first, 0)
            for s in range(slots):
                mine = here & (place == s + (SIDE if rest else 0))
                lows[s] = jnp.where(mine, low, lows[s])
                highs[s] = jnp.where(mine, ends[d] - 1 - first, highs[s])
            place = place + here.astype(jnp.int32)
            device = (ends[d] - 1) // rows
            rank = jnp.where(device == previous, rank + 1, 0)
            previous = device
            late = ((rank >= SIDE) & (ends[d] != (device + 1) * rows)).astype(jnp.int32)
            crowded = jnp.maximum(crowded, late)
            owned_in = jnp.where(own_ref[d] == me, device, owned_in)
        at = iota((heads, rows), 1)
        cum = crow_ref[...]
        total = jnp.zeros((heads, rows), F32)
        for s in range(slots):
            total = total + span_weights(cum, at, lows[s], highs[s])
        if rest:
            row_at = iota((16, rows), 1)
            for s in range(slots):
                inside = (row_at >= lows[s]) & (row_at <= highs[s])
                keep_ref[s] = jnp.where(inside, 1.0, 0.0).astype(BF16)
        else:
            total = total + span_weights(cum, at, jnp.maximum(run_start(ends, last) - first, 0), rows - 1)
            flag_ref[0] = owned_in // MEMBERS
            flag_ref[1] = crowded
            high = jnp.int32(-1)
            for s in range(slots):
                high = jnp.maximum(high, highs[s])
                high_ref[s] = high
            stop = jnp.minimum(run_end(ends, first) - 1 - first, rows - 1)
            goes_on = (run_start(ends, first) < first).astype(F32)
            first_ref[...] = jnp.broadcast_to(jnp.exp2(value_at(cum, at, stop)) * goes_on, (heads, 128))
        w_ref[...] = total

    def own(states, j):
        return states[j * 128 : (j + 1) * 128, j * 128 : (j + 1) * 128]

    if rest:
        for i in range(0, hp, 2):
            lanes = slice(i * 128, (i + 2) * 128)
            weighted = weigh(k_ref[:, lanes].T, w_ref, step * hp + i).reshape(16, 16, rows)
            for s in range(slots):
                states = dot((weighted * keep_ref[s][None]).reshape(256, rows), v_ref[:, lanes])
                for j in range(2):
                    at = (s * hp + i + j) * 128
                    side_ref[0, at : at + 128, :] = own(states, j).astype(BF16)
        return

    pairs = range(0, hp, 2)
    lanes = {i: slice(i * 128, (i + 2) * 128) for i in pairs}
    for i in pairs:
        weighted_ref[lanes[i], :] = weigh(k_ref[:, lanes[i]].T, w_ref, step * hp + i)
    totals = {}
    for i in pairs:
        sums = [jnp.zeros((128, 128), F32)] * 2
        for t in range(rows // TILE):
            span = slice(t * TILE, (t + 1) * TILE)
            states = dot(weighted_ref[lanes[i], span], v_ref[span, lanes[i]])
            for j in range(2):
                prefix_ref[t, i + j] = sums[j]
                sums[j] = sums[j] + own(states, j)
        totals[i] = sums
    ended = {i: [jnp.zeros((128, 128), F32)] * 2 for i in pairs}
    for s in range(slots):
        high = high_ref[s]
        tile = jnp.maximum(high, 0) // TILE
        start = pl.multiple_of(tile * TILE, TILE)
        keep = jnp.where(start + iota((16, TILE), 1) <= high, 1.0, 0.0).astype(BF16)
        for i in pairs:
            kept = weighted_ref[lanes[i], pl.ds(start, TILE)].reshape(16, 16, TILE) * keep[None]
            states = dot(kept.reshape(256, TILE), v_ref[pl.ds(start, TILE), lanes[i]])
            for j in range(2):
                until = own(states, j) + prefix_ref[tile, i + j]
                at = (s * hp + i + j) * 128
                side_ref[0, at : at + 128, :] = (until - ended[i][j]).astype(BF16)
                ended[i][j] = until
    rate = first_ref[pl.ds(step * hp, hp), :]
    high = rate.astype(BF16).astype(F32)
    pad = jnp.zeros((EXTRA - 2 * hp, 128), F32)
    tail = jnp.concatenate([high, rate - high, pad], axis=0).astype(BF16)
    last_states = [(totals[i][j] - ended[i][j]).astype(BF16) for i in pairs for j in range(2)]
    for x, last_ref in enumerate(last_refs):

        @pl.when((step ^ (me % MEMBERS)) == x)
        def _():
            for i in range(hp):
                last_ref[i * 128 : (i + 1) * 128, :] = last_states[i]
            last_ref[hp * 128 :, :] = tail


def piece_states(doc_lengths, owner_ids, decay_rows, keys, values, slots):
    heads, rows = decay_rows.shape
    rest = slots > SIDE
    count = slots - SIDE if rest else slots
    hp = heads // MEMBERS
    wide = pl.BlockSpec((rows, hp * 128), lambda j: (0, j))
    side = (count * hp * 128, 128)
    shapes = [jax.ShapeDtypeStruct((MEMBERS,) + side, BF16), jax.ShapeDtypeStruct((heads, rows), F32)]
    specs = [pl.BlockSpec((1,) + side, lambda j: (j, 0, 0)), whole((heads, rows))]
    scratch = [pltpu.VMEM((heads, rows), F32)]
    if rest:
        scratch.append(pltpu.VMEM((count, 16, rows), BF16))
    else:
        last = (hp * 128 + EXTRA, 128)
        shapes += [jax.ShapeDtypeStruct((2,), jnp.int32)] + [jax.ShapeDtypeStruct(last, BF16)] * MEMBERS
        specs += [SMEM] + [whole(last)] * MEMBERS
        scratch += [
            pltpu.VMEM((heads, 128), F32),
            pltpu.SMEM((SIDE,), jnp.int32),
            pltpu.VMEM((hp * 128, rows), BF16),
            pltpu.VMEM((rows // TILE, hp, 128, 128), F32),
        ]
    return pl.pallas_call(
        functools.partial(pieces_kernel, rest),
        grid=(MEMBERS,),
        in_specs=[SMEM, SMEM, whole((heads, rows)), wide, wide],
        out_specs=specs,
        out_shape=shapes,
        scratch_shapes=scratch,
        compiler_params=LIMIT,
        cost_estimate=pl.CostEstimate(
            flops=2 * heads * rows * 128 * 256, bytes_accessed=rows * heads * 128 * 4, transcendentals=heads * rows
        ),
        name="piece_states",
    )(doc_lengths, owner_ids, decay_rows, keys, values)


def head_column(ccol_ref, h):
    cols = ccol_ref[...]
    return jnp.sum(jnp.where(iota(cols.shape, 1) == h, cols, 0.0), axis=1, keepdims=True)


def fill_columns(crow_ref, ccol_ref):
    heads, rows = crow_ref.shape
    for r0 in range(0, rows, 128):
        part = crow_ref[:, r0 : r0 + 128]
        part = jnp.concatenate([part, jnp.zeros((128 - heads, 128), F32)], axis=0)
        ccol_ref[r0 : r0 + 128, :] = part.T


def fill_bias(first, ends, bias_ref):
    for c in range(bias_ref.shape[0] // CHUNK):
        base = first + c * CHUNK
        t_pos = base + iota((CHUNK, 1), 0)
        start = run_start(ends, t_pos)
        s_pos = base + iota((CHUNK, CHUNK), 1)
        keep = (s_pos <= t_pos) & (s_pos >= start)
        bias_ref[c * CHUNK : (c + 1) * CHUNK, :] = jnp.where(keep, math.log2(SCALE), NEG)


def attend(first, ends, q_ref, k_ref, v_ref, h, crow_ref, ccol_ref, bias_ref, states, emit):
    rows = q_ref.shape[0]
    pair = range(2)
    half = CHUNK // 2
    lanes = [slice(i * 128, (i + 1) * 128) for i in pair]
    row_all = [crow_ref[pl.ds(h + i, 1), :] for i in pair]
    col_all = [head_column(ccol_ref, h + i) for i in pair]
    starts = range(0, rows, CHUNK)
    spans = [slice(r0, r0 + CHUNK) for r0 in starts]
    reach = [run_end(ends, first + r0 - 1) - (first + r0) for r0 in starts]
    base = [[row_all[i][:, r0 - 1 : r0] if r0 else jnp.zeros((1, 1), F32) for r0 in starts] for i in pair]

    fresh = [[], []]
    for c, r0 in enumerate(starts[:-1]):
        since = run_start(ends, first + r0 + CHUNK - 1) - (first + r0)
        inside = iota((1, CHUNK), 1) >= since
        for i in pair:
            row = row_all[i][:, spans[c]]
            weight = jnp.exp2(jnp.where(inside, row[:, CHUNK - 1 :] - row, NEG) + math.log2(SCALE))
            flipped = k_ref[spans[c], lanes[i]].T
            fresh[i].append(dot((flipped.astype(F32) * weight).astype(BF16), v_ref[spans[c], lanes[i]]))
    carried = []
    for i in pair:
        state = None if states is None else states[i]
        chain = [None if state is None else state.astype(BF16)]
        for c in range(len(starts) - 1):
            if state is None:
                state = fresh[i][c]
            else:
                total = row_all[i][:, starts[c] + CHUNK - 1 : starts[c] + CHUNK]
                state = fresh[i][c] + state * jnp.exp2(jnp.where(CHUNK <= reach[c], total - base[i][c], NEG))
            chain.append(state.astype(BF16))
        carried.append(chain)

    def products(c):
        result = []
        for i in pair:
            query = q_ref[spans[c], lanes[i]]
            scores = dot(query, k_ref[spans[c], lanes[i]], ((1,), (1,)))
            result.append((scores, None if carried[i][c] is None else dot(query, carried[i][c])))
        return result

    ahead = products(0)
    for c, r0 in enumerate(starts):
        current = ahead
        if c + 1 < len(starts):
            ahead = products(c + 1)
        for part in range(2):
            t0, width = part * half, (part + 1) * half
            rows_here = slice(r0 + t0, r0 + t0 + half)
            for i in pair:
                scores, carry = current[i]
                col = col_all[i][rows_here]
                decay = jnp.exp2((col - row_all[i][:, r0 : r0 + width]) + bias_ref[rows_here, :width])
                weights = (scores[t0 : t0 + half, :width] * decay).astype(BF16)
                att = dot(weights, v_ref[r0 : r0 + width, lanes[i]])
                if carry is not None:
                    lead = jnp.exp2(jnp.where(t0 + iota((half, 1), 0) < reach[c], col - base[i][c], NEG))
                    att = att + lead * carry[t0 : t0 + half]
                emit(lanes[i], r0 + t0, half, att)


def early_kernel(pairs_before, len_ref, q_ref, k_ref, v_ref, crow_ref, *refs):
    out_ref, bias_ref, ccol_ref = refs[-3:]
    rows = q_ref.shape[0]
    step = pl.program_id(0)
    first = lax.axis_index("seq") * rows
    ends = read_ends(len_ref, len_ref.shape[0])

    @pl.when(step == 0)
    def _():
        fill_bias(first, ends, bias_ref)
        fill_columns(crow_ref, ccol_ref)

    def emit(lanes, t0, size, att):
        out_ref[t0 : t0 + size, lanes] = att

    attend(first, ends, q_ref, k_ref, v_ref, (step + pairs_before) * 2, crow_ref, ccol_ref, bias_ref, None, emit)


def early_attention(doc_lengths, queries, keys, values, crow, before, part):
    heads, rows = crow.shape
    skip = sum(EARLY[:part]) // 2
    wide = pl.BlockSpec((rows, 256), lambda j: (0, j + skip))
    count = EARLY[part]
    return pl.pallas_call(
        functools.partial(early_kernel, skip),
        grid=(count // 2,),
        in_specs=[SMEM, wide, wide, wide, whole((heads, rows))] + [pl.BlockSpec(memory_space=pl.ANY)] * len(before),
        out_specs=wide,
        out_shape=jax.ShapeDtypeStruct((rows, sum(EARLY) * 128), F32),
        input_output_aliases={5: 0} if before else {},
        scratch_shapes=[pltpu.VMEM((rows, CHUNK), F32), pltpu.VMEM((rows, 128), F32)],
        compiler_params=LIMIT,
        cost_estimate=pl.CostEstimate(
            flops=count * rows * CHUNK * 128 * 8, bytes_accessed=rows * count * 128 * 10, transcendentals=count * rows * CHUNK
        ),
        name="early_attention",
    )(doc_lengths, queries, keys, values, crow, *before)


def gather_last(refs, last_ref):
    me = lax.axis_index("seq") % MEMBERS
    for x, ref in enumerate(refs):
        last_ref[me ^ x] = ref[...]


def decay_of(last_ref, e, i, hp):
    extra = last_ref[e, hp * 128 :, :].astype(F32)
    return extra[i : i + 1, :] + extra[hp + i : hp + i + 1, :]


def scan_quad(rows, len_ref, last_ref, state, i, hp, note):
    members = last_ref.shape[0]
    ends = read_ends(len_ref, len_ref.shape[0])
    base = lax.axis_index("seq") // members * members
    for e in range(members):
        note(e, state)
        low = (base + e) * rows
        inner = jnp.int32(0)
        for end in ends:
            inner = inner + ((end > low) & (end < low + rows)).astype(jnp.int32)
        passes = (inner == 0).astype(F32)
        piece = last_ref[e, i * 128 : (i + 1) * 128, :].astype(F32)
        state = state * (decay_of(last_ref, e, i, hp) * passes) + piece
    return state


def leave_kernel(rows, len_ref, *refs):
    out_ref, last_ref = refs[-2:]
    gather_last(refs[:MEMBERS], last_ref)
    hp = out_ref.shape[0]
    for i in range(hp):
        state = jnp.zeros((128, 128), F32)
        if len(refs) > MEMBERS + 2:
            state = refs[MEMBERS][i].astype(F32)
        state = scan_quad(rows, len_ref, last_ref, state, i, hp, lambda e, x: None)
        out_ref[i] = state.astype(BF16)


def leave_quad(doc_lengths, last, coming, rows, hp):
    return pl.pallas_call(
        functools.partial(leave_kernel, rows),
        in_specs=[SMEM] + [VMEM] * (MEMBERS + len(coming)),
        out_specs=VMEM,
        out_shape=jax.ShapeDtypeStruct((hp, 128, 128), BF16),
        scratch_shapes=[pltpu.VMEM((MEMBERS,) + last[0].shape, BF16)],
        compiler_params=SMALL,
        name="leave_quad",
    )(doc_lengths, *last, *coming)


def enter_kernel(rows, len_ref, *refs):
    in_ref, out_refs, last_ref, state_ref = refs[MEMBERS], refs[MEMBERS + 1 : -2], refs[-2], refs[-1]
    gather_last(refs[:MEMBERS], last_ref)
    hp = in_ref.shape[0]

    def note(i, e, state):
        state_ref[e, i] = state

    for i in range(hp):
        scan_quad(rows, len_ref, last_ref, in_ref[i].astype(F32), i, hp, functools.partial(note, i))
    me = lax.axis_index("seq") % MEMBERS
    for x, out_ref in enumerate(out_refs):
        out_ref[...] = state_ref[me ^ x].astype(BF16)


def enter_states(doc_lengths, last, coming, rows):
    return pl.pallas_call(
        functools.partial(enter_kernel, rows),
        in_specs=[SMEM] + [VMEM] * (MEMBERS + 1),
        out_specs=[VMEM] * MEMBERS,
        out_shape=[jax.ShapeDtypeStruct(coming.shape, BF16)] * MEMBERS,
        scratch_shapes=[
            pltpu.VMEM((MEMBERS,) + last[0].shape, BF16),
            pltpu.VMEM((MEMBERS,) + coming.shape, F32),
        ],
        compiler_params=SMALL,
        name="enter_states",
    )(doc_lengths, *last, coming)


def final_kernel(rows, len_ref, own_ref, *refs):
    side_ref, rest_ref, in_ref, out_ref, last_ref, state_ref, piece_ref = refs[MEMBERS:]
    gather_last(refs[:MEMBERS], last_ref)
    hp = in_ref.shape[0]
    ends = read_ends(len_ref, len_ref.shape[0])
    base = lax.axis_index("seq") // MEMBERS * MEMBERS

    def note(i, e, state):
        state_ref[e, i] = state

    for i in range(hp):
        scan_quad(rows, len_ref, last_ref, in_ref[i].astype(F32), i, hp, functools.partial(note, i))
    out_ref[...] = jnp.zeros_like(out_ref)
    place, previous = jnp.int32(0), jnp.int32(-1)
    for d in range(len(ends)):
        device = (ends[d] - 1) // rows
        place = jnp.where(device == previous, place + 1, 0)
        previous = device
        at_end = ends[d] == (device + 1) * rows
        enters = (place == 0).astype(F32)
        mine = device // MEMBERS * MEMBERS == base
        e = device - base

        def put(i, local):
            state = local.astype(F32) + state_ref[e, i] * (decay_of(last_ref, e, i, hp) * enters)
            out_ref[own_ref[d], i] = state.astype(BF16)

        @pl.when(mine & at_end)
        def _():
            for i in range(hp):
                put(i, last_ref[e, i * 128 : (i + 1) * 128, :])

        @pl.when(mine & jnp.logical_not(at_end) & (place < SIDE))
        def _():
            for i in range(hp):
                put(i, side_ref[e, pl.ds(pl.multiple_of((place * hp + i) * 128, 128), 128), :])

        @pl.when(mine & jnp.logical_not(at_end) & (place >= SIDE))
        def _():
            for i in range(hp):
                row = pl.multiple_of(((place - SIDE) * hp + i) * 128, 128)
                pltpu.sync_copy(rest_ref.at[e, pl.ds(row, 128), :], piece_ref)
                put(i, piece_ref[...])


def final_states(doc_lengths, owner_ids, last, side, rest, coming, rows, spread):
    return pl.pallas_call(
        functools.partial(final_kernel, rows),
        in_specs=[SMEM, SMEM] + [VMEM] * (MEMBERS + 1) + [pl.BlockSpec(memory_space=pl.ANY), VMEM],
        out_specs=VMEM,
        out_shape=jax.ShapeDtypeStruct((spread,) + coming.shape, BF16),
        scratch_shapes=[
            pltpu.VMEM((MEMBERS,) + last[0].shape, BF16),
            pltpu.VMEM((MEMBERS,) + coming.shape, F32),
            pltpu.VMEM((128, 128), BF16),
        ],
        compiler_params=SMALL,
        name="final_states",
    )(doc_lengths, owner_ids, *last, side, rest, coming)


def finish_kernel(
    len_ref, q_ref, k_ref, v_ref, e0, e1, e2, e3, local_ref, gate_ref, gain_ref, crow_ref, out_ref, bias_ref, ccol_ref
):
    rows = q_ref.shape[0]
    step = pl.program_id(0)
    me = lax.axis_index("seq")
    first = me * rows
    ends = read_ends(len_ref, len_ref.shape[0])
    hp = e0.shape[0]
    pairs = sum(EARLY) // 2

    def entering(h):
        far = (h // hp) ^ (me % MEMBERS)
        state = e0[h % hp]
        for x, ref in ((1, e1), (2, e2), (3, e3)):
            state = jnp.where(far == x, ref[h % hp], state)
        return state

    def emit(lanes, t0, size, att):
        mean = jnp.mean(att * att, axis=1, keepdims=True)
        gate = 0.5 + 0.5 * jnp.tanh(0.5 * gate_ref[t0 : t0 + size, lanes].astype(F32))
        gain = gain_ref[:, lanes].astype(F32)
        out_ref[t0 : t0 + size, lanes] = (att * lax.rsqrt(mean + 1e-06) * (gain * gate)).astype(BF16)

    @pl.when(step == 0)
    def _():
        fill_bias(first, ends, bias_ref)
        fill_columns(crow_ref, ccol_ref)

    @pl.when(step < pairs)
    def _():
        reach = run_end(ends, first - 1) - first
        cols = [head_column(ccol_ref, step * 2 + i) for i in range(2)]
        states = [entering(step * 2 + i) for i in range(2)]
        lanes = [slice(i * 128, (i + 1) * 128) for i in range(2)]
        for t0 in range(0, rows, 256):
            carry = [dot(q_ref[t0 : t0 + 256, lanes[i]], states[i]) for i in range(2)]
            at = t0 + iota((256, 1), 0)
            for i in range(2):
                lead = jnp.exp2(jnp.where(at < reach, cols[i][t0 : t0 + 256], NEG))
                emit(lanes[i], t0, 256, local_ref[t0 : t0 + 256, lanes[i]] + lead * carry[i])

    @pl.when(step >= pairs)
    def _():
        states = [entering(step * 2 + i).astype(F32) for i in range(2)]
        attend(first, ends, q_ref, k_ref, v_ref, step * 2, crow_ref, ccol_ref, bias_ref, states, emit)


def finish(doc_lengths, queries, keys, values, entering, local, gate, gain, crow):
    heads, rows = crow.shape
    pairs = sum(EARLY) // 2
    wide = pl.BlockSpec((rows, 256), lambda j: (0, j))
    late = pl.BlockSpec((rows, 256), lambda j: (0, jnp.maximum(j, pairs)))
    return pl.pallas_call(
        finish_kernel,
        grid=(heads // 2,),
        in_specs=[SMEM, wide, late, late]
        + [whole(e.shape) for e in entering]
        + [
            pl.BlockSpec((rows, 256), lambda j: (0, jnp.minimum(j, pairs - 1))),
            wide,
            pl.BlockSpec((1, 256), lambda j: (0, j)),
            whole((heads, rows)),
        ],
        out_specs=wide,
        out_shape=jax.ShapeDtypeStruct((rows, heads * 128), BF16),
        scratch_shapes=[pltpu.VMEM((rows, CHUNK), F32), pltpu.VMEM((rows, 128), F32)],
        compiler_params=LIMIT,
        cost_estimate=pl.CostEstimate(
            flops=heads * rows * CHUNK * 128 * 8, bytes_accessed=rows * heads * 128 * 10, transcendentals=heads * rows * CHUNK
        ),
        name="finish",
    )(doc_lengths, queries, keys, values, *entering, local, gate, gain, crow)


def swap(x, groups=None):
    return lax.all_to_all(x, "seq", split_axis=0, concat_axis=0, axis_index_groups=groups, tiled=True)


def by_distance(parcels, spread):
    return [parcels[0]] + [
        lax.ppermute(parcels[x], "seq", [(s, s ^ x) for s in range(spread)]) for x in range(1, MEMBERS)
    ]


def on_device(spread, queries, keys, values, log_decay, gate, gain, doc_lengths, owner_ids):
    rows, heads = log_decay.shape
    quads = spread // MEMBERS
    hp = heads // MEMBERS
    near = [[q * MEMBERS + m for m in range(MEMBERS)] for q in range(quads)]
    onward = [(s, s + MEMBERS) for s in range(spread - MEMBERS)]
    decay_rows = log_decay.T
    barrier = lax.optimization_barrier

    side, crow, flags, *last = piece_states(doc_lengths, owner_ids, decay_rows, keys, values, SIDE)
    last = by_distance(last, spread)
    gain = gain.reshape(1, -1)
    crowded = flags[1] > 0
    from_quad = [flags[0] == q for q in range(1, quads)]
    slots = max(doc_lengths.shape[0] - 1, SIDE + 1)

    def send_rest():
        return swap(piece_states(doc_lengths, owner_ids, decay_rows, keys, values, slots)[0], near)

    none = jnp.zeros((MEMBERS, (slots - SIDE) * hp * 128, 128), BF16)
    rest = lax.cond(crowded, send_rest, lambda: none)
    side, gain, rest, from_quad = barrier((side, gain, rest, from_quad))

    side = swap(side, near)
    coming = []
    for _ in range(quads - 1):
        leaving = leave_quad(doc_lengths, last, coming, rows, hp)
        coming = [lax.ppermute(leaving, "seq", onward)]
    crow_1, leaving = barrier((crow, leaving))
    local = early_attention(doc_lengths, queries, keys, values, crow_1, [], 0)
    coming, local, side = barrier((coming[0], local, side))

    entering = by_distance(enter_states(doc_lengths, last, coming, rows), spread)
    finals = final_states(doc_lengths, owner_ids, last, side, rest, coming, rows, spread)
    entering, finals = barrier((entering, finals))
    arrived = swap(finals).reshape(quads, 1, heads, 128, 128)
    mixed = finish(doc_lengths, queries, keys, values, entering, local, gate, gain, crow)
    owned = arrived[0]
    for q in range(1, quads):
        owned = jnp.where(from_quad[q - 1], arrived[q], owned)
    return mixed, owned


def solution(mesh):
    placed = (
        P(("groups", "seq"), "tp"),
        P(("groups", "seq"), "tp"),
        P(("groups", "seq"), "tp"),
        P(("groups", "seq"), "tp"),
        P(("groups", "seq"), "tp"),
        P("tp"),
        P("groups"),
        P("groups"),
    )
    return jax.shard_map(
        functools.partial(on_device, mesh.shape["seq"]),
        mesh=mesh,
        in_specs=placed,
        out_specs=(P(("groups", "seq"), "tp"), P(("groups", "seq"), "tp", None, None)),
        check_vma=False,
    )
```

```python
import functools
import math

import jax
import jax.numpy as jnp
from jax import lax
from jax.experimental import pallas as pl
from jax.experimental.pallas import tpu as pltpu
from jax.sharding import PartitionSpec as P

BLK = 512
SIDE = 3
EXTRA = 16
CHUNK = 256
MEMBERS = 4
TILE = 256
EARLY = (8,)
NEG = -1e30
LOG2E = math.log2(math.e)
SCALE = 128**-0.5
F32, BF16 = jnp.float32, jnp.bfloat16
SMEM = pl.BlockSpec(memory_space=pltpu.SMEM)
VMEM = pl.BlockSpec(memory_space=pltpu.VMEM)
LIMIT = pltpu.CompilerParams(vmem_limit_bytes=60 * 2**20)
SMALL = pltpu.CompilerParams(vmem_limit_bytes=48 * 2**20)


def dot(a, b, contract=((1,), (0,))):
    return lax.dot_general(a, b, (contract, ((), ())), preferred_element_type=F32)


def iota(shape, dim):
    return lax.broadcasted_iota(jnp.int32, shape, dim)


def read_ends(len_ref, count):
    ends, total = [], jnp.int32(0)
    for d in range(count):
        total = total + len_ref[d]
        ends.append(total)
    return ends


def run_end(ends, pos):
    best = ends[-1]
    for e in reversed(ends[:-1]):
        best = jnp.where(e > pos, e, best)
    return best


def run_start(ends, pos):
    best = jnp.zeros_like(pos)
    for e in ends[:-1]:
        best = jnp.where(e <= pos, e, best)
    return best


def split3(x):
    hi = x.astype(BF16)
    rest = x - hi.astype(F32)
    mid = rest.astype(BF16)
    return hi, mid, (rest - mid.astype(F32)).astype(BF16)


def cum_rows(ld_ref, crow_ref):
    heads, rows = ld_ref.shape
    upper = (iota((BLK, BLK), 0) <= iota((BLK, BLK), 1)).astype(F32).astype(BF16)
    base = jnp.zeros((heads, 1), F32)
    for b in range(rows // BLK):
        part = ld_ref[:, b * BLK : (b + 1) * BLK] * LOG2E
        sums = dot(jnp.concatenate(split3(part), axis=0), upper)
        row = sums[2 * heads :] + sums[heads : 2 * heads] + sums[:heads] + base
        crow_ref[:, b * BLK : (b + 1) * BLK] = row
        base = row[:, BLK - 1 :]


def value_at(cum, at, index):
    return jnp.sum(jnp.where(at == index, cum, 0.0), axis=1, keepdims=True)


def span_weights(cum, at, low, high):
    inside = (at >= low) & (at <= high)
    return jnp.exp2(jnp.where(inside, value_at(cum, at, high) - cum, NEG) + math.log2(SCALE))


def weigh(flipped, w_ref, h):
    weights = [jnp.broadcast_to(w_ref[pl.ds(h + j, 1), :], (128, flipped.shape[1])) for j in range(2)]
    return (flipped.astype(F32) * jnp.concatenate(weights, axis=0)).astype(BF16)


def whole(shape):
    return pl.BlockSpec(shape, lambda j: (0,) * len(shape))


def pieces_kernel(rest, len_ref, own_ref, ld_ref, k_ref, v_ref, *refs):
    if rest:
        side_ref, crow_ref, w_ref, keep_ref = refs
        slots = keep_ref.shape[0]
    else:
        crow_ref, flag_ref = refs[:2]
        side_refs, last_refs = refs[2 : 2 + MEMBERS], refs[2 + MEMBERS : 2 + 2 * MEMBERS]
        w_ref, first_ref, high_ref, weighted_ref, prefix_ref, parcel_ref = refs[2 + 2 * MEMBERS :]
        slots = SIDE
    heads, rows = crow_ref.shape
    step = pl.program_id(0)
    hp = v_ref.shape[1] // 128
    me = lax.axis_index("seq")

    @pl.when(step == 0)
    def _():
        cum_rows(ld_ref, crow_ref)
        first = me * rows
        last = first + rows - 1
        ends = read_ends(len_ref, len_ref.shape[0])
        starts = [jnp.int32(0)] + ends[:-1]
        lows = [jnp.int32(0)] * slots
        highs = [jnp.int32(-1)] * slots
        place, rank, previous = jnp.int32(0), jnp.int32(0), jnp.int32(-1)
        crowded, owned_in = jnp.int32(0), jnp.int32(0)
        for d in range(len(ends)):
            here = (ends[d] > first) & (ends[d] <= last)
            low = jnp.maximum(starts[d] - first, 0)
            for s in range(slots):
                mine = here & (place == s + (SIDE if rest else 0))
                lows[s] = jnp.where(mine, low, lows[s])
                highs[s] = jnp.where(mine, ends[d] - 1 - first, highs[s])
            place = place + here.astype(jnp.int32)
            device = (ends[d] - 1) // rows
            rank = jnp.where(device == previous, rank + 1, 0)
            previous = device
            late = ((rank >= SIDE) & (ends[d] != (device + 1) * rows)).astype(jnp.int32)
            crowded = jnp.maximum(crowded, late)
            owned_in = jnp.where(own_ref[d] == me, device, owned_in)
        at = iota((heads, rows), 1)
        cum = crow_ref[...]
        total = jnp.zeros((heads, rows), F32)
        for s in range(slots):
            total = total + span_weights(cum, at, lows[s], highs[s])
        if rest:
            row_at = iota((16, rows), 1)
            for s in range(slots):
                inside = (row_at >= lows[s]) & (row_at <= highs[s])
                keep_ref[s] = jnp.where(inside, 1.0, 0.0).astype(BF16)
        else:
            total = total + span_weights(cum, at, jnp.maximum(run_start(ends, last) - first, 0), rows - 1)
            flag_ref[0] = owned_in // MEMBERS
            flag_ref[1] = crowded
            high = jnp.int32(-1)
            for s in range(slots):
                high = jnp.maximum(high, highs[s])
                high_ref[s] = high
            stop = jnp.minimum(run_end(ends, first) - 1 - first, rows - 1)
            goes_on = (run_start(ends, first) < first).astype(F32)
            first_ref[...] = jnp.broadcast_to(jnp.exp2(value_at(cum, at, stop)) * goes_on, (heads, 128))
        w_ref[...] = total

    def own(states, j):
        return states[j * 128 : (j + 1) * 128, j * 128 : (j + 1) * 128]

    if rest:
        for i in range(0, hp, 2):
            lanes = slice(i * 128, (i + 2) * 128)
            weighted = weigh(k_ref[:, lanes].T, w_ref, step * hp + i).reshape(16, 16, rows)
            for s in range(slots):
                states = dot((weighted * keep_ref[s][None]).reshape(256, rows), v_ref[:, lanes])
                for j in range(2):
                    at = (s * hp + i + j) * 128
                    side_ref[0, at : at + 128, :] = own(states, j).astype(BF16)
        return

    pairs = range(0, hp, 2)
    lanes = {i: slice(i * 128, (i + 2) * 128) for i in pairs}
    for i in pairs:
        weighted_ref[lanes[i], :] = weigh(k_ref[:, lanes[i]].T, w_ref, step * hp + i)
    totals = {}
    for i in pairs:
        sums = [jnp.zeros((128, 128), F32)] * 2
        for t in range(rows // TILE):
            span = slice(t * TILE, (t + 1) * TILE)
            states = dot(weighted_ref[lanes[i], span], v_ref[span, lanes[i]])
            for j in range(2):
                prefix_ref[t, i + j] = sums[j]
                sums[j] = sums[j] + own(states, j)
        totals[i] = sums
    ended = {i: [jnp.zeros((128, 128), F32)] * 2 for i in pairs}
    for s in range(slots):
        high = high_ref[s]
        tile = jnp.maximum(high, 0) // TILE
        start = pl.multiple_of(tile * TILE, TILE)
        keep = jnp.where(start + iota((16, TILE), 1) <= high, 1.0, 0.0).astype(BF16)
        for i in pairs:
            kept = weighted_ref[lanes[i], pl.ds(start, TILE)].reshape(16, 16, TILE) * keep[None]
            states = dot(kept.reshape(256, TILE), v_ref[pl.ds(start, TILE), lanes[i]])
            for j in range(2):
                until = own(states, j) + prefix_ref[tile, i + j]
                at = (s * hp + i + j) * 128
                parcel_ref[at : at + 128, :] = (until - ended[i][j]).astype(BF16)
                ended[i][j] = until
    rate = first_ref[pl.ds(step * hp, hp), :]
    high = rate.astype(BF16).astype(F32)
    pad = jnp.zeros((EXTRA - 2 * hp, 128), F32)
    tail = jnp.concatenate([high, rate - high, pad], axis=0).astype(BF16)
    cut = SIDE * hp * 128
    for i in pairs:
        for j in range(2):
            at = cut + (i + j) * 128
            parcel_ref[at : at + 128, :] = (totals[i][j] - ended[i][j]).astype(BF16)
    parcel_ref[cut + hp * 128 :, :] = tail
    for x in range(MEMBERS):

        @pl.when((step ^ (me % MEMBERS)) == x)
        def _():
            side_refs[x][...] = parcel_ref[:cut, :]
            last_refs[x][...] = parcel_ref[cut:, :]


def piece_states(doc_lengths, owner_ids, decay_rows, keys, values, slots):
    heads, rows = decay_rows.shape
    rest = slots > SIDE
    count = slots - SIDE if rest else slots
    hp = heads // MEMBERS
    wide = pl.BlockSpec((rows, hp * 128), lambda j: (0, j))
    side = (count * hp * 128, 128)
    shapes, specs = [jax.ShapeDtypeStruct((heads, rows), F32)], [whole((heads, rows))]
    scratch = [pltpu.VMEM((heads, rows), F32)]
    if rest:
        shapes.insert(0, jax.ShapeDtypeStruct((MEMBERS,) + side, BF16))
        specs.insert(0, pl.BlockSpec((1,) + side, lambda j: (j, 0, 0)))
        scratch.append(pltpu.VMEM((count, 16, rows), BF16))
    else:
        last = (hp * 128 + EXTRA, 128)
        shapes += [jax.ShapeDtypeStruct((2,), jnp.int32)]
        shapes += [jax.ShapeDtypeStruct(shape, BF16) for shape in (side, last) for _ in range(MEMBERS)]
        specs += [SMEM] + [whole(shape) for shape in (side, last) for _ in range(MEMBERS)]
        scratch += [
            pltpu.VMEM((heads, 128), F32),
            pltpu.SMEM((SIDE,), jnp.int32),
            pltpu.VMEM((hp * 128, rows), BF16),
            pltpu.VMEM((rows // TILE, hp, 128, 128), F32),
            pltpu.VMEM((side[0] + last[0], 128), BF16),
        ]
    return pl.pallas_call(
        functools.partial(pieces_kernel, rest),
        grid=(MEMBERS,),
        in_specs=[SMEM, SMEM, whole((heads, rows)), wide, wide],
        out_specs=specs,
        out_shape=shapes,
        scratch_shapes=scratch,
        compiler_params=LIMIT,
        cost_estimate=pl.CostEstimate(
            flops=2 * heads * rows * 128 * 256, bytes_accessed=rows * heads * 128 * 4, transcendentals=heads * rows
        ),
        name="piece_states",
    )(doc_lengths, owner_ids, decay_rows, keys, values)


def head_column(ccol_ref, h):
    cols = ccol_ref[...]
    return jnp.sum(jnp.where(iota(cols.shape, 1) == h, cols, 0.0), axis=1, keepdims=True)


def fill_columns(crow_ref, ccol_ref):
    heads, rows = crow_ref.shape
    for r0 in range(0, rows, 128):
        part = crow_ref[:, r0 : r0 + 128]
        part = jnp.concatenate([part, jnp.zeros((128 - heads, 128), F32)], axis=0)
        ccol_ref[r0 : r0 + 128, :] = part.T


def fill_bias(first, ends, bias_ref):
    for c in range(bias_ref.shape[0] // CHUNK):
        base = first + c * CHUNK
        t_pos = base + iota((CHUNK, 1), 0)
        start = run_start(ends, t_pos)
        s_pos = base + iota((CHUNK, CHUNK), 1)
        keep = (s_pos <= t_pos) & (s_pos >= start)
        bias_ref[c * CHUNK : (c + 1) * CHUNK, :] = jnp.where(keep, math.log2(SCALE), NEG)


def attend(first, ends, q_ref, k_ref, v_ref, h, crow_ref, ccol_ref, bias_ref, states, emit):
    rows = q_ref.shape[0]
    pair = range(2)
    half = CHUNK // 2
    lanes = [slice(i * 128, (i + 1) * 128) for i in pair]
    row_all = [crow_ref[pl.ds(h + i, 1), :] for i in pair]
    col_all = [head_column(ccol_ref, h + i) for i in pair]
    starts = range(0, rows, CHUNK)
    spans = [slice(r0, r0 + CHUNK) for r0 in starts]
    reach = [run_end(ends, first + r0 - 1) - (first + r0) for r0 in starts]
    base = [[row_all[i][:, r0 - 1 : r0] if r0 else jnp.zeros((1, 1), F32) for r0 in starts] for i in pair]

    fresh = [[], []]
    for c, r0 in enumerate(starts[:-1]):
        since = run_start(ends, first + r0 + CHUNK - 1) - (first + r0)
        inside = iota((1, CHUNK), 1) >= since
        for i in pair:
            row = row_all[i][:, spans[c]]
            weight = jnp.exp2(jnp.where(inside, row[:, CHUNK - 1 :] - row, NEG) + math.log2(SCALE))
            flipped = k_ref[spans[c], lanes[i]].T
            fresh[i].append(dot((flipped.astype(F32) * weight).astype(BF16), v_ref[spans[c], lanes[i]]))
    carried = []
    for i in pair:
        state = None if states is None else states[i]
        chain = [None if state is None else state.astype(BF16)]
        for c in range(len(starts) - 1):
            if state is None:
                state = fresh[i][c]
            else:
                total = row_all[i][:, starts[c] + CHUNK - 1 : starts[c] + CHUNK]
                state = fresh[i][c] + state * jnp.exp2(jnp.where(CHUNK <= reach[c], total - base[i][c], NEG))
            chain.append(state.astype(BF16))
        carried.append(chain)

    def products(c):
        result = []
        for i in pair:
            query = q_ref[spans[c], lanes[i]]
            scores = dot(query, k_ref[spans[c], lanes[i]], ((1,), (1,)))
            result.append((scores, None if carried[i][c] is None else dot(query, carried[i][c])))
        return result

    ahead = products(0)
    for c, r0 in enumerate(starts):
        current = ahead
        if c + 1 < len(starts):
            ahead = products(c + 1)
        for part in range(2):
            t0, width = part * half, (part + 1) * half
            rows_here = slice(r0 + t0, r0 + t0 + half)
            for i in pair:
                scores, carry = current[i]
                col = col_all[i][rows_here]
                decay = jnp.exp2((col - row_all[i][:, r0 : r0 + width]) + bias_ref[rows_here, :width])
                weights = (scores[t0 : t0 + half, :width] * decay).astype(BF16)
                att = dot(weights, v_ref[r0 : r0 + width, lanes[i]])
                if carry is not None:
                    lead = jnp.exp2(jnp.where(t0 + iota((half, 1), 0) < reach[c], col - base[i][c], NEG))
                    att = att + lead * carry[t0 : t0 + half]
                emit(lanes[i], r0 + t0, half, att)


def early_kernel(pairs_before, len_ref, q_ref, k_ref, v_ref, crow_ref, *refs):
    out_ref, bias_ref, ccol_ref = refs[-3:]
    rows = q_ref.shape[0]
    step = pl.program_id(0)
    first = lax.axis_index("seq") * rows
    ends = read_ends(len_ref, len_ref.shape[0])

    @pl.when(step == 0)
    def _():
        fill_bias(first, ends, bias_ref)
        fill_columns(crow_ref, ccol_ref)

    def emit(lanes, t0, size, att):
        out_ref[t0 : t0 + size, lanes] = att

    attend(first, ends, q_ref, k_ref, v_ref, (step + pairs_before) * 2, crow_ref, ccol_ref, bias_ref, None, emit)


def early_attention(doc_lengths, queries, keys, values, crow, before, part):
    heads, rows = crow.shape
    skip = sum(EARLY[:part]) // 2
    wide = pl.BlockSpec((rows, 256), lambda j: (0, j + skip))
    count = EARLY[part]
    return pl.pallas_call(
        functools.partial(early_kernel, skip),
        grid=(count // 2,),
        in_specs=[SMEM, wide, wide, wide, whole((heads, rows))] + [pl.BlockSpec(memory_space=pl.ANY)] * len(before),
        out_specs=wide,
        out_shape=jax.ShapeDtypeStruct((rows, sum(EARLY) * 128), F32),
        input_output_aliases={5: 0} if before else {},
        scratch_shapes=[pltpu.VMEM((rows, CHUNK), F32), pltpu.VMEM((rows, 128), F32)],
        compiler_params=LIMIT,
        cost_estimate=pl.CostEstimate(
            flops=count * rows * CHUNK * 128 * 8, bytes_accessed=rows * count * 128 * 10, transcendentals=count * rows * CHUNK
        ),
        name="early_attention",
    )(doc_lengths, queries, keys, values, crow, *before)


def gather_last(refs, last_ref):
    me = lax.axis_index("seq") % MEMBERS
    for x, ref in enumerate(refs):
        last_ref[me ^ x] = ref[...]


def decay_of(last_ref, e, i, hp):
    extra = last_ref[e, hp * 128 :, :].astype(F32)
    return extra[i : i + 1, :] + extra[hp + i : hp + i + 1, :]


def scan_quad(rows, len_ref, last_ref, state, i, hp, note):
    members = last_ref.shape[0]
    ends = read_ends(len_ref, len_ref.shape[0])
    base = lax.axis_index("seq") // members * members
    for e in range(members):
        note(e, state)
        low = (base + e) * rows
        inner = jnp.int32(0)
        for end in ends:
            inner = inner + ((end > low) & (end < low + rows)).astype(jnp.int32)
        passes = (inner == 0).astype(F32)
        piece = last_ref[e, i * 128 : (i + 1) * 128, :].astype(F32)
        state = state * (decay_of(last_ref, e, i, hp) * passes) + piece
    return state


def leave_kernel(rows, len_ref, *refs):
    out_ref, last_ref = refs[-2:]
    gather_last(refs[:MEMBERS], last_ref)
    hp = out_ref.shape[0]
    for i in range(hp):
        state = jnp.zeros((128, 128), F32)
        if len(refs) > MEMBERS + 2:
            state = refs[MEMBERS][i].astype(F32)
        state = scan_quad(rows, len_ref, last_ref, state, i, hp, lambda e, x: None)
        out_ref[i] = state.astype(BF16)


def leave_quad(doc_lengths, last, coming, rows, hp):
    return pl.pallas_call(
        functools.partial(leave_kernel, rows),
        in_specs=[SMEM] + [VMEM] * (MEMBERS + len(coming)),
        out_specs=VMEM,
        out_shape=jax.ShapeDtypeStruct((hp, 128, 128), BF16),
        scratch_shapes=[pltpu.VMEM((MEMBERS,) + last[0].shape, BF16)],
        compiler_params=SMALL,
        name="leave_quad",
    )(doc_lengths, *last, *coming)


def enter_kernel(rows, len_ref, *refs):
    in_ref, out_refs, last_ref, state_ref = refs[MEMBERS], refs[MEMBERS + 1 : -2], refs[-2], refs[-1]
    gather_last(refs[:MEMBERS], last_ref)
    hp = in_ref.shape[0]

    def note(i, e, state):
        state_ref[e, i] = state

    for i in range(hp):
        scan_quad(rows, len_ref, last_ref, in_ref[i].astype(F32), i, hp, functools.partial(note, i))
    me = lax.axis_index("seq") % MEMBERS
    for x, out_ref in enumerate(out_refs):
        out_ref[...] = state_ref[me ^ x].astype(BF16)


def enter_states(doc_lengths, last, coming, rows):
    return pl.pallas_call(
        functools.partial(enter_kernel, rows),
        in_specs=[SMEM] + [VMEM] * (MEMBERS + 1),
        out_specs=[VMEM] * MEMBERS,
        out_shape=[jax.ShapeDtypeStruct(coming.shape, BF16)] * MEMBERS,
        scratch_shapes=[
            pltpu.VMEM((MEMBERS,) + last[0].shape, BF16),
            pltpu.VMEM((MEMBERS,) + coming.shape, F32),
        ],
        compiler_params=SMALL,
        name="enter_states",
    )(doc_lengths, *last, coming)


def final_kernel(rows, len_ref, own_ref, *refs):
    side_refs = refs[MEMBERS : 2 * MEMBERS]
    rest_ref, in_ref = refs[2 * MEMBERS : 2 * MEMBERS + 2]
    out_refs, (last_ref, state_ref, piece_ref, final_ref) = refs[2 * MEMBERS + 2 : -4], refs[-4:]
    gather_last(refs[:MEMBERS], last_ref)
    hp = in_ref.shape[0]
    ends = read_ends(len_ref, len_ref.shape[0])
    me = lax.axis_index("seq")
    base = me // MEMBERS * MEMBERS

    def note(i, e, state):
        state_ref[e, i] = state

    for i in range(hp):
        scan_quad(rows, len_ref, last_ref, in_ref[i].astype(F32), i, hp, functools.partial(note, i))
    final_ref[...] = jnp.zeros_like(final_ref)
    place, previous = jnp.int32(0), jnp.int32(-1)
    for d in range(len(ends)):
        device = (ends[d] - 1) // rows
        place = jnp.where(device == previous, place + 1, 0)
        previous = device
        at_end = ends[d] == (device + 1) * rows
        enters = (place == 0).astype(F32)
        mine = device // MEMBERS * MEMBERS == base
        inner = mine & jnp.logical_not(at_end)
        e = device - base

        @pl.when(mine & at_end)
        def _():
            piece_ref[...] = last_ref[e, : hp * 128, :]

        for x, side_ref in enumerate(side_refs):

            @pl.when(inner & (place < SIDE) & ((e ^ (me % MEMBERS)) == x))
            def _():
                piece_ref[...] = side_ref[pl.ds(pl.multiple_of(place * hp * 128, 128), hp * 128), :]

        @pl.when(inner & (place >= SIDE))
        def _():
            row = pl.multiple_of((place - SIDE) * hp * 128, 128)
            pltpu.sync_copy(rest_ref.at[e, pl.ds(row, hp * 128), :], piece_ref)

        @pl.when(mine)
        def _():
            for i in range(hp):
                local = piece_ref[i * 128 : (i + 1) * 128, :].astype(F32)
                state = local + state_ref[e, i] * (decay_of(last_ref, e, i, hp) * enters)
                final_ref[own_ref[d], i] = state.astype(BF16)

    for x, out_ref in enumerate(out_refs):
        out_ref[...] = final_ref[me ^ x]


def final_states(doc_lengths, owner_ids, last, side, rest, coming, rows, spread):
    return pl.pallas_call(
        functools.partial(final_kernel, rows),
        in_specs=[SMEM, SMEM] + [VMEM] * (2 * MEMBERS) + [pl.BlockSpec(memory_space=pl.ANY), VMEM],
        out_specs=[VMEM] * spread,
        out_shape=[jax.ShapeDtypeStruct(coming.shape, BF16)] * spread,
        scratch_shapes=[
            pltpu.VMEM((MEMBERS,) + last[0].shape, BF16),
            pltpu.VMEM((MEMBERS,) + coming.shape, F32),
            pltpu.VMEM((coming.shape[0] * 128, 128), BF16),
            pltpu.VMEM((spread,) + coming.shape, BF16),
        ],
        compiler_params=SMALL,
        name="final_states",
    )(doc_lengths, owner_ids, *last, *side, rest, coming)


def pick_kernel(flag_ref, *refs):
    in_refs, out_ref = refs[:-1], refs[-1]
    me = lax.axis_index("seq")
    hp = in_refs[0].shape[0]
    for x, ref in enumerate(in_refs):
        source = me ^ x

        @pl.when(source // MEMBERS == flag_ref[0])
        def _():
            out_ref[0, pl.ds(source % MEMBERS * hp, hp)] = ref[...]


def pick_owned(flags, arrived, heads):
    return pl.pallas_call(
        pick_kernel,
        in_specs=[SMEM] + [VMEM] * len(arrived),
        out_specs=VMEM,
        out_shape=jax.ShapeDtypeStruct((1, heads, 128, 128), BF16),
        compiler_params=SMALL,
        name="pick_owned",
    )(flags, *arrived)


def finish_kernel(
    len_ref, q_ref, k_ref, v_ref, e0, e1, e2, e3, local_ref, gate_ref, gain_ref, crow_ref, out_ref, bias_ref, ccol_ref
):
    rows = q_ref.shape[0]
    step = pl.program_id(0)
    me = lax.axis_index("seq")
    first = me * rows
    ends = read_ends(len_ref, len_ref.shape[0])
    hp = e0.shape[0]
    pairs = sum(EARLY) // 2

    def entering(h):
        far = (h // hp) ^ (me % MEMBERS)
        state = e0[h % hp]
        for x, ref in ((1, e1), (2, e2), (3, e3)):
            state = jnp.where(far == x, ref[h % hp], state)
        return state

    def emit(lanes, t0, size, att):
        mean = jnp.mean(att * att, axis=1, keepdims=True)
        gate = 0.5 + 0.5 * jnp.tanh(0.5 * gate_ref[t0 : t0 + size, lanes].astype(F32))
        gain = gain_ref[:, lanes].astype(F32)
        out_ref[t0 : t0 + size, lanes] = (att * lax.rsqrt(mean + 1e-06) * (gain * gate)).astype(BF16)

    @pl.when(step == 0)
    def _():
        fill_bias(first, ends, bias_ref)
        fill_columns(crow_ref, ccol_ref)

    @pl.when(step < pairs)
    def _():
        reach = run_end(ends, first - 1) - first
        cols = [head_column(ccol_ref, step * 2 + i) for i in range(2)]
        states = [entering(step * 2 + i) for i in range(2)]
        lanes = [slice(i * 128, (i + 1) * 128) for i in range(2)]
        for t0 in range(0, rows, 256):
            carry = [dot(q_ref[t0 : t0 + 256, lanes[i]], states[i]) for i in range(2)]
            at = t0 + iota((256, 1), 0)
            for i in range(2):
                lead = jnp.exp2(jnp.where(at < reach, cols[i][t0 : t0 + 256], NEG))
                emit(lanes[i], t0, 256, local_ref[t0 : t0 + 256, lanes[i]] + lead * carry[i])

    @pl.when(step >= pairs)
    def _():
        states = [entering(step * 2 + i).astype(F32) for i in range(2)]
        attend(first, ends, q_ref, k_ref, v_ref, step * 2, crow_ref, ccol_ref, bias_ref, states, emit)


def finish(doc_lengths, queries, keys, values, entering, local, gate, gain, crow):
    heads, rows = crow.shape
    pairs = sum(EARLY) // 2
    wide = pl.BlockSpec((rows, 256), lambda j: (0, j))
    late = pl.BlockSpec((rows, 256), lambda j: (0, jnp.maximum(j, pairs)))
    return pl.pallas_call(
        finish_kernel,
        grid=(heads // 2,),
        in_specs=[SMEM, wide, late, late]
        + [whole(e.shape) for e in entering]
        + [
            pl.BlockSpec((rows, 256), lambda j: (0, jnp.minimum(j, pairs - 1))),
            wide,
            pl.BlockSpec((1, 256), lambda j: (0, j)),
            whole((heads, rows)),
        ],
        out_specs=wide,
        out_shape=jax.ShapeDtypeStruct((rows, heads * 128), BF16),
        scratch_shapes=[pltpu.VMEM((rows, CHUNK), F32), pltpu.VMEM((rows, 128), F32)],
        compiler_params=LIMIT,
        cost_estimate=pl.CostEstimate(
            flops=heads * rows * CHUNK * 128 * 8, bytes_accessed=rows * heads * 128 * 10, transcendentals=heads * rows * CHUNK
        ),
        name="finish",
    )(doc_lengths, queries, keys, values, *entering, local, gate, gain, crow)


def swap(x, groups=None):
    return lax.all_to_all(x, "seq", split_axis=0, concat_axis=0, axis_index_groups=groups, tiled=True)


def by_distance(parcels, spread):
    moved = {0: parcels[0]}
    for x in sorted(range(1, len(parcels)), key=lambda x: (x < MEMBERS, x)):
        moved[x] = lax.ppermute(parcels[x], "seq", [(s, s ^ x) for s in range(spread)])
    return [moved[x] for x in range(len(parcels))]


def on_device(spread, queries, keys, values, log_decay, gate, gain, doc_lengths, owner_ids):
    rows, heads = log_decay.shape
    quads = spread // MEMBERS
    hp = heads // MEMBERS
    near = [[q * MEMBERS + m for m in range(MEMBERS)] for q in range(quads)]
    onward = [(s, s + MEMBERS) for s in range(spread - MEMBERS)]
    decay_rows = log_decay.T
    barrier = lax.optimization_barrier

    crow, flags, *parcels = piece_states(doc_lengths, owner_ids, decay_rows, keys, values, SIDE)
    side, last = parcels[:MEMBERS], parcels[MEMBERS:]
    last = by_distance(last, spread)
    gain = gain.reshape(1, -1)
    crowded = flags[1] > 0
    slots = max(doc_lengths.shape[0] - 1, SIDE + 1)

    def send_rest():
        return swap(piece_states(doc_lengths, owner_ids, decay_rows, keys, values, slots)[0], near)

    none = jnp.zeros((MEMBERS, (slots - SIDE) * hp * 128, 128), BF16)
    rest = lax.cond(crowded, send_rest, lambda: none)
    last, side, gain, rest = barrier((last, side, gain, rest))

    side = by_distance(side, spread)
    coming = []
    for _ in range(quads - 1):
        leaving = leave_quad(doc_lengths, last, coming, rows, hp)
        coming = [lax.ppermute(leaving, "seq", onward)]
    crow_1, leaving = barrier((crow, leaving))
    local = early_attention(doc_lengths, queries, keys, values, crow_1, [], 0)
    coming, local, side = barrier((coming[0], local, side))

    entering = by_distance(enter_states(doc_lengths, last, coming, rows), spread)
    finals = final_states(doc_lengths, owner_ids, last, side, rest, coming, rows, spread)
    entering, finals = barrier((entering, finals))
    arrived = by_distance(finals, spread)
    mixed = finish(doc_lengths, queries, keys, values, entering, local, gate, gain, crow)
    return mixed, pick_owned(flags, arrived, heads)


def solution(mesh):
    placed = (
        P(("groups", "seq"), "tp"),
        P(("groups", "seq"), "tp"),
        P(("groups", "seq"), "tp"),
        P(("groups", "seq"), "tp"),
        P(("groups", "seq"), "tp"),
        P("tp"),
        P("groups"),
        P("groups"),
    )
    return jax.shard_map(
        functools.partial(on_device, mesh.shape["seq"]),
        mesh=mesh,
        in_specs=placed,
        out_specs=(P(("groups", "seq"), "tp"), P(("groups", "seq"), "tp", None, None)),
        check_vma=False,
    )
```

```python
import functools
import math

import jax
import jax.numpy as jnp
from jax import lax
from jax.experimental import pallas as pl
from jax.experimental.pallas import tpu as pltpu
from jax.sharding import PartitionSpec as P

BLK = 512
SIDE = 3
EXTRA = 16
CHUNK = 256
MEMBERS = 4
TILE = 256
NEG = -1e30
LOG2E = math.log2(math.e)
SCALE = 128**-0.5
F32, BF16 = jnp.float32, jnp.bfloat16
SMEM = pl.BlockSpec(memory_space=pltpu.SMEM)
VMEM = pl.BlockSpec(memory_space=pltpu.VMEM)
LIMIT = pltpu.CompilerParams(vmem_limit_bytes=60 * 2**20)
SMALL = pltpu.CompilerParams(vmem_limit_bytes=48 * 2**20)


def dot(a, b, contract=((1,), (0,))):
    return lax.dot_general(a, b, (contract, ((), ())), preferred_element_type=F32)


def iota(shape, dim):
    return lax.broadcasted_iota(jnp.int32, shape, dim)


def read_ends(len_ref, count):
    ends, total = [], jnp.int32(0)
    for d in range(count):
        total = total + len_ref[d]
        ends.append(total)
    return ends


def run_end(ends, pos):
    best = ends[-1]
    for e in reversed(ends[:-1]):
        best = jnp.where(e > pos, e, best)
    return best


def run_start(ends, pos):
    best = jnp.zeros_like(pos)
    for e in ends[:-1]:
        best = jnp.where(e <= pos, e, best)
    return best


def split3(x):
    hi = x.astype(BF16)
    rest = x - hi.astype(F32)
    mid = rest.astype(BF16)
    return hi, mid, (rest - mid.astype(F32)).astype(BF16)


def cum_rows(ld_ref, crow_ref):
    heads, rows = ld_ref.shape
    upper = (iota((BLK, BLK), 0) <= iota((BLK, BLK), 1)).astype(F32).astype(BF16)
    base = jnp.zeros((heads, 1), F32)
    for b in range(rows // BLK):
        part = ld_ref[:, b * BLK : (b + 1) * BLK] * LOG2E
        sums = dot(jnp.concatenate(split3(part), axis=0), upper)
        row = sums[2 * heads :] + sums[heads : 2 * heads] + sums[:heads] + base
        crow_ref[:, b * BLK : (b + 1) * BLK] = row
        base = row[:, BLK - 1 :]


def value_at(cum, at, index):
    return jnp.sum(jnp.where(at == index, cum, 0.0), axis=1, keepdims=True)


def span_weights(cum, at, low, high):
    inside = (at >= low) & (at <= high)
    return jnp.exp2(jnp.where(inside, value_at(cum, at, high) - cum, NEG) + math.log2(SCALE))


def weigh(flipped, w_ref, h):
    weights = [jnp.broadcast_to(w_ref[pl.ds(h + j, 1), :], (128, flipped.shape[1])) for j in range(2)]
    return (flipped.astype(F32) * jnp.concatenate(weights, axis=0)).astype(BF16)


def whole(shape):
    return pl.BlockSpec(shape, lambda j: (0,) * len(shape))


def pieces_kernel(rest, len_ref, own_ref, ld_ref, k_ref, v_ref, *refs):
    if rest:
        side_ref, crow_ref, w_ref, keep_ref = refs
        slots = keep_ref.shape[0]
    else:
        crow_ref, flag_ref = refs[:2]
        side_refs, last_refs = refs[2 : 2 + MEMBERS], refs[2 + MEMBERS : 2 + 2 * MEMBERS]
        w_ref, first_ref, high_ref, weighted_ref, prefix_ref, parcel_ref = refs[2 + 2 * MEMBERS :]
        slots = SIDE
    heads, rows = crow_ref.shape
    step = pl.program_id(0)
    hp = v_ref.shape[1] // 128
    me = lax.axis_index("seq")

    @pl.when(step == 0)
    def _():
        cum_rows(ld_ref, crow_ref)
        first = me * rows
        last = first + rows - 1
        ends = read_ends(len_ref, len_ref.shape[0])
        starts = [jnp.int32(0)] + ends[:-1]
        lows = [jnp.int32(0)] * slots
        highs = [jnp.int32(-1)] * slots
        place, rank, previous = jnp.int32(0), jnp.int32(0), jnp.int32(-1)
        crowded, owned_in = jnp.int32(0), jnp.int32(0)
        for d in range(len(ends)):
            here = (ends[d] > first) & (ends[d] <= last)
            low = jnp.maximum(starts[d] - first, 0)
            for s in range(slots):
                mine = here & (place == s + (SIDE if rest else 0))
                lows[s] = jnp.where(mine, low, lows[s])
                highs[s] = jnp.where(mine, ends[d] - 1 - first, highs[s])
            place = place + here.astype(jnp.int32)
            device = (ends[d] - 1) // rows
            rank = jnp.where(device == previous, rank + 1, 0)
            previous = device
            late = ((rank >= SIDE) & (ends[d] != (device + 1) * rows)).astype(jnp.int32)
            crowded = jnp.maximum(crowded, late)
            owned_in = jnp.where(own_ref[d] == me, device, owned_in)
        at = iota((heads, rows), 1)
        cum = crow_ref[...]
        total = jnp.zeros((heads, rows), F32)
        for s in range(slots):
            total = total + span_weights(cum, at, lows[s], highs[s])
        if rest:
            row_at = iota((16, rows), 1)
            for s in range(slots):
                inside = (row_at >= lows[s]) & (row_at <= highs[s])
                keep_ref[s] = jnp.where(inside, 1.0, 0.0).astype(BF16)
        else:
            total = total + span_weights(cum, at, jnp.maximum(run_start(ends, last) - first, 0), rows - 1)
            flag_ref[0] = owned_in // MEMBERS
            flag_ref[1] = crowded
            high = jnp.int32(-1)
            for s in range(slots):
                high = jnp.maximum(high, highs[s])
                high_ref[s] = high
            stop = jnp.minimum(run_end(ends, first) - 1 - first, rows - 1)
            goes_on = (run_start(ends, first) < first).astype(F32)
            first_ref[...] = jnp.broadcast_to(jnp.exp2(value_at(cum, at, stop)) * goes_on, (heads, 128))
        w_ref[...] = total

    def own(states, j):
        return states[j * 128 : (j + 1) * 128, j * 128 : (j + 1) * 128]

    if rest:
        for i in range(0, hp, 2):
            lanes = slice(i * 128, (i + 2) * 128)
            weighted = weigh(k_ref[:, lanes].T, w_ref, step * hp + i).reshape(16, 16, rows)
            for s in range(slots):
                states = dot((weighted * keep_ref[s][None]).reshape(256, rows), v_ref[:, lanes])
                for j in range(2):
                    at = (s * hp + i + j) * 128
                    side_ref[0, at : at + 128, :] = own(states, j).astype(BF16)
        return

    pairs = range(0, hp, 2)
    lanes = {i: slice(i * 128, (i + 2) * 128) for i in pairs}
    for i in pairs:
        weighted_ref[lanes[i], :] = weigh(k_ref[:, lanes[i]].T, w_ref, step * hp + i)
    totals = {}
    for i in pairs:
        sums = [jnp.zeros((128, 128), F32)] * 2
        for t in range(rows // TILE):
            span = slice(t * TILE, (t + 1) * TILE)
            states = dot(weighted_ref[lanes[i], span], v_ref[span, lanes[i]])
            for j in range(2):
                prefix_ref[t, i + j] = sums[j]
                sums[j] = sums[j] + own(states, j)
        totals[i] = sums
    ended = {i: [jnp.zeros((128, 128), F32)] * 2 for i in pairs}
    for s in range(slots):
        high = high_ref[s]
        tile = jnp.maximum(high, 0) // TILE
        start = pl.multiple_of(tile * TILE, TILE)
        keep = jnp.where(start + iota((16, TILE), 1) <= high, 1.0, 0.0).astype(BF16)
        for i in pairs:
            kept = weighted_ref[lanes[i], pl.ds(start, TILE)].reshape(16, 16, TILE) * keep[None]
            states = dot(kept.reshape(256, TILE), v_ref[pl.ds(start, TILE), lanes[i]])
            for j in range(2):
                until = own(states, j) + prefix_ref[tile, i + j]
                at = (s * hp + i + j) * 128
                parcel_ref[at : at + 128, :] = (until - ended[i][j]).astype(BF16)
                ended[i][j] = until
    rate = first_ref[pl.ds(step * hp, hp), :]
    high = rate.astype(BF16).astype(F32)
    pad = jnp.zeros((EXTRA - 2 * hp, 128), F32)
    tail = jnp.concatenate([high, rate - high, pad], axis=0).astype(BF16)
    cut = SIDE * hp * 128
    for i in pairs:
        for j in range(2):
            at = cut + (i + j) * 128
            parcel_ref[at : at + 128, :] = (totals[i][j] - ended[i][j]).astype(BF16)
    parcel_ref[cut + hp * 128 :, :] = tail
    for x in range(MEMBERS):

        @pl.when((step ^ (me % MEMBERS)) == x)
        def _():
            side_refs[x][...] = parcel_ref[:cut, :]
            last_refs[x][...] = parcel_ref[cut:, :]


def piece_states(doc_lengths, owner_ids, decay_rows, keys, values, slots):
    heads, rows = decay_rows.shape
    rest = slots > SIDE
    count = slots - SIDE if rest else slots
    hp = heads // MEMBERS
    wide = pl.BlockSpec((rows, hp * 128), lambda j: (0, j))
    side = (count * hp * 128, 128)
    shapes, specs = [jax.ShapeDtypeStruct((heads, rows), F32)], [whole((heads, rows))]
    scratch = [pltpu.VMEM((heads, rows), F32)]
    if rest:
        shapes.insert(0, jax.ShapeDtypeStruct((MEMBERS,) + side, BF16))
        specs.insert(0, pl.BlockSpec((1,) + side, lambda j: (j, 0, 0)))
        scratch.append(pltpu.VMEM((count, 16, rows), BF16))
    else:
        last = (hp * 128 + EXTRA, 128)
        shapes += [jax.ShapeDtypeStruct((2,), jnp.int32)]
        shapes += [jax.ShapeDtypeStruct(shape, BF16) for shape in (side, last) for _ in range(MEMBERS)]
        specs += [SMEM] + [whole(shape) for shape in (side, last) for _ in range(MEMBERS)]
        scratch += [
            pltpu.VMEM((heads, 128), F32),
            pltpu.SMEM((SIDE,), jnp.int32),
            pltpu.VMEM((hp * 128, rows), BF16),
            pltpu.VMEM((rows // TILE, hp, 128, 128), F32),
            pltpu.VMEM((side[0] + last[0], 128), BF16),
        ]
    return pl.pallas_call(
        functools.partial(pieces_kernel, rest),
        grid=(MEMBERS,),
        in_specs=[SMEM, SMEM, whole((heads, rows)), wide, wide],
        out_specs=specs,
        out_shape=shapes,
        scratch_shapes=scratch,
        compiler_params=LIMIT,
        cost_estimate=pl.CostEstimate(
            flops=2 * heads * rows * 128 * 256, bytes_accessed=rows * heads * 128 * 4, transcendentals=heads * rows
        ),
        name="piece_states",
    )(doc_lengths, owner_ids, decay_rows, keys, values)


def head_column(ccol_ref, h):
    cols = ccol_ref[...]
    return jnp.sum(jnp.where(iota(cols.shape, 1) == h, cols, 0.0), axis=1, keepdims=True)


def fill_columns(crow_ref, ccol_ref):
    heads, rows = crow_ref.shape
    for r0 in range(0, rows, 128):
        part = crow_ref[:, r0 : r0 + 128]
        part = jnp.concatenate([part, jnp.zeros((128 - heads, 128), F32)], axis=0)
        ccol_ref[r0 : r0 + 128, :] = part.T


def fill_bias(first, ends, bias_ref):
    for c in range(bias_ref.shape[0] // CHUNK):
        base = first + c * CHUNK
        t_pos = base + iota((CHUNK, 1), 0)
        start = run_start(ends, t_pos)
        s_pos = base + iota((CHUNK, CHUNK), 1)
        keep = (s_pos <= t_pos) & (s_pos >= start)
        bias_ref[c * CHUNK : (c + 1) * CHUNK, :] = jnp.where(keep, math.log2(SCALE), NEG)


def attend(first, ends, q_ref, k_ref, v_ref, h, crow_ref, ccol_ref, bias_ref, out_ref):
    rows = q_ref.shape[0]
    pair = range(2)
    half = CHUNK // 2
    lanes = [slice(i * 128, (i + 1) * 128) for i in pair]
    row_all = [crow_ref[pl.ds(h + i, 1), :] for i in pair]
    col_all = [head_column(ccol_ref, h + i) for i in pair]
    starts = range(0, rows, CHUNK)
    spans = [slice(r0, r0 + CHUNK) for r0 in starts]
    reach = [run_end(ends, first + r0 - 1) - (first + r0) for r0 in starts]
    base = [[row_all[i][:, r0 - 1 : r0] if r0 else None for r0 in starts] for i in pair]

    fresh = [[], []]
    for c, r0 in enumerate(starts[:-1]):
        since = run_start(ends, first + r0 + CHUNK - 1) - (first + r0)
        inside = iota((1, CHUNK), 1) >= since
        for i in pair:
            row = row_all[i][:, spans[c]]
            weight = jnp.exp2(jnp.where(inside, row[:, CHUNK - 1 :] - row, NEG) + math.log2(SCALE))
            flipped = k_ref[spans[c], lanes[i]].T
            fresh[i].append(dot((flipped.astype(F32) * weight).astype(BF16), v_ref[spans[c], lanes[i]]))
    carried = []
    for i in pair:
        state = fresh[i][0]
        chain = [None, state.astype(BF16)]
        for c in range(1, len(starts) - 1):
            total = row_all[i][:, starts[c] + CHUNK - 1 : starts[c] + CHUNK]
            state = fresh[i][c] + state * jnp.exp2(jnp.where(CHUNK <= reach[c], total - base[i][c], NEG))
            chain.append(state.astype(BF16))
        carried.append(chain)

    def products(c):
        result = []
        for i in pair:
            query = q_ref[spans[c], lanes[i]]
            scores = dot(query, k_ref[spans[c], lanes[i]], ((1,), (1,)))
            result.append((scores, dot(query, carried[i][c]) if c else None))
        return result

    ahead = products(0)
    for c, r0 in enumerate(starts):
        current = ahead
        if c + 1 < len(starts):
            ahead = products(c + 1)
        for part in range(2):
            t0, width = part * half, (part + 1) * half
            rows_here = slice(r0 + t0, r0 + t0 + half)
            for i in pair:
                scores, carry = current[i]
                col = col_all[i][rows_here]
                decay = jnp.exp2((col - row_all[i][:, r0 : r0 + width]) + bias_ref[rows_here, :width])
                weights = (scores[t0 : t0 + half, :width] * decay).astype(BF16)
                att = dot(weights, v_ref[r0 : r0 + width, lanes[i]])
                if c:
                    lead = jnp.exp2(jnp.where(t0 + iota((half, 1), 0) < reach[c], col - base[i][c], NEG))
                    att = att + lead * carry[t0 : t0 + half]
                out_ref[rows_here, lanes[i]] = att


def local_kernel(len_ref, q_ref, k_ref, v_ref, crow_ref, out_ref, bias_ref, ccol_ref):
    rows = q_ref.shape[0]
    step = pl.program_id(0)
    first = lax.axis_index("seq") * rows
    ends = read_ends(len_ref, len_ref.shape[0])

    @pl.when(step == 0)
    def _():
        fill_bias(first, ends, bias_ref)
        fill_columns(crow_ref, ccol_ref)

    attend(first, ends, q_ref, k_ref, v_ref, step * 2, crow_ref, ccol_ref, bias_ref, out_ref)


def local_attention(doc_lengths, queries, keys, values, crow):
    heads, rows = crow.shape
    wide = pl.BlockSpec((rows, 256), lambda j: (0, j))
    return pl.pallas_call(
        local_kernel,
        grid=(heads // 2,),
        in_specs=[SMEM, wide, wide, wide, whole((heads, rows))],
        out_specs=wide,
        out_shape=jax.ShapeDtypeStruct((rows, heads * 128), F32),
        scratch_shapes=[pltpu.VMEM((rows, CHUNK), F32), pltpu.VMEM((rows, 128), F32)],
        compiler_params=LIMIT,
        cost_estimate=pl.CostEstimate(
            flops=heads * rows * CHUNK * 128 * 8, bytes_accessed=rows * heads * 128 * 10, transcendentals=heads * rows * CHUNK
        ),
        name="local_attention",
    )(doc_lengths, queries, keys, values, crow)


def gather_last(refs, last_ref):
    me = lax.axis_index("seq") % MEMBERS
    for x, ref in enumerate(refs):
        last_ref[me ^ x] = ref[...]


def decay_of(last_ref, e, i, hp):
    extra = last_ref[e, hp * 128 :, :].astype(F32)
    return extra[i : i + 1, :] + extra[hp + i : hp + i + 1, :]


def scan_quad(rows, len_ref, last_ref, state, i, hp, note):
    members = last_ref.shape[0]
    ends = read_ends(len_ref, len_ref.shape[0])
    base = lax.axis_index("seq") // members * members
    for e in range(members):
        note(e, state)
        low = (base + e) * rows
        inner = jnp.int32(0)
        for end in ends:
            inner = inner + ((end > low) & (end < low + rows)).astype(jnp.int32)
        passes = (inner == 0).astype(F32)
        piece = last_ref[e, i * 128 : (i + 1) * 128, :].astype(F32)
        state = state * (decay_of(last_ref, e, i, hp) * passes) + piece
    return state


def leave_kernel(rows, len_ref, *refs):
    out_ref, last_ref = refs[-2:]
    gather_last(refs[:MEMBERS], last_ref)
    hp = out_ref.shape[0]
    for i in range(hp):
        state = jnp.zeros((128, 128), F32)
        if len(refs) > MEMBERS + 2:
            state = refs[MEMBERS][i].astype(F32)
        state = scan_quad(rows, len_ref, last_ref, state, i, hp, lambda e, x: None)
        out_ref[i] = state.astype(BF16)


def leave_quad(doc_lengths, last, coming, rows, hp):
    return pl.pallas_call(
        functools.partial(leave_kernel, rows),
        in_specs=[SMEM] + [VMEM] * (MEMBERS + len(coming)),
        out_specs=VMEM,
        out_shape=jax.ShapeDtypeStruct((hp, 128, 128), BF16),
        scratch_shapes=[pltpu.VMEM((MEMBERS,) + last[0].shape, BF16)],
        compiler_params=SMALL,
        name="leave_quad",
    )(doc_lengths, *last, *coming)


def enter_kernel(rows, len_ref, *refs):
    in_ref, out_refs, last_ref, state_ref = refs[MEMBERS], refs[MEMBERS + 1 : -2], refs[-2], refs[-1]
    gather_last(refs[:MEMBERS], last_ref)
    hp = in_ref.shape[0]

    def note(i, e, state):
        state_ref[e, i] = state

    for i in range(hp):
        scan_quad(rows, len_ref, last_ref, in_ref[i].astype(F32), i, hp, functools.partial(note, i))
    me = lax.axis_index("seq") % MEMBERS
    for x, out_ref in enumerate(out_refs):
        out_ref[...] = state_ref[me ^ x].astype(BF16)


def enter_states(doc_lengths, last, coming, rows):
    return pl.pallas_call(
        functools.partial(enter_kernel, rows),
        in_specs=[SMEM] + [VMEM] * (MEMBERS + 1),
        out_specs=[VMEM] * MEMBERS,
        out_shape=[jax.ShapeDtypeStruct(coming.shape, BF16)] * MEMBERS,
        scratch_shapes=[
            pltpu.VMEM((MEMBERS,) + last[0].shape, BF16),
            pltpu.VMEM((MEMBERS,) + coming.shape, F32),
        ],
        compiler_params=SMALL,
        name="enter_states",
    )(doc_lengths, *last, coming)


def final_kernel(rows, len_ref, own_ref, *refs):
    side_refs = refs[MEMBERS : 2 * MEMBERS]
    rest_ref, in_ref = refs[2 * MEMBERS : 2 * MEMBERS + 2]
    out_refs, (last_ref, state_ref, piece_ref, final_ref) = refs[2 * MEMBERS + 2 : -4], refs[-4:]
    gather_last(refs[:MEMBERS], last_ref)
    hp = in_ref.shape[0]
    ends = read_ends(len_ref, len_ref.shape[0])
    me = lax.axis_index("seq")
    base = me // MEMBERS * MEMBERS

    def note(i, e, state):
        state_ref[e, i] = state

    for i in range(hp):
        scan_quad(rows, len_ref, last_ref, in_ref[i].astype(F32), i, hp, functools.partial(note, i))
    final_ref[...] = jnp.zeros_like(final_ref)
    place, previous = jnp.int32(0), jnp.int32(-1)
    for d in range(len(ends)):
        device = (ends[d] - 1) // rows
        place = jnp.where(device == previous, place + 1, 0)
        previous = device
        at_end = ends[d] == (device + 1) * rows
        enters = (place == 0).astype(F32)
        mine = device // MEMBERS * MEMBERS == base
        inner = mine & jnp.logical_not(at_end)
        e = device - base

        @pl.when(mine & at_end)
        def _():
            piece_ref[...] = last_ref[e, : hp * 128, :]

        for x, side_ref in enumerate(side_refs):

            @pl.when(inner & (place < SIDE) & ((e ^ (me % MEMBERS)) == x))
            def _():
                piece_ref[...] = side_ref[pl.ds(pl.multiple_of(place * hp * 128, 128), hp * 128), :]

        @pl.when(inner & (place >= SIDE))
        def _():
            row = pl.multiple_of((place - SIDE) * hp * 128, 128)
            pltpu.sync_copy(rest_ref.at[e, pl.ds(row, hp * 128), :], piece_ref)

        @pl.when(mine)
        def _():
            for i in range(hp):
                local = piece_ref[i * 128 : (i + 1) * 128, :].astype(F32)
                state = local + state_ref[e, i] * (decay_of(last_ref, e, i, hp) * enters)
                final_ref[own_ref[d], i] = state.astype(BF16)

    for x, out_ref in enumerate(out_refs):
        out_ref[...] = final_ref[me ^ x]


def final_states(doc_lengths, owner_ids, last, side, rest, coming, rows, spread):
    return pl.pallas_call(
        functools.partial(final_kernel, rows),
        in_specs=[SMEM, SMEM] + [VMEM] * (2 * MEMBERS) + [pl.BlockSpec(memory_space=pl.ANY), VMEM],
        out_specs=[VMEM] * spread,
        out_shape=[jax.ShapeDtypeStruct(coming.shape, BF16)] * spread,
        scratch_shapes=[
            pltpu.VMEM((MEMBERS,) + last[0].shape, BF16),
            pltpu.VMEM((MEMBERS,) + coming.shape, F32),
            pltpu.VMEM((coming.shape[0] * 128, 128), BF16),
            pltpu.VMEM((spread,) + coming.shape, BF16),
        ],
        compiler_params=SMALL,
        name="final_states",
    )(doc_lengths, owner_ids, *last, *side, rest, coming)


def pick_kernel(flag_ref, *refs):
    in_refs, out_ref = refs[:-1], refs[-1]
    me = lax.axis_index("seq")
    hp = in_refs[0].shape[0]
    for x, ref in enumerate(in_refs):
        source = me ^ x

        @pl.when(source // MEMBERS == flag_ref[0])
        def _():
            out_ref[0, pl.ds(source % MEMBERS * hp, hp)] = ref[...]


def pick_owned(flags, arrived, heads):
    return pl.pallas_call(
        pick_kernel,
        in_specs=[SMEM] + [VMEM] * len(arrived),
        out_specs=VMEM,
        out_shape=jax.ShapeDtypeStruct((1, heads, 128, 128), BF16),
        compiler_params=SMALL,
        name="pick_owned",
    )(flags, *arrived)


def finish_kernel(len_ref, q_ref, e0, e1, e2, e3, local_ref, gate_ref, gain_ref, crow_ref, out_ref, ccol_ref):
    rows = q_ref.shape[0]
    step = pl.program_id(0)
    me = lax.axis_index("seq")
    hp = e0.shape[0]

    @pl.when(step == 0)
    def _():
        fill_columns(crow_ref, ccol_ref)

    def entering(h):
        far = (h // hp) ^ (me % MEMBERS)
        state = e0[h % hp]
        for x, ref in ((1, e1), (2, e2), (3, e3)):
            state = jnp.where(far == x, ref[h % hp], state)
        return state

    first = me * rows
    reach = run_end(read_ends(len_ref, len_ref.shape[0]), first - 1) - first
    cols = [head_column(ccol_ref, step * 2 + i) for i in range(2)]
    states = [entering(step * 2 + i) for i in range(2)]
    for t0 in range(0, rows, 256):
        span = slice(t0, t0 + 256)
        carry = [dot(q_ref[span, i * 128 : (i + 1) * 128], states[i]) for i in range(2)]
        inside = t0 + iota((256, 1), 0) < reach
        for i in range(2):
            lanes = slice(i * 128, (i + 1) * 128)
            lead = jnp.exp2(jnp.where(inside, cols[i][span], NEG))
            att = local_ref[span, lanes] + lead * carry[i]
            mean = jnp.mean(att * att, axis=1, keepdims=True)
            gate = 0.5 + 0.5 * jnp.tanh(0.5 * gate_ref[span, lanes].astype(F32))
            gain = gain_ref[:, lanes].astype(F32)
            out_ref[span, lanes] = (att * lax.rsqrt(mean + 1e-06) * (gain * gate)).astype(BF16)


def finish(doc_lengths, queries, entering, local, gate, gain, crow):
    heads, rows = crow.shape
    wide = pl.BlockSpec((rows, 256), lambda j: (0, j))
    return pl.pallas_call(
        finish_kernel,
        grid=(heads // 2,),
        in_specs=[SMEM, wide]
        + [whole(e.shape) for e in entering]
        + [wide, wide, pl.BlockSpec((1, 256), lambda j: (0, j)), whole((heads, rows))],
        out_specs=wide,
        out_shape=jax.ShapeDtypeStruct((rows, heads * 128), BF16),
        scratch_shapes=[pltpu.VMEM((rows, 128), F32)],
        compiler_params=pltpu.CompilerParams(vmem_limit_bytes=54 * 2**20),
        cost_estimate=pl.CostEstimate(
            flops=heads * rows * 128 * 256, bytes_accessed=rows * heads * 128 * 10, transcendentals=heads * rows * 256
        ),
        name="finish",
    )(doc_lengths, queries, *entering, local, gate, gain, crow)


def swap(x, groups=None):
    return lax.all_to_all(x, "seq", split_axis=0, concat_axis=0, axis_index_groups=groups, tiled=True)


def by_distance(parcels, spread):
    moved = {0: parcels[0]}
    for x in sorted(range(1, len(parcels)), key=lambda x: (x < MEMBERS, x)):
        moved[x] = lax.ppermute(parcels[x], "seq", [(s, s ^ x) for s in range(spread)])
    return [moved[x] for x in range(len(parcels))]


def on_device(spread, queries, keys, values, log_decay, gate, gain, doc_lengths, owner_ids):
    rows, heads = log_decay.shape
    quads = spread // MEMBERS
    hp = heads // MEMBERS
    near = [[q * MEMBERS + m for m in range(MEMBERS)] for q in range(quads)]
    onward = [(s, s + MEMBERS) for s in range(spread - MEMBERS)]
    decay_rows = log_decay.T
    barrier = lax.optimization_barrier

    crow, flags, *parcels = piece_states(doc_lengths, owner_ids, decay_rows, keys, values, SIDE)
    side, last = parcels[:MEMBERS], parcels[MEMBERS:]
    last = by_distance(last, spread)
    gain = gain.reshape(1, -1)
    crowded = flags[1] > 0
    slots = max(doc_lengths.shape[0] - 1, SIDE + 1)

    def send_rest():
        return swap(piece_states(doc_lengths, owner_ids, decay_rows, keys, values, slots)[0], near)

    none = jnp.zeros((MEMBERS, (slots - SIDE) * hp * 128, 128), BF16)
    rest = lax.cond(crowded, send_rest, lambda: none)
    last, side, gain, rest = barrier((last, side, gain, rest))

    side = by_distance(side, spread)
    coming = []
    for _ in range(quads - 1):
        leaving = leave_quad(doc_lengths, last, coming, rows, hp)
        coming = [lax.ppermute(leaving, "seq", onward)]
    crow_1, leaving = barrier((crow, leaving))
    local = local_attention(doc_lengths, queries, keys, values, crow_1)
    coming, local, side = barrier((coming[0], local, side))

    entering = by_distance(enter_states(doc_lengths, last, coming, rows), spread)
    finals = final_states(doc_lengths, owner_ids, last, side, rest, coming, rows, spread)
    entering, finals = barrier((entering, finals))
    arrived = by_distance(finals, spread)
    mixed = finish(doc_lengths, queries, entering, local, gate, gain, crow)
    return mixed, pick_owned(flags, arrived, heads)


def solution(mesh):
    placed = (
        P(("groups", "seq"), "tp"),
        P(("groups", "seq"), "tp"),
        P(("groups", "seq"), "tp"),
        P(("groups", "seq"), "tp"),
        P(("groups", "seq"), "tp"),
        P("tp"),
        P("groups"),
        P("groups"),
    )
    return jax.shard_map(
        functools.partial(on_device, mesh.shape["seq"]),
        mesh=mesh,
        in_specs=placed,
        out_specs=(P(("groups", "seq"), "tp"), P(("groups", "seq"), "tp", None, None)),
        check_vma=False,
    )
```

```python
import functools
import math

import jax
import jax.numpy as jnp
from jax import lax
from jax.experimental import pallas as pl
from jax.experimental.pallas import tpu as pltpu
from jax.sharding import PartitionSpec as P

BLK = 512
SIDE = 3
EXTRA = 16
CHUNK = 256
MEMBERS = 4
TILE = 256
PARTS = (4, 12)
NEG = -1e30
LOG2E = math.log2(math.e)
SCALE = 128**-0.5
F32, BF16 = jnp.float32, jnp.bfloat16
SMEM = pl.BlockSpec(memory_space=pltpu.SMEM)
VMEM = pl.BlockSpec(memory_space=pltpu.VMEM)
LIMIT = pltpu.CompilerParams(vmem_limit_bytes=60 * 2**20)
SMALL = pltpu.CompilerParams(vmem_limit_bytes=48 * 2**20)


def dot(a, b, contract=((1,), (0,))):
    return lax.dot_general(a, b, (contract, ((), ())), preferred_element_type=F32)


def iota(shape, dim):
    return lax.broadcasted_iota(jnp.int32, shape, dim)


def read_ends(len_ref, count):
    ends, total = [], jnp.int32(0)
    for d in range(count):
        total = total + len_ref[d]
        ends.append(total)
    return ends


def run_end(ends, pos):
    best = ends[-1]
    for e in reversed(ends[:-1]):
        best = jnp.where(e > pos, e, best)
    return best


def run_start(ends, pos):
    best = jnp.zeros_like(pos)
    for e in ends[:-1]:
        best = jnp.where(e <= pos, e, best)
    return best


def split3(x):
    hi = x.astype(BF16)
    rest = x - hi.astype(F32)
    mid = rest.astype(BF16)
    return hi, mid, (rest - mid.astype(F32)).astype(BF16)


def cum_rows(ld_ref, crow_ref):
    heads, rows = ld_ref.shape
    upper = (iota((BLK, BLK), 0) <= iota((BLK, BLK), 1)).astype(F32).astype(BF16)
    base = jnp.zeros((heads, 1), F32)
    for b in range(rows // BLK):
        part = ld_ref[:, b * BLK : (b + 1) * BLK] * LOG2E
        sums = dot(jnp.concatenate(split3(part), axis=0), upper)
        row = sums[2 * heads :] + sums[heads : 2 * heads] + sums[:heads] + base
        crow_ref[:, b * BLK : (b + 1) * BLK] = row
        base = row[:, BLK - 1 :]


def value_at(cum, at, index):
    return jnp.sum(jnp.where(at == index, cum, 0.0), axis=1, keepdims=True)


def span_weights(cum, at, low, high):
    inside = (at >= low) & (at <= high)
    return jnp.exp2(jnp.where(inside, value_at(cum, at, high) - cum, NEG) + math.log2(SCALE))


def weigh(flipped, w_ref, h):
    weights = [jnp.broadcast_to(w_ref[pl.ds(h + j, 1), :], (128, flipped.shape[1])) for j in range(2)]
    return (flipped.astype(F32) * jnp.concatenate(weights, axis=0)).astype(BF16)


def whole(shape):
    return pl.BlockSpec(shape, lambda j: (0,) * len(shape))


def pieces_kernel(rest, len_ref, own_ref, ld_ref, k_ref, v_ref, *refs):
    if rest:
        side_ref, crow_ref, w_ref, keep_ref = refs
        slots = keep_ref.shape[0]
    else:
        crow_ref, flag_ref = refs[:2]
        side_refs, last_refs = refs[2 : 2 + MEMBERS], refs[2 + MEMBERS : 2 + 2 * MEMBERS]
        w_ref, first_ref, high_ref, weighted_ref, prefix_ref, parcel_ref = refs[2 + 2 * MEMBERS :]
        slots = SIDE
    heads, rows = crow_ref.shape
    step = pl.program_id(0)
    hp = v_ref.shape[1] // 128
    me = lax.axis_index("seq")

    @pl.when(step == 0)
    def _():
        cum_rows(ld_ref, crow_ref)
        first = me * rows
        last = first + rows - 1
        ends = read_ends(len_ref, len_ref.shape[0])
        starts = [jnp.int32(0)] + ends[:-1]
        lows = [jnp.int32(0)] * slots
        highs = [jnp.int32(-1)] * slots
        place, rank, previous = jnp.int32(0), jnp.int32(0), jnp.int32(-1)
        crowded, owned_in = jnp.int32(0), jnp.int32(0)
        for d in range(len(ends)):
            here = (ends[d] > first) & (ends[d] <= last)
            low = jnp.maximum(starts[d] - first, 0)
            for s in range(slots):
                mine = here & (place == s + (SIDE if rest else 0))
                lows[s] = jnp.where(mine, low, lows[s])
                highs[s] = jnp.where(mine, ends[d] - 1 - first, highs[s])
            place = place + here.astype(jnp.int32)
            device = (ends[d] - 1) // rows
            rank = jnp.where(device == previous, rank + 1, 0)
            previous = device
            late = ((rank >= SIDE) & (ends[d] != (device + 1) * rows)).astype(jnp.int32)
            crowded = jnp.maximum(crowded, late)
            owned_in = jnp.where(own_ref[d] == me, device, owned_in)
        at = iota((heads, rows), 1)
        cum = crow_ref[...]
        total = jnp.zeros((heads, rows), F32)
        for s in range(slots):
            total = total + span_weights(cum, at, lows[s], highs[s])
        if rest:
            row_at = iota((16, rows), 1)
            for s in range(slots):
                inside = (row_at >= lows[s]) & (row_at <= highs[s])
                keep_ref[s] = jnp.where(inside, 1.0, 0.0).astype(BF16)
        else:
            total = total + span_weights(cum, at, jnp.maximum(run_start(ends, last) - first, 0), rows - 1)
            flag_ref[0] = owned_in // MEMBERS
            flag_ref[1] = crowded
            high = jnp.int32(-1)
            for s in range(slots):
                high = jnp.maximum(high, highs[s])
                high_ref[s] = high
            stop = jnp.minimum(run_end(ends, first) - 1 - first, rows - 1)
            goes_on = (run_start(ends, first) < first).astype(F32)
            first_ref[...] = jnp.broadcast_to(jnp.exp2(value_at(cum, at, stop)) * goes_on, (heads, 128))
        w_ref[...] = total

    def own(states, j):
        return states[j * 128 : (j + 1) * 128, j * 128 : (j + 1) * 128]

    if rest:
        for i in range(0, hp, 2):
            lanes = slice(i * 128, (i + 2) * 128)
            weighted = weigh(k_ref[:, lanes].T, w_ref, step * hp + i).reshape(16, 16, rows)
            for s in range(slots):
                states = dot((weighted * keep_ref[s][None]).reshape(256, rows), v_ref[:, lanes])
                for j in range(2):
                    at = (s * hp + i + j) * 128
                    side_ref[0, at : at + 128, :] = own(states, j).astype(BF16)
        return

    pairs = range(0, hp, 2)
    lanes = {i: slice(i * 128, (i + 2) * 128) for i in pairs}
    for i in pairs:
        weighted_ref[lanes[i], :] = weigh(k_ref[:, lanes[i]].T, w_ref, step * hp + i)
    totals = {}
    for i in pairs:
        sums = [jnp.zeros((128, 128), F32)] * 2
        for t in range(rows // TILE):
            span = slice(t * TILE, (t + 1) * TILE)
            states = dot(weighted_ref[lanes[i], span], v_ref[span, lanes[i]])
            for j in range(2):
                prefix_ref[t, i + j] = sums[j]
                sums[j] = sums[j] + own(states, j)
        totals[i] = sums
    ended = {i: [jnp.zeros((128, 128), F32)] * 2 for i in pairs}
    for s in range(slots):
        high = high_ref[s]
        tile = jnp.maximum(high, 0) // TILE
        start = pl.multiple_of(tile * TILE, TILE)
        keep = jnp.where(start + iota((16, TILE), 1) <= high, 1.0, 0.0).astype(BF16)
        for i in pairs:
            kept = weighted_ref[lanes[i], pl.ds(start, TILE)].reshape(16, 16, TILE) * keep[None]
            states = dot(kept.reshape(256, TILE), v_ref[pl.ds(start, TILE), lanes[i]])
            for j in range(2):
                until = own(states, j) + prefix_ref[tile, i + j]
                at = (s * hp + i + j) * 128
                parcel_ref[at : at + 128, :] = (until - ended[i][j]).astype(BF16)
                ended[i][j] = until
    rate = first_ref[pl.ds(step * hp, hp), :]
    high = rate.astype(BF16).astype(F32)
    pad = jnp.zeros((EXTRA - 2 * hp, 128), F32)
    tail = jnp.concatenate([high, rate - high, pad], axis=0).astype(BF16)
    cut = SIDE * hp * 128
    for i in pairs:
        for j in range(2):
            at = cut + (i + j) * 128
            parcel_ref[at : at + 128, :] = (totals[i][j] - ended[i][j]).astype(BF16)
    parcel_ref[cut + hp * 128 :, :] = tail
    for x in range(MEMBERS):

        @pl.when((step ^ (me % MEMBERS)) == x)
        def _():
            side_refs[x][...] = parcel_ref[:cut, :]
            last_refs[x][...] = parcel_ref[cut:, :]


def piece_states(doc_lengths, owner_ids, decay_rows, keys, values, slots):
    heads, rows = decay_rows.shape
    rest = slots > SIDE
    count = slots - SIDE if rest else slots
    hp = heads // MEMBERS
    wide = pl.BlockSpec((rows, hp * 128), lambda j: (0, j))
    side = (count * hp * 128, 128)
    shapes, specs = [jax.ShapeDtypeStruct((heads, rows), F32)], [whole((heads, rows))]
    scratch = [pltpu.VMEM((heads, rows), F32)]
    if rest:
        shapes.insert(0, jax.ShapeDtypeStruct((MEMBERS,) + side, BF16))
        specs.insert(0, pl.BlockSpec((1,) + side, lambda j: (j, 0, 0)))
        scratch.append(pltpu.VMEM((count, 16, rows), BF16))
    else:
        last = (hp * 128 + EXTRA, 128)
        shapes += [jax.ShapeDtypeStruct((2,), jnp.int32)]
        shapes += [jax.ShapeDtypeStruct(shape, BF16) for shape in (side, last) for _ in range(MEMBERS)]
        specs += [SMEM] + [whole(shape) for shape in (side, last) for _ in range(MEMBERS)]
        scratch += [
            pltpu.VMEM((heads, 128), F32),
            pltpu.SMEM((SIDE,), jnp.int32),
            pltpu.VMEM((hp * 128, rows), BF16),
            pltpu.VMEM((rows // TILE, hp, 128, 128), F32),
            pltpu.VMEM((side[0] + last[0], 128), BF16),
        ]
    return pl.pallas_call(
        functools.partial(pieces_kernel, rest),
        grid=(MEMBERS,),
        in_specs=[SMEM, SMEM, whole((heads, rows)), wide, wide],
        out_specs=specs,
        out_shape=shapes,
        scratch_shapes=scratch,
        compiler_params=LIMIT,
        cost_estimate=pl.CostEstimate(
            flops=2 * heads * rows * 128 * 256, bytes_accessed=rows * heads * 128 * 4, transcendentals=heads * rows
        ),
        name="piece_states",
    )(doc_lengths, owner_ids, decay_rows, keys, values)


def head_column(ccol_ref, h, heads):
    row = iota((128, 128), 0)
    pick = (row == h) | (row == h + heads) | (row == h + 2 * heads)
    return dot(ccol_ref[...], pick.astype(F32).astype(BF16))


def fill_columns(crow_ref, ccol_ref):
    heads, rows = crow_ref.shape
    for r0 in range(0, rows, 128):
        parts = [part.astype(F32) for part in split3(crow_ref[:, r0 : r0 + 128])]
        parts.append(jnp.zeros((128 - 3 * heads, 128), F32))
        ccol_ref[r0 : r0 + 128, :] = jnp.concatenate(parts, axis=0).T.astype(BF16)


def fill_bias(first, ends, bias_ref):
    for c in range(bias_ref.shape[0] // CHUNK):
        base = first + c * CHUNK
        t_pos = base + iota((CHUNK, 1), 0)
        start = run_start(ends, t_pos)
        s_pos = base + iota((CHUNK, CHUNK), 1)
        keep = (s_pos <= t_pos) & (s_pos >= start)
        bias_ref[c * CHUNK : (c + 1) * CHUNK, :] = jnp.where(keep, math.log2(SCALE), NEG)


def attend(first, ends, q_ref, k_ref, v_ref, h, crow_ref, ccol_ref, bias_ref, out_ref):
    rows = q_ref.shape[0]
    pair = range(2)
    half = CHUNK // 2
    lanes = [slice(i * 128, (i + 1) * 128) for i in pair]
    row_all = [crow_ref[pl.ds(h + i, 1), :] for i in pair]
    col_all = [head_column(ccol_ref, h + i, crow_ref.shape[0]) for i in pair]
    starts = range(0, rows, CHUNK)
    spans = [slice(r0, r0 + CHUNK) for r0 in starts]
    reach = [run_end(ends, first + r0 - 1) - (first + r0) for r0 in starts]
    base = [[row_all[i][:, r0 - 1 : r0] if r0 else None for r0 in starts] for i in pair]

    fresh = [[], []]
    for c, r0 in enumerate(starts[:-1]):
        since = run_start(ends, first + r0 + CHUNK - 1) - (first + r0)
        inside = iota((1, CHUNK), 1) >= since
        for i in pair:
            row = row_all[i][:, spans[c]]
            weight = jnp.exp2(jnp.where(inside, row[:, CHUNK - 1 :] - row, NEG) + math.log2(SCALE))
            flipped = k_ref[spans[c], lanes[i]].T
            fresh[i].append(dot((flipped.astype(F32) * weight).astype(BF16), v_ref[spans[c], lanes[i]]))
    carried = []
    for i in pair:
        state = fresh[i][0]
        chain = [None, state.astype(BF16)]
        for c in range(1, len(starts) - 1):
            total = row_all[i][:, starts[c] + CHUNK - 1 : starts[c] + CHUNK]
            state = fresh[i][c] + state * jnp.exp2(jnp.where(CHUNK <= reach[c], total - base[i][c], NEG))
            chain.append(state.astype(BF16))
        carried.append(chain)

    def products(c):
        result = []
        for i in pair:
            query = q_ref[spans[c], lanes[i]]
            scores = dot(query, k_ref[spans[c], lanes[i]], ((1,), (1,)))
            result.append((scores, dot(query, carried[i][c]) if c else None))
        return result

    ahead = products(0)
    for c, r0 in enumerate(starts):
        current = ahead
        if c + 1 < len(starts):
            ahead = products(c + 1)
        for part in range(2):
            t0, width = part * half, (part + 1) * half
            rows_here = slice(r0 + t0, r0 + t0 + half)
            for i in pair:
                scores, carry = current[i]
                col = col_all[i][rows_here]
                cols = jnp.concatenate([col] * (width // half), axis=1)
                decay = jnp.exp2((cols - row_all[i][:, r0 : r0 + width]) + bias_ref[rows_here, :width])
                weights = (scores[t0 : t0 + half, :width] * decay).astype(BF16)
                att = dot(weights, v_ref[r0 : r0 + width, lanes[i]])
                if c:
                    lead = jnp.exp2(jnp.where(t0 + iota((half, 1), 0) < reach[c], col - base[i][c], NEG))
                    att = att + lead * carry[t0 : t0 + half]
                out_ref[rows_here, lanes[i]] = att


def local_kernel(pairs_before, len_ref, q_ref, k_ref, v_ref, crow_ref, *refs):
    out_ref, bias_ref, ccol_ref = refs[-3:]
    rows = q_ref.shape[0]
    step = pl.program_id(0)
    first = lax.axis_index("seq") * rows
    ends = read_ends(len_ref, len_ref.shape[0])

    @pl.when(step == 0)
    def _():
        fill_bias(first, ends, bias_ref)
        fill_columns(crow_ref, ccol_ref)

    attend(first, ends, q_ref, k_ref, v_ref, (step + pairs_before) * 2, crow_ref, ccol_ref, bias_ref, out_ref)


def local_attention(doc_lengths, queries, keys, values, crow, before, part):
    heads, rows = crow.shape
    skip, count = sum(PARTS[:part]) // 2, PARTS[part]
    wide = pl.BlockSpec((rows, 256), lambda j: (0, j + skip))
    return pl.pallas_call(
        functools.partial(local_kernel, skip),
        grid=(count // 2,),
        in_specs=[SMEM, wide, wide, wide, whole((heads, rows))] + [pl.BlockSpec(memory_space=pl.ANY)] * len(before),
        input_output_aliases={5: 0} if before else {},
        out_specs=wide,
        out_shape=jax.ShapeDtypeStruct((rows, heads * 128), F32),
        scratch_shapes=[pltpu.VMEM((rows, CHUNK), F32), pltpu.VMEM((rows, 128), BF16)],
        compiler_params=LIMIT,
        cost_estimate=pl.CostEstimate(
            flops=count * rows * CHUNK * 128 * 8, bytes_accessed=rows * count * 128 * 10, transcendentals=count * rows * CHUNK
        ),
        name="local_attention",
    )(doc_lengths, queries, keys, values, crow, *before)


def gather_last(refs, last_ref):
    me = lax.axis_index("seq") % MEMBERS
    for x, ref in enumerate(refs):
        last_ref[me ^ x] = ref[...]


def decay_of(last_ref, e, i, hp):
    extra = last_ref[e, hp * 128 :, :].astype(F32)
    return extra[i : i + 1, :] + extra[hp + i : hp + i + 1, :]


def scan_quad(rows, len_ref, last_ref, state, i, hp, note):
    members = last_ref.shape[0]
    ends = read_ends(len_ref, len_ref.shape[0])
    base = lax.axis_index("seq") // members * members
    for e in range(members):
        note(e, state)
        low = (base + e) * rows
        inner = jnp.int32(0)
        for end in ends:
            inner = inner + ((end > low) & (end < low + rows)).astype(jnp.int32)
        passes = (inner == 0).astype(F32)
        piece = last_ref[e, i * 128 : (i + 1) * 128, :].astype(F32)
        state = state * (decay_of(last_ref, e, i, hp) * passes) + piece
    return state


def leave_kernel(rows, len_ref, *refs):
    out_ref, last_ref = refs[-2:]
    gather_last(refs[:MEMBERS], last_ref)
    hp = out_ref.shape[0]
    for i in range(hp):
        state = jnp.zeros((128, 128), F32)
        if len(refs) > MEMBERS + 2:
            state = refs[MEMBERS][i].astype(F32)
        state = scan_quad(rows, len_ref, last_ref, state, i, hp, lambda e, x: None)
        out_ref[i] = state.astype(BF16)


def leave_quad(doc_lengths, last, coming, rows, hp):
    return pl.pallas_call(
        functools.partial(leave_kernel, rows),
        in_specs=[SMEM] + [VMEM] * (MEMBERS + len(coming)),
        out_specs=VMEM,
        out_shape=jax.ShapeDtypeStruct((hp, 128, 128), BF16),
        scratch_shapes=[pltpu.VMEM((MEMBERS,) + last[0].shape, BF16)],
        compiler_params=SMALL,
        name="leave_quad",
    )(doc_lengths, *last, *coming)


def enter_kernel(rows, len_ref, *refs):
    in_ref, out_refs, last_ref, state_ref = refs[MEMBERS], refs[MEMBERS + 1 : -2], refs[-2], refs[-1]
    gather_last(refs[:MEMBERS], last_ref)
    hp = in_ref.shape[0]

    def note(i, e, state):
        state_ref[e, i] = state

    for i in range(hp):
        scan_quad(rows, len_ref, last_ref, in_ref[i].astype(F32), i, hp, functools.partial(note, i))
    me = lax.axis_index("seq") % MEMBERS
    for x, out_ref in enumerate(out_refs):
        out_ref[...] = state_ref[me ^ x].astype(BF16)


def enter_states(doc_lengths, last, coming, rows):
    return pl.pallas_call(
        functools.partial(enter_kernel, rows),
        in_specs=[SMEM] + [VMEM] * (MEMBERS + 1),
        out_specs=[VMEM] * MEMBERS,
        out_shape=[jax.ShapeDtypeStruct(coming.shape, BF16)] * MEMBERS,
        scratch_shapes=[
            pltpu.VMEM((MEMBERS,) + last[0].shape, BF16),
            pltpu.VMEM((MEMBERS,) + coming.shape, F32),
        ],
        compiler_params=SMALL,
        name="enter_states",
    )(doc_lengths, *last, coming)


def final_kernel(rows, len_ref, own_ref, *refs):
    side_refs = refs[MEMBERS : 2 * MEMBERS]
    rest_ref, in_ref = refs[2 * MEMBERS : 2 * MEMBERS + 2]
    out_refs, (last_ref, state_ref, piece_ref, final_ref) = refs[2 * MEMBERS + 2 : -4], refs[-4:]
    gather_last(refs[:MEMBERS], last_ref)
    hp = in_ref.shape[0]
    ends = read_ends(len_ref, len_ref.shape[0])
    me = lax.axis_index("seq")
    base = me // MEMBERS * MEMBERS

    def note(i, e, state):
        state_ref[e, i] = state

    for i in range(hp):
        scan_quad(rows, len_ref, last_ref, in_ref[i].astype(F32), i, hp, functools.partial(note, i))
    final_ref[...] = jnp.zeros_like(final_ref)
    place, previous = jnp.int32(0), jnp.int32(-1)
    for d in range(len(ends)):
        device = (ends[d] - 1) // rows
        place = jnp.where(device == previous, place + 1, 0)
        previous = device
        at_end = ends[d] == (device + 1) * rows
        enters = (place == 0).astype(F32)
        mine = device // MEMBERS * MEMBERS == base
        inner = mine & jnp.logical_not(at_end)
        e = device - base

        @pl.when(mine & at_end)
        def _():
            piece_ref[...] = last_ref[e, : hp * 128, :]

        for x, side_ref in enumerate(side_refs):

            @pl.when(inner & (place < SIDE) & ((e ^ (me % MEMBERS)) == x))
            def _():
                piece_ref[...] = side_ref[pl.ds(pl.multiple_of(place * hp * 128, 128), hp * 128), :]

        @pl.when(inner & (place >= SIDE))
        def _():
            row = pl.multiple_of((place - SIDE) * hp * 128, 128)
            pltpu.sync_copy(rest_ref.at[e, pl.ds(row, hp * 128), :], piece_ref)

        @pl.when(mine)
        def _():
            for i in range(hp):
                local = piece_ref[i * 128 : (i + 1) * 128, :].astype(F32)
                state = local + state_ref[e, i] * (decay_of(last_ref, e, i, hp) * enters)
                final_ref[own_ref[d], i] = state.astype(BF16)

    for x, out_ref in enumerate(out_refs):
        out_ref[...] = final_ref[me ^ x]


def final_states(doc_lengths, owner_ids, last, side, rest, coming, rows, spread):
    return pl.pallas_call(
        functools.partial(final_kernel, rows),
        in_specs=[SMEM, SMEM] + [VMEM] * (2 * MEMBERS) + [pl.BlockSpec(memory_space=pl.ANY), VMEM],
        out_specs=[VMEM] * spread,
        out_shape=[jax.ShapeDtypeStruct(coming.shape, BF16)] * spread,
        scratch_shapes=[
            pltpu.VMEM((MEMBERS,) + last[0].shape, BF16),
            pltpu.VMEM((MEMBERS,) + coming.shape, F32),
            pltpu.VMEM((coming.shape[0] * 128, 128), BF16),
            pltpu.VMEM((spread,) + coming.shape, BF16),
        ],
        compiler_params=SMALL,
        name="final_states",
    )(doc_lengths, owner_ids, *last, *side, rest, coming)


def pick_kernel(flag_ref, *refs):
    in_refs, out_ref = refs[:-1], refs[-1]
    me = lax.axis_index("seq")
    hp = in_refs[0].shape[0]
    for x, ref in enumerate(in_refs):
        source = me ^ x

        @pl.when(source // MEMBERS == flag_ref[0])
        def _():
            out_ref[0, pl.ds(source % MEMBERS * hp, hp)] = ref[...]


def pick_owned(flags, arrived, heads):
    return pl.pallas_call(
        pick_kernel,
        in_specs=[SMEM] + [VMEM] * len(arrived),
        out_specs=VMEM,
        out_shape=jax.ShapeDtypeStruct((1, heads, 128, 128), BF16),
        compiler_params=SMALL,
        name="pick_owned",
    )(flags, *arrived)


def finish_kernel(len_ref, q_ref, e0, e1, e2, e3, local_ref, gate_ref, gain_ref, crow_ref, out_ref, ccol_ref):
    rows = q_ref.shape[0]
    step = pl.program_id(0)
    me = lax.axis_index("seq")
    hp = e0.shape[0]

    @pl.when(step == 0)
    def _():
        fill_columns(crow_ref, ccol_ref)

    def entering(h):
        far = (h // hp) ^ (me % MEMBERS)
        state = e0[h % hp]
        for x, ref in ((1, e1), (2, e2), (3, e3)):
            state = jnp.where(far == x, ref[h % hp], state)
        return state

    first = me * rows
    reach = run_end(read_ends(len_ref, len_ref.shape[0]), first - 1) - first
    ones = jnp.ones((128, 128), BF16)
    cols = [head_column(ccol_ref, step * 2 + i, crow_ref.shape[0]) for i in range(2)]
    states = [entering(step * 2 + i) for i in range(2)]
    for t0 in range(0, rows, 256):
        span = slice(t0, t0 + 256)
        carry = [dot(q_ref[span, i * 128 : (i + 1) * 128], states[i]) for i in range(2)]
        inside = t0 + iota((256, 1), 0) < reach
        for i in range(2):
            lanes = slice(i * 128, (i + 1) * 128)
            lead = jnp.exp2(jnp.where(inside, cols[i][span], NEG))
            att = local_ref[span, lanes] + lead * carry[i]
            mean = dot((att * att).astype(BF16), ones) * (1 / 128)
            gate = 0.5 + 0.5 * jnp.tanh(0.5 * gate_ref[span, lanes].astype(F32))
            gain = gain_ref[:, lanes].astype(F32)
            out_ref[span, lanes] = (att * lax.rsqrt(mean + 1e-06) * (gain * gate)).astype(BF16)


def finish(doc_lengths, queries, entering, local, gate, gain, crow):
    heads, rows = crow.shape
    wide = pl.BlockSpec((rows, 256), lambda j: (0, j))
    return pl.pallas_call(
        finish_kernel,
        grid=(heads // 2,),
        in_specs=[SMEM, wide]
        + [whole(e.shape) for e in entering]
        + [wide, wide, pl.BlockSpec((1, 256), lambda j: (0, j)), whole((heads, rows))],
        out_specs=wide,
        out_shape=jax.ShapeDtypeStruct((rows, heads * 128), BF16),
        scratch_shapes=[pltpu.VMEM((rows, 128), BF16)],
        compiler_params=pltpu.CompilerParams(vmem_limit_bytes=54 * 2**20),
        cost_estimate=pl.CostEstimate(
            flops=heads * rows * 128 * 256, bytes_accessed=rows * heads * 128 * 10, transcendentals=heads * rows * 256
        ),
        name="finish",
    )(doc_lengths, queries, *entering, local, gate, gain, crow)


def swap(x, groups=None):
    return lax.all_to_all(x, "seq", split_axis=0, concat_axis=0, axis_index_groups=groups, tiled=True)


def by_distance(parcels, spread):
    moved = {0: parcels[0]}
    for x in sorted(range(1, len(parcels)), key=lambda x: (x < MEMBERS, x)):
        moved[x] = lax.ppermute(parcels[x], "seq", [(s, s ^ x) for s in range(spread)])
    return [moved[x] for x in range(len(parcels))]


def on_device(spread, queries, keys, values, log_decay, gate, gain, doc_lengths, owner_ids):
    rows, heads = log_decay.shape
    quads = spread // MEMBERS
    hp = heads // MEMBERS
    near = [[q * MEMBERS + m for m in range(MEMBERS)] for q in range(quads)]
    onward = [(s, s + MEMBERS) for s in range(spread - MEMBERS)]
    decay_rows = log_decay.T
    barrier = lax.optimization_barrier

    crow, flags, *parcels = piece_states(doc_lengths, owner_ids, decay_rows, keys, values, SIDE)
    side, last = parcels[:MEMBERS], parcels[MEMBERS:]
    last = by_distance(last, spread)
    gain = gain.reshape(1, -1)
    crowded = flags[1] > 0
    slots = max(doc_lengths.shape[0] - 1, SIDE + 1)

    def send_rest():
        return swap(piece_states(doc_lengths, owner_ids, decay_rows, keys, values, slots)[0], near)

    none = jnp.zeros((MEMBERS, (slots - SIDE) * hp * 128, 128), BF16)
    rest = lax.cond(crowded, send_rest, lambda: none)
    last, side, gain, rest = barrier((last, side, gain, rest))

    side = by_distance(side, spread)
    coming = []
    for _ in range(quads - 1):
        leaving = leave_quad(doc_lengths, last, coming, rows, hp)
        coming = [lax.ppermute(leaving, "seq", onward)]
    local = functools.partial(local_attention, doc_lengths, queries, keys, values)
    crow_1, leaving = barrier((crow, leaving))
    done = local(crow_1, [], 0)
    coming, done = barrier((coming[0], done))

    entering = enter_states(doc_lengths, last, coming, rows)
    crow_2, entering = barrier((crow_1, entering))
    entering = by_distance(entering, spread)
    done = local(crow_2, [done], 1)
    side, done, entering = barrier((side, done, entering))
    finals = final_states(doc_lengths, owner_ids, last, side, rest, coming, rows, spread)
    arrived = by_distance(finals, spread)
    mixed = finish(doc_lengths, queries, entering, done, gate, gain, crow)
    return mixed, pick_owned(flags, arrived, heads)


def solution(mesh):
    placed = (
        P(("groups", "seq"), "tp"),
        P(("groups", "seq"), "tp"),
        P(("groups", "seq"), "tp"),
        P(("groups", "seq"), "tp"),
        P(("groups", "seq"), "tp"),
        P("tp"),
        P("groups"),
        P("groups"),
    )
    return jax.shard_map(
        functools.partial(on_device, mesh.shape["seq"]),
        mesh=mesh,
        in_specs=placed,
        out_specs=(P(("groups", "seq"), "tp"), P(("groups", "seq"), "tp", None, None)),
        check_vma=False,
    )
```

```python
import functools
import math

import jax
import jax.numpy as jnp
from jax import lax
from jax.experimental import pallas as pl
from jax.experimental.pallas import tpu as pltpu
from jax.sharding import PartitionSpec as P

BLK = 512
SIDE = 3
EXTRA = 16
CHUNK = 256
MEMBERS = 4
TILE = 256
NEG = -1e30
LOG2E = math.log2(math.e)
SCALE = 128**-0.5
F32, BF16 = jnp.float32, jnp.bfloat16
SMEM = pl.BlockSpec(memory_space=pltpu.SMEM)
VMEM = pl.BlockSpec(memory_space=pltpu.VMEM)
LIMIT = pltpu.CompilerParams(vmem_limit_bytes=60 * 2**20)
SMALL = pltpu.CompilerParams(vmem_limit_bytes=48 * 2**20)


def dot(a, b, contract=((1,), (0,))):
    return lax.dot_general(a, b, (contract, ((), ())), preferred_element_type=F32)


def iota(shape, dim):
    return lax.broadcasted_iota(jnp.int32, shape, dim)


def read_ends(len_ref, count):
    ends, total = [], jnp.int32(0)
    for d in range(count):
        total = total + len_ref[d]
        ends.append(total)
    return ends


def run_end(ends, pos):
    best = ends[-1]
    for e in reversed(ends[:-1]):
        best = jnp.where(e > pos, e, best)
    return best


def run_start(ends, pos):
    best = jnp.zeros_like(pos)
    for e in ends[:-1]:
        best = jnp.where(e <= pos, e, best)
    return best


def split3(x):
    hi = x.astype(BF16)
    rest = x - hi.astype(F32)
    mid = rest.astype(BF16)
    return hi, mid, (rest - mid.astype(F32)).astype(BF16)


def cum_rows(ld_ref, crow_ref):
    heads, rows = ld_ref.shape
    upper = (iota((BLK, BLK), 0) <= iota((BLK, BLK), 1)).astype(F32).astype(BF16)
    base = jnp.zeros((heads, 1), F32)
    for b in range(rows // BLK):
        part = ld_ref[:, b * BLK : (b + 1) * BLK] * LOG2E
        sums = dot(jnp.concatenate(split3(part), axis=0), upper)
        row = sums[2 * heads :] + sums[heads : 2 * heads] + sums[:heads] + base
        crow_ref[:, b * BLK : (b + 1) * BLK] = row
        base = row[:, BLK - 1 :]


def value_at(cum, at, index):
    return jnp.sum(jnp.where(at == index, cum, 0.0), axis=1, keepdims=True)


def span_weights(cum, at, low, high):
    inside = (at >= low) & (at <= high)
    return jnp.exp2(jnp.where(inside, value_at(cum, at, high) - cum, NEG) + math.log2(SCALE))


def weigh(flipped, w_ref, h):
    weights = [jnp.broadcast_to(w_ref[pl.ds(h + j, 1), :], (128, flipped.shape[1])) for j in range(2)]
    return (flipped.astype(F32) * jnp.concatenate(weights, axis=0)).astype(BF16)


def whole(shape):
    return pl.BlockSpec(shape, lambda j: (0,) * len(shape))


def pieces_kernel(rest, len_ref, own_ref, ld_ref, k_ref, v_ref, *refs):
    if rest:
        side_ref, crow_ref, w_ref, keep_ref = refs
        slots = keep_ref.shape[0]
    else:
        crow_ref, flag_ref = refs[:2]
        side_refs, last_refs = refs[2 : 2 + MEMBERS], refs[2 + MEMBERS : 2 + 2 * MEMBERS]
        w_ref, first_ref, high_ref, weighted_ref, prefix_ref, parcel_ref = refs[2 + 2 * MEMBERS :]
        slots = SIDE
    heads, rows = crow_ref.shape
    step = pl.program_id(0)
    hp = v_ref.shape[1] // 128
    me = lax.axis_index("seq")

    @pl.when(step == 0)
    def _():
        cum_rows(ld_ref, crow_ref)
        first = me * rows
        last = first + rows - 1
        ends = read_ends(len_ref, len_ref.shape[0])
        starts = [jnp.int32(0)] + ends[:-1]
        lows = [jnp.int32(0)] * slots
        highs = [jnp.int32(-1)] * slots
        place, rank, previous = jnp.int32(0), jnp.int32(0), jnp.int32(-1)
        crowded, owned_in = jnp.int32(0), jnp.int32(0)
        for d in range(len(ends)):
            here = (ends[d] > first) & (ends[d] <= last)
            low = jnp.maximum(starts[d] - first, 0)
            for s in range(slots):
                mine = here & (place == s + (SIDE if rest else 0))
                lows[s] = jnp.where(mine, low, lows[s])
                highs[s] = jnp.where(mine, ends[d] - 1 - first, highs[s])
            place = place + here.astype(jnp.int32)
            device = (ends[d] - 1) // rows
            rank = jnp.where(device == previous, rank + 1, 0)
            previous = device
            late = ((rank >= SIDE) & (ends[d] != (device + 1) * rows)).astype(jnp.int32)
            crowded = jnp.maximum(crowded, late)
            owned_in = jnp.where(own_ref[d] == me, device, owned_in)
        at = iota((heads, rows), 1)
        cum = crow_ref[...]
        total = jnp.zeros((heads, rows), F32)
        for s in range(slots):
            total = total + span_weights(cum, at, lows[s], highs[s])
        if rest:
            row_at = iota((16, rows), 1)
            for s in range(slots):
                inside = (row_at >= lows[s]) & (row_at <= highs[s])
                keep_ref[s] = jnp.where(inside, 1.0, 0.0).astype(BF16)
        else:
            total = total + span_weights(cum, at, jnp.maximum(run_start(ends, last) - first, 0), rows - 1)
            flag_ref[0] = owned_in // MEMBERS
            flag_ref[1] = crowded
            high = jnp.int32(-1)
            for s in range(slots):
                high = jnp.maximum(high, highs[s])
                high_ref[s] = high
            stop = jnp.minimum(run_end(ends, first) - 1 - first, rows - 1)
            goes_on = (run_start(ends, first) < first).astype(F32)
            first_ref[...] = jnp.broadcast_to(jnp.exp2(value_at(cum, at, stop)) * goes_on, (heads, 128))
        w_ref[...] = total

    def own(states, j):
        return states[j * 128 : (j + 1) * 128, j * 128 : (j + 1) * 128]

    if rest:
        for i in range(0, hp, 2):
            lanes = slice(i * 128, (i + 2) * 128)
            weighted = weigh(k_ref[:, lanes].T, w_ref, step * hp + i).reshape(16, 16, rows)
            for s in range(slots):
                states = dot((weighted * keep_ref[s][None]).reshape(256, rows), v_ref[:, lanes])
                for j in range(2):
                    at = (s * hp + i + j) * 128
                    side_ref[0, at : at + 128, :] = own(states, j).astype(BF16)
        return

    pairs = range(0, hp, 2)
    lanes = {i: slice(i * 128, (i + 2) * 128) for i in pairs}
    for i in pairs:
        weighted_ref[lanes[i], :] = weigh(k_ref[:, lanes[i]].T, w_ref, step * hp + i)
    totals = {}
    for i in pairs:
        sums = [jnp.zeros((128, 128), F32)] * 2
        for t in range(rows // TILE):
            span = slice(t * TILE, (t + 1) * TILE)
            states = dot(weighted_ref[lanes[i], span], v_ref[span, lanes[i]])
            for j in range(2):
                prefix_ref[t, i + j] = sums[j]
                sums[j] = sums[j] + own(states, j)
        totals[i] = sums
    ended = {i: [jnp.zeros((128, 128), F32)] * 2 for i in pairs}
    for s in range(slots):
        high = high_ref[s]
        tile = jnp.maximum(high, 0) // TILE
        start = pl.multiple_of(tile * TILE, TILE)
        keep = jnp.where(start + iota((16, TILE), 1) <= high, 1.0, 0.0).astype(BF16)
        for i in pairs:
            kept = weighted_ref[lanes[i], pl.ds(start, TILE)].reshape(16, 16, TILE) * keep[None]
            states = dot(kept.reshape(256, TILE), v_ref[pl.ds(start, TILE), lanes[i]])
            for j in range(2):
                until = own(states, j) + prefix_ref[tile, i + j]
                at = (s * hp + i + j) * 128
                parcel_ref[at : at + 128, :] = (until - ended[i][j]).astype(BF16)
                ended[i][j] = until
    rate = first_ref[pl.ds(step * hp, hp), :]
    high = rate.astype(BF16).astype(F32)
    pad = jnp.zeros((EXTRA - 2 * hp, 128), F32)
    tail = jnp.concatenate([high, rate - high, pad], axis=0).astype(BF16)
    cut = SIDE * hp * 128
    for i in pairs:
        for j in range(2):
            at = cut + (i + j) * 128
            parcel_ref[at : at + 128, :] = (totals[i][j] - ended[i][j]).astype(BF16)
    parcel_ref[cut + hp * 128 :, :] = tail
    for x in range(MEMBERS):

        @pl.when((step ^ (me % MEMBERS)) == x)
        def _():
            side_refs[x][...] = parcel_ref[:cut, :]
            last_refs[x][...] = parcel_ref[cut:, :]


def piece_states(doc_lengths, owner_ids, decay_rows, keys, values, slots):
    heads, rows = decay_rows.shape
    rest = slots > SIDE
    count = slots - SIDE if rest else slots
    hp = heads // MEMBERS
    wide = pl.BlockSpec((rows, hp * 128), lambda j: (0, j))
    side = (count * hp * 128, 128)
    shapes, specs = [jax.ShapeDtypeStruct((heads, rows), F32)], [whole((heads, rows))]
    scratch = [pltpu.VMEM((heads, rows), F32)]
    if rest:
        shapes.insert(0, jax.ShapeDtypeStruct((MEMBERS,) + side, BF16))
        specs.insert(0, pl.BlockSpec((1,) + side, lambda j: (j, 0, 0)))
        scratch.append(pltpu.VMEM((count, 16, rows), BF16))
    else:
        last = (hp * 128 + EXTRA, 128)
        shapes += [jax.ShapeDtypeStruct((2,), jnp.int32)]
        shapes += [jax.ShapeDtypeStruct(shape, BF16) for shape in (side, last) for _ in range(MEMBERS)]
        specs += [SMEM] + [whole(shape) for shape in (side, last) for _ in range(MEMBERS)]
        scratch += [
            pltpu.VMEM((heads, 128), F32),
            pltpu.SMEM((SIDE,), jnp.int32),
            pltpu.VMEM((hp * 128, rows), BF16),
            pltpu.VMEM((rows // TILE, hp, 128, 128), F32),
            pltpu.VMEM((side[0] + last[0], 128), BF16),
        ]
    return pl.pallas_call(
        functools.partial(pieces_kernel, rest),
        grid=(MEMBERS,),
        in_specs=[SMEM, SMEM, whole((heads, rows)), wide, wide],
        out_specs=specs,
        out_shape=shapes,
        scratch_shapes=scratch,
        compiler_params=LIMIT,
        cost_estimate=pl.CostEstimate(
            flops=2 * heads * rows * 128 * 256, bytes_accessed=rows * heads * 128 * 4, transcendentals=heads * rows
        ),
        name="piece_states",
    )(doc_lengths, owner_ids, decay_rows, keys, values)


def head_column(ccol_ref, h):
    cols = ccol_ref[...]
    return jnp.sum(jnp.where(iota(cols.shape, 1) == h, cols, 0.0), axis=1, keepdims=True)


def fill_columns(crow_ref, ccol_ref):
    heads, rows = crow_ref.shape
    for r0 in range(0, rows, 128):
        part = crow_ref[:, r0 : r0 + 128]
        part = jnp.concatenate([part, jnp.zeros((128 - heads, 128), F32)], axis=0)
        ccol_ref[r0 : r0 + 128, :] = part.T


def fill_bias(first, ends, bias_ref):
    for c in range(bias_ref.shape[0] // CHUNK):
        base = first + c * CHUNK
        t_pos = base + iota((CHUNK, 1), 0)
        start = run_start(ends, t_pos)
        s_pos = base + iota((CHUNK, CHUNK), 1)
        keep = (s_pos <= t_pos) & (s_pos >= start)
        bias_ref[c * CHUNK : (c + 1) * CHUNK, :] = jnp.where(keep, math.log2(SCALE), NEG)


def attend(first, ends, q_ref, k_ref, v_ref, h, crow_ref, ccol_ref, bias_ref, out_ref):
    rows = q_ref.shape[0]
    pair = range(2)
    half = CHUNK // 2
    lanes = [slice(i * 128, (i + 1) * 128) for i in pair]
    row_all = [crow_ref[pl.ds(h + i, 1), :] for i in pair]
    col_all = [head_column(ccol_ref, h + i) for i in pair]
    starts = range(0, rows, CHUNK)
    spans = [slice(r0, r0 + CHUNK) for r0 in starts]
    reach = [run_end(ends, first + r0 - 1) - (first + r0) for r0 in starts]
    base = [[row_all[i][:, r0 - 1 : r0] if r0 else None for r0 in starts] for i in pair]

    fresh = [[], []]
    for c, r0 in enumerate(starts[:-1]):
        since = run_start(ends, first + r0 + CHUNK - 1) - (first + r0)
        inside = iota((1, CHUNK), 1) >= since
        for i in pair:
            row = row_all[i][:, spans[c]]
            weight = jnp.exp2(jnp.where(inside, row[:, CHUNK - 1 :] - row, NEG) + math.log2(SCALE))
            flipped = k_ref[spans[c], lanes[i]].T
            fresh[i].append(dot((flipped.astype(F32) * weight).astype(BF16), v_ref[spans[c], lanes[i]]))
    carried = []
    for i in pair:
        state = fresh[i][0]
        chain = [None, state.astype(BF16)]
        for c in range(1, len(starts) - 1):
            total = row_all[i][:, starts[c] + CHUNK - 1 : starts[c] + CHUNK]
            state = fresh[i][c] + state * jnp.exp2(jnp.where(CHUNK <= reach[c], total - base[i][c], NEG))
            chain.append(state.astype(BF16))
        carried.append(chain)

    def products(c):
        result = []
        for i in pair:
            query = q_ref[spans[c], lanes[i]]
            scores = dot(query, k_ref[spans[c], lanes[i]], ((1,), (1,)))
            result.append((scores, dot(query, carried[i][c]) if c else None))
        return result

    ahead = products(0)
    for c, r0 in enumerate(starts):
        current = ahead
        if c + 1 < len(starts):
            ahead = products(c + 1)
        for part in range(2):
            t0, width = part * half, (part + 1) * half
            rows_here = slice(r0 + t0, r0 + t0 + half)
            for i in pair:
                scores, carry = current[i]
                col = col_all[i][rows_here]
                decay = jnp.exp2((col - row_all[i][:, r0 : r0 + width]) + bias_ref[rows_here, :width])
                weights = (scores[t0 : t0 + half, :width] * decay).astype(BF16)
                att = dot(weights, v_ref[r0 : r0 + width, lanes[i]])
                if c:
                    lead = jnp.exp2(jnp.where(t0 + iota((half, 1), 0) < reach[c], col - base[i][c], NEG))
                    att = att + lead * carry[t0 : t0 + half]
                out_ref[rows_here, lanes[i]] = att


def local_kernel(len_ref, q_ref, k_ref, v_ref, crow_ref, out_ref, bias_ref, ccol_ref):
    rows = q_ref.shape[0]
    step = pl.program_id(0)
    first = lax.axis_index("seq") * rows
    ends = read_ends(len_ref, len_ref.shape[0])

    @pl.when(step == 0)
    def _():
        fill_bias(first, ends, bias_ref)
        fill_columns(crow_ref, ccol_ref)

    attend(first, ends, q_ref, k_ref, v_ref, step * 2, crow_ref, ccol_ref, bias_ref, out_ref)


def local_attention(doc_lengths, queries, keys, values, crow):
    heads, rows = crow.shape
    wide = pl.BlockSpec((rows, 256), lambda j: (0, j))
    return pl.pallas_call(
        local_kernel,
        grid=(heads // 2,),
        in_specs=[SMEM, wide, wide, wide, whole((heads, rows))],
        out_specs=wide,
        out_shape=jax.ShapeDtypeStruct((rows, heads * 128), F32),
        scratch_shapes=[pltpu.VMEM((rows, CHUNK), F32), pltpu.VMEM((rows, 128), F32)],
        compiler_params=LIMIT,
        cost_estimate=pl.CostEstimate(
            flops=heads * rows * CHUNK * 128 * 8, bytes_accessed=rows * heads * 128 * 10, transcendentals=heads * rows * CHUNK
        ),
        name="local_attention",
    )(doc_lengths, queries, keys, values, crow)


def gather_last(refs, last_ref):
    me = lax.axis_index("seq") % MEMBERS
    for x, ref in enumerate(refs):
        last_ref[me ^ x] = ref[...]


def decay_of(last_ref, e, i, hp):
    extra = last_ref[e, hp * 128 :, :].astype(F32)
    return extra[i : i + 1, :] + extra[hp + i : hp + i + 1, :]


def scan_quad(rows, len_ref, last_ref, state, i, hp, note):
    members = last_ref.shape[0]
    ends = read_ends(len_ref, len_ref.shape[0])
    base = lax.axis_index("seq") // members * members
    for e in range(members):
        note(e, state)
        low = (base + e) * rows
        inner = jnp.int32(0)
        for end in ends:
            inner = inner + ((end > low) & (end < low + rows)).astype(jnp.int32)
        passes = (inner == 0).astype(F32)
        piece = last_ref[e, i * 128 : (i + 1) * 128, :].astype(F32)
        state = state * (decay_of(last_ref, e, i, hp) * passes) + piece
    return state


def leave_kernel(rows, len_ref, *refs):
    out_ref, last_ref = refs[-2:]
    gather_last(refs[:MEMBERS], last_ref)
    hp = out_ref.shape[0]
    for i in range(hp):
        state = jnp.zeros((128, 128), F32)
        if len(refs) > MEMBERS + 2:
            state = refs[MEMBERS][i].astype(F32)
        state = scan_quad(rows, len_ref, last_ref, state, i, hp, lambda e, x: None)
        out_ref[i] = state.astype(BF16)


def leave_quad(doc_lengths, last, coming, rows, hp):
    return pl.pallas_call(
        functools.partial(leave_kernel, rows),
        in_specs=[SMEM] + [VMEM] * (MEMBERS + len(coming)),
        out_specs=VMEM,
        out_shape=jax.ShapeDtypeStruct((hp, 128, 128), BF16),
        scratch_shapes=[pltpu.VMEM((MEMBERS,) + last[0].shape, BF16)],
        compiler_params=SMALL,
        name="leave_quad",
    )(doc_lengths, *last, *coming)


def enter_kernel(rows, len_ref, *refs):
    in_ref, out_ref, last_ref = refs[MEMBERS:]
    gather_last(refs[:MEMBERS], last_ref)
    hp = in_ref.shape[0]

    def note(i, e, state):
        out_ref[e, i] = state.astype(BF16)

    for i in range(hp):
        scan_quad(rows, len_ref, last_ref, in_ref[i].astype(F32), i, hp, functools.partial(note, i))


def enter_states(doc_lengths, last, coming, rows):
    return pl.pallas_call(
        functools.partial(enter_kernel, rows),
        in_specs=[SMEM] + [VMEM] * (MEMBERS + 1),
        out_specs=VMEM,
        out_shape=jax.ShapeDtypeStruct((MEMBERS,) + coming.shape, BF16),
        scratch_shapes=[pltpu.VMEM((MEMBERS,) + last[0].shape, BF16)],
        compiler_params=SMALL,
        name="enter_states",
    )(doc_lengths, *last, coming)


def final_kernel(rows, len_ref, own_ref, *refs):
    side_refs = refs[MEMBERS : 2 * MEMBERS]
    rest_ref, in_ref = refs[2 * MEMBERS : 2 * MEMBERS + 2]
    out_refs, (last_ref, state_ref, piece_ref, final_ref) = refs[2 * MEMBERS + 2 : -4], refs[-4:]
    gather_last(refs[:MEMBERS], last_ref)
    hp = in_ref.shape[0]
    ends = read_ends(len_ref, len_ref.shape[0])
    me = lax.axis_index("seq")
    base = me // MEMBERS * MEMBERS

    def note(i, e, state):
        state_ref[e, i] = state

    for i in range(hp):
        scan_quad(rows, len_ref, last_ref, in_ref[i].astype(F32), i, hp, functools.partial(note, i))
    final_ref[...] = jnp.zeros_like(final_ref)
    place, previous = jnp.int32(0), jnp.int32(-1)
    for d in range(len(ends)):
        device = (ends[d] - 1) // rows
        place = jnp.where(device == previous, place + 1, 0)
        previous = device
        at_end = ends[d] == (device + 1) * rows
        enters = (place == 0).astype(F32)
        mine = device // MEMBERS * MEMBERS == base
        inner = mine & jnp.logical_not(at_end)
        e = device - base

        @pl.when(mine & at_end)
        def _():
            piece_ref[...] = last_ref[e, : hp * 128, :]

        for x, side_ref in enumerate(side_refs):

            @pl.when(inner & (place < SIDE) & ((e ^ (me % MEMBERS)) == x))
            def _():
                piece_ref[...] = side_ref[pl.ds(pl.multiple_of(place * hp * 128, 128), hp * 128), :]

        @pl.when(inner & (place >= SIDE))
        def _():
            row = pl.multiple_of((place - SIDE) * hp * 128, 128)
            pltpu.sync_copy(rest_ref.at[e, pl.ds(row, hp * 128), :], piece_ref)

        @pl.when(mine)
        def _():
            for i in range(hp):
                local = piece_ref[i * 128 : (i + 1) * 128, :].astype(F32)
                state = local + state_ref[e, i] * (decay_of(last_ref, e, i, hp) * enters)
                final_ref[own_ref[d], i] = state.astype(BF16)

    for x, out_ref in enumerate(out_refs):
        out_ref[...] = final_ref[me ^ x]


def final_states(doc_lengths, owner_ids, last, side, rest, coming, rows, spread):
    return pl.pallas_call(
        functools.partial(final_kernel, rows),
        in_specs=[SMEM, SMEM] + [VMEM] * (2 * MEMBERS) + [pl.BlockSpec(memory_space=pl.ANY), VMEM],
        out_specs=[VMEM] * spread,
        out_shape=[jax.ShapeDtypeStruct(coming.shape, BF16)] * spread,
        scratch_shapes=[
            pltpu.VMEM((MEMBERS,) + last[0].shape, BF16),
            pltpu.VMEM((MEMBERS,) + coming.shape, F32),
            pltpu.VMEM((coming.shape[0] * 128, 128), BF16),
            pltpu.VMEM((spread,) + coming.shape, BF16),
        ],
        compiler_params=SMALL,
        name="final_states",
    )(doc_lengths, owner_ids, *last, *side, rest, coming)


def pick_kernel(flag_ref, *refs):
    in_refs, out_ref = refs[:-1], refs[-1]
    me = lax.axis_index("seq")
    hp = in_refs[0].shape[0]
    for x, ref in enumerate(in_refs):
        source = me ^ x

        @pl.when(source // MEMBERS == flag_ref[0])
        def _():
            out_ref[0, pl.ds(source % MEMBERS * hp, hp)] = ref[...]


def pick_owned(flags, arrived, heads):
    return pl.pallas_call(
        pick_kernel,
        in_specs=[SMEM] + [VMEM] * len(arrived),
        out_specs=VMEM,
        out_shape=jax.ShapeDtypeStruct((1, heads, 128, 128), BF16),
        compiler_params=SMALL,
        name="pick_owned",
    )(flags, *arrived)


def finish_kernel(len_ref, q_ref, enter_ref, local_ref, gate_ref, gain_ref, crow_ref, out_ref, ccol_ref):
    rows = q_ref.shape[0]
    step = pl.program_id(0)
    first = lax.axis_index("seq") * rows

    @pl.when(step == 0)
    def _():
        fill_columns(crow_ref, ccol_ref)

    reach = run_end(read_ends(len_ref, len_ref.shape[0]), first - 1) - first
    cols = [head_column(ccol_ref, step * 2 + i) for i in range(2)]
    for t0 in range(0, rows, 256):
        span = slice(t0, t0 + 256)
        carry = [dot(q_ref[span, i * 128 : (i + 1) * 128], enter_ref[i]) for i in range(2)]
        inside = t0 + iota((256, 1), 0) < reach
        for i in range(2):
            lanes = slice(i * 128, (i + 1) * 128)
            lead = jnp.exp2(jnp.where(inside, cols[i][span], NEG))
            att = local_ref[span, lanes] + lead * carry[i]
            mean = jnp.mean(att * att, axis=1, keepdims=True)
            gate = 0.5 + 0.5 * jnp.tanh(0.5 * gate_ref[span, lanes].astype(F32))
            gain = gain_ref[:, lanes].astype(F32)
            out_ref[span, lanes] = (att * lax.rsqrt(mean + 1e-06) * (gain * gate)).astype(BF16)


def finish(doc_lengths, queries, entering, local, gate, gain, crow):
    heads, rows = crow.shape
    wide = pl.BlockSpec((rows, 256), lambda j: (0, j))
    return pl.pallas_call(
        finish_kernel,
        grid=(heads // 2,),
        in_specs=[
            SMEM,
            wide,
            pl.BlockSpec((2, 128, 128), lambda j: (j, 0, 0)),
            wide,
            wide,
            pl.BlockSpec((1, 256), lambda j: (0, j)),
            whole((heads, rows)),
        ],
        out_specs=wide,
        out_shape=jax.ShapeDtypeStruct((rows, heads * 128), BF16),
        scratch_shapes=[pltpu.VMEM((rows, 128), F32)],
        compiler_params=pltpu.CompilerParams(vmem_limit_bytes=54 * 2**20),
        cost_estimate=pl.CostEstimate(
            flops=heads * rows * 128 * 256, bytes_accessed=rows * heads * 128 * 10, transcendentals=heads * rows * 256
        ),
        name="finish",
    )(doc_lengths, queries, entering, local, gate, gain, crow)


def swap(x, groups=None):
    return lax.all_to_all(x, "seq", split_axis=0, concat_axis=0, axis_index_groups=groups, tiled=True)


def by_distance(parcels, spread):
    moved = {0: parcels[0]}
    for x in sorted(range(1, len(parcels)), key=lambda x: (x < MEMBERS, x)):
        moved[x] = lax.ppermute(parcels[x], "seq", [(s, s ^ x) for s in range(spread)])
    return [moved[x] for x in range(len(parcels))]


def on_device(spread, queries, keys, values, log_decay, gate, gain, doc_lengths, owner_ids):
    rows, heads = log_decay.shape
    quads = spread // MEMBERS
    hp = heads // MEMBERS
    near = [[q * MEMBERS + m for m in range(MEMBERS)] for q in range(quads)]
    onward = [(s, s + MEMBERS) for s in range(spread - MEMBERS)]
    decay_rows = log_decay.T
    barrier = lax.optimization_barrier

    crow, flags, *parcels = piece_states(doc_lengths, owner_ids, decay_rows, keys, values, SIDE)
    side, last = parcels[:MEMBERS], parcels[MEMBERS:]
    last = by_distance(last, spread)
    gain = gain.reshape(1, -1)
    crowded = flags[1] > 0
    slots = max(doc_lengths.shape[0] - 1, SIDE + 1)

    def send_rest():
        return swap(piece_states(doc_lengths, owner_ids, decay_rows, keys, values, slots)[0], near)

    none = jnp.zeros((MEMBERS, (slots - SIDE) * hp * 128, 128), BF16)
    rest = lax.cond(crowded, send_rest, lambda: none)
    last, side, gain, rest = barrier((last, side, gain, rest))

    side = by_distance(side, spread)
    coming = []
    for _ in range(quads - 1):
        leaving = leave_quad(doc_lengths, last, coming, rows, hp)
        coming = [lax.ppermute(leaving, "seq", onward)]
    crow_1, leaving = barrier((crow, leaving))
    local = local_attention(doc_lengths, queries, keys, values, crow_1)
    coming, local, side = barrier((coming[0], local, side))

    entering = swap(enter_states(doc_lengths, last, coming, rows), near).reshape(heads, 128, 128)
    finals = final_states(doc_lengths, owner_ids, last, side, rest, coming, rows, spread)
    arrived = by_distance(finals, spread)
    mixed = finish(doc_lengths, queries, entering, local, gate, gain, crow)
    return mixed, pick_owned(flags, arrived, heads)


def solution(mesh):
    placed = (
        P(("groups", "seq"), "tp"),
        P(("groups", "seq"), "tp"),
        P(("groups", "seq"), "tp"),
        P(("groups", "seq"), "tp"),
        P(("groups", "seq"), "tp"),
        P("tp"),
        P("groups"),
        P("groups"),
    )
    return jax.shard_map(
        functools.partial(on_device, mesh.shape["seq"]),
        mesh=mesh,
        in_specs=placed,
        out_specs=(P(("groups", "seq"), "tp"), P(("groups", "seq"), "tp", None, None)),
        check_vma=False,
    )
```

```python
import functools
import math

import jax
import jax.numpy as jnp
from jax import lax
from jax.experimental import pallas as pl
from jax.experimental.pallas import tpu as pltpu
from jax.sharding import PartitionSpec as P

BLK = 512
SIDE = 3
EXTRA = 16
CHUNK = 256
MEMBERS = 4
TILE = 256
NEG = -1e30
LOG2E = math.log2(math.e)
SCALE = 128**-0.5
F32, BF16 = jnp.float32, jnp.bfloat16
SMEM = pl.BlockSpec(memory_space=pltpu.SMEM)
VMEM = pl.BlockSpec(memory_space=pltpu.VMEM)
LIMIT = pltpu.CompilerParams(vmem_limit_bytes=60 * 2**20)
SMALL = pltpu.CompilerParams(vmem_limit_bytes=48 * 2**20)


def dot(a, b, contract=((1,), (0,))):
    return lax.dot_general(a, b, (contract, ((), ())), preferred_element_type=F32)


def iota(shape, dim):
    return lax.broadcasted_iota(jnp.int32, shape, dim)


def read_ends(len_ref, count):
    ends, total = [], jnp.int32(0)
    for d in range(count):
        total = total + len_ref[d]
        ends.append(total)
    return ends


def run_end(ends, pos):
    best = ends[-1]
    for e in reversed(ends[:-1]):
        best = jnp.where(e > pos, e, best)
    return best


def run_start(ends, pos):
    best = jnp.zeros_like(pos)
    for e in ends[:-1]:
        best = jnp.where(e <= pos, e, best)
    return best


def split3(x):
    hi = x.astype(BF16)
    rest = x - hi.astype(F32)
    mid = rest.astype(BF16)
    return hi, mid, (rest - mid.astype(F32)).astype(BF16)


def cum_rows(ld_ref, crow_ref):
    heads, rows = ld_ref.shape
    upper = (iota((BLK, BLK), 0) <= iota((BLK, BLK), 1)).astype(F32).astype(BF16)
    base = jnp.zeros((heads, 1), F32)
    for b in range(rows // BLK):
        part = ld_ref[:, b * BLK : (b + 1) * BLK] * LOG2E
        sums = dot(jnp.concatenate(split3(part), axis=0), upper)
        row = sums[2 * heads :] + sums[heads : 2 * heads] + sums[:heads] + base
        crow_ref[:, b * BLK : (b + 1) * BLK] = row
        base = row[:, BLK - 1 :]


def value_at(cum, at, index):
    return jnp.sum(jnp.where(at == index, cum, 0.0), axis=1, keepdims=True)


def span_weights(cum, at, low, high):
    inside = (at >= low) & (at <= high)
    return jnp.exp2(jnp.where(inside, value_at(cum, at, high) - cum, NEG) + math.log2(SCALE))


def weigh(flipped, w_ref, h):
    weights = [jnp.broadcast_to(w_ref[pl.ds(h + j, 1), :], (128, flipped.shape[1])) for j in range(2)]
    return (flipped.astype(F32) * jnp.concatenate(weights, axis=0)).astype(BF16)


def whole(shape):
    return pl.BlockSpec(shape, lambda j: (0,) * len(shape))


def pieces_kernel(rest, len_ref, own_ref, ld_ref, k_ref, v_ref, *refs):
    if rest:
        side_ref, crow_ref, w_ref, keep_ref = refs
        slots = keep_ref.shape[0]
    else:
        crow_ref, flag_ref = refs[:2]
        side_refs, last_refs = refs[2 : 2 + MEMBERS], refs[2 + MEMBERS : 2 + 2 * MEMBERS]
        w_ref, first_ref, high_ref, weighted_ref, prefix_ref, parcel_ref = refs[2 + 2 * MEMBERS :]
        slots = SIDE
    heads, rows = crow_ref.shape
    step = pl.program_id(0)
    hp = v_ref.shape[1] // 128
    me = lax.axis_index("seq")

    @pl.when(step == 0)
    def _():
        cum_rows(ld_ref, crow_ref)
        first = me * rows
        last = first + rows - 1
        ends = read_ends(len_ref, len_ref.shape[0])
        starts = [jnp.int32(0)] + ends[:-1]
        lows = [jnp.int32(0)] * slots
        highs = [jnp.int32(-1)] * slots
        place, rank, previous = jnp.int32(0), jnp.int32(0), jnp.int32(-1)
        crowded, owned_in = jnp.int32(0), jnp.int32(0)
        for d in range(len(ends)):
            here = (ends[d] > first) & (ends[d] <= last)
            low = jnp.maximum(starts[d] - first, 0)
            for s in range(slots):
                mine = here & (place == s + (SIDE if rest else 0))
                lows[s] = jnp.where(mine, low, lows[s])
                highs[s] = jnp.where(mine, ends[d] - 1 - first, highs[s])
            place = place + here.astype(jnp.int32)
            device = (ends[d] - 1) // rows
            rank = jnp.where(device == previous, rank + 1, 0)
            previous = device
            late = ((rank >= SIDE) & (ends[d] != (device + 1) * rows)).astype(jnp.int32) + (rank > SIDE).astype(jnp.int32)
            crowded = jnp.maximum(crowded, late)
            owned_in = jnp.where(own_ref[d] == me, device, owned_in)
        at = iota((heads, rows), 1)
        cum = crow_ref[...]
        total = jnp.zeros((heads, rows), F32)
        for s in range(slots):
            total = total + span_weights(cum, at, lows[s], highs[s])
        if rest:
            row_at = iota((16, rows), 1)
            for s in range(slots):
                inside = (row_at >= lows[s]) & (row_at <= highs[s])
                keep_ref[s] = jnp.where(inside, 1.0, 0.0).astype(BF16)
        else:
            total = total + span_weights(cum, at, jnp.maximum(run_start(ends, last) - first, 0), rows - 1)
            flag_ref[0] = owned_in // MEMBERS
            flag_ref[1] = crowded
            high = jnp.int32(-1)
            for s in range(slots):
                high = jnp.maximum(high, highs[s])
                high_ref[s] = high
            stop = jnp.minimum(run_end(ends, first) - 1 - first, rows - 1)
            goes_on = (run_start(ends, first) < first).astype(F32)
            first_ref[...] = jnp.broadcast_to(jnp.exp2(value_at(cum, at, stop)) * goes_on, (heads, 128))
        w_ref[...] = total

    def own(states, j):
        return states[j * 128 : (j + 1) * 128, j * 128 : (j + 1) * 128]

    if rest:
        for i in range(0, hp, 2):
            lanes = slice(i * 128, (i + 2) * 128)
            weighted = weigh(k_ref[:, lanes].T, w_ref, step * hp + i).reshape(16, 16, rows)
            for s in range(slots):
                states = dot((weighted * keep_ref[s][None]).reshape(256, rows), v_ref[:, lanes])
                for j in range(2):
                    at = (s * hp + i + j) * 128
                    side_ref[0, at : at + 128, :] = own(states, j).astype(BF16)
        return

    pairs = range(0, hp, 2)
    lanes = {i: slice(i * 128, (i + 2) * 128) for i in pairs}
    for i in pairs:
        weighted_ref[lanes[i], :] = weigh(k_ref[:, lanes[i]].T, w_ref, step * hp + i)
    totals = {}
    for i in pairs:
        sums = [jnp.zeros((128, 128), F32)] * 2
        for t in range(rows // TILE):
            span = slice(t * TILE, (t + 1) * TILE)
            states = dot(weighted_ref[lanes[i], span], v_ref[span, lanes[i]])
            for j in range(2):
                prefix_ref[t, i + j] = sums[j]
                sums[j] = sums[j] + own(states, j)
        totals[i] = sums
    ended = {i: [jnp.zeros((128, 128), F32)] * 2 for i in pairs}
    for s in range(slots):
        high = high_ref[s]
        tile = jnp.maximum(high, 0) // TILE
        start = pl.multiple_of(tile * TILE, TILE)
        keep = jnp.where(start + iota((16, TILE), 1) <= high, 1.0, 0.0).astype(BF16)
        for i in pairs:
            kept = weighted_ref[lanes[i], pl.ds(start, TILE)].reshape(16, 16, TILE) * keep[None]
            states = dot(kept.reshape(256, TILE), v_ref[pl.ds(start, TILE), lanes[i]])
            for j in range(2):
                until = own(states, j) + prefix_ref[tile, i + j]
                at = (s * hp + i + j) * 128
                parcel_ref[at : at + 128, :] = (until - ended[i][j]).astype(BF16)
                ended[i][j] = until
    rate = first_ref[pl.ds(step * hp, hp), :]
    high = rate.astype(BF16).astype(F32)
    pad = jnp.zeros((EXTRA - 2 * hp, 128), F32)
    tail = jnp.concatenate([high, rate - high, pad], axis=0).astype(BF16)
    cut = SIDE * hp * 128
    for i in pairs:
        for j in range(2):
            at = cut + (i + j) * 128
            parcel_ref[at : at + 128, :] = (totals[i][j] - ended[i][j]).astype(BF16)
    parcel_ref[cut + hp * 128 :, :] = tail
    for x in range(MEMBERS):

        @pl.when((step ^ (me % MEMBERS)) == x)
        def _():
            side_refs[x][...] = parcel_ref[:cut, :]
            last_refs[x][...] = parcel_ref[cut:, :]


def piece_states(doc_lengths, owner_ids, decay_rows, keys, values, slots):
    heads, rows = decay_rows.shape
    rest = slots > SIDE
    count = slots - SIDE if rest else slots
    hp = heads // MEMBERS
    wide = pl.BlockSpec((rows, hp * 128), lambda j: (0, j))
    side = (count * hp * 128, 128)
    shapes, specs = [jax.ShapeDtypeStruct((heads, rows), F32)], [whole((heads, rows))]
    scratch = [pltpu.VMEM((heads, rows), F32)]
    if rest:
        shapes.insert(0, jax.ShapeDtypeStruct((MEMBERS,) + side, BF16))
        specs.insert(0, pl.BlockSpec((1,) + side, lambda j: (j, 0, 0)))
        scratch.append(pltpu.VMEM((count, 16, rows), BF16))
    else:
        last = (hp * 128 + EXTRA, 128)
        shapes += [jax.ShapeDtypeStruct((2,), jnp.int32)]
        shapes += [jax.ShapeDtypeStruct(shape, BF16) for shape in (side, last) for _ in range(MEMBERS)]
        specs += [SMEM] + [whole(shape) for shape in (side, last) for _ in range(MEMBERS)]
        scratch += [
            pltpu.VMEM((heads, 128), F32),
            pltpu.SMEM((SIDE,), jnp.int32),
            pltpu.VMEM((hp * 128, rows), BF16),
            pltpu.VMEM((rows // TILE, hp, 128, 128), F32),
            pltpu.VMEM((side[0] + last[0], 128), BF16),
        ]
    return pl.pallas_call(
        functools.partial(pieces_kernel, rest),
        grid=(MEMBERS,),
        in_specs=[SMEM, SMEM, whole((heads, rows)), wide, wide],
        out_specs=specs,
        out_shape=shapes,
        scratch_shapes=scratch,
        compiler_params=LIMIT,
        cost_estimate=pl.CostEstimate(
            flops=2 * heads * rows * 128 * 256, bytes_accessed=rows * heads * 128 * 4, transcendentals=heads * rows
        ),
        name="piece_states",
    )(doc_lengths, owner_ids, decay_rows, keys, values)


def head_column(ccol_ref, h):
    cols = ccol_ref[...]
    return jnp.sum(jnp.where(iota(cols.shape, 1) == h, cols, 0.0), axis=1, keepdims=True)


def fill_columns(crow_ref, ccol_ref):
    heads, rows = crow_ref.shape
    for r0 in range(0, rows, 128):
        part = crow_ref[:, r0 : r0 + 128]
        part = jnp.concatenate([part, jnp.zeros((128 - heads, 128), F32)], axis=0)
        ccol_ref[r0 : r0 + 128, :] = part.T


def fill_bias(first, ends, bias_ref):
    for c in range(bias_ref.shape[0] // CHUNK):
        base = first + c * CHUNK
        t_pos = base + iota((CHUNK, 1), 0)
        start = run_start(ends, t_pos)
        s_pos = base + iota((CHUNK, CHUNK), 1)
        keep = (s_pos <= t_pos) & (s_pos >= start)
        bias_ref[c * CHUNK : (c + 1) * CHUNK, :] = jnp.where(keep, math.log2(SCALE), NEG)


def attend(first, ends, q_ref, k_ref, v_ref, h, crow_ref, ccol_ref, bias_ref, out_ref):
    rows = q_ref.shape[0]
    pair = range(2)
    half = CHUNK // 2
    lanes = [slice(i * 128, (i + 1) * 128) for i in pair]
    row_all = [crow_ref[pl.ds(h + i, 1), :] for i in pair]
    col_all = [head_column(ccol_ref, h + i) for i in pair]
    starts = range(0, rows, CHUNK)
    spans = [slice(r0, r0 + CHUNK) for r0 in starts]
    reach = [run_end(ends, first + r0 - 1) - (first + r0) for r0 in starts]
    base = [[row_all[i][:, r0 - 1 : r0] if r0 else None for r0 in starts] for i in pair]

    fresh = [[], []]
    for c, r0 in enumerate(starts[:-1]):
        since = run_start(ends, first + r0 + CHUNK - 1) - (first + r0)
        inside = iota((1, CHUNK), 1) >= since
        for i in pair:
            row = row_all[i][:, spans[c]]
            weight = jnp.exp2(jnp.where(inside, row[:, CHUNK - 1 :] - row, NEG) + math.log2(SCALE))
            flipped = k_ref[spans[c], lanes[i]].T
            fresh[i].append(dot((flipped.astype(F32) * weight).astype(BF16), v_ref[spans[c], lanes[i]]))
    carried = []
    for i in pair:
        state = fresh[i][0]
        chain = [None, state.astype(BF16)]
        for c in range(1, len(starts) - 1):
            total = row_all[i][:, starts[c] + CHUNK - 1 : starts[c] + CHUNK]
            state = fresh[i][c] + state * jnp.exp2(jnp.where(CHUNK <= reach[c], total - base[i][c], NEG))
            chain.append(state.astype(BF16))
        carried.append(chain)

    def products(c):
        result = []
        for i in pair:
            query = q_ref[spans[c], lanes[i]]
            scores = dot(query, k_ref[spans[c], lanes[i]], ((1,), (1,)))
            result.append((scores, dot(query, carried[i][c]) if c else None))
        return result

    ahead = products(0)
    for c, r0 in enumerate(starts):
        current = ahead
        if c + 1 < len(starts):
            ahead = products(c + 1)
        for part in range(2):
            t0, width = part * half, (part + 1) * half
            rows_here = slice(r0 + t0, r0 + t0 + half)
            for i in pair:
                scores, carry = current[i]
                col = col_all[i][rows_here]
                decay = jnp.exp2((col - row_all[i][:, r0 : r0 + width]) + bias_ref[rows_here, :width])
                weights = (scores[t0 : t0 + half, :width] * decay).astype(BF16)
                att = dot(weights, v_ref[r0 : r0 + width, lanes[i]])
                if c:
                    lead = jnp.exp2(jnp.where(t0 + iota((half, 1), 0) < reach[c], col - base[i][c], NEG))
                    att = att + lead * carry[t0 : t0 + half]
                out_ref[rows_here, lanes[i]] = att


def local_kernel(len_ref, q_ref, k_ref, v_ref, crow_ref, out_ref, bias_ref, ccol_ref):
    rows = q_ref.shape[0]
    step = pl.program_id(0)
    first = lax.axis_index("seq") * rows
    ends = read_ends(len_ref, len_ref.shape[0])

    @pl.when(step == 0)
    def _():
        fill_bias(first, ends, bias_ref)
        fill_columns(crow_ref, ccol_ref)

    attend(first, ends, q_ref, k_ref, v_ref, step * 2, crow_ref, ccol_ref, bias_ref, out_ref)


def local_attention(doc_lengths, queries, keys, values, crow):
    heads, rows = crow.shape
    wide = pl.BlockSpec((rows, 256), lambda j: (0, j))
    return pl.pallas_call(
        local_kernel,
        grid=(heads // 2,),
        in_specs=[SMEM, wide, wide, wide, whole((heads, rows))],
        out_specs=wide,
        out_shape=jax.ShapeDtypeStruct((rows, heads * 128), F32),
        scratch_shapes=[pltpu.VMEM((rows, CHUNK), F32), pltpu.VMEM((rows, 128), F32)],
        compiler_params=LIMIT,
        cost_estimate=pl.CostEstimate(
            flops=heads * rows * CHUNK * 128 * 8, bytes_accessed=rows * heads * 128 * 10, transcendentals=heads * rows * CHUNK
        ),
        name="local_attention",
    )(doc_lengths, queries, keys, values, crow)


def gather_last(refs, last_ref):
    me = lax.axis_index("seq") % MEMBERS
    for x, ref in enumerate(refs):
        last_ref[me ^ x] = ref[...]


def decay_of(last_ref, e, i, hp):
    extra = last_ref[e, hp * 128 :, :].astype(F32)
    return extra[i : i + 1, :] + extra[hp + i : hp + i + 1, :]


def scan_quad(rows, len_ref, last_ref, state, i, hp, note):
    members = last_ref.shape[0]
    ends = read_ends(len_ref, len_ref.shape[0])
    base = lax.axis_index("seq") // members * members
    for e in range(members):
        note(e, state)
        low = (base + e) * rows
        inner = jnp.int32(0)
        for end in ends:
            inner = inner + ((end > low) & (end < low + rows)).astype(jnp.int32)
        passes = (inner == 0).astype(F32)
        piece = last_ref[e, i * 128 : (i + 1) * 128, :].astype(F32)
        state = state * (decay_of(last_ref, e, i, hp) * passes) + piece
    return state


def leave_kernel(rows, len_ref, *refs):
    out_ref, last_ref = refs[-2:]
    gather_last(refs[:MEMBERS], last_ref)
    hp = out_ref.shape[0]
    for i in range(hp):
        state = jnp.zeros((128, 128), F32)
        if len(refs) > MEMBERS + 2:
            state = refs[MEMBERS][i].astype(F32)
        state = scan_quad(rows, len_ref, last_ref, state, i, hp, lambda e, x: None)
        out_ref[i] = state.astype(BF16)


def leave_quad(doc_lengths, last, coming, rows, hp):
    return pl.pallas_call(
        functools.partial(leave_kernel, rows),
        in_specs=[SMEM] + [VMEM] * (MEMBERS + len(coming)),
        out_specs=VMEM,
        out_shape=jax.ShapeDtypeStruct((hp, 128, 128), BF16),
        scratch_shapes=[pltpu.VMEM((MEMBERS,) + last[0].shape, BF16)],
        compiler_params=SMALL,
        name="leave_quad",
    )(doc_lengths, *last, *coming)


def enter_kernel(rows, len_ref, *refs):
    in_ref, out_refs, last_ref, state_ref = refs[MEMBERS], refs[MEMBERS + 1 : -2], refs[-2], refs[-1]
    gather_last(refs[:MEMBERS], last_ref)
    hp = in_ref.shape[0]

    def note(i, e, state):
        state_ref[e, i] = state

    for i in range(hp):
        scan_quad(rows, len_ref, last_ref, in_ref[i].astype(F32), i, hp, functools.partial(note, i))
    me = lax.axis_index("seq") % MEMBERS
    for x, out_ref in enumerate(out_refs):
        out_ref[...] = state_ref[me ^ x].astype(BF16)


def enter_states(doc_lengths, last, coming, rows):
    return pl.pallas_call(
        functools.partial(enter_kernel, rows),
        in_specs=[SMEM] + [VMEM] * (MEMBERS + 1),
        out_specs=[VMEM] * MEMBERS,
        out_shape=[jax.ShapeDtypeStruct(coming.shape, BF16)] * MEMBERS,
        scratch_shapes=[
            pltpu.VMEM((MEMBERS,) + last[0].shape, BF16),
            pltpu.VMEM((MEMBERS,) + coming.shape, F32),
        ],
        compiler_params=SMALL,
        name="enter_states",
    )(doc_lengths, *last, coming)


def final_kernel(rows, len_ref, own_ref, *refs):
    side_refs = refs[MEMBERS : 2 * MEMBERS]
    rest_ref, in_ref = refs[2 * MEMBERS : 2 * MEMBERS + 2]
    out_refs, (last_ref, state_ref, piece_ref, final_ref) = refs[2 * MEMBERS + 2 : -4], refs[-4:]
    gather_last(refs[:MEMBERS], last_ref)
    hp = in_ref.shape[0]
    ends = read_ends(len_ref, len_ref.shape[0])
    me = lax.axis_index("seq")
    base = me // MEMBERS * MEMBERS

    def note(i, e, state):
        state_ref[e, i] = state

    for i in range(hp):
        scan_quad(rows, len_ref, last_ref, in_ref[i].astype(F32), i, hp, functools.partial(note, i))
    final_ref[...] = jnp.zeros_like(final_ref)
    place, previous = jnp.int32(0), jnp.int32(-1)
    for d in range(len(ends)):
        device = (ends[d] - 1) // rows
        place = jnp.where(device == previous, place + 1, 0)
        previous = device
        at_end = ends[d] == (device + 1) * rows
        enters = (place == 0).astype(F32)
        mine = device // MEMBERS * MEMBERS == base
        inner = mine & jnp.logical_not(at_end)
        e = device - base

        @pl.when(mine & at_end)
        def _():
            piece_ref[...] = last_ref[e, : hp * 128, :]

        for x, side_ref in enumerate(side_refs):

            @pl.when(inner & (place < SIDE) & ((e ^ (me % MEMBERS)) == x))
            def _():
                piece_ref[...] = side_ref[pl.ds(pl.multiple_of(place * hp * 128, 128), hp * 128), :]

        @pl.when(inner & (place >= SIDE))
        def _():
            row = pl.multiple_of((place - SIDE) * hp * 128, 128)
            pltpu.sync_copy(rest_ref.at[e, pl.ds(row, hp * 128), :], piece_ref)

        @pl.when(mine)
        def _():
            for i in range(hp):
                local = piece_ref[i * 128 : (i + 1) * 128, :].astype(F32)
                state = local + state_ref[e, i] * (decay_of(last_ref, e, i, hp) * enters)
                final_ref[own_ref[d], i] = state.astype(BF16)

    for x, out_ref in enumerate(out_refs):
        out_ref[...] = final_ref[me ^ x]


def final_states(doc_lengths, owner_ids, last, side, rest, coming, rows, spread):
    return pl.pallas_call(
        functools.partial(final_kernel, rows),
        in_specs=[SMEM, SMEM] + [VMEM] * (2 * MEMBERS) + [pl.BlockSpec(memory_space=pl.ANY), VMEM],
        out_specs=[VMEM] * spread,
        out_shape=[jax.ShapeDtypeStruct(coming.shape, BF16)] * spread,
        scratch_shapes=[
            pltpu.VMEM((MEMBERS,) + last[0].shape, BF16),
            pltpu.VMEM((MEMBERS,) + coming.shape, F32),
            pltpu.VMEM((coming.shape[0] * 128, 128), BF16),
            pltpu.VMEM((spread,) + coming.shape, BF16),
        ],
        compiler_params=SMALL,
        name="final_states",
    )(doc_lengths, owner_ids, *last, *side, rest, coming)


def turns(spread):
    far, near = list(range(MEMBERS, spread)), list(range(1, MEMBERS))
    order = [0]
    while far:
        order += far[:1] + near[:1]
        far, near = far[1:], near[1:]
    return order + near


def pick_kernel(flag_ref, *refs):
    in_refs, out_ref = refs[:-1], refs[-1]
    me = lax.axis_index("seq")
    hp = in_refs[0].shape[0]
    for x, ref in zip(turns(len(in_refs)), in_refs):
        source = me ^ x

        @pl.when(source // MEMBERS == flag_ref[0])
        def _():
            out_ref[0, pl.ds(source % MEMBERS * hp, hp)] = ref[...]


def pick_owned(flags, arrived, heads):
    return pl.pallas_call(
        pick_kernel,
        in_specs=[SMEM] + [VMEM] * len(arrived),
        out_specs=VMEM,
        out_shape=jax.ShapeDtypeStruct((1, heads, 128, 128), BF16),
        compiler_params=SMALL,
        name="pick_owned",
    )(flags, *[arrived[x] for x in turns(len(arrived))])


def finish_kernel(len_ref, q_ref, e0, e1, e2, e3, local_ref, gate_ref, gain_ref, crow_ref, out_ref, ccol_ref):
    rows = q_ref.shape[0]
    step = pl.program_id(0)
    me = lax.axis_index("seq")
    hp = e0.shape[0]

    @pl.when(step == 0)
    def _():
        fill_columns(crow_ref, ccol_ref)

    def entering(h):
        far = (h // hp) ^ (me % MEMBERS)
        state = e0[h % hp]
        for x, ref in ((1, e1), (2, e2), (3, e3)):
            state = jnp.where(far == x, ref[h % hp], state)
        return state

    first = me * rows
    reach = run_end(read_ends(len_ref, len_ref.shape[0]), first - 1) - first
    cols = [head_column(ccol_ref, step * 2 + i) for i in range(2)]
    states = [entering(step * 2 + i) for i in range(2)]
    for t0 in range(0, rows, 256):
        span = slice(t0, t0 + 256)
        carry = [dot(q_ref[span, i * 128 : (i + 1) * 128], states[i]) for i in range(2)]
        inside = t0 + iota((256, 1), 0) < reach
        for i in range(2):
            lanes = slice(i * 128, (i + 1) * 128)
            lead = jnp.exp2(jnp.where(inside, cols[i][span], NEG))
            att = local_ref[span, lanes] + lead * carry[i]
            mean = jnp.mean(att * att, axis=1, keepdims=True)
            gate = 0.5 + 0.5 * jnp.tanh(0.5 * gate_ref[span, lanes].astype(F32))
            gain = gain_ref[:, lanes].astype(F32)
            out_ref[span, lanes] = (att * lax.rsqrt(mean + 1e-06) * (gain * gate)).astype(BF16)


def finish(doc_lengths, queries, entering, local, gate, gain, crow):
    heads, rows = crow.shape
    wide = pl.BlockSpec((rows, 256), lambda j: (0, j))
    return pl.pallas_call(
        finish_kernel,
        grid=(heads // 2,),
        in_specs=[SMEM, wide]
        + [whole(e.shape) for e in entering]
        + [wide, wide, pl.BlockSpec((1, 256), lambda j: (0, j)), whole((heads, rows))],
        out_specs=wide,
        out_shape=jax.ShapeDtypeStruct((rows, heads * 128), BF16),
        scratch_shapes=[pltpu.VMEM((rows, 128), F32)],
        compiler_params=pltpu.CompilerParams(vmem_limit_bytes=54 * 2**20),
        cost_estimate=pl.CostEstimate(
            flops=heads * rows * 128 * 256, bytes_accessed=rows * heads * 128 * 10, transcendentals=heads * rows * 256
        ),
        name="finish",
    )(doc_lengths, queries, *entering, local, gate, gain, crow)


def swap(x, groups=None):
    return lax.all_to_all(x, "seq", split_axis=0, concat_axis=0, axis_index_groups=groups, tiled=True)


def by_distance(parcels, spread):
    moved = {0: parcels[0]}
    for x in turns(len(parcels))[1:]:
        moved[x] = lax.ppermute(parcels[x], "seq", [(s, s ^ x) for s in range(spread)])
    return [moved[x] for x in range(len(parcels))]


def on_device(spread, queries, keys, values, log_decay, gate, gain, doc_lengths, owner_ids):
    rows, heads = log_decay.shape
    quads = spread // MEMBERS
    hp = heads // MEMBERS
    near = [[q * MEMBERS + m for m in range(MEMBERS)] for q in range(quads)]
    onward = [(s, s + MEMBERS) for s in range(spread - MEMBERS)]
    decay_rows = log_decay.T
    barrier = lax.optimization_barrier

    crow, flags, *parcels = piece_states(doc_lengths, owner_ids, decay_rows, keys, values, SIDE)
    side, last = parcels[:MEMBERS], parcels[MEMBERS:]
    last = by_distance(last, spread)
    gain = gain.reshape(1, -1)
    slots = max(doc_lengths.shape[0] - 1, SIDE + 1)

    def none(count):
        return jnp.zeros((MEMBERS, count * hp * 128, 128), BF16)

    def send_rest(count):
        sent = swap(piece_states(doc_lengths, owner_ids, decay_rows, keys, values, count)[0], near)
        return jnp.concatenate([sent, none(slots - count)], axis=1) if count < slots else sent

    branches = [lambda: none(slots - SIDE), lambda: send_rest(SIDE + 1), lambda: send_rest(slots)]
    rest = lax.switch(flags[1], branches)
    last, side, gain, rest = barrier((last, side, gain, rest))

    side = by_distance(side, spread)
    coming = []
    for _ in range(quads - 1):
        leaving = leave_quad(doc_lengths, last, coming, rows, hp)
        coming = [lax.ppermute(leaving, "seq", onward)]
    crow_1, leaving = barrier((crow, leaving))
    local = local_attention(doc_lengths, queries, keys, values, crow_1)
    coming, local, side = barrier((coming[0], local, side))

    entering = by_distance(enter_states(doc_lengths, last, coming, rows), spread)
    finals = final_states(doc_lengths, owner_ids, last, side, rest, coming, rows, spread)
    entering, finals = barrier((entering, finals))
    arrived = by_distance(finals, spread)
    mixed = finish(doc_lengths, queries, entering, local, gate, gain, crow)
    return mixed, pick_owned(flags, arrived, heads)


def solution(mesh):
    placed = (
        P(("groups", "seq"), "tp"),
        P(("groups", "seq"), "tp"),
        P(("groups", "seq"), "tp"),
        P(("groups", "seq"), "tp"),
        P(("groups", "seq"), "tp"),
        P("tp"),
        P("groups"),
        P("groups"),
    )
    return jax.shard_map(
        functools.partial(on_device, mesh.shape["seq"]),
        mesh=mesh,
        in_specs=placed,
        out_specs=(P(("groups", "seq"), "tp"), P(("groups", "seq"), "tp", None, None)),
        check_vma=False,
    )
```

```python
import functools
import math

import jax
import jax.numpy as jnp
from jax import lax
from jax.experimental import pallas as pl
from jax.experimental.pallas import tpu as pltpu
from jax.sharding import PartitionSpec as P

BLK = 512
SIDE = 3
EXTRA = 16
CHUNK = 256
MEMBERS = 4
TILE = 256
NEG = -1e30
LOG2E = math.log2(math.e)
SCALE = 128**-0.5
F32, BF16 = jnp.float32, jnp.bfloat16
SMEM = pl.BlockSpec(memory_space=pltpu.SMEM)
VMEM = pl.BlockSpec(memory_space=pltpu.VMEM)
LIMIT = pltpu.CompilerParams(vmem_limit_bytes=60 * 2**20)
SMALL = pltpu.CompilerParams(vmem_limit_bytes=48 * 2**20)


def dot(a, b, contract=((1,), (0,))):
    return lax.dot_general(a, b, (contract, ((), ())), preferred_element_type=F32)


def iota(shape, dim):
    return lax.broadcasted_iota(jnp.int32, shape, dim)


def read_ends(len_ref, count):
    ends, total = [], jnp.int32(0)
    for d in range(count):
        total = total + len_ref[d]
        ends.append(total)
    return ends


def run_end(ends, pos):
    best = ends[-1]
    for e in reversed(ends[:-1]):
        best = jnp.where(e > pos, e, best)
    return best


def run_start(ends, pos):
    best = jnp.zeros_like(pos)
    for e in ends[:-1]:
        best = jnp.where(e <= pos, e, best)
    return best


def split3(x):
    hi = x.astype(BF16)
    rest = x - hi.astype(F32)
    mid = rest.astype(BF16)
    return hi, mid, (rest - mid.astype(F32)).astype(BF16)


def cum_rows(ld_ref, crow_ref):
    heads, rows = ld_ref.shape
    upper = (iota((TILE, TILE), 0) <= iota((TILE, TILE), 1)).astype(F32).astype(BF16)
    spans = [slice(r0, r0 + TILE) for r0 in range(0, rows, TILE)]
    parts = [part for span in spans for part in split3(ld_ref[:, span] * LOG2E)]
    sums = dot(jnp.concatenate(parts, axis=0), upper)
    base = jnp.zeros((heads, 1), F32)
    for t, span in enumerate(spans):
        high, mid, low = [sums[(3 * t + j) * heads : (3 * t + j + 1) * heads] for j in range(3)]
        row = low + mid + high + base
        crow_ref[:, span] = row
        base = row[:, TILE - 1 :]


def value_at(cum, at, index):
    return jnp.sum(jnp.where(at == index, cum, 0.0), axis=1, keepdims=True)


def span_weights(cum, at, low, high):
    inside = (at >= low) & (at <= high)
    return jnp.exp2(jnp.where(inside, value_at(cum, at, high) - cum, NEG) + math.log2(SCALE))


def weigh(flipped, w_ref, h):
    weights = [jnp.broadcast_to(w_ref[pl.ds(h + j, 1), :], (128, flipped.shape[1])) for j in range(2)]
    return (flipped.astype(F32) * jnp.concatenate(weights, axis=0)).astype(BF16)


def whole(shape):
    return pl.BlockSpec(shape, lambda j: (0,) * len(shape))


def pieces_kernel(rest, len_ref, own_ref, ld_ref, k_ref, v_ref, *refs):
    if rest:
        side_ref, crow_ref, w_ref, keep_ref = refs
        slots = keep_ref.shape[0]
    else:
        crow_ref, flag_ref = refs[:2]
        side_refs, last_refs = refs[2 : 2 + MEMBERS], refs[2 + MEMBERS : 2 + 2 * MEMBERS]
        w_ref, first_ref, high_ref, weighted_ref, prefix_ref, parcel_ref = refs[2 + 2 * MEMBERS :]
        slots = SIDE
    heads, rows = crow_ref.shape
    step = pl.program_id(0)
    hp = v_ref.shape[1] // 128
    me = lax.axis_index("seq")

    @pl.when(step == 0)
    def _():
        cum_rows(ld_ref, crow_ref)
        first = me * rows
        last = first + rows - 1
        ends = read_ends(len_ref, len_ref.shape[0])
        starts = [jnp.int32(0)] + ends[:-1]
        lows = [jnp.int32(0)] * slots
        highs = [jnp.int32(-1)] * slots
        place, rank, previous = jnp.int32(0), jnp.int32(0), jnp.int32(-1)
        crowded, owned_in = jnp.int32(0), jnp.int32(0)
        for d in range(len(ends)):
            here = (ends[d] > first) & (ends[d] <= last)
            low = jnp.maximum(starts[d] - first, 0)
            for s in range(slots):
                mine = here & (place == s + (SIDE if rest else 0))
                lows[s] = jnp.where(mine, low, lows[s])
                highs[s] = jnp.where(mine, ends[d] - 1 - first, highs[s])
            place = place + here.astype(jnp.int32)
            device = (ends[d] - 1) // rows
            rank = jnp.where(device == previous, rank + 1, 0)
            previous = device
            late = ((rank >= SIDE) & (ends[d] != (device + 1) * rows)).astype(jnp.int32) + (rank > SIDE).astype(jnp.int32)
            crowded = jnp.maximum(crowded, late)
            owned_in = jnp.where(own_ref[d] == me, device, owned_in)
        at = iota((heads, rows), 1)
        cum = crow_ref[...]
        total = jnp.zeros((heads, rows), F32)
        for s in range(slots):
            total = total + span_weights(cum, at, lows[s], highs[s])
        if rest:
            row_at = iota((16, rows), 1)
            for s in range(slots):
                inside = (row_at >= lows[s]) & (row_at <= highs[s])
                keep_ref[s] = jnp.where(inside, 1.0, 0.0).astype(BF16)
        else:
            total = total + span_weights(cum, at, jnp.maximum(run_start(ends, last) - first, 0), rows - 1)
            flag_ref[0] = owned_in // MEMBERS
            flag_ref[1] = crowded
            high = jnp.int32(-1)
            for s in range(slots):
                high = jnp.maximum(high, highs[s])
                high_ref[s] = high
            stop = jnp.minimum(run_end(ends, first) - 1 - first, rows - 1)
            goes_on = (run_start(ends, first) < first).astype(F32)
            first_ref[...] = jnp.broadcast_to(jnp.exp2(value_at(cum, at, stop)) * goes_on, (heads, 128))
        w_ref[...] = total

    def own(states, j):
        return states[j * 128 : (j + 1) * 128, j * 128 : (j + 1) * 128]

    if rest:
        for i in range(0, hp, 2):
            lanes = slice(i * 128, (i + 2) * 128)
            weighted = weigh(k_ref[:, lanes].T, w_ref, step * hp + i).reshape(16, 16, rows)
            for s in range(slots):
                states = dot((weighted * keep_ref[s][None]).reshape(256, rows), v_ref[:, lanes])
                for j in range(2):
                    at = (s * hp + i + j) * 128
                    side_ref[0, at : at + 128, :] = own(states, j).astype(BF16)
        return

    pairs = range(0, hp, 2)
    lanes = {i: slice(i * 128, (i + 2) * 128) for i in pairs}
    for i in pairs:
        weighted_ref[lanes[i], :] = weigh(k_ref[:, lanes[i]].T, w_ref, step * hp + i)
    totals = {}
    for i in pairs:
        sums = [jnp.zeros((128, 128), F32)] * 2
        for t in range(rows // TILE):
            span = slice(t * TILE, (t + 1) * TILE)
            states = dot(weighted_ref[lanes[i], span], v_ref[span, lanes[i]])
            for j in range(2):
                prefix_ref[t, i + j] = sums[j]
                sums[j] = sums[j] + own(states, j)
        totals[i] = sums
    ended = {i: [jnp.zeros((128, 128), F32)] * 2 for i in pairs}
    for s in range(slots):
        high = high_ref[s]
        tile = jnp.maximum(high, 0) // TILE
        start = pl.multiple_of(tile * TILE, TILE)
        keep = jnp.where(start + iota((16, TILE), 1) <= high, 1.0, 0.0).astype(BF16)
        for i in pairs:
            kept = weighted_ref[lanes[i], pl.ds(start, TILE)].reshape(16, 16, TILE) * keep[None]
            states = dot(kept.reshape(256, TILE), v_ref[pl.ds(start, TILE), lanes[i]])
            for j in range(2):
                until = own(states, j) + prefix_ref[tile, i + j]
                at = (s * hp + i + j) * 128
                parcel_ref[at : at + 128, :] = (until - ended[i][j]).astype(BF16)
                ended[i][j] = until
    rate = first_ref[pl.ds(step * hp, hp), :]
    high = rate.astype(BF16).astype(F32)
    pad = jnp.zeros((EXTRA - 2 * hp, 128), F32)
    tail = jnp.concatenate([high, rate - high, pad], axis=0).astype(BF16)
    cut = SIDE * hp * 128
    for i in pairs:
        for j in range(2):
            at = cut + (i + j) * 128
            parcel_ref[at : at + 128, :] = (totals[i][j] - ended[i][j]).astype(BF16)
    parcel_ref[cut + hp * 128 :, :] = tail
    for x in range(MEMBERS):

        @pl.when((step ^ (me % MEMBERS)) == x)
        def _():
            side_refs[x][...] = parcel_ref[:cut, :]
            last_refs[x][...] = parcel_ref[cut:, :]


def piece_states(doc_lengths, owner_ids, decay_rows, keys, values, slots):
    heads, rows = decay_rows.shape
    rest = slots > SIDE
    count = slots - SIDE if rest else slots
    hp = heads // MEMBERS
    wide = pl.BlockSpec((rows, hp * 128), lambda j: (0, j))
    side = (count * hp * 128, 128)
    shapes, specs = [jax.ShapeDtypeStruct((heads, rows), F32)], [whole((heads, rows))]
    scratch = [pltpu.VMEM((heads, rows), F32)]
    if rest:
        shapes.insert(0, jax.ShapeDtypeStruct((MEMBERS,) + side, BF16))
        specs.insert(0, pl.BlockSpec((1,) + side, lambda j: (j, 0, 0)))
        scratch.append(pltpu.VMEM((count, 16, rows), BF16))
    else:
        last = (hp * 128 + EXTRA, 128)
        shapes += [jax.ShapeDtypeStruct((2,), jnp.int32)]
        shapes += [jax.ShapeDtypeStruct(shape, BF16) for shape in (side, last) for _ in range(MEMBERS)]
        specs += [SMEM] + [whole(shape) for shape in (side, last) for _ in range(MEMBERS)]
        scratch += [
            pltpu.VMEM((heads, 128), F32),
            pltpu.SMEM((SIDE,), jnp.int32),
            pltpu.VMEM((hp * 128, rows), BF16),
            pltpu.VMEM((rows // TILE, hp, 128, 128), F32),
            pltpu.VMEM((side[0] + last[0], 128), BF16),
        ]
    return pl.pallas_call(
        functools.partial(pieces_kernel, rest),
        grid=(MEMBERS,),
        in_specs=[SMEM, SMEM, whole((heads, rows)), wide, wide],
        out_specs=specs,
        out_shape=shapes,
        scratch_shapes=scratch,
        compiler_params=LIMIT,
        cost_estimate=pl.CostEstimate(
            flops=2 * heads * rows * 128 * 256, bytes_accessed=rows * heads * 128 * 4, transcendentals=heads * rows
        ),
        name="piece_states",
    )(doc_lengths, owner_ids, decay_rows, keys, values)


def head_column(ccol_ref, h):
    cols = ccol_ref[...]
    return jnp.sum(jnp.where(iota(cols.shape, 1) == h, cols, 0.0), axis=1, keepdims=True)


def fill_columns(crow_ref, ccol_ref):
    heads, rows = crow_ref.shape
    for r0 in range(0, rows, 128):
        part = crow_ref[:, r0 : r0 + 128]
        part = jnp.concatenate([part, jnp.zeros((128 - heads, 128), F32)], axis=0)
        ccol_ref[r0 : r0 + 128, :] = part.T


def fill_bias(first, ends, bias_ref):
    for c in range(bias_ref.shape[0] // CHUNK):
        base = first + c * CHUNK
        t_pos = base + iota((CHUNK, 1), 0)
        start = run_start(ends, t_pos)
        s_pos = base + iota((CHUNK, CHUNK), 1)
        keep = (s_pos <= t_pos) & (s_pos >= start)
        bias_ref[c * CHUNK : (c + 1) * CHUNK, :] = jnp.where(keep, math.log2(SCALE), NEG)


def attend(first, ends, q_ref, k_ref, v_ref, h, crow_ref, ccol_ref, bias_ref, out_ref):
    rows = q_ref.shape[0]
    pair = range(2)
    half = CHUNK // 2
    lanes = [slice(i * 128, (i + 1) * 128) for i in pair]
    row_all = [crow_ref[pl.ds(h + i, 1), :] for i in pair]
    col_all = [head_column(ccol_ref, h + i) for i in pair]
    starts = range(0, rows, CHUNK)
    spans = [slice(r0, r0 + CHUNK) for r0 in starts]
    reach = [run_end(ends, first + r0 - 1) - (first + r0) for r0 in starts]
    base = [[row_all[i][:, r0 - 1 : r0] if r0 else None for r0 in starts] for i in pair]

    fresh = [[], []]
    for c, r0 in enumerate(starts[:-1]):
        since = run_start(ends, first + r0 + CHUNK - 1) - (first + r0)
        inside = iota((1, CHUNK), 1) >= since
        for i in pair:
            row = row_all[i][:, spans[c]]
            weight = jnp.exp2(jnp.where(inside, row[:, CHUNK - 1 :] - row, NEG) + math.log2(SCALE))
            flipped = k_ref[spans[c], lanes[i]].T
            fresh[i].append(dot((flipped.astype(F32) * weight).astype(BF16), v_ref[spans[c], lanes[i]]))
    carried = []
    for i in pair:
        state = fresh[i][0]
        chain = [None, state.astype(BF16)]
        for c in range(1, len(starts) - 1):
            total = row_all[i][:, starts[c] + CHUNK - 1 : starts[c] + CHUNK]
            state = fresh[i][c] + state * jnp.exp2(jnp.where(CHUNK <= reach[c], total - base[i][c], NEG))
            chain.append(state.astype(BF16))
        carried.append(chain)

    def products(c):
        result = []
        for i in pair:
            query = q_ref[spans[c], lanes[i]]
            scores = dot(query, k_ref[spans[c], lanes[i]], ((1,), (1,)))
            result.append((scores, dot(query, carried[i][c]) if c else None))
        return result

    ahead = products(0)
    for c, r0 in enumerate(starts):
        current = ahead
        if c + 1 < len(starts):
            ahead = products(c + 1)
        for part in range(2):
            t0, width = part * half, (part + 1) * half
            rows_here = slice(r0 + t0, r0 + t0 + half)
            for i in pair:
                scores, carry = current[i]
                col = col_all[i][rows_here]
                decay = jnp.exp2((col - row_all[i][:, r0 : r0 + width]) + bias_ref[rows_here, :width])
                weights = (scores[t0 : t0 + half, :width] * decay).astype(BF16)
                att = dot(weights, v_ref[r0 : r0 + width, lanes[i]])
                if c:
                    lead = jnp.exp2(jnp.where(t0 + iota((half, 1), 0) < reach[c], col - base[i][c], NEG))
                    att = att + lead * carry[t0 : t0 + half]
                out_ref[rows_here, lanes[i]] = att


def local_kernel(len_ref, q_ref, k_ref, v_ref, crow_ref, out_ref, bias_ref, ccol_ref):
    rows = q_ref.shape[0]
    step = pl.program_id(0)
    first = lax.axis_index("seq") * rows
    ends = read_ends(len_ref, len_ref.shape[0])

    @pl.when(step == 0)
    def _():
        fill_bias(first, ends, bias_ref)
        fill_columns(crow_ref, ccol_ref)

    attend(first, ends, q_ref, k_ref, v_ref, step * 2, crow_ref, ccol_ref, bias_ref, out_ref)


def local_attention(doc_lengths, queries, keys, values, crow):
    heads, rows = crow.shape
    wide = pl.BlockSpec((rows, 256), lambda j: (0, j))
    return pl.pallas_call(
        local_kernel,
        grid=(heads // 2,),
        in_specs=[SMEM, wide, wide, wide, whole((heads, rows))],
        out_specs=wide,
        out_shape=jax.ShapeDtypeStruct((rows, heads * 128), F32),
        scratch_shapes=[pltpu.VMEM((rows, CHUNK), F32), pltpu.VMEM((rows, 128), F32)],
        compiler_params=LIMIT,
        cost_estimate=pl.CostEstimate(
            flops=heads * rows * CHUNK * 128 * 8, bytes_accessed=rows * heads * 128 * 10, transcendentals=heads * rows * CHUNK
        ),
        name="local_attention",
    )(doc_lengths, queries, keys, values, crow)


def gather_last(refs, last_ref):
    me = lax.axis_index("seq") % MEMBERS
    for x, ref in enumerate(refs):
        last_ref[me ^ x] = ref[...]


def decay_of(last_ref, e, i, hp):
    extra = last_ref[e, hp * 128 :, :].astype(F32)
    return extra[i : i + 1, :] + extra[hp + i : hp + i + 1, :]


def scan_quad(rows, len_ref, last_ref, state, i, hp, note):
    members = last_ref.shape[0]
    ends = read_ends(len_ref, len_ref.shape[0])
    base = lax.axis_index("seq") // members * members
    for e in range(members):
        note(e, state)
        low = (base + e) * rows
        inner = jnp.int32(0)
        for end in ends:
            inner = inner + ((end > low) & (end < low + rows)).astype(jnp.int32)
        passes = (inner == 0).astype(F32)
        piece = last_ref[e, i * 128 : (i + 1) * 128, :].astype(F32)
        state = state * (decay_of(last_ref, e, i, hp) * passes) + piece
    return state


def leave_kernel(rows, len_ref, *refs):
    out_ref, last_ref = refs[-2:]
    gather_last(refs[:MEMBERS], last_ref)
    hp = out_ref.shape[0]
    for i in range(hp):
        state = jnp.zeros((128, 128), F32)
        if len(refs) > MEMBERS + 2:
            state = refs[MEMBERS][i].astype(F32)
        state = scan_quad(rows, len_ref, last_ref, state, i, hp, lambda e, x: None)
        out_ref[i] = state.astype(BF16)


def leave_quad(doc_lengths, last, coming, rows, hp):
    return pl.pallas_call(
        functools.partial(leave_kernel, rows),
        in_specs=[SMEM] + [VMEM] * (MEMBERS + len(coming)),
        out_specs=VMEM,
        out_shape=jax.ShapeDtypeStruct((hp, 128, 128), BF16),
        scratch_shapes=[pltpu.VMEM((MEMBERS,) + last[0].shape, BF16)],
        compiler_params=SMALL,
        name="leave_quad",
    )(doc_lengths, *last, *coming)


def enter_kernel(rows, len_ref, *refs):
    in_ref, out_refs, last_ref, state_ref = refs[MEMBERS], refs[MEMBERS + 1 : -2], refs[-2], refs[-1]
    gather_last(refs[:MEMBERS], last_ref)
    hp = in_ref.shape[0]

    def note(i, e, state):
        state_ref[e, i] = state

    for i in range(hp):
        scan_quad(rows, len_ref, last_ref, in_ref[i].astype(F32), i, hp, functools.partial(note, i))
    me = lax.axis_index("seq") % MEMBERS
    for x, out_ref in enumerate(out_refs):
        out_ref[...] = state_ref[me ^ x].astype(BF16)


def enter_states(doc_lengths, last, coming, rows):
    return pl.pallas_call(
        functools.partial(enter_kernel, rows),
        in_specs=[SMEM] + [VMEM] * (MEMBERS + 1),
        out_specs=[VMEM] * MEMBERS,
        out_shape=[jax.ShapeDtypeStruct(coming.shape, BF16)] * MEMBERS,
        scratch_shapes=[
            pltpu.VMEM((MEMBERS,) + last[0].shape, BF16),
            pltpu.VMEM((MEMBERS,) + coming.shape, F32),
        ],
        compiler_params=SMALL,
        name="enter_states",
    )(doc_lengths, *last, coming)


def final_kernel(rows, len_ref, own_ref, *refs):
    side_refs = refs[MEMBERS : 2 * MEMBERS]
    rest_ref, in_ref = refs[2 * MEMBERS : 2 * MEMBERS + 2]
    out_refs, (last_ref, state_ref, piece_ref, final_ref) = refs[2 * MEMBERS + 2 : -4], refs[-4:]
    gather_last(refs[:MEMBERS], last_ref)
    hp = in_ref.shape[0]
    ends = read_ends(len_ref, len_ref.shape[0])
    me = lax.axis_index("seq")
    base = me // MEMBERS * MEMBERS

    def note(i, e, state):
        state_ref[e, i] = state

    for i in range(hp):
        scan_quad(rows, len_ref, last_ref, in_ref[i].astype(F32), i, hp, functools.partial(note, i))
    final_ref[...] = jnp.zeros_like(final_ref)
    place, previous = jnp.int32(0), jnp.int32(-1)
    for d in range(len(ends)):
        device = (ends[d] - 1) // rows
        place = jnp.where(device == previous, place + 1, 0)
        previous = device
        at_end = ends[d] == (device + 1) * rows
        enters = (place == 0).astype(F32)
        mine = device // MEMBERS * MEMBERS == base
        inner = mine & jnp.logical_not(at_end)
        e = device - base

        @pl.when(mine & at_end)
        def _():
            piece_ref[...] = last_ref[e, : hp * 128, :]

        for x, side_ref in enumerate(side_refs):

            @pl.when(inner & (place < SIDE) & ((e ^ (me % MEMBERS)) == x))
            def _():
                piece_ref[...] = side_ref[pl.ds(pl.multiple_of(place * hp * 128, 128), hp * 128), :]

        @pl.when(inner & (place >= SIDE))
        def _():
            row = pl.multiple_of((place - SIDE) * hp * 128, 128)
            pltpu.sync_copy(rest_ref.at[e, pl.ds(row, hp * 128), :], piece_ref)

        @pl.when(mine)
        def _():
            for i in range(hp):
                local = piece_ref[i * 128 : (i + 1) * 128, :].astype(F32)
                state = local + state_ref[e, i] * (decay_of(last_ref, e, i, hp) * enters)
                final_ref[own_ref[d], i] = state.astype(BF16)

    for x, out_ref in enumerate(out_refs):
        out_ref[...] = final_ref[me ^ x]


def final_states(doc_lengths, owner_ids, last, side, rest, coming, rows, spread):
    return pl.pallas_call(
        functools.partial(final_kernel, rows),
        in_specs=[SMEM, SMEM] + [VMEM] * (2 * MEMBERS) + [pl.BlockSpec(memory_space=pl.ANY), VMEM],
        out_specs=[VMEM] * spread,
        out_shape=[jax.ShapeDtypeStruct(coming.shape, BF16)] * spread,
        scratch_shapes=[
            pltpu.VMEM((MEMBERS,) + last[0].shape, BF16),
            pltpu.VMEM((MEMBERS,) + coming.shape, F32),
            pltpu.VMEM((coming.shape[0] * 128, 128), BF16),
            pltpu.VMEM((spread,) + coming.shape, BF16),
        ],
        compiler_params=SMALL,
        name="final_states",
    )(doc_lengths, owner_ids, *last, *side, rest, coming)


def turns(spread):
    far, near = list(range(MEMBERS, spread)), list(range(1, MEMBERS))
    order = [0] + near[:1]
    near = near[1:]
    while far:
        order += far[:2] + near[:1]
        far, near = far[2:], near[1:]
    return order + near


def pick_kernel(flag_ref, *refs):
    in_refs, out_ref = refs[:-1], refs[-1]
    me = lax.axis_index("seq")
    hp = in_refs[0].shape[0]
    for x, ref in zip(turns(len(in_refs)), in_refs):
        source = me ^ x

        @pl.when(source // MEMBERS == flag_ref[0])
        def _():
            out_ref[0, pl.ds(source % MEMBERS * hp, hp)] = ref[...]


def pick_owned(flags, arrived, heads):
    return pl.pallas_call(
        pick_kernel,
        in_specs=[SMEM] + [VMEM] * len(arrived),
        out_specs=VMEM,
        out_shape=jax.ShapeDtypeStruct((1, heads, 128, 128), BF16),
        compiler_params=SMALL,
        name="pick_owned",
    )(flags, *[arrived[x] for x in turns(len(arrived))])


def finish_kernel(len_ref, q_ref, e0, e1, e2, e3, local_ref, gate_ref, gain_ref, crow_ref, out_ref, ccol_ref):
    rows = q_ref.shape[0]
    step = pl.program_id(0)
    me = lax.axis_index("seq")
    hp = e0.shape[0]

    @pl.when(step == 0)
    def _():
        fill_columns(crow_ref, ccol_ref)

    def entering(h):
        far = (h // hp) ^ (me % MEMBERS)
        state = e0[h % hp]
        for x, ref in ((1, e1), (2, e2), (3, e3)):
            state = jnp.where(far == x, ref[h % hp], state)
        return state

    first = me * rows
    reach = run_end(read_ends(len_ref, len_ref.shape[0]), first - 1) - first
    cols = [head_column(ccol_ref, step * 2 + i) for i in range(2)]
    states = [entering(step * 2 + i) for i in range(2)]
    spans = [slice(t0, t0 + 256) for t0 in range(0, rows, 256)]
    carries = [[dot(q_ref[span, i * 128 : (i + 1) * 128], states[i]) for i in range(2)] for span in spans]
    for span, carry in zip(spans, carries):
        inside = span.start + iota((256, 1), 0) < reach
        for i in range(2):
            lanes = slice(i * 128, (i + 1) * 128)
            lead = jnp.exp2(jnp.where(inside, cols[i][span], NEG))
            att = local_ref[span, lanes] + lead * carry[i]
            mean = jnp.mean(att * att, axis=1, keepdims=True)
            gate = 0.5 + 0.5 * jnp.tanh(0.5 * gate_ref[span, lanes].astype(F32))
            gain = gain_ref[:, lanes].astype(F32)
            out_ref[span, lanes] = (att * lax.rsqrt(mean + 1e-06) * (gain * gate)).astype(BF16)


def finish(doc_lengths, queries, entering, local, gate, gain, crow):
    heads, rows = crow.shape
    wide = pl.BlockSpec((rows, 256), lambda j: (0, j))
    return pl.pallas_call(
        finish_kernel,
        grid=(heads // 2,),
        in_specs=[SMEM, wide]
        + [whole(e.shape) for e in entering]
        + [wide, wide, pl.BlockSpec((1, 256), lambda j: (0, j)), whole((heads, rows))],
        out_specs=wide,
        out_shape=jax.ShapeDtypeStruct((rows, heads * 128), BF16),
        scratch_shapes=[pltpu.VMEM((rows, 128), F32)],
        compiler_params=pltpu.CompilerParams(vmem_limit_bytes=54 * 2**20),
        cost_estimate=pl.CostEstimate(
            flops=heads * rows * 128 * 256, bytes_accessed=rows * heads * 128 * 10, transcendentals=heads * rows * 256
        ),
        name="finish",
    )(doc_lengths, queries, *entering, local, gate, gain, crow)


def swap(x, groups=None):
    return lax.all_to_all(x, "seq", split_axis=0, concat_axis=0, axis_index_groups=groups, tiled=True)


def by_distance(parcels, spread):
    moved = {0: parcels[0]}
    for x in turns(len(parcels))[1:]:
        moved[x] = lax.ppermute(parcels[x], "seq", [(s, s ^ x) for s in range(spread)])
    return [moved[x] for x in range(len(parcels))]


def on_device(spread, queries, keys, values, log_decay, gate, gain, doc_lengths, owner_ids):
    rows, heads = log_decay.shape
    quads = spread // MEMBERS
    hp = heads // MEMBERS
    near = [[q * MEMBERS + m for m in range(MEMBERS)] for q in range(quads)]
    onward = [(s, s + MEMBERS) for s in range(spread - MEMBERS)]
    decay_rows = log_decay.T
    barrier = lax.optimization_barrier

    crow, flags, *parcels = piece_states(doc_lengths, owner_ids, decay_rows, keys, values, SIDE)
    side, last = parcels[:MEMBERS], parcels[MEMBERS:]
    last = by_distance(last, spread)
    gain = gain.reshape(1, -1)
    slots = max(doc_lengths.shape[0] - 1, SIDE + 1)

    def none(count):
        return jnp.zeros((MEMBERS, count * hp * 128, 128), BF16)

    def send_rest(count):
        sent = swap(piece_states(doc_lengths, owner_ids, decay_rows, keys, values, count)[0], near)
        return jnp.concatenate([sent, none(slots - count)], axis=1) if count < slots else sent

    branches = [lambda: none(slots - SIDE), lambda: send_rest(SIDE + 1), lambda: send_rest(slots)]
    rest = lax.switch(flags[1], branches)
    last, side, gain, rest = barrier((last, side, gain, rest))

    side = by_distance(side, spread)
    coming = []
    for _ in range(quads - 1):
        leaving = leave_quad(doc_lengths, last, coming, rows, hp)
        coming = [lax.ppermute(leaving, "seq", onward)]
    crow_1, leaving = barrier((crow, leaving))
    local = local_attention(doc_lengths, queries, keys, values, crow_1)
    coming, local, side = barrier((coming[0], local, side))

    entering = by_distance(enter_states(doc_lengths, last, coming, rows), spread)
    finals = final_states(doc_lengths, owner_ids, last, side, rest, coming, rows, spread)
    entering, finals = barrier((entering, finals))
    arrived = by_distance(finals, spread)
    mixed = finish(doc_lengths, queries, entering, local, gate, gain, crow)
    return mixed, pick_owned(flags, arrived, heads)


def solution(mesh):
    placed = (
        P(("groups", "seq"), "tp"),
        P(("groups", "seq"), "tp"),
        P(("groups", "seq"), "tp"),
        P(("groups", "seq"), "tp"),
        P(("groups", "seq"), "tp"),
        P("tp"),
        P("groups"),
        P("groups"),
    )
    return jax.shard_map(
        functools.partial(on_device, mesh.shape["seq"]),
        mesh=mesh,
        in_specs=placed,
        out_specs=(P(("groups", "seq"), "tp"), P(("groups", "seq"), "tp", None, None)),
        check_vma=False,
    )
```

```python
import functools
import math

import jax
import jax.numpy as jnp
from jax import lax
from jax.experimental import pallas as pl
from jax.experimental.pallas import tpu as pltpu
from jax.sharding import PartitionSpec as P

BLK = 512
SIDE = 3
EXTRA = 16
CHUNK = 256
MEMBERS = 4
TILE = 256
EARLY = (8,)
NEG = -1e30
LOG2E = math.log2(math.e)
SCALE = 128**-0.5
F32, BF16 = jnp.float32, jnp.bfloat16
SMEM = pl.BlockSpec(memory_space=pltpu.SMEM)
VMEM = pl.BlockSpec(memory_space=pltpu.VMEM)
LIMIT = pltpu.CompilerParams(vmem_limit_bytes=60 * 2**20)
SMALL = pltpu.CompilerParams(vmem_limit_bytes=48 * 2**20)


def dot(a, b, contract=((1,), (0,))):
    return lax.dot_general(a, b, (contract, ((), ())), preferred_element_type=F32)


def iota(shape, dim):
    return lax.broadcasted_iota(jnp.int32, shape, dim)


def read_ends(len_ref, count):
    ends, total = [], jnp.int32(0)
    for d in range(count):
        total = total + len_ref[d]
        ends.append(total)
    return ends


def run_end(ends, pos):
    best = ends[-1]
    for e in reversed(ends[:-1]):
        best = jnp.where(e > pos, e, best)
    return best


def run_start(ends, pos):
    best = jnp.zeros_like(pos)
    for e in ends[:-1]:
        best = jnp.where(e <= pos, e, best)
    return best


def split3(x):
    hi = x.astype(BF16)
    rest = x - hi.astype(F32)
    mid = rest.astype(BF16)
    return hi, mid, (rest - mid.astype(F32)).astype(BF16)


def cum_rows(ld_ref, crow_ref):
    heads, rows = ld_ref.shape
    upper = (iota((BLK, BLK), 0) <= iota((BLK, BLK), 1)).astype(F32).astype(BF16)
    base = jnp.zeros((heads, 1), F32)
    for b in range(rows // BLK):
        part = ld_ref[:, b * BLK : (b + 1) * BLK] * LOG2E
        sums = dot(jnp.concatenate(split3(part), axis=0), upper)
        row = sums[2 * heads :] + sums[heads : 2 * heads] + sums[:heads] + base
        crow_ref[:, b * BLK : (b + 1) * BLK] = row
        base = row[:, BLK - 1 :]


def value_at(cum, at, index):
    return jnp.sum(jnp.where(at == index, cum, 0.0), axis=1, keepdims=True)


def span_weights(cum, at, low, high):
    inside = (at >= low) & (at <= high)
    return jnp.exp2(jnp.where(inside, value_at(cum, at, high) - cum, NEG) + math.log2(SCALE))


def weigh(flipped, w_ref, h):
    weights = [jnp.broadcast_to(w_ref[pl.ds(h + j, 1), :], (128, flipped.shape[1])) for j in range(2)]
    return (flipped.astype(F32) * jnp.concatenate(weights, axis=0)).astype(BF16)


def whole(shape):
    return pl.BlockSpec(shape, lambda j: (0,) * len(shape))


def pieces_kernel(rest, len_ref, own_ref, ld_ref, k_ref, v_ref, *refs):
    if rest:
        side_ref, crow_ref, w_ref, keep_ref = refs
        slots = keep_ref.shape[0]
    else:
        side_ref, crow_ref, flag_ref = refs[:3]
        last_refs = refs[3 : 3 + MEMBERS]
        w_ref, first_ref, high_ref, weighted_ref, prefix_ref = refs[3 + MEMBERS :]
        slots = SIDE
    heads, rows = crow_ref.shape
    step = pl.program_id(0)
    hp = v_ref.shape[1] // 128
    me = lax.axis_index("seq")

    @pl.when(step == 0)
    def _():
        cum_rows(ld_ref, crow_ref)
        first = me * rows
        last = first + rows - 1
        ends = read_ends(len_ref, len_ref.shape[0])
        starts = [jnp.int32(0)] + ends[:-1]
        lows = [jnp.int32(0)] * slots
        highs = [jnp.int32(-1)] * slots
        place, rank, previous = jnp.int32(0), jnp.int32(0), jnp.int32(-1)
        crowded, owned_in = jnp.int32(0), jnp.int32(0)
        for d in range(len(ends)):
            here = (ends[d] > first) & (ends[d] <= last)
            low = jnp.maximum(starts[d] - first, 0)
            for s in range(slots):
                mine = here & (place == s + (SIDE if rest else 0))
                lows[s] = jnp.where(mine, low, lows[s])
                highs[s] = jnp.where(mine, ends[d] - 1 - first, highs[s])
            place = place + here.astype(jnp.int32)
            device = (ends[d] - 1) // rows
            rank = jnp.where(device == previous, rank + 1, 0)
            previous = device
            late = ((rank >= SIDE) & (ends[d] != (device + 1) * rows)).astype(jnp.int32) + (rank > SIDE).astype(jnp.int32)
            crowded = jnp.maximum(crowded, late)
            owned_in = jnp.where(own_ref[d] == me, device, owned_in)
        at = iota((heads, rows), 1)
        cum = crow_ref[...]
        total = jnp.zeros((heads, rows), F32)
        for s in range(slots):
            total = total + span_weights(cum, at, lows[s], highs[s])
        if rest:
            row_at = iota((16, rows), 1)
            for s in range(slots):
                inside = (row_at >= lows[s]) & (row_at <= highs[s])
                keep_ref[s] = jnp.where(inside, 1.0, 0.0).astype(BF16)
        else:
            total = total + span_weights(cum, at, jnp.maximum(run_start(ends, last) - first, 0), rows - 1)
            flag_ref[0] = owned_in // MEMBERS
            flag_ref[1] = crowded
            high = jnp.int32(-1)
            for s in range(slots):
                high = jnp.maximum(high, highs[s])
                high_ref[s] = high
            stop = jnp.minimum(run_end(ends, first) - 1 - first, rows - 1)
            goes_on = (run_start(ends, first) < first).astype(F32)
            first_ref[...] = jnp.broadcast_to(jnp.exp2(value_at(cum, at, stop)) * goes_on, (heads, 128))
        w_ref[...] = total

    def own(states, j):
        return states[j * 128 : (j + 1) * 128, j * 128 : (j + 1) * 128]

    if rest:
        for i in range(0, hp, 2):
            lanes = slice(i * 128, (i + 2) * 128)
            weighted = weigh(k_ref[:, lanes].T, w_ref, step * hp + i).reshape(16, 16, rows)
            for s in range(slots):
                states = dot((weighted * keep_ref[s][None]).reshape(256, rows), v_ref[:, lanes])
                for j in range(2):
                    at = (s * hp + i + j) * 128
                    side_ref[0, at : at + 128, :] = own(states, j).astype(BF16)
        return

    pairs = range(0, hp, 2)
    lanes = {i: slice(i * 128, (i + 2) * 128) for i in pairs}
    for i in pairs:
        weighted_ref[lanes[i], :] = weigh(k_ref[:, lanes[i]].T, w_ref, step * hp + i)
    totals = {}
    for i in pairs:
        sums = [jnp.zeros((128, 128), F32)] * 2
        for t in range(rows // TILE):
            span = slice(t * TILE, (t + 1) * TILE)
            states = dot(weighted_ref[lanes[i], span], v_ref[span, lanes[i]])
            for j in range(2):
                prefix_ref[t, i + j] = sums[j]
                sums[j] = sums[j] + own(states, j)
        totals[i] = sums
    ended = {i: [jnp.zeros((128, 128), F32)] * 2 for i in pairs}
    for s in range(slots):
        high = high_ref[s]
        tile = jnp.maximum(high, 0) // TILE
        start = pl.multiple_of(tile * TILE, TILE)
        keep = jnp.where(start + iota((16, TILE), 1) <= high, 1.0, 0.0).astype(BF16)
        for i in pairs:
            kept = weighted_ref[lanes[i], pl.ds(start, TILE)].reshape(16, 16, TILE) * keep[None]
            states = dot(kept.reshape(256, TILE), v_ref[pl.ds(start, TILE), lanes[i]])
            for j in range(2):
                until = own(states, j) + prefix_ref[tile, i + j]
                at = (s * hp + i + j) * 128
                side_ref[0, at : at + 128, :] = (until - ended[i][j]).astype(BF16)
                ended[i][j] = until
    rate = first_ref[pl.ds(step * hp, hp), :]
    high = rate.astype(BF16).astype(F32)
    pad = jnp.zeros((EXTRA - 2 * hp, 128), F32)
    tail = jnp.concatenate([high, rate - high, pad], axis=0).astype(BF16)
    last_states = [(totals[i][j] - ended[i][j]).astype(BF16) for i in pairs for j in range(2)]
    for x, last_ref in enumerate(last_refs):

        @pl.when((step ^ (me % MEMBERS)) == x)
        def _():
            for i in range(hp):
                last_ref[i * 128 : (i + 1) * 128, :] = last_states[i]
            last_ref[hp * 128 :, :] = tail


def piece_states(doc_lengths, owner_ids, decay_rows, keys, values, slots):
    heads, rows = decay_rows.shape
    rest = slots > SIDE
    count = slots - SIDE if rest else slots
    hp = heads // MEMBERS
    wide = pl.BlockSpec((rows, hp * 128), lambda j: (0, j))
    side = (count * hp * 128, 128)
    shapes = [jax.ShapeDtypeStruct((MEMBERS,) + side, BF16), jax.ShapeDtypeStruct((heads, rows), F32)]
    specs = [pl.BlockSpec((1,) + side, lambda j: (j, 0, 0)), whole((heads, rows))]
    scratch = [pltpu.VMEM((heads, rows), F32)]
    if rest:
        scratch.append(pltpu.VMEM((count, 16, rows), BF16))
    else:
        last = (hp * 128 + EXTRA, 128)
        shapes += [jax.ShapeDtypeStruct((2,), jnp.int32)] + [jax.ShapeDtypeStruct(last, BF16)] * MEMBERS
        specs += [SMEM] + [whole(last)] * MEMBERS
        scratch += [
            pltpu.VMEM((heads, 128), F32),
            pltpu.SMEM((SIDE,), jnp.int32),
            pltpu.VMEM((hp * 128, rows), BF16),
            pltpu.VMEM((rows // TILE, hp, 128, 128), F32),
        ]
    return pl.pallas_call(
        functools.partial(pieces_kernel, rest),
        grid=(MEMBERS,),
        in_specs=[SMEM, SMEM, whole((heads, rows)), wide, wide],
        out_specs=specs,
        out_shape=shapes,
        scratch_shapes=scratch,
        compiler_params=LIMIT,
        cost_estimate=pl.CostEstimate(
            flops=2 * heads * rows * 128 * 256, bytes_accessed=rows * heads * 128 * 4, transcendentals=heads * rows
        ),
        name="piece_states",
    )(doc_lengths, owner_ids, decay_rows, keys, values)


def head_column(ccol_ref, h):
    cols = ccol_ref[...]
    return jnp.sum(jnp.where(iota(cols.shape, 1) == h, cols, 0.0), axis=1, keepdims=True)


def fill_columns(crow_ref, ccol_ref):
    heads, rows = crow_ref.shape
    for r0 in range(0, rows, 128):
        part = crow_ref[:, r0 : r0 + 128]
        part = jnp.concatenate([part, jnp.zeros((128 - heads, 128), F32)], axis=0)
        ccol_ref[r0 : r0 + 128, :] = part.T


def fill_bias(first, ends, bias_ref):
    for c in range(bias_ref.shape[0] // CHUNK):
        base = first + c * CHUNK
        t_pos = base + iota((CHUNK, 1), 0)
        start = run_start(ends, t_pos)
        s_pos = base + iota((CHUNK, CHUNK), 1)
        keep = (s_pos <= t_pos) & (s_pos >= start)
        bias_ref[c * CHUNK : (c + 1) * CHUNK, :] = jnp.where(keep, math.log2(SCALE), NEG)


def attend(first, ends, q_ref, k_ref, v_ref, h, crow_ref, ccol_ref, bias_ref, states, emit):
    rows = q_ref.shape[0]
    pair = range(2)
    half = CHUNK // 2
    lanes = [slice(i * 128, (i + 1) * 128) for i in pair]
    row_all = [crow_ref[pl.ds(h + i, 1), :] for i in pair]
    col_all = [head_column(ccol_ref, h + i) for i in pair]
    starts = range(0, rows, CHUNK)
    spans = [slice(r0, r0 + CHUNK) for r0 in starts]
    reach = [run_end(ends, first + r0 - 1) - (first + r0) for r0 in starts]
    base = [[row_all[i][:, r0 - 1 : r0] if r0 else jnp.zeros((1, 1), F32) for r0 in starts] for i in pair]

    fresh = [[], []]
    for c, r0 in enumerate(starts[:-1]):
        since = run_start(ends, first + r0 + CHUNK - 1) - (first + r0)
        inside = iota((1, CHUNK), 1) >= since
        for i in pair:
            row = row_all[i][:, spans[c]]
            weight = jnp.exp2(jnp.where(inside, row[:, CHUNK - 1 :] - row, NEG) + math.log2(SCALE))
            flipped = k_ref[spans[c], lanes[i]].T
            fresh[i].append(dot((flipped.astype(F32) * weight).astype(BF16), v_ref[spans[c], lanes[i]]))
    carried = []
    for i in pair:
        state = None if states is None else states[i]
        chain = [None if state is None else state.astype(BF16)]
        for c in range(len(starts) - 1):
            if state is None:
                state = fresh[i][c]
            else:
                total = row_all[i][:, starts[c] + CHUNK - 1 : starts[c] + CHUNK]
                state = fresh[i][c] + state * jnp.exp2(jnp.where(CHUNK <= reach[c], total - base[i][c], NEG))
            chain.append(state.astype(BF16))
        carried.append(chain)

    def products(c):
        result = []
        for i in pair:
            query = q_ref[spans[c], lanes[i]]
            scores = dot(query, k_ref[spans[c], lanes[i]], ((1,), (1,)))
            result.append((scores, None if carried[i][c] is None else dot(query, carried[i][c])))
        return result

    ahead = products(0)
    for c, r0 in enumerate(starts):
        current = ahead
        if c + 1 < len(starts):
            ahead = products(c + 1)
        for part in range(2):
            t0, width = part * half, (part + 1) * half
            rows_here = slice(r0 + t0, r0 + t0 + half)
            for i in pair:
                scores, carry = current[i]
                col = col_all[i][rows_here]
                decay = jnp.exp2((col - row_all[i][:, r0 : r0 + width]) + bias_ref[rows_here, :width])
                weights = (scores[t0 : t0 + half, :width] * decay).astype(BF16)
                att = dot(weights, v_ref[r0 : r0 + width, lanes[i]])
                if carry is not None:
                    lead = jnp.exp2(jnp.where(t0 + iota((half, 1), 0) < reach[c], col - base[i][c], NEG))
                    att = att + lead * carry[t0 : t0 + half]
                emit(lanes[i], r0 + t0, half, att)


def early_kernel(pairs_before, len_ref, q_ref, k_ref, v_ref, crow_ref, *refs):
    out_ref, bias_ref, ccol_ref = refs[-3:]
    rows = q_ref.shape[0]
    step = pl.program_id(0)
    first = lax.axis_index("seq") * rows
    ends = read_ends(len_ref, len_ref.shape[0])

    @pl.when(step == 0)
    def _():
        fill_bias(first, ends, bias_ref)
        fill_columns(crow_ref, ccol_ref)

    def emit(lanes, t0, size, att):
        out_ref[t0 : t0 + size, lanes] = att

    attend(first, ends, q_ref, k_ref, v_ref, (step + pairs_before) * 2, crow_ref, ccol_ref, bias_ref, None, emit)


def early_attention(doc_lengths, queries, keys, values, crow, before, part):
    heads, rows = crow.shape
    skip = sum(EARLY[:part]) // 2
    wide = pl.BlockSpec((rows, 256), lambda j: (0, j + skip))
    count = EARLY[part]
    return pl.pallas_call(
        functools.partial(early_kernel, skip),
        grid=(count // 2,),
        in_specs=[SMEM, wide, wide, wide, whole((heads, rows))] + [pl.BlockSpec(memory_space=pl.ANY)] * len(before),
        out_specs=wide,
        out_shape=jax.ShapeDtypeStruct((rows, sum(EARLY) * 128), F32),
        input_output_aliases={5: 0} if before else {},
        scratch_shapes=[pltpu.VMEM((rows, CHUNK), F32), pltpu.VMEM((rows, 128), F32)],
        compiler_params=LIMIT,
        cost_estimate=pl.CostEstimate(
            flops=count * rows * CHUNK * 128 * 8, bytes_accessed=rows * count * 128 * 10, transcendentals=count * rows * CHUNK
        ),
        name="early_attention",
    )(doc_lengths, queries, keys, values, crow, *before)


def gather_last(refs, last_ref):
    me = lax.axis_index("seq") % MEMBERS
    for x, ref in enumerate(refs):
        last_ref[me ^ x] = ref[...]


def decay_of(last_ref, e, i, hp):
    extra = last_ref[e, hp * 128 :, :].astype(F32)
    return extra[i : i + 1, :] + extra[hp + i : hp + i + 1, :]


def scan_quad(rows, len_ref, last_ref, state, i, hp, note):
    members = last_ref.shape[0]
    ends = read_ends(len_ref, len_ref.shape[0])
    base = lax.axis_index("seq") // members * members
    for e in range(members):
        note(e, state)
        low = (base + e) * rows
        inner = jnp.int32(0)
        for end in ends:
            inner = inner + ((end > low) & (end < low + rows)).astype(jnp.int32)
        passes = (inner == 0).astype(F32)
        piece = last_ref[e, i * 128 : (i + 1) * 128, :].astype(F32)
        state = state * (decay_of(last_ref, e, i, hp) * passes) + piece
    return state


def leave_kernel(rows, len_ref, *refs):
    out_ref, last_ref = refs[-2:]
    gather_last(refs[:MEMBERS], last_ref)
    hp = out_ref.shape[0]
    for i in range(hp):
        state = jnp.zeros((128, 128), F32)
        if len(refs) > MEMBERS + 2:
            state = refs[MEMBERS][i].astype(F32)
        state = scan_quad(rows, len_ref, last_ref, state, i, hp, lambda e, x: None)
        out_ref[i] = state.astype(BF16)


def leave_quad(doc_lengths, last, coming, rows, hp):
    return pl.pallas_call(
        functools.partial(leave_kernel, rows),
        in_specs=[SMEM] + [VMEM] * (MEMBERS + len(coming)),
        out_specs=VMEM,
        out_shape=jax.ShapeDtypeStruct((hp, 128, 128), BF16),
        scratch_shapes=[pltpu.VMEM((MEMBERS,) + last[0].shape, BF16)],
        compiler_params=SMALL,
        name="leave_quad",
    )(doc_lengths, *last, *coming)


def enter_kernel(rows, len_ref, *refs):
    in_ref, out_refs, last_ref, state_ref = refs[MEMBERS], refs[MEMBERS + 1 : -2], refs[-2], refs[-1]
    gather_last(refs[:MEMBERS], last_ref)
    hp = in_ref.shape[0]

    def note(i, e, state):
        state_ref[e, i] = state

    for i in range(hp):
        scan_quad(rows, len_ref, last_ref, in_ref[i].astype(F32), i, hp, functools.partial(note, i))
    me = lax.axis_index("seq") % MEMBERS
    for x, out_ref in enumerate(out_refs):
        out_ref[...] = state_ref[me ^ x].astype(BF16)


def enter_states(doc_lengths, last, coming, rows):
    return pl.pallas_call(
        functools.partial(enter_kernel, rows),
        in_specs=[SMEM] + [VMEM] * (MEMBERS + 1),
        out_specs=[VMEM] * MEMBERS,
        out_shape=[jax.ShapeDtypeStruct(coming.shape, BF16)] * MEMBERS,
        scratch_shapes=[
            pltpu.VMEM((MEMBERS,) + last[0].shape, BF16),
            pltpu.VMEM((MEMBERS,) + coming.shape, F32),
        ],
        compiler_params=SMALL,
        name="enter_states",
    )(doc_lengths, *last, coming)


def final_kernel(rows, len_ref, own_ref, *refs):
    side_ref, rest_ref, in_ref, out_ref, last_ref, state_ref, piece_ref = refs[MEMBERS:]
    gather_last(refs[:MEMBERS], last_ref)
    hp = in_ref.shape[0]
    ends = read_ends(len_ref, len_ref.shape[0])
    base = lax.axis_index("seq") // MEMBERS * MEMBERS

    def note(i, e, state):
        state_ref[e, i] = state

    for i in range(hp):
        scan_quad(rows, len_ref, last_ref, in_ref[i].astype(F32), i, hp, functools.partial(note, i))
    out_ref[...] = jnp.zeros_like(out_ref)
    place, previous = jnp.int32(0), jnp.int32(-1)
    for d in range(len(ends)):
        device = (ends[d] - 1) // rows
        place = jnp.where(device == previous, place + 1, 0)
        previous = device
        at_end = ends[d] == (device + 1) * rows
        enters = (place == 0).astype(F32)
        mine = device // MEMBERS * MEMBERS == base
        e = device - base

        def put(i, local):
            state = local.astype(F32) + state_ref[e, i] * (decay_of(last_ref, e, i, hp) * enters)
            out_ref[own_ref[d], i] = state.astype(BF16)

        @pl.when(mine & at_end)
        def _():
            for i in range(hp):
                put(i, last_ref[e, i * 128 : (i + 1) * 128, :])

        @pl.when(mine & jnp.logical_not(at_end) & (place < SIDE))
        def _():
            for i in range(hp):
                put(i, side_ref[e, pl.ds(pl.multiple_of((place * hp + i) * 128, 128), 128), :])

        @pl.when(mine & jnp.logical_not(at_end) & (place >= SIDE))
        def _():
            for i in range(hp):
                row = pl.multiple_of(((place - SIDE) * hp + i) * 128, 128)
                pltpu.sync_copy(rest_ref.at[e, pl.ds(row, 128), :], piece_ref)
                put(i, piece_ref[...])


def final_states(doc_lengths, owner_ids, last, side, rest, coming, rows, spread):
    return pl.pallas_call(
        functools.partial(final_kernel, rows),
        in_specs=[SMEM, SMEM] + [VMEM] * (MEMBERS + 1) + [pl.BlockSpec(memory_space=pl.ANY), VMEM],
        out_specs=VMEM,
        out_shape=jax.ShapeDtypeStruct((spread,) + coming.shape, BF16),
        scratch_shapes=[
            pltpu.VMEM((MEMBERS,) + last[0].shape, BF16),
            pltpu.VMEM((MEMBERS,) + coming.shape, F32),
            pltpu.VMEM((128, 128), BF16),
        ],
        compiler_params=SMALL,
        name="final_states",
    )(doc_lengths, owner_ids, *last, side, rest, coming)


def finish_kernel(
    len_ref, q_ref, k_ref, v_ref, e0, e1, e2, e3, local_ref, gate_ref, gain_ref, crow_ref, out_ref, bias_ref, ccol_ref
):
    rows = q_ref.shape[0]
    step = pl.program_id(0)
    me = lax.axis_index("seq")
    first = me * rows
    ends = read_ends(len_ref, len_ref.shape[0])
    hp = e0.shape[0]
    pairs = sum(EARLY) // 2

    def entering(h):
        far = (h // hp) ^ (me % MEMBERS)
        state = e0[h % hp]
        for x, ref in ((1, e1), (2, e2), (3, e3)):
            state = jnp.where(far == x, ref[h % hp], state)
        return state

    def emit(lanes, t0, size, att):
        mean = jnp.mean(att * att, axis=1, keepdims=True)
        gate = 0.5 + 0.5 * jnp.tanh(0.5 * gate_ref[t0 : t0 + size, lanes].astype(F32))
        gain = gain_ref[:, lanes].astype(F32)
        out_ref[t0 : t0 + size, lanes] = (att * lax.rsqrt(mean + 1e-06) * (gain * gate)).astype(BF16)

    @pl.when(step == 0)
    def _():
        fill_bias(first, ends, bias_ref)
        fill_columns(crow_ref, ccol_ref)

    @pl.when(step < pairs)
    def _():
        reach = run_end(ends, first - 1) - first
        cols = [head_column(ccol_ref, step * 2 + i) for i in range(2)]
        states = [entering(step * 2 + i) for i in range(2)]
        lanes = [slice(i * 128, (i + 1) * 128) for i in range(2)]
        for t0 in range(0, rows, 256):
            carry = [dot(q_ref[t0 : t0 + 256, lanes[i]], states[i]) for i in range(2)]
            at = t0 + iota((256, 1), 0)
            for i in range(2):
                lead = jnp.exp2(jnp.where(at < reach, cols[i][t0 : t0 + 256], NEG))
                emit(lanes[i], t0, 256, local_ref[t0 : t0 + 256, lanes[i]] + lead * carry[i])

    @pl.when(step >= pairs)
    def _():
        states = [entering(step * 2 + i).astype(F32) for i in range(2)]
        attend(first, ends, q_ref, k_ref, v_ref, step * 2, crow_ref, ccol_ref, bias_ref, states, emit)


def finish(doc_lengths, queries, keys, values, entering, local, gate, gain, crow):
    heads, rows = crow.shape
    pairs = sum(EARLY) // 2
    wide = pl.BlockSpec((rows, 256), lambda j: (0, j))
    late = pl.BlockSpec((rows, 256), lambda j: (0, jnp.maximum(j, pairs)))
    return pl.pallas_call(
        finish_kernel,
        grid=(heads // 2,),
        in_specs=[SMEM, wide, late, late]
        + [whole(e.shape) for e in entering]
        + [
            pl.BlockSpec((rows, 256), lambda j: (0, jnp.minimum(j, pairs - 1))),
            wide,
            pl.BlockSpec((1, 256), lambda j: (0, j)),
            whole((heads, rows)),
        ],
        out_specs=wide,
        out_shape=jax.ShapeDtypeStruct((rows, heads * 128), BF16),
        scratch_shapes=[pltpu.VMEM((rows, CHUNK), F32), pltpu.VMEM((rows, 128), F32)],
        compiler_params=LIMIT,
        cost_estimate=pl.CostEstimate(
            flops=heads * rows * CHUNK * 128 * 8, bytes_accessed=rows * heads * 128 * 10, transcendentals=heads * rows * CHUNK
        ),
        name="finish",
    )(doc_lengths, queries, keys, values, *entering, local, gate, gain, crow)


def swap(x, groups=None):
    return lax.all_to_all(x, "seq", split_axis=0, concat_axis=0, axis_index_groups=groups, tiled=True)


def by_distance(parcels, spread):
    return [parcels[0]] + [
        lax.ppermute(parcels[x], "seq", [(s, s ^ x) for s in range(spread)]) for x in range(1, MEMBERS)
    ]


def on_device(spread, queries, keys, values, log_decay, gate, gain, doc_lengths, owner_ids):
    rows, heads = log_decay.shape
    quads = spread // MEMBERS
    hp = heads // MEMBERS
    near = [[q * MEMBERS + m for m in range(MEMBERS)] for q in range(quads)]
    onward = [(s, s + MEMBERS) for s in range(spread - MEMBERS)]
    decay_rows = log_decay.T
    barrier = lax.optimization_barrier

    side, crow, flags, *last = piece_states(doc_lengths, owner_ids, decay_rows, keys, values, SIDE)
    last = by_distance(last, spread)
    gain = gain.reshape(1, -1)
    from_quad = [flags[0] == q for q in range(1, quads)]
    slots = max(doc_lengths.shape[0] - 1, SIDE + 1)

    def none(count):
        return jnp.zeros((MEMBERS, count * hp * 128, 128), BF16)

    def send_rest(count):
        sent = swap(piece_states(doc_lengths, owner_ids, decay_rows, keys, values, count)[0], near)
        return jnp.concatenate([sent, none(slots - count)], axis=1) if count < slots else sent

    branches = [lambda: none(slots - SIDE), lambda: send_rest(SIDE + 1), lambda: send_rest(slots)]
    rest = lax.switch(flags[1], branches)
    last, side, gain, rest, from_quad = barrier((last, side, gain, rest, from_quad))

    side = swap(side, near)
    coming = []
    for _ in range(quads - 1):
        leaving = leave_quad(doc_lengths, last, coming, rows, hp)
        coming = [lax.ppermute(leaving, "seq", onward)]
    crow_1, leaving = barrier((crow, leaving))
    local = early_attention(doc_lengths, queries, keys, values, crow_1, [], 0)
    coming, local, side = barrier((coming[0], local, side))

    entering = by_distance(enter_states(doc_lengths, last, coming, rows), spread)
    finals = final_states(doc_lengths, owner_ids, last, side, rest, coming, rows, spread)
    entering, finals = barrier((entering, finals))
    arrived = swap(finals).reshape(quads, 1, heads, 128, 128)
    mixed = finish(doc_lengths, queries, keys, values, entering, local, gate, gain, crow)
    owned = arrived[0]
    for q in range(1, quads):
        owned = jnp.where(from_quad[q - 1], arrived[q], owned)
    return mixed, owned


def solution(mesh):
    placed = (
        P(("groups", "seq"), "tp"),
        P(("groups", "seq"), "tp"),
        P(("groups", "seq"), "tp"),
        P(("groups", "seq"), "tp"),
        P(("groups", "seq"), "tp"),
        P("tp"),
        P("groups"),
        P("groups"),
    )
    return jax.shard_map(
        functools.partial(on_device, mesh.shape["seq"]),
        mesh=mesh,
        in_specs=placed,
        out_specs=(P(("groups", "seq"), "tp"), P(("groups", "seq"), "tp", None, None)),
        check_vma=False,
    )
```

```python
import functools
import math

import jax
import jax.numpy as jnp
from jax import lax
from jax.experimental import pallas as pl
from jax.experimental.pallas import tpu as pltpu
from jax.sharding import PartitionSpec as P

BLK = 512
SIDE = 3
EXTRA = 16
CHUNK = 256
MEMBERS = 4
TILE = 256
EARLY = (8,)
NEG = -1e30
LOG2E = math.log2(math.e)
SCALE = 128**-0.5
F32, BF16 = jnp.float32, jnp.bfloat16
SMEM = pl.BlockSpec(memory_space=pltpu.SMEM)
VMEM = pl.BlockSpec(memory_space=pltpu.VMEM)
LIMIT = pltpu.CompilerParams(vmem_limit_bytes=60 * 2**20)
SMALL = pltpu.CompilerParams(vmem_limit_bytes=48 * 2**20)


def dot(a, b, contract=((1,), (0,))):
    return lax.dot_general(a, b, (contract, ((), ())), preferred_element_type=F32)


def iota(shape, dim):
    return lax.broadcasted_iota(jnp.int32, shape, dim)


def read_ends(len_ref, count):
    ends, total = [], jnp.int32(0)
    for d in range(count):
        total = total + len_ref[d]
        ends.append(total)
    return ends


def run_end(ends, pos):
    best = ends[-1]
    for e in reversed(ends[:-1]):
        best = jnp.where(e > pos, e, best)
    return best


def run_start(ends, pos):
    best = jnp.zeros_like(pos)
    for e in ends[:-1]:
        best = jnp.where(e <= pos, e, best)
    return best


def split3(x):
    hi = x.astype(BF16)
    rest = x - hi.astype(F32)
    mid = rest.astype(BF16)
    return hi, mid, (rest - mid.astype(F32)).astype(BF16)


def cum_rows(ld_ref, crow_ref):
    heads, rows = ld_ref.shape
    upper = (iota((BLK, BLK), 0) <= iota((BLK, BLK), 1)).astype(F32).astype(BF16)
    base = jnp.zeros((heads, 1), F32)
    for b in range(rows // BLK):
        part = ld_ref[:, b * BLK : (b + 1) * BLK] * LOG2E
        sums = dot(jnp.concatenate(split3(part), axis=0), upper)
        row = sums[2 * heads :] + sums[heads : 2 * heads] + sums[:heads] + base
        crow_ref[:, b * BLK : (b + 1) * BLK] = row
        base = row[:, BLK - 1 :]


def value_at(cum, at, index):
    return jnp.sum(jnp.where(at == index, cum, 0.0), axis=1, keepdims=True)


def span_weights(cum, at, low, high):
    inside = (at >= low) & (at <= high)
    return jnp.exp2(jnp.where(inside, value_at(cum, at, high) - cum, NEG) + math.log2(SCALE))


def weigh(flipped, w_ref, h):
    weights = [jnp.broadcast_to(w_ref[pl.ds(h + j, 1), :], (128, flipped.shape[1])) for j in range(2)]
    return (flipped.astype(F32) * jnp.concatenate(weights, axis=0)).astype(BF16)


def whole(shape):
    return pl.BlockSpec(shape, lambda j: (0,) * len(shape))


def pieces_kernel(rest, len_ref, own_ref, ld_ref, k_ref, v_ref, *refs):
    if rest:
        side_ref, crow_ref, w_ref, keep_ref = refs
        slots = keep_ref.shape[0]
    else:
        side_ref, crow_ref, flag_ref, spare_ref = refs[:4]
        last_refs = refs[4 : 4 + MEMBERS]
        w_ref, first_ref, high_ref, weighted_ref, prefix_ref = refs[4 + MEMBERS :]
        slots = SIDE + 1
    heads, rows = crow_ref.shape
    step = pl.program_id(0)
    hp = v_ref.shape[1] // 128
    me = lax.axis_index("seq")

    @pl.when(step == 0)
    def _():
        cum_rows(ld_ref, crow_ref)
        first = me * rows
        last = first + rows - 1
        ends = read_ends(len_ref, len_ref.shape[0])
        starts = [jnp.int32(0)] + ends[:-1]
        lows = [jnp.int32(0)] * slots
        highs = [jnp.int32(-1)] * slots
        place, rank, previous = jnp.int32(0), jnp.int32(0), jnp.int32(-1)
        crowded, owned_in = jnp.int32(0), jnp.int32(0)
        for d in range(len(ends)):
            here = (ends[d] > first) & (ends[d] <= last)
            low = jnp.maximum(starts[d] - first, 0)
            for s in range(slots):
                mine = here & (place == s + (SIDE if rest else 0))
                lows[s] = jnp.where(mine, low, lows[s])
                highs[s] = jnp.where(mine, ends[d] - 1 - first, highs[s])
            place = place + here.astype(jnp.int32)
            device = (ends[d] - 1) // rows
            rank = jnp.where(device == previous, rank + 1, 0)
            previous = device
            late = ((rank >= SIDE) & (ends[d] != (device + 1) * rows)).astype(jnp.int32) + (rank > SIDE).astype(jnp.int32)
            crowded = jnp.maximum(crowded, late)
            owned_in = jnp.where(own_ref[d] == me, device, owned_in)
        at = iota((heads, rows), 1)
        cum = crow_ref[...]
        total = jnp.zeros((heads, rows), F32)
        for s in range(slots):
            total = total + span_weights(cum, at, lows[s], highs[s])
        if rest:
            row_at = iota((16, rows), 1)
            for s in range(slots):
                inside = (row_at >= lows[s]) & (row_at <= highs[s])
                keep_ref[s] = jnp.where(inside, 1.0, 0.0).astype(BF16)
        else:
            total = total + span_weights(cum, at, jnp.maximum(run_start(ends, last) - first, 0), rows - 1)
            flag_ref[0] = owned_in // MEMBERS
            flag_ref[1] = crowded
            high = jnp.int32(-1)
            for s in range(slots):
                high = jnp.maximum(high, highs[s])
                high_ref[s] = high
            stop = jnp.minimum(run_end(ends, first) - 1 - first, rows - 1)
            goes_on = (run_start(ends, first) < first).astype(F32)
            first_ref[...] = jnp.broadcast_to(jnp.exp2(value_at(cum, at, stop)) * goes_on, (heads, 128))
        w_ref[...] = total

    def own(states, j):
        return states[j * 128 : (j + 1) * 128, j * 128 : (j + 1) * 128]

    if rest:
        for i in range(0, hp, 2):
            lanes = slice(i * 128, (i + 2) * 128)
            weighted = weigh(k_ref[:, lanes].T, w_ref, step * hp + i).reshape(16, 16, rows)
            for s in range(slots):
                states = dot((weighted * keep_ref[s][None]).reshape(256, rows), v_ref[:, lanes])
                for j in range(2):
                    at = (s * hp + i + j) * 128
                    side_ref[0, at : at + 128, :] = own(states, j).astype(BF16)
        return

    pairs = range(0, hp, 2)
    lanes = {i: slice(i * 128, (i + 2) * 128) for i in pairs}
    for i in pairs:
        weighted_ref[lanes[i], :] = weigh(k_ref[:, lanes[i]].T, w_ref, step * hp + i)
    totals = {}
    for i in pairs:
        sums = [jnp.zeros((128, 128), F32)] * 2
        for t in range(rows // TILE):
            span = slice(t * TILE, (t + 1) * TILE)
            states = dot(weighted_ref[lanes[i], span], v_ref[span, lanes[i]])
            for j in range(2):
                prefix_ref[t, i + j] = sums[j]
                sums[j] = sums[j] + own(states, j)
        totals[i] = sums
    ended = {i: [jnp.zeros((128, 128), F32)] * 2 for i in pairs}
    for s in range(slots):
        high = high_ref[s]
        tile = jnp.maximum(high, 0) // TILE
        start = pl.multiple_of(tile * TILE, TILE)
        keep = jnp.where(start + iota((16, TILE), 1) <= high, 1.0, 0.0).astype(BF16)
        for i in pairs:
            kept = weighted_ref[lanes[i], pl.ds(start, TILE)].reshape(16, 16, TILE) * keep[None]
            states = dot(kept.reshape(256, TILE), v_ref[pl.ds(start, TILE), lanes[i]])
            for j in range(2):
                until = own(states, j) + prefix_ref[tile, i + j]
                out_ref, at = (side_ref, (s * hp + i + j) * 128) if s < SIDE else (spare_ref, (i + j) * 128)
                out_ref[0, at : at + 128, :] = (until - ended[i][j]).astype(BF16)
                ended[i][j] = until
    rate = first_ref[pl.ds(step * hp, hp), :]
    high = rate.astype(BF16).astype(F32)
    pad = jnp.zeros((EXTRA - 2 * hp, 128), F32)
    tail = jnp.concatenate([high, rate - high, pad], axis=0).astype(BF16)
    last_states = [(totals[i][j] - ended[i][j]).astype(BF16) for i in pairs for j in range(2)]
    for x, last_ref in enumerate(last_refs):

        @pl.when((step ^ (me % MEMBERS)) == x)
        def _():
            for i in range(hp):
                last_ref[i * 128 : (i + 1) * 128, :] = last_states[i]
            last_ref[hp * 128 :, :] = tail


def piece_states(doc_lengths, owner_ids, decay_rows, keys, values, slots):
    heads, rows = decay_rows.shape
    rest = slots > SIDE
    count = slots - SIDE if rest else slots
    hp = heads // MEMBERS
    wide = pl.BlockSpec((rows, hp * 128), lambda j: (0, j))
    side = (count * hp * 128, 128)
    shapes = [jax.ShapeDtypeStruct((MEMBERS,) + side, BF16), jax.ShapeDtypeStruct((heads, rows), F32)]
    specs = [pl.BlockSpec((1,) + side, lambda j: (j, 0, 0)), whole((heads, rows))]
    scratch = [pltpu.VMEM((heads, rows), F32)]
    if rest:
        scratch.append(pltpu.VMEM((count, 16, rows), BF16))
    else:
        last = (hp * 128 + EXTRA, 128)
        spare = (hp * 128, 128)
        shapes += [jax.ShapeDtypeStruct((2,), jnp.int32), jax.ShapeDtypeStruct((MEMBERS,) + spare, BF16)]
        shapes += [jax.ShapeDtypeStruct(last, BF16)] * MEMBERS
        specs += [SMEM, pl.BlockSpec((1,) + spare, lambda j: (j, 0, 0))] + [whole(last)] * MEMBERS
        scratch += [
            pltpu.VMEM((heads, 128), F32),
            pltpu.SMEM((SIDE + 1,), jnp.int32),
            pltpu.VMEM((hp * 128, rows), BF16),
            pltpu.VMEM((rows // TILE, hp, 128, 128), F32),
        ]
    return pl.pallas_call(
        functools.partial(pieces_kernel, rest),
        grid=(MEMBERS,),
        in_specs=[SMEM, SMEM, whole((heads, rows)), wide, wide],
        out_specs=specs,
        out_shape=shapes,
        scratch_shapes=scratch,
        compiler_params=LIMIT,
        cost_estimate=pl.CostEstimate(
            flops=2 * heads * rows * 128 * 256, bytes_accessed=rows * heads * 128 * 4, transcendentals=heads * rows
        ),
        name="piece_states",
    )(doc_lengths, owner_ids, decay_rows, keys, values)


def head_column(ccol_ref, h):
    cols = ccol_ref[...]
    return jnp.sum(jnp.where(iota(cols.shape, 1) == h, cols, 0.0), axis=1, keepdims=True)


def fill_columns(crow_ref, ccol_ref):
    heads, rows = crow_ref.shape
    for r0 in range(0, rows, 128):
        part = crow_ref[:, r0 : r0 + 128]
        part = jnp.concatenate([part, jnp.zeros((128 - heads, 128), F32)], axis=0)
        ccol_ref[r0 : r0 + 128, :] = part.T


def fill_bias(first, ends, bias_ref):
    for c in range(bias_ref.shape[0] // CHUNK):
        base = first + c * CHUNK
        t_pos = base + iota((CHUNK, 1), 0)
        start = run_start(ends, t_pos)
        s_pos = base + iota((CHUNK, CHUNK), 1)
        keep = (s_pos <= t_pos) & (s_pos >= start)
        bias_ref[c * CHUNK : (c + 1) * CHUNK, :] = jnp.where(keep, math.log2(SCALE), NEG)


def attend(first, ends, q_ref, k_ref, v_ref, h, crow_ref, ccol_ref, bias_ref, states, emit):
    rows = q_ref.shape[0]
    pair = range(2)
    half = CHUNK // 2
    lanes = [slice(i * 128, (i + 1) * 128) for i in pair]
    row_all = [crow_ref[pl.ds(h + i, 1), :] for i in pair]
    col_all = [head_column(ccol_ref, h + i) for i in pair]
    starts = range(0, rows, CHUNK)
    spans = [slice(r0, r0 + CHUNK) for r0 in starts]
    reach = [run_end(ends, first + r0 - 1) - (first + r0) for r0 in starts]
    base = [[row_all[i][:, r0 - 1 : r0] if r0 else jnp.zeros((1, 1), F32) for r0 in starts] for i in pair]

    fresh = [[], []]
    for c, r0 in enumerate(starts[:-1]):
        since = run_start(ends, first + r0 + CHUNK - 1) - (first + r0)
        inside = iota((1, CHUNK), 1) >= since
        for i in pair:
            row = row_all[i][:, spans[c]]
            weight = jnp.exp2(jnp.where(inside, row[:, CHUNK - 1 :] - row, NEG) + math.log2(SCALE))
            flipped = k_ref[spans[c], lanes[i]].T
            fresh[i].append(dot((flipped.astype(F32) * weight).astype(BF16), v_ref[spans[c], lanes[i]]))
    carried = []
    for i in pair:
        state = None if states is None else states[i]
        chain = [None if state is None else state.astype(BF16)]
        for c in range(len(starts) - 1):
            if state is None:
                state = fresh[i][c]
            else:
                total = row_all[i][:, starts[c] + CHUNK - 1 : starts[c] + CHUNK]
                state = fresh[i][c] + state * jnp.exp2(jnp.where(CHUNK <= reach[c], total - base[i][c], NEG))
            chain.append(state.astype(BF16))
        carried.append(chain)

    def products(c):
        result = []
        for i in pair:
            query = q_ref[spans[c], lanes[i]]
            scores = dot(query, k_ref[spans[c], lanes[i]], ((1,), (1,)))
            result.append((scores, None if carried[i][c] is None else dot(query, carried[i][c])))
        return result

    ahead = products(0)
    for c, r0 in enumerate(starts):
        current = ahead
        if c + 1 < len(starts):
            ahead = products(c + 1)
        for part in range(2):
            t0, width = part * half, (part + 1) * half
            rows_here = slice(r0 + t0, r0 + t0 + half)
            for i in pair:
                scores, carry = current[i]
                col = col_all[i][rows_here]
                decay = jnp.exp2((col - row_all[i][:, r0 : r0 + width]) + bias_ref[rows_here, :width])
                weights = (scores[t0 : t0 + half, :width] * decay).astype(BF16)
                att = dot(weights, v_ref[r0 : r0 + width, lanes[i]])
                if carry is not None:
                    lead = jnp.exp2(jnp.where(t0 + iota((half, 1), 0) < reach[c], col - base[i][c], NEG))
                    att = att + lead * carry[t0 : t0 + half]
                emit(lanes[i], r0 + t0, half, att)


def early_kernel(pairs_before, len_ref, q_ref, k_ref, v_ref, crow_ref, *refs):
    out_ref, bias_ref, ccol_ref = refs[-3:]
    rows = q_ref.shape[0]
    step = pl.program_id(0)
    first = lax.axis_index("seq") * rows
    ends = read_ends(len_ref, len_ref.shape[0])

    @pl.when(step == 0)
    def _():
        fill_bias(first, ends, bias_ref)
        fill_columns(crow_ref, ccol_ref)

    def emit(lanes, t0, size, att):
        out_ref[t0 : t0 + size, lanes] = att

    attend(first, ends, q_ref, k_ref, v_ref, (step + pairs_before) * 2, crow_ref, ccol_ref, bias_ref, None, emit)


def early_attention(doc_lengths, queries, keys, values, crow, before, part):
    heads, rows = crow.shape
    skip = sum(EARLY[:part]) // 2
    wide = pl.BlockSpec((rows, 256), lambda j: (0, j + skip))
    count = EARLY[part]
    return pl.pallas_call(
        functools.partial(early_kernel, skip),
        grid=(count // 2,),
        in_specs=[SMEM, wide, wide, wide, whole((heads, rows))] + [pl.BlockSpec(memory_space=pl.ANY)] * len(before),
        out_specs=wide,
        out_shape=jax.ShapeDtypeStruct((rows, sum(EARLY) * 128), F32),
        input_output_aliases={5: 0} if before else {},
        scratch_shapes=[pltpu.VMEM((rows, CHUNK), F32), pltpu.VMEM((rows, 128), F32)],
        compiler_params=LIMIT,
        cost_estimate=pl.CostEstimate(
            flops=count * rows * CHUNK * 128 * 8, bytes_accessed=rows * count * 128 * 10, transcendentals=count * rows * CHUNK
        ),
        name="early_attention",
    )(doc_lengths, queries, keys, values, crow, *before)


def gather_last(refs, last_ref):
    me = lax.axis_index("seq") % MEMBERS
    for x, ref in enumerate(refs):
        last_ref[me ^ x] = ref[...]


def decay_of(last_ref, e, i, hp):
    extra = last_ref[e, hp * 128 :, :].astype(F32)
    return extra[i : i + 1, :] + extra[hp + i : hp + i + 1, :]


def scan_quad(rows, len_ref, last_ref, state, i, hp, note):
    members = last_ref.shape[0]
    ends = read_ends(len_ref, len_ref.shape[0])
    base = lax.axis_index("seq") // members * members
    for e in range(members):
        note(e, state)
        low = (base + e) * rows
        inner = jnp.int32(0)
        for end in ends:
            inner = inner + ((end > low) & (end < low + rows)).astype(jnp.int32)
        passes = (inner == 0).astype(F32)
        piece = last_ref[e, i * 128 : (i + 1) * 128, :].astype(F32)
        state = state * (decay_of(last_ref, e, i, hp) * passes) + piece
    return state


def leave_kernel(rows, len_ref, *refs):
    out_ref, last_ref = refs[-2:]
    gather_last(refs[:MEMBERS], last_ref)
    hp = out_ref.shape[0]
    for i in range(hp):
        state = jnp.zeros((128, 128), F32)
        if len(refs) > MEMBERS + 2:
            state = refs[MEMBERS][i].astype(F32)
        state = scan_quad(rows, len_ref, last_ref, state, i, hp, lambda e, x: None)
        out_ref[i] = state.astype(BF16)


def leave_quad(doc_lengths, last, coming, rows, hp):
    return pl.pallas_call(
        functools.partial(leave_kernel, rows),
        in_specs=[SMEM] + [VMEM] * (MEMBERS + len(coming)),
        out_specs=VMEM,
        out_shape=jax.ShapeDtypeStruct((hp, 128, 128), BF16),
        scratch_shapes=[pltpu.VMEM((MEMBERS,) + last[0].shape, BF16)],
        compiler_params=SMALL,
        name="leave_quad",
    )(doc_lengths, *last, *coming)


def enter_kernel(rows, len_ref, *refs):
    in_ref, out_refs, last_ref, state_ref = refs[MEMBERS], refs[MEMBERS + 1 : -2], refs[-2], refs[-1]
    gather_last(refs[:MEMBERS], last_ref)
    hp = in_ref.shape[0]

    def note(i, e, state):
        state_ref[e, i] = state

    for i in range(hp):
        scan_quad(rows, len_ref, last_ref, in_ref[i].astype(F32), i, hp, functools.partial(note, i))
    me = lax.axis_index("seq") % MEMBERS
    for x, out_ref in enumerate(out_refs):
        out_ref[...] = state_ref[me ^ x].astype(BF16)


def enter_states(doc_lengths, last, coming, rows):
    return pl.pallas_call(
        functools.partial(enter_kernel, rows),
        in_specs=[SMEM] + [VMEM] * (MEMBERS + 1),
        out_specs=[VMEM] * MEMBERS,
        out_shape=[jax.ShapeDtypeStruct(coming.shape, BF16)] * MEMBERS,
        scratch_shapes=[
            pltpu.VMEM((MEMBERS,) + last[0].shape, BF16),
            pltpu.VMEM((MEMBERS,) + coming.shape, F32),
        ],
        compiler_params=SMALL,
        name="enter_states",
    )(doc_lengths, *last, coming)


def final_kernel(rows, len_ref, own_ref, *refs):
    side_ref, rest_ref, in_ref, out_ref, last_ref, state_ref, piece_ref = refs[MEMBERS:]
    gather_last(refs[:MEMBERS], last_ref)
    hp = in_ref.shape[0]
    ends = read_ends(len_ref, len_ref.shape[0])
    base = lax.axis_index("seq") // MEMBERS * MEMBERS

    def note(i, e, state):
        state_ref[e, i] = state

    for i in range(hp):
        scan_quad(rows, len_ref, last_ref, in_ref[i].astype(F32), i, hp, functools.partial(note, i))
    out_ref[...] = jnp.zeros_like(out_ref)
    place, previous = jnp.int32(0), jnp.int32(-1)
    for d in range(len(ends)):
        device = (ends[d] - 1) // rows
        place = jnp.where(device == previous, place + 1, 0)
        previous = device
        at_end = ends[d] == (device + 1) * rows
        enters = (place == 0).astype(F32)
        mine = device // MEMBERS * MEMBERS == base
        e = device - base

        def put(i, local):
            state = local.astype(F32) + state_ref[e, i] * (decay_of(last_ref, e, i, hp) * enters)
            out_ref[own_ref[d], i] = state.astype(BF16)

        @pl.when(mine & at_end)
        def _():
            for i in range(hp):
                put(i, last_ref[e, i * 128 : (i + 1) * 128, :])

        @pl.when(mine & jnp.logical_not(at_end) & (place < SIDE))
        def _():
            for i in range(hp):
                put(i, side_ref[e, pl.ds(pl.multiple_of((place * hp + i) * 128, 128), 128), :])

        @pl.when(mine & jnp.logical_not(at_end) & (place >= SIDE))
        def _():
            for i in range(hp):
                row = pl.multiple_of(((place - SIDE) * hp + i) * 128, 128)
                pltpu.sync_copy(rest_ref.at[e, pl.ds(row, 128), :], piece_ref)
                put(i, piece_ref[...])


def final_states(doc_lengths, owner_ids, last, side, rest, coming, rows, spread):
    return pl.pallas_call(
        functools.partial(final_kernel, rows),
        in_specs=[SMEM, SMEM] + [VMEM] * (MEMBERS + 1) + [pl.BlockSpec(memory_space=pl.ANY), VMEM],
        out_specs=VMEM,
        out_shape=jax.ShapeDtypeStruct((spread,) + coming.shape, BF16),
        scratch_shapes=[
            pltpu.VMEM((MEMBERS,) + last[0].shape, BF16),
            pltpu.VMEM((MEMBERS,) + coming.shape, F32),
            pltpu.VMEM((128, 128), BF16),
        ],
        compiler_params=SMALL,
        name="final_states",
    )(doc_lengths, owner_ids, *last, side, rest, coming)


def finish_kernel(
    len_ref, q_ref, k_ref, v_ref, e0, e1, e2, e3, local_ref, gate_ref, gain_ref, crow_ref, out_ref, bias_ref, ccol_ref
):
    rows = q_ref.shape[0]
    step = pl.program_id(0)
    me = lax.axis_index("seq")
    first = me * rows
    ends = read_ends(len_ref, len_ref.shape[0])
    hp = e0.shape[0]
    pairs = sum(EARLY) // 2

    def entering(h):
        far = (h // hp) ^ (me % MEMBERS)
        state = e0[h % hp]
        for x, ref in ((1, e1), (2, e2), (3, e3)):
            state = jnp.where(far == x, ref[h % hp], state)
        return state

    def emit(lanes, t0, size, att):
        mean = jnp.mean(att * att, axis=1, keepdims=True)
        gate = 0.5 + 0.5 * jnp.tanh(0.5 * gate_ref[t0 : t0 + size, lanes].astype(F32))
        gain = gain_ref[:, lanes].astype(F32)
        out_ref[t0 : t0 + size, lanes] = (att * lax.rsqrt(mean + 1e-06) * (gain * gate)).astype(BF16)

    @pl.when(step == 0)
    def _():
        fill_bias(first, ends, bias_ref)
        fill_columns(crow_ref, ccol_ref)

    @pl.when(step < pairs)
    def _():
        reach = run_end(ends, first - 1) - first
        cols = [head_column(ccol_ref, step * 2 + i) for i in range(2)]
        states = [entering(step * 2 + i) for i in range(2)]
        lanes = [slice(i * 128, (i + 1) * 128) for i in range(2)]
        for t0 in range(0, rows, 256):
            carry = [dot(q_ref[t0 : t0 + 256, lanes[i]], states[i]) for i in range(2)]
            at = t0 + iota((256, 1), 0)
            for i in range(2):
                lead = jnp.exp2(jnp.where(at < reach, cols[i][t0 : t0 + 256], NEG))
                emit(lanes[i], t0, 256, local_ref[t0 : t0 + 256, lanes[i]] + lead * carry[i])

    @pl.when(step >= pairs)
    def _():
        states = [entering(step * 2 + i).astype(F32) for i in range(2)]
        attend(first, ends, q_ref, k_ref, v_ref, step * 2, crow_ref, ccol_ref, bias_ref, states, emit)


def finish(doc_lengths, queries, keys, values, entering, local, gate, gain, crow):
    heads, rows = crow.shape
    pairs = sum(EARLY) // 2
    wide = pl.BlockSpec((rows, 256), lambda j: (0, j))
    late = pl.BlockSpec((rows, 256), lambda j: (0, jnp.maximum(j, pairs)))
    return pl.pallas_call(
        finish_kernel,
        grid=(heads // 2,),
        in_specs=[SMEM, wide, late, late]
        + [whole(e.shape) for e in entering]
        + [
            pl.BlockSpec((rows, 256), lambda j: (0, jnp.minimum(j, pairs - 1))),
            wide,
            pl.BlockSpec((1, 256), lambda j: (0, j)),
            whole((heads, rows)),
        ],
        out_specs=wide,
        out_shape=jax.ShapeDtypeStruct((rows, heads * 128), BF16),
        scratch_shapes=[pltpu.VMEM((rows, CHUNK), F32), pltpu.VMEM((rows, 128), F32)],
        compiler_params=LIMIT,
        cost_estimate=pl.CostEstimate(
            flops=heads * rows * CHUNK * 128 * 8, bytes_accessed=rows * heads * 128 * 10, transcendentals=heads * rows * CHUNK
        ),
        name="finish",
    )(doc_lengths, queries, keys, values, *entering, local, gate, gain, crow)


def swap(x, groups=None):
    return lax.all_to_all(x, "seq", split_axis=0, concat_axis=0, axis_index_groups=groups, tiled=True)


def by_distance(parcels, spread):
    return [parcels[0]] + [
        lax.ppermute(parcels[x], "seq", [(s, s ^ x) for s in range(spread)]) for x in range(1, MEMBERS)
    ]


def on_device(spread, queries, keys, values, log_decay, gate, gain, doc_lengths, owner_ids):
    rows, heads = log_decay.shape
    quads = spread // MEMBERS
    hp = heads // MEMBERS
    near = [[q * MEMBERS + m for m in range(MEMBERS)] for q in range(quads)]
    onward = [(s, s + MEMBERS) for s in range(spread - MEMBERS)]
    decay_rows = log_decay.T
    barrier = lax.optimization_barrier

    side, crow, flags, spare, *last = piece_states(doc_lengths, owner_ids, decay_rows, keys, values, SIDE)
    last = by_distance(last, spread)
    gain = gain.reshape(1, -1)
    from_quad = [flags[0] == q for q in range(1, quads)]
    slots = max(doc_lengths.shape[0] - 1, SIDE + 1)

    def none(count):
        return jnp.zeros((MEMBERS, count * hp * 128, 128), BF16)

    def send_one():
        return jnp.concatenate([swap(spare, near), none(slots - SIDE - 1)], axis=1)

    def send_rest():
        return swap(piece_states(doc_lengths, owner_ids, decay_rows, keys, values, slots)[0], near)

    branches = [lambda: none(slots - SIDE), send_one, send_rest]
    rest = lax.switch(flags[1], branches)
    last, side, gain, rest, from_quad = barrier((last, side, gain, rest, from_quad))

    side = swap(side, near)
    coming = []
    for _ in range(quads - 1):
        leaving = leave_quad(doc_lengths, last, coming, rows, hp)
        coming = [lax.ppermute(leaving, "seq", onward)]
    crow_1, leaving = barrier((crow, leaving))
    local = early_attention(doc_lengths, queries, keys, values, crow_1, [], 0)
    coming, local, side = barrier((coming[0], local, side))

    entering = by_distance(enter_states(doc_lengths, last, coming, rows), spread)
    finals = final_states(doc_lengths, owner_ids, last, side, rest, coming, rows, spread)
    entering, finals = barrier((entering, finals))
    arrived = swap(finals).reshape(quads, 1, heads, 128, 128)
    mixed = finish(doc_lengths, queries, keys, values, entering, local, gate, gain, crow)
    owned = arrived[0]
    for q in range(1, quads):
        owned = jnp.where(from_quad[q - 1], arrived[q], owned)
    return mixed, owned


def solution(mesh):
    placed = (
        P(("groups", "seq"), "tp"),
        P(("groups", "seq"), "tp"),
        P(("groups", "seq"), "tp"),
        P(("groups", "seq"), "tp"),
        P(("groups", "seq"), "tp"),
        P("tp"),
        P("groups"),
        P("groups"),
    )
    return jax.shard_map(
        functools.partial(on_device, mesh.shape["seq"]),
        mesh=mesh,
        in_specs=placed,
        out_specs=(P(("groups", "seq"), "tp"), P(("groups", "seq"), "tp", None, None)),
        check_vma=False,
    )
```
